32 devices in a mesh: grp: 2 (over y), ma: 4 (over z), af: 2 (over x), pa: 2 (over core).
Axes of the slice: x: 2, y: 2, z: 4, core: 2. Of those that a mesh axis runs over, the one named last changes fastest.
Arguments:
- panels: bfloat16 [64, 512, 2048], P('grp', ('af', 'ma'), 'pa'), parts along dimension 0, may hold values from -6 to 6
- svd_basis: bfloat16 [512, 2048, 256], P(('af', 'ma'), 'pa'), may hold values from -0.125 to 0.125
- kl_basis: bfloat16 [32, 128, 512], P(('pa', 'ma'), None, 'af'), may hold values from -0.25 to 0.25
- slot_of_m: int32 [32], replicated, may hold values from 0 to 31, as said below
- svd_keep: int32 [32], replicated, may hold values from 32 to 256, as said below
- kl_keep: int32 [32], replicated, may hold values from 16 to 128, as said below
Outputs:
- klmodes: float32 [64, 128, 256], P(('grp', 'pa', 'ma'), 'af'), parts along dimension 0
The draws below stay inside these ranges and needn't reach their ends.
There are 2 independent parts, one for each index of `grp`. The reference program is written for one: setup_inputs(seed, part) draws one part's arguments, and reference() takes and returns one part's arrays. A program takes and returns all parts, laid end to end along the dimension named above; an argument that names none is the same for every part. Nothing has to cross between parts.
Inputs may be any that keep to these rules, and one draw needn't show every extreme that they name: `slot_of_m`: each slot 0 to 31 belongs to exactly one m-mode. `svd_keep`: over the m-modes of slots 4 * i to 4 * i + 3 the counts sum to at most 576, exactly 576 for some i. `kl_keep`: m-mode 0 keeps all 128; counts tend to fall with m.
All inputs are finite; a program needn't handle non-finite values.
Results may differ from the reference program's by a relative error of at most 0.0029.
Values may be sent and summed in bfloat16 or wider, within the bound.
No kernel may reach another device: no remote copies, remote signals or barrier semaphores. Data moves between devices by JAX's collectives and lax.ppermute only.
A program may use at most 128 MiB of HBM per device.

```python
import jax
import jax.numpy as jnp
from jax import lax

B = 2048
F = 512
R = 256
K = 128
M_DEV = 4
M = 32


def falling_counts(key, length, highest):
    index = jnp.arange(length, dtype=jnp.int32)
    noise = jax.random.randint(key, (length,), 0, highest // 8 + 1)
    counts = highest - index * highest // length - noise
    counts = jnp.maximum(counts, highest // 8)
    return jnp.where(index == 0, highest, counts).astype(jnp.int32)


def slot_table(key):
    return jax.random.permutation(key, M).astype(jnp.int32)


def draw_slot_of_m(key, part):
    return slot_table(key)


def draw_svd_keep(key, part):
    table = slot_table(key)
    key = jax.random.fold_in(key, 11)
    upper = 7 * R // 8
    budget = M_DEV * upper // 2
    owners = M // M_DEV
    extra = jax.random.randint(key, (owners, M_DEV), 0, upper + 1).astype(jnp.int32)
    total = jnp.sum(extra, axis=1, keepdims=True)
    scaled = jnp.where(total > budget, extra * budget // jnp.maximum(total, 1), extra)
    first = min(upper, budget)
    rest = budget - first
    others = max(M_DEV - 1, 1)
    place = jnp.arange(M_DEV, dtype=jnp.int32)
    filled = jnp.where(place == 0, first, rest // others)
    filled = jnp.where((place == M_DEV - 1) & (place > 0), rest - (M_DEV - 2) * (rest // others), filled)
    chosen = jax.random.randint(jax.random.fold_in(key, 5), (), 0, owners)
    owner_index = jnp.arange(owners, dtype=jnp.int32)
    extra = jnp.where(owner_index[:, None] == chosen, filled[None, :], scaled)
    keep_slot = (R // 8 + extra).reshape(M).astype(jnp.int32)
    return jnp.take(keep_slot, table, axis=0).astype(jnp.int32)


def draw_kl_keep(key, part):
    key = jax.random.fold_in(key, 12)
    return falling_counts(key, M, K)


def shard_levels(key, dims, pieces, low, top_value):
    factor_of, own = 1.0, jax.random.fold_in(key, 6)
    for position, shards_of in pieces:
        heights = jnp.exp(jax.random.uniform(jax.random.fold_in(own, position), (shards_of,), jnp.float32, low / len(pieces), top_value / len(pieces)))
        factor_of = factor_of * jnp.repeat(heights, dims[position] // shards_of).reshape([-1 if axis == position else 1 for axis in range(len(dims))])
    return factor_of


def normal_values(key, extent, width, limit, split=(), kind=jnp.bfloat16):
    result = jax.random.normal(key, extent, jnp.float32) * width
    if len(split) > 0:
        result = shard_levels(key, extent, split, -0.22, 0.18) * result
    return jnp.clip(result, min=-limit, max=limit).astype(kind)


def setup_inputs(seed: int = 0, part: int = 0) -> dict:
    key_list = jax.random.split(jax.random.key(seed), 7)
    part_splits = jax.random.split(jax.random.fold_in(key_list[6], part), 7)
    panels = normal_values(part_splits[0], (M, F, B), 1.0, 6.0, ((1, 8), (2, 2)))
    svd_basis = normal_values(key_list[1], (F, B, R), B ** -0.5, 0.125, ((0, 8), (1, 2)))
    kl_basis = normal_values(key_list[2], (M, K, F), F ** -0.5, 0.25, ((0, 8), (2, 2)))
    slot_of_m = draw_slot_of_m(jax.random.fold_in(key_list[6], 71), part)
    svd_keep = draw_svd_keep(jax.random.fold_in(key_list[6], 71), part)
    kl_keep = draw_kl_keep(jax.random.fold_in(key_list[6], 71), part)
    return {"panels": panels, "svd_basis": svd_basis, "kl_basis": kl_basis, "slot_of_m": slot_of_m, "svd_keep": svd_keep, "kl_keep": kl_keep}


def project_frequency(pair):
    rows_frequency, basis_frequency = pair
    return jnp.dot(rows_frequency, basis_frequency, preferred_element_type=jnp.float32)


def reference(panels, svd_basis, kl_basis, slot_of_m, svd_keep, kl_keep):
    order_slots = jnp.argsort(slot_of_m).astype(jnp.int32)
    projected = lax.map(project_frequency, (jnp.transpose(panels, (1, 0, 2)), svd_basis))
    slotted = jnp.take(jnp.transpose(projected, (1, 0, 2)), order_slots, axis=0)
    columns = jnp.arange(svd_basis.shape[2], dtype=jnp.int32)
    keep_slots = jnp.take(svd_keep, order_slots, axis=0)
    retained = jnp.where(columns[None, None, :] < keep_slots[:, None, None], slotted, jnp.zeros_like(slotted))
    retained = retained.astype(jnp.bfloat16)
    amplitudes = jnp.einsum("mkf,mfr->mkr", kl_basis.astype(jnp.float32), retained.astype(jnp.float32))
    modes = jnp.arange(kl_basis.shape[1], dtype=jnp.int32)
    modes_slots = jnp.take(kl_keep, order_slots, axis=0)
    return jnp.where(modes[None, :, None] < modes_slots[:, None, None], amplitudes, jnp.zeros_like(amplitudes))
```

```python
import functools

import jax
import jax.numpy as jnp
from jax import lax
from jax.experimental import pallas as pl
from jax.experimental.pallas import tpu as pltpu
from jax.sharding import PartitionSpec as P

LANES = 128
GROUP = 16
OWNER_BUDGET = 576
MIB = 2**20


def shards_plain(panels, svd_basis, kl_basis, slot_of_m, svd_keep, kl_keep):
    slot_count = slot_of_m.shape[0]
    order_slots = jnp.argsort(slot_of_m)
    keep_slots = jnp.take(svd_keep, order_slots, axis=0)
    modes_slots = jnp.take(kl_keep, order_slots, axis=0)
    width_modes = svd_basis.shape[2]
    owner_rows = kl_basis.shape[0]
    slot_rows = slot_count // lax.axis_size("pa")
    slot_start = lax.axis_index("pa") * slot_rows
    owner_start = slot_start + lax.axis_index("ma") * owner_rows
    modes_owner = lax.dynamic_slice_in_dim(modes_slots, owner_start, owner_rows, 0)
    chosen = jnp.take(panels, order_slots, axis=0)
    summed = lax.psum_scatter(
        jnp.einsum("mfb,fbr->mfr", chosen, svd_basis, preferred_element_type=jnp.float32),
        "pa",
        scatter_dimension=0,
        tiled=True,
    )
    keep_here = lax.dynamic_slice_in_dim(keep_slots, slot_start, slot_rows, 0)
    columns = jnp.arange(width_modes, dtype=jnp.int32)
    retained = jnp.where(columns[None, None, :] < keep_here[:, None, None], summed, 0.0).astype(
        jnp.bfloat16
    )
    relaid = lax.all_to_all(retained, "ma", split_axis=0, concat_axis=1, tiled=True)
    partial_sums = jnp.einsum("mkf,mfr->mkr", kl_basis, relaid, preferred_element_type=jnp.float32)
    modes = jnp.arange(kl_basis.shape[1], dtype=jnp.int32)
    partial_sums = jnp.where(modes[None, :, None] < modes_owner[:, None, None], partial_sums, 0.0)
    return lax.psum_scatter(partial_sums, "af", scatter_dimension=1, tiled=True)


def cyclic(value, count):
    return lax.rem(value + count, count)


def packed_place(offset, width, span):
    last = (width - span) // LANES
    tile = jnp.minimum(lax.div(offset, LANES), last)
    return pl.multiple_of(tile * LANES, LANES), offset - tile * LANES


def project_kernel(
    start, owner_slots, slot_hbm, keep_hbm, panels, basis, mine, send,
    slot_s, keep_s, place_s, panels_v, basis_v, lhs_v, out_v, small_sem, panel_sem, basis_sem,
):
    slots = panels_v.shape[0]
    freqs = panels_v.shape[1]
    per_copy = freqs // basis_sem.shape[0]
    halves, owners = lax.axis_size("pa"), lax.axis_size("ma")
    my_half, my_owner = lax.axis_index("pa"), lax.axis_index("ma")
    half_slots = slots // halves
    width, modes = mine.shape[-1], basis.shape[-1]
    span = modes + LANES

    table_copies = [
        pltpu.make_async_copy(slot_hbm, slot_s, small_sem.at[0]),
        pltpu.make_async_copy(keep_hbm, keep_s, small_sem.at[1]),
    ]
    for copy in table_copies:
        copy.start()

    def basis_copy(i):
        return pltpu.make_async_copy(
            basis.at[pl.ds(start + i * per_copy, per_copy)],
            basis_v.at[pl.ds(i * per_copy, per_copy)],
            basis_sem.at[i],
        )

    for i in range(basis_sem.shape[0]):
        basis_copy(i).start()
    for copy in table_copies:
        copy.wait()

    @pl.loop(0, slots)
    def _(m):
        slot = slot_s[m]
        half = cyclic(lax.div(slot, half_slots) - my_half, halves)
        within = lax.rem(slot, half_slots)
        owner = cyclic(lax.div(within, owner_slots) - my_owner, owners)
        place = half * half_slots + owner * owner_slots + lax.rem(within, owner_slots)
        place_s[place] = keep_s[m]
        pltpu.make_async_copy(
            panels.at[m, pl.ds(start, freqs)], panels_v.at[place], panel_sem
        ).start()

    side = GROUP * GROUP
    row = lax.broadcasted_iota(jnp.int32, (side, side), 0)
    column = lax.broadcasted_iota(jnp.int32, (side, side), 1)
    swap = (column == (row % GROUP) * GROUP + row // GROUP).astype(jnp.float32).astype(jnp.bfloat16)
    lane = lax.broadcasted_iota(jnp.int32, (GROUP, modes), 1)
    blank = jnp.zeros((GROUP, LANES), jnp.float32)

    pltpu.make_async_copy(panels_v, panels_v, panel_sem).wait()

    for group in range(freqs // GROUP):
        here = slice(group * GROUP, (group + 1) * GROUP)
        for block in range(slots // GROUP):
            blocks = slice(block * GROUP, (block + 1) * GROUP)
            tile = panels_v[blocks, here, :].reshape(side, panels_v.shape[2])
            turned = jnp.dot(swap, tile, preferred_element_type=jnp.float32).astype(jnp.bfloat16)
            lhs_v[:, blocks, :] = turned.reshape(GROUP, GROUP, panels_v.shape[2])
        copies = GROUP // per_copy

        @pl.loop(0, copies)
        def _(i):
            basis_copy(group * copies + i).wait()
            for k in range(per_copy):
                f = i * per_copy + k
                out_v[f] = jnp.dot(
                    lhs_v[f], basis_v[group * GROUP + f], preferred_element_type=jnp.float32
                )

        for half in range(halves):
            to = (mine, send)[half]
            for owner in range(owners):
                to[owner, here, :] = jnp.zeros((GROUP, width), jnp.float32)
                offset = jnp.int32(0)
                for j in range(owner_slots):
                    place = half * half_slots + owner * owner_slots + j
                    keep = place_s[place]
                    kept = jnp.where(lane < keep, out_v[:, place, :], 0.0)
                    first, shift = packed_place(offset, width, span)
                    wide = jnp.concatenate([kept, blank], axis=1)
                    to[owner, here, pl.ds(first, span)] += pltpu.roll(wide, shift, 1)
                    offset = offset + keep


def owner_tables(slot_s, keep_s, table_s, slots):
    @pl.loop(0, slots)
    def _(m):
        table_s[slot_s[m]] = keep_s[m]


def kl_kernel(
    starts, counts, mine_too, slot_hbm, keep_hbm, rows_hbm, kl, *refs
):
    blocks = refs[: len(starts) * counts]
    rest = refs[len(starts) * counts :]
    send, mine, slot_s, keep_s, rows_s, keep_t, rows_t, packed_v, small_sem = rest
    owner_slots, rows, freqs = kl.shape
    slots = slot_s.shape[0]
    owners, shares = lax.axis_size("ma"), lax.axis_size("af")
    per_source = freqs // owners
    copies = [
        pltpu.make_async_copy(slot_hbm, slot_s, small_sem.at[0]),
        pltpu.make_async_copy(keep_hbm, keep_s, small_sem.at[1]),
        pltpu.make_async_copy(rows_hbm, rows_s, small_sem.at[2]),
    ]
    for copy in copies:
        copy.start()
    me = lax.axis_index("ma")
    for c, begin in enumerate(starts):
        for step in range(owners):
            block = blocks[c * owners + step]
            source = cyclic(me - step, owners)
            at = pl.multiple_of(source * per_source + begin, GROUP)
            packed_v[pl.ds(at, block.shape[0]), :] = block[...]
    for copy in copies:
        copy.wait()

    @pl.loop(0, slots)
    def _(m):
        keep_t[slot_s[m]] = keep_s[m]
        rows_t[slot_s[m]] = rows_s[m]

    width = send.shape[1]
    share_rows = rows // shares
    my_share = lax.axis_index("af")
    first = (lax.axis_index("pa") * owners + me) * owner_slots
    lane = lax.broadcasted_iota(jnp.int32, (share_rows, width), 1)
    line = lax.broadcasted_iota(jnp.int32, (share_rows, width), 0)
    for part, out in ((1, send), (0, mine)):
        share = cyclic(my_share + part, shares)
        at = pl.multiple_of(share * share_rows, GROUP)
        total = jnp.zeros((share_rows, width), jnp.float32)
        offset = jnp.int32(0)
        for j in range(owner_slots):
            keep = keep_t[first + j]
            product = jnp.dot(
                kl[j, pl.ds(at, share_rows), :], packed_v[...], preferred_element_type=jnp.float32
            )
            within = (lane >= offset) & (lane < offset + keep) & (line < rows_t[first + j] - at)
            total = jnp.where(within, product, total)
            offset = offset + keep
        out[...] = total.astype(out.dtype)


def final_kernel(slot_hbm, keep_hbm, mine, got, out, slot_s, keep_s, keep_t, sum_v, small_sem):
    owner_slots, rows, modes = out.shape
    slots = slot_s.shape[0]
    width = mine.shape[1]
    span = modes + LANES
    copies = [
        pltpu.make_async_copy(slot_hbm, slot_s, small_sem.at[0]),
        pltpu.make_async_copy(keep_hbm, keep_s, small_sem.at[1]),
    ]
    for copy in copies:
        copy.start()
    sum_v[...] = mine[...] + got[...].astype(jnp.float32)
    for copy in copies:
        copy.wait()

    @pl.loop(0, slots)
    def _(m):
        keep_t[slot_s[m]] = keep_s[m]

    first = (lax.axis_index("pa") * lax.axis_size("ma") + lax.axis_index("ma")) * owner_slots
    lane = lax.broadcasted_iota(jnp.int32, (rows, modes), 1)
    offset = jnp.int32(0)
    for j in range(owner_slots):
        keep = keep_t[first + j]
        at, shift = packed_place(offset, width, span)
        window = pltpu.roll(sum_v[:, pl.ds(at, span)], lax.rem(span - shift, span), 1)
        out[j] = jnp.where(lane < keep, window[:, :modes], 0.0)
        offset = offset + keep


ANY = pl.BlockSpec(memory_space=pl.ANY)
VMEM = pl.BlockSpec(memory_space=pltpu.VMEM)


def project(panels, svd_basis, slot_of_m, svd_keep, start, freqs, owner_slots, width):
    slots, _, depth = panels.shape
    modes = svd_basis.shape[2]
    owners = lax.axis_size("ma")
    shape = jax.ShapeDtypeStruct((owners, freqs, width), jnp.float32)
    return pl.pallas_call(
        functools.partial(project_kernel, start, owner_slots),
        out_shape=(shape, shape),
        in_specs=[ANY] * 4,
        out_specs=(VMEM, VMEM),
        scratch_shapes=[
            pltpu.SMEM((slots,), jnp.int32),
            pltpu.SMEM((slots,), jnp.int32),
            pltpu.SMEM((slots,), jnp.int32),
            pltpu.VMEM((slots, freqs, depth), jnp.bfloat16),
            pltpu.VMEM((freqs, depth, modes), jnp.bfloat16),
            pltpu.VMEM((GROUP, slots, depth), jnp.bfloat16),
            pltpu.VMEM((GROUP, slots, modes), jnp.float32),
            pltpu.SemaphoreType.DMA((2,)),
            pltpu.SemaphoreType.DMA,
            pltpu.SemaphoreType.DMA((freqs // 4,)),
        ],
        compiler_params=pltpu.CompilerParams(vmem_limit_bytes=40 * MIB),
        cost_estimate=pl.CostEstimate(
            flops=2 * slots * freqs * depth * modes,
            bytes_accessed=2 * freqs * depth * (modes + slots),
            transcendentals=0,
        ),
        name="project",
    )(slot_of_m, svd_keep, panels, svd_basis)


def kl_project(kl_basis, slot_of_m, svd_keep, kl_keep, blocks, starts, width):
    owners, shares = lax.axis_size("ma"), lax.axis_size("af")
    slots = slot_of_m.shape[0]
    rows, freqs = kl_basis.shape[1:]
    return pl.pallas_call(
        functools.partial(kl_kernel, starts, owners, True),
        out_shape=(
            jax.ShapeDtypeStruct((rows // shares, width), jnp.bfloat16),
            jax.ShapeDtypeStruct((rows // shares, width), jnp.float32),
        ),
        in_specs=[ANY] * 3 + [VMEM] * (1 + len(blocks)),
        out_specs=(VMEM, VMEM),
        scratch_shapes=[pltpu.SMEM((slots,), jnp.int32)] * 5
        + [pltpu.VMEM((freqs, width), jnp.bfloat16), pltpu.SemaphoreType.DMA((3,))],
        cost_estimate=pl.CostEstimate(
            flops=2 * kl_basis.size * width, bytes_accessed=2 * kl_basis.size, transcendentals=0
        ),
        name="kl_project",
    )(slot_of_m, svd_keep, kl_keep, kl_basis, *blocks)


def unpack(mine, got, slot_of_m, svd_keep, owner_slots, modes):
    slots = slot_of_m.shape[0]
    rows, width = mine.shape
    return pl.pallas_call(
        final_kernel,
        out_shape=jax.ShapeDtypeStruct((owner_slots, rows, modes), jnp.float32),
        in_specs=[ANY] * 2 + [VMEM] * 2,
        out_specs=VMEM,
        scratch_shapes=[pltpu.SMEM((slots,), jnp.int32)] * 3
        + [pltpu.VMEM((rows, width), jnp.float32), pltpu.SemaphoreType.DMA((2,))],
        cost_estimate=pl.CostEstimate(
            flops=rows * width, bytes_accessed=10 * rows * width, transcendentals=0
        ),
        name="unpack",
    )(slot_of_m, svd_keep, mine, got)


def ring(axis, step):
    size = lax.axis_size(axis)
    return [(i, (i + step) % size) for i in range(size)]


def shards(panels, svd_basis, kl_basis, slot_of_m, svd_keep, kl_keep):
    freqs = svd_basis.shape[0]
    owner_slots, modes = kl_basis.shape[0], svd_basis.shape[2]
    owners = lax.axis_size("ma")
    width = -(-min(OWNER_BUDGET, owner_slots * modes) // LANES) * LANES
    chunk = GROUP
    starts = tuple(range(0, freqs, chunk))
    blocks = []
    for start in starts:
        mine, send = project(
            panels, svd_basis, slot_of_m, svd_keep, start, chunk, owner_slots, width
        )
        got = lax.ppermute(send, "pa", ring("pa", 1))
        summed = [(mine[step] + got[step]).astype(jnp.bfloat16) for step in range(owners)]
        blocks += [summed[0]] + [
            lax.ppermute(summed[step], "ma", ring("ma", step)) for step in range(1, owners)
        ]
    send, mine = kl_project(kl_basis, slot_of_m, svd_keep, kl_keep, blocks, starts, width)
    got = lax.ppermute(send, "af", ring("af", 1))
    return unpack(mine, got, slot_of_m, svd_keep, owner_slots, modes)


def kernels_fit(mesh, args):
    panels, svd_basis, kl_basis = args[:3]
    slots = panels.shape[0] // mesh.shape["grp"]
    freqs = svd_basis.shape[0] // (mesh.shape["af"] * mesh.shape["ma"])
    owner_slots = kl_basis.shape[0] // (mesh.shape["pa"] * mesh.shape["ma"])
    share_rows = kl_basis.shape[1] // mesh.shape["af"]
    return (
        freqs % GROUP == 0
        and slots % (GROUP * mesh.shape["pa"]) == 0
        and owner_slots == 4
        and svd_basis.shape[2] == 2 * LANES
        and share_rows % GROUP == 0
        and mesh.shape["pa"] == 2
        and mesh.shape["af"] == 2
        and mesh.shape["ma"] <= 4
    )


def solution(mesh):
    in_specs = (
        P("grp", ("af", "ma"), "pa"),
        P(("af", "ma"), "pa", None),
        P(("pa", "ma"), None, "af"),
        P(),
        P(),
        P(),
    )
    out_specs = P(("grp", "pa", "ma"), "af", None)

    def run(*args):
        body = shards if kernels_fit(mesh, args) else shards_plain
        mapped = jax.shard_map(
            body, mesh=mesh, in_specs=in_specs, out_specs=out_specs, check_vma=False
        )
        return mapped(*args)

    return run
```

```python
import functools

import jax
import jax.numpy as jnp
from jax import lax
from jax.experimental import pallas as pl
from jax.experimental.pallas import tpu as pltpu
from jax.sharding import PartitionSpec as P

LANES = 128
GROUP = 16
OWNER_BUDGET = 576
MIB = 2**20


def shards_plain(panels, svd_basis, kl_basis, slot_of_m, svd_keep, kl_keep):
    slot_count = slot_of_m.shape[0]
    order_slots = jnp.argsort(slot_of_m)
    keep_slots = jnp.take(svd_keep, order_slots, axis=0)
    modes_slots = jnp.take(kl_keep, order_slots, axis=0)
    width_modes = svd_basis.shape[2]
    owner_rows = kl_basis.shape[0]
    slot_rows = slot_count // lax.axis_size("pa")
    slot_start = lax.axis_index("pa") * slot_rows
    owner_start = slot_start + lax.axis_index("ma") * owner_rows
    modes_owner = lax.dynamic_slice_in_dim(modes_slots, owner_start, owner_rows, 0)
    chosen = jnp.take(panels, order_slots, axis=0)
    summed = lax.psum_scatter(
        jnp.einsum("mfb,fbr->mfr", chosen, svd_basis, preferred_element_type=jnp.float32),
        "pa",
        scatter_dimension=0,
        tiled=True,
    )
    keep_here = lax.dynamic_slice_in_dim(keep_slots, slot_start, slot_rows, 0)
    columns = jnp.arange(width_modes, dtype=jnp.int32)
    retained = jnp.where(columns[None, None, :] < keep_here[:, None, None], summed, 0.0).astype(
        jnp.bfloat16
    )
    relaid = lax.all_to_all(retained, "ma", split_axis=0, concat_axis=1, tiled=True)
    partial_sums = jnp.einsum("mkf,mfr->mkr", kl_basis, relaid, preferred_element_type=jnp.float32)
    modes = jnp.arange(kl_basis.shape[1], dtype=jnp.int32)
    partial_sums = jnp.where(modes[None, :, None] < modes_owner[:, None, None], partial_sums, 0.0)
    return lax.psum_scatter(partial_sums, "af", scatter_dimension=1, tiled=True)


def cyclic(value, count):
    return lax.rem(value + count, count)


def shifted(tiles, shift, lane):
    low, high = (pltpu.roll(tile, shift, 1) for tile in tiles)
    left = lane < shift
    return jnp.where(left, 0.0, low), jnp.where(left, low, high), jnp.where(left, high, 0.0)


def project_kernel(
    owner_slots, slot_hbm, keep_hbm, rows_hbm, panels, basis,
    mine, send, slot_column, rows_column, scalars,
    slot_s, keep_s, rows_s, keep_place, rows_place,
    panels_v, basis_v, lhs_v, out_v, pack_v, small_sem, panel_sem, basis_sem,
):
    slots, freqs, depth = panels_v.shape
    groups = freqs // GROUP
    copies = basis_sem.shape[0] // groups
    per_copy = GROUP // copies
    halves, owners = lax.axis_size("pa"), lax.axis_size("ma")
    my_half, my_owner = lax.axis_index("pa"), lax.axis_index("ma")
    half_slots = slots // halves
    width, modes = mine.shape[-1], basis.shape[-1]

    table_copies = [
        pltpu.make_async_copy(slot_hbm, slot_s, small_sem.at[0]),
        pltpu.make_async_copy(keep_hbm, keep_s, small_sem.at[1]),
        pltpu.make_async_copy(rows_hbm, rows_s, small_sem.at[2]),
    ]
    for copy in table_copies:
        copy.start()

    def basis_copy(i):
        part = pl.ds(i * per_copy, per_copy)
        return pltpu.make_async_copy(basis.at[part], basis_v.at[part], basis_sem.at[i])

    ahead = 2
    for i in range(ahead):
        basis_copy(i).start()
    for copy in table_copies:
        copy.wait()

    for group in range(groups):
        part = pl.ds(group * GROUP, GROUP)

        @pl.loop(0, slots)
        def _(m):
            slot = slot_s[m]
            half = cyclic(lax.div(slot, half_slots) - my_half, halves)
            within = lax.rem(slot, half_slots)
            owner = cyclic(lax.div(within, owner_slots) - my_owner, owners)
            place = half * half_slots + owner * owner_slots + lax.rem(within, owner_slots)
            if group == 0:
                keep_place[place] = keep_s[m]
                rows_place[place] = rows_s[m]
            pltpu.make_async_copy(
                panels.at[m, part], panels_v.at[place, part], panel_sem.at[group]
            ).start()

        for i in range(ahead + group * copies, min(ahead + (group + 1) * copies, groups * copies)):
            basis_copy(i).start()

    column = lax.broadcasted_iota(jnp.int32, slot_column.shape, 1)
    slot_at = jnp.full(slot_column.shape, owner_slots, jnp.int32)
    rows_at = jnp.zeros(slot_column.shape, jnp.int32)
    offset = jnp.int32(0)
    for j in range(owner_slots):
        keep = keep_place[j]
        within = (column >= offset) & (column < offset + keep)
        slot_at = jnp.where(within, j, slot_at)
        rows_at = jnp.where(within, rows_place[j], rows_at)
        scalars[j : j + 1, :] = jnp.full((1, LANES), offset, jnp.int32)
        scalars[owner_slots + j : owner_slots + j + 1, :] = jnp.full((1, LANES), keep, jnp.int32)
        offset = offset + keep
    slot_column[...] = slot_at
    rows_column[...] = rows_at

    side = GROUP * GROUP
    row = lax.broadcasted_iota(jnp.int32, (side, side), 0)
    column = lax.broadcasted_iota(jnp.int32, (side, side), 1)
    swap = (column == (row % GROUP) * GROUP + row // GROUP).astype(jnp.float32).astype(jnp.bfloat16)
    lane = lax.broadcasted_iota(jnp.int32, (GROUP, LANES), 1)

    @pl.loop(0, groups)
    def _(group):
        here = pl.ds(pl.multiple_of(group * GROUP, GROUP), GROUP)
        pltpu.make_async_copy(
            panels_v.at[:, here], panels_v.at[:, here], panel_sem.at[group]
        ).wait()
        for block in range(slots // GROUP):
            blocks = slice(block * GROUP, (block + 1) * GROUP)
            tile = panels_v[blocks, here, :].reshape(side, depth)
            turned = jnp.dot(swap, tile, preferred_element_type=jnp.float32).astype(jnp.bfloat16)
            lhs_v[:, blocks, :] = turned.reshape(GROUP, GROUP, depth)

        @pl.loop(0, copies)
        def _(i):
            basis_copy(group * copies + i).wait()
            for k in range(per_copy):
                f = i * per_copy + k
                out_v[f] = jnp.dot(
                    lhs_v[f], basis_v[group * GROUP + f], preferred_element_type=jnp.float32
                )

        pack_v[...] = jnp.zeros(pack_v.shape, jnp.float32)
        for half in range(halves):
            to = (mine, send)[half]
            for owner in range(owners):
                offset = jnp.int32(0)
                at = half * owners + owner
                for j in range(owner_slots):
                    place = at * owner_slots + j
                    keep = keep_place[place]
                    tiles = [
                        jnp.where(
                            lane < keep - t * LANES,
                            out_v[:, place, t * LANES : (t + 1) * LANES],
                            0.0,
                        )
                        for t in range(modes // LANES)
                    ]
                    tile = lax.div(offset, LANES)
                    moved = shifted(tiles, offset - tile * LANES, lane)
                    for t, value in enumerate(moved):
                        lanes = pl.ds(pl.multiple_of((tile + t) * LANES, LANES), LANES)
                        pack_v[at, :, lanes] += value
                    offset = offset + keep
                to[owner, here, :] = pack_v[at, :, :width]


def kl_kernel(part, owners, slot_column, rows_column, kl, *refs):
    blocks, (out, packed_v) = refs[:owners], refs[owners:]
    owner_slots, rows, freqs = kl.shape
    shares = lax.axis_size("af")
    per_source = freqs // owners
    me = lax.axis_index("ma")
    for step in range(owners):
        source = cyclic(me - step, owners)
        at = pl.multiple_of(source * per_source, GROUP)
        packed_v[pl.ds(at, per_source), :] = blocks[step][...]
    share_rows, width = out.shape
    at = pl.multiple_of(cyclic(lax.axis_index("af") + part, shares) * share_rows, GROUP)
    lhs = kl[:, pl.ds(at, share_rows), :].reshape(owner_slots * share_rows, freqs)
    product = jnp.dot(lhs, packed_v[...], preferred_element_type=jnp.float32)
    line = lax.broadcasted_iota(jnp.int32, (share_rows, width), 0) + at
    slot_at = slot_column[0:1, :]
    total = jnp.zeros((share_rows, width), jnp.float32)
    for j in range(owner_slots):
        here = product[j * share_rows : (j + 1) * share_rows]
        total = jnp.where(slot_at == j, here, total)
    out[...] = jnp.where(line < rows_column[0:1, :], total, 0.0).astype(out.dtype)


def unpack_kernel(scalars, mine, got, out, sum_v):
    owner_slots, rows, modes = out.shape
    width = mine.shape[1]
    sum_v[:, :width] = mine[...] + got[...].astype(jnp.float32)
    lane = lax.broadcasted_iota(jnp.int32, (rows, LANES), 1)
    for j in range(owner_slots):
        offset = jnp.max(scalars[j : j + 1, :])
        keep = jnp.max(scalars[owner_slots + j : owner_slots + j + 1, :])
        tile = lax.div(offset, LANES)
        shift = offset - tile * LANES
        back = lax.rem(LANES - shift, LANES)
        turned = [
            pltpu.roll(
                sum_v[:, pl.ds(pl.multiple_of((tile + t) * LANES, LANES), LANES)], back, 1
            )
            for t in range(modes // LANES + 1)
        ]
        for t in range(modes // LANES):
            value = jnp.where(lane < LANES - shift, turned[t], turned[t + 1])
            value = jnp.where(lane < keep - t * LANES, value, 0.0)
            out[j, :, t * LANES : (t + 1) * LANES] = value


HBM = pl.BlockSpec(memory_space=pltpu.HBM)
VMEM = pl.BlockSpec(memory_space=pltpu.VMEM)


def in_hbm(operand):
    return pltpu.with_memory_space_constraint(operand, pltpu.HBM)


def project(panels, svd_basis, slot_of_m, svd_keep, kl_keep, owner_slots, width):
    slots, freqs, depth = panels.shape
    modes = svd_basis.shape[2]
    owners, halves = lax.axis_size("ma"), lax.axis_size("pa")
    packed = jax.ShapeDtypeStruct((owners, freqs, width), jnp.float32)
    column = jax.ShapeDtypeStruct((8, width), jnp.int32)
    table = pltpu.SMEM((slots,), jnp.int32)
    wide = width + modes + LANES
    return pl.pallas_call(
        functools.partial(project_kernel, owner_slots),
        out_shape=(packed, packed, column, column, jax.ShapeDtypeStruct((8, LANES), jnp.int32)),
        in_specs=[HBM] * 5,
        out_specs=(VMEM,) * 5,
        scratch_shapes=[table] * 5
        + [
            pltpu.VMEM((slots, freqs, depth), jnp.bfloat16),
            pltpu.VMEM((freqs, depth, modes), jnp.bfloat16),
            pltpu.VMEM((GROUP, slots, depth), jnp.bfloat16),
            pltpu.VMEM((GROUP, slots, modes), jnp.float32),
            pltpu.VMEM((halves * owners, GROUP, wide), jnp.float32),
            pltpu.SemaphoreType.DMA((3,)),
            pltpu.SemaphoreType.DMA((freqs // GROUP,)),
            pltpu.SemaphoreType.DMA((freqs // 4,)),
        ],
        compiler_params=pltpu.CompilerParams(vmem_limit_bytes=48 * MIB),
        cost_estimate=pl.CostEstimate(
            flops=2 * slots * freqs * depth * modes,
            bytes_accessed=2 * freqs * depth * (modes + slots),
            transcendentals=0,
        ),
        name="project",
    )(*map(in_hbm, (slot_of_m, svd_keep, kl_keep, panels, svd_basis)))


def kl_project(part, kind, slot_column, rows_column, kl_basis, blocks):
    owners, shares = lax.axis_size("ma"), lax.axis_size("af")
    rows, freqs = kl_basis.shape[1:]
    width = slot_column.shape[1]
    return pl.pallas_call(
        functools.partial(kl_kernel, part, owners),
        out_shape=jax.ShapeDtypeStruct((rows // shares, width), kind),
        in_specs=[VMEM] * (3 + owners),
        out_specs=VMEM,
        scratch_shapes=[pltpu.VMEM((freqs, width), jnp.bfloat16)],
        cost_estimate=pl.CostEstimate(
            flops=2 * kl_basis.size * width // shares,
            bytes_accessed=2 * kl_basis.size,
            transcendentals=0,
        ),
        name="kl_project",
    )(slot_column, rows_column, kl_basis, *blocks)


def unpack(scalars, mine, got, owner_slots, modes):
    rows, width = mine.shape
    return pl.pallas_call(
        unpack_kernel,
        out_shape=jax.ShapeDtypeStruct((owner_slots, rows, modes), jnp.float32),
        in_specs=[VMEM] * 3,
        out_specs=VMEM,
        scratch_shapes=[pltpu.VMEM((rows, width + modes + LANES), jnp.float32)],
        cost_estimate=pl.CostEstimate(
            flops=rows * width, bytes_accessed=10 * rows * width, transcendentals=0
        ),
        name="unpack",
    )(scalars, mine, got)


def ring(axis, step):
    size = lax.axis_size(axis)
    return [(i, (i + step) % size) for i in range(size)]


def shards(panels, svd_basis, kl_basis, slot_of_m, svd_keep, kl_keep):
    owner_slots, modes = kl_basis.shape[0], svd_basis.shape[2]
    owners = lax.axis_size("ma")
    width = -(-min(OWNER_BUDGET, owner_slots * modes) // LANES) * LANES
    mine, send, slot_column, rows_column, scalars = project(
        panels, svd_basis, slot_of_m, svd_keep, kl_keep, owner_slots, width
    )
    got = lax.ppermute(send, "pa", ring("pa", 1))
    summed = [(mine[step] + got[step]).astype(jnp.bfloat16) for step in range(owners)]
    blocks = [summed[0]] + [
        lax.ppermute(summed[step], "ma", ring("ma", step)) for step in range(1, owners)
    ]
    send = kl_project(1, jnp.bfloat16, slot_column, rows_column, kl_basis, blocks)
    got = lax.ppermute(send, "af", ring("af", 1))
    mine = kl_project(0, jnp.float32, slot_column, rows_column, kl_basis, blocks)
    return unpack(scalars, mine, got, owner_slots, modes)


def kernels_fit(mesh, args):
    panels, svd_basis, kl_basis = args[:3]
    slots = panels.shape[0] // mesh.shape["grp"]
    freqs = svd_basis.shape[0] // (mesh.shape["af"] * mesh.shape["ma"])
    owner_slots = kl_basis.shape[0] // (mesh.shape["pa"] * mesh.shape["ma"])
    share_rows = kl_basis.shape[1] // mesh.shape["af"]
    return (
        freqs % GROUP == 0
        and slots % (GROUP * mesh.shape["pa"]) == 0
        and owner_slots == 4
        and svd_basis.shape[2] == 2 * LANES
        and share_rows % GROUP == 0
        and mesh.shape["pa"] == 2
        and mesh.shape["af"] == 2
        and mesh.shape["ma"] <= 4
    )


def solution(mesh):
    in_specs = (
        P("grp", ("af", "ma"), "pa"),
        P(("af", "ma"), "pa", None),
        P(("pa", "ma"), None, "af"),
        P(),
        P(),
        P(),
    )
    out_specs = P(("grp", "pa", "ma"), "af", None)

    def run(*args):
        body = shards if kernels_fit(mesh, args) else shards_plain
        mapped = jax.shard_map(
            body, mesh=mesh, in_specs=in_specs, out_specs=out_specs, check_vma=False
        )
        return mapped(*args)

    return run
```

```python
import functools

import jax
import jax.numpy as jnp
from jax import lax
from jax.experimental import pallas as pl
from jax.experimental.pallas import tpu as pltpu
from jax.sharding import PartitionSpec as P

LANES = 128
GROUP = 16
OWNER_BUDGET = 576
MIB = 2**20


def shards_plain(panels, svd_basis, kl_basis, slot_of_m, svd_keep, kl_keep):
    slot_count = slot_of_m.shape[0]
    order_slots = jnp.argsort(slot_of_m)
    keep_slots = jnp.take(svd_keep, order_slots, axis=0)
    modes_slots = jnp.take(kl_keep, order_slots, axis=0)
    width_modes = svd_basis.shape[2]
    owner_rows = kl_basis.shape[0]
    slot_rows = slot_count // lax.axis_size("pa")
    slot_start = lax.axis_index("pa") * slot_rows
    owner_start = slot_start + lax.axis_index("ma") * owner_rows
    modes_owner = lax.dynamic_slice_in_dim(modes_slots, owner_start, owner_rows, 0)
    chosen = jnp.take(panels, order_slots, axis=0)
    summed = lax.psum_scatter(
        jnp.einsum("mfb,fbr->mfr", chosen, svd_basis, preferred_element_type=jnp.float32),
        "pa",
        scatter_dimension=0,
        tiled=True,
    )
    keep_here = lax.dynamic_slice_in_dim(keep_slots, slot_start, slot_rows, 0)
    columns = jnp.arange(width_modes, dtype=jnp.int32)
    retained = jnp.where(columns[None, None, :] < keep_here[:, None, None], summed, 0.0).astype(
        jnp.bfloat16
    )
    relaid = lax.all_to_all(retained, "ma", split_axis=0, concat_axis=1, tiled=True)
    partial_sums = jnp.einsum("mkf,mfr->mkr", kl_basis, relaid, preferred_element_type=jnp.float32)
    modes = jnp.arange(kl_basis.shape[1], dtype=jnp.int32)
    partial_sums = jnp.where(modes[None, :, None] < modes_owner[:, None, None], partial_sums, 0.0)
    return lax.psum_scatter(partial_sums, "af", scatter_dimension=1, tiled=True)


def cyclic(value, count):
    return lax.rem(value + count, count)


def shifted(tiles, shift, lane):
    low, high = (pltpu.roll(tile, shift, 1) for tile in tiles)
    left = lane < shift
    return jnp.where(left, 0.0, low), jnp.where(left, low, high), jnp.where(left, high, 0.0)


def project_kernel(
    owner_slots, slot_hbm, keep_hbm, rows_hbm, panels, basis,
    mine, send, slot_column, rows_column, scalars,
    slot_s, keep_s, rows_s, keep_place, rows_place,
    panels_v, basis_v, lhs_v, out_v, pack_v, small_sem, panel_sem, basis_sem,
):
    slots, freqs, depth = panels_v.shape
    groups = freqs // GROUP
    copies = basis_sem.shape[0] // groups
    per_copy = GROUP // copies
    halves, owners = lax.axis_size("pa"), lax.axis_size("ma")
    my_half, my_owner = lax.axis_index("pa"), lax.axis_index("ma")
    half_slots = slots // halves
    width, modes = mine.shape[-1], basis.shape[-1]

    table_copies = [
        pltpu.make_async_copy(slot_hbm, slot_s, small_sem.at[0]),
        pltpu.make_async_copy(keep_hbm, keep_s, small_sem.at[1]),
        pltpu.make_async_copy(rows_hbm, rows_s, small_sem.at[2]),
    ]
    for copy in table_copies:
        copy.start()

    def basis_copy(i):
        part = pl.ds(i * per_copy, per_copy)
        return pltpu.make_async_copy(basis.at[part], basis_v.at[part], basis_sem.at[i])

    ahead = 2
    for i in range(ahead):
        basis_copy(i).start()
    for copy in table_copies:
        copy.wait()

    for group in range(groups):
        part = pl.ds(group * GROUP, GROUP)

        @pl.loop(0, slots)
        def _(m):
            slot = slot_s[m]
            half = cyclic(lax.div(slot, half_slots) - my_half, halves)
            within = lax.rem(slot, half_slots)
            owner = lax.div(within, owner_slots) ^ my_owner
            place = half * half_slots + owner * owner_slots + lax.rem(within, owner_slots)
            if group == 0:
                keep_place[place] = keep_s[m]
                rows_place[place] = rows_s[m]
            pltpu.make_async_copy(
                panels.at[m, part], panels_v.at[place, part], panel_sem.at[group]
            ).start()

        for i in range(ahead + group * copies, min(ahead + (group + 1) * copies, groups * copies)):
            basis_copy(i).start()

    column = lax.broadcasted_iota(jnp.int32, slot_column.shape, 1)
    slot_at = jnp.full(slot_column.shape, owner_slots, jnp.int32)
    rows_at = jnp.zeros(slot_column.shape, jnp.int32)
    offset = jnp.int32(0)
    for j in range(owner_slots):
        keep = keep_place[j]
        within = (column >= offset) & (column < offset + keep)
        slot_at = jnp.where(within, j, slot_at)
        rows_at = jnp.where(within, rows_place[j], rows_at)
        scalars[j : j + 1, :] = jnp.full((1, LANES), offset, jnp.int32)
        scalars[owner_slots + j : owner_slots + j + 1, :] = jnp.full((1, LANES), keep, jnp.int32)
        offset = offset + keep
    slot_column[...] = slot_at
    rows_column[...] = rows_at

    side = GROUP * GROUP
    row = lax.broadcasted_iota(jnp.int32, (side, side), 0)
    column = lax.broadcasted_iota(jnp.int32, (side, side), 1)
    swap = (column == (row % GROUP) * GROUP + row // GROUP).astype(jnp.float32).astype(jnp.bfloat16)
    lane = lax.broadcasted_iota(jnp.int32, (GROUP, LANES), 1)

    @pl.loop(0, groups)
    def _(group):
        here = pl.ds(pl.multiple_of(group * GROUP, GROUP), GROUP)
        pltpu.make_async_copy(
            panels_v.at[:, here], panels_v.at[:, here], panel_sem.at[group]
        ).wait()
        for block in range(slots // GROUP):
            blocks = slice(block * GROUP, (block + 1) * GROUP)
            tile = panels_v[blocks, here, :].reshape(side, depth)
            turned = jnp.dot(swap, tile, preferred_element_type=jnp.float32).astype(jnp.bfloat16)
            lhs_v[:, blocks, :] = turned.reshape(GROUP, GROUP, depth)

        @pl.loop(0, copies)
        def _(i):
            basis_copy(group * copies + i).wait()
            for k in range(per_copy):
                f = i * per_copy + k
                out_v[f] = jnp.dot(
                    lhs_v[f], basis_v[group * GROUP + f], preferred_element_type=jnp.float32
                )

        pack_v[...] = jnp.zeros(pack_v.shape, jnp.float32)
        for half in range(halves):
            to = (mine, send)[half]
            for owner in range(owners):
                offset = jnp.int32(0)
                at = half * owners + owner
                for j in range(owner_slots):
                    place = at * owner_slots + j
                    keep = keep_place[place]
                    tiles = [
                        jnp.where(
                            lane < keep - t * LANES,
                            out_v[:, place, t * LANES : (t + 1) * LANES],
                            0.0,
                        )
                        for t in range(modes // LANES)
                    ]
                    tile = lax.div(offset, LANES)
                    moved = shifted(tiles, offset - tile * LANES, lane)
                    for t, value in enumerate(moved):
                        lanes = pl.ds(pl.multiple_of((tile + t) * LANES, LANES), LANES)
                        pack_v[at, :, lanes] += value
                    offset = offset + keep
                to[owner, here, :] = pack_v[at, :, :width]


def kl_kernel(part, owners, slot_column, rows_column, kl, *refs):
    blocks, (out, packed_v) = refs[:owners], refs[owners:]
    owner_slots, rows, freqs = kl.shape
    shares = lax.axis_size("af")
    per_source = freqs // owners
    me = lax.axis_index("ma")
    for step in range(owners):
        source = me ^ step
        at = pl.multiple_of(source * per_source, GROUP)
        packed_v[pl.ds(at, per_source), :] = blocks[step][...]
    share_rows, width = out.shape
    at = pl.multiple_of(cyclic(lax.axis_index("af") + part, shares) * share_rows, GROUP)
    lhs = kl[:, pl.ds(at, share_rows), :].reshape(owner_slots * share_rows, freqs)
    product = jnp.dot(lhs, packed_v[...], preferred_element_type=jnp.float32)
    line = lax.broadcasted_iota(jnp.int32, (share_rows, width), 0) + at
    slot_at = slot_column[0:1, :]
    total = jnp.zeros((share_rows, width), jnp.float32)
    for j in range(owner_slots):
        here = product[j * share_rows : (j + 1) * share_rows]
        total = jnp.where(slot_at == j, here, total)
    out[...] = jnp.where(line < rows_column[0:1, :], total, 0.0).astype(out.dtype)


def unpack_kernel(scalars, mine, got, out, sum_v):
    owner_slots, rows, modes = out.shape
    width = mine.shape[1]
    sum_v[:, :width] = mine[...] + got[...].astype(jnp.float32)
    lane = lax.broadcasted_iota(jnp.int32, (rows, LANES), 1)
    for j in range(owner_slots):
        offset = jnp.max(scalars[j : j + 1, :])
        keep = jnp.max(scalars[owner_slots + j : owner_slots + j + 1, :])
        tile = lax.div(offset, LANES)
        shift = offset - tile * LANES
        back = lax.rem(LANES - shift, LANES)
        turned = [
            pltpu.roll(
                sum_v[:, pl.ds(pl.multiple_of((tile + t) * LANES, LANES), LANES)], back, 1
            )
            for t in range(modes // LANES + 1)
        ]
        for t in range(modes // LANES):
            value = jnp.where(lane < LANES - shift, turned[t], turned[t + 1])
            value = jnp.where(lane < keep - t * LANES, value, 0.0)
            out[j, :, t * LANES : (t + 1) * LANES] = value


HBM = pl.BlockSpec(memory_space=pltpu.HBM)
VMEM = pl.BlockSpec(memory_space=pltpu.VMEM)
SMALL = pltpu.CompilerParams(vmem_limit_bytes=8 * MIB)


def in_hbm(operand):
    return pltpu.with_memory_space_constraint(operand, pltpu.HBM)


def project(panels, svd_basis, slot_of_m, svd_keep, kl_keep, owner_slots, width):
    slots, freqs, depth = panels.shape
    modes = svd_basis.shape[2]
    owners, halves = lax.axis_size("ma"), lax.axis_size("pa")
    packed = jax.ShapeDtypeStruct((owners, freqs, width), jnp.float32)
    column = jax.ShapeDtypeStruct((8, width), jnp.int32)
    table = pltpu.SMEM((slots,), jnp.int32)
    wide = width + modes + LANES
    return pl.pallas_call(
        functools.partial(project_kernel, owner_slots),
        out_shape=(packed, packed, column, column, jax.ShapeDtypeStruct((8, LANES), jnp.int32)),
        in_specs=[HBM] * 5,
        out_specs=(VMEM,) * 5,
        scratch_shapes=[table] * 5
        + [
            pltpu.VMEM((slots, freqs, depth), jnp.bfloat16),
            pltpu.VMEM((freqs, depth, modes), jnp.bfloat16),
            pltpu.VMEM((GROUP, slots, depth), jnp.bfloat16),
            pltpu.VMEM((GROUP, slots, modes), jnp.float32),
            pltpu.VMEM((halves * owners, GROUP, wide), jnp.float32),
            pltpu.SemaphoreType.DMA((3,)),
            pltpu.SemaphoreType.DMA((freqs // GROUP,)),
            pltpu.SemaphoreType.DMA((freqs // 4,)),
        ],
        compiler_params=pltpu.CompilerParams(vmem_limit_bytes=48 * MIB),
        cost_estimate=pl.CostEstimate(
            flops=2 * slots * freqs * depth * modes,
            bytes_accessed=2 * freqs * depth * (modes + slots),
            transcendentals=0,
        ),
        name="project",
    )(*map(in_hbm, (slot_of_m, svd_keep, kl_keep, panels, svd_basis)))


def kl_project(part, kind, slot_column, rows_column, kl_basis, blocks):
    owners, shares = lax.axis_size("ma"), lax.axis_size("af")
    rows, freqs = kl_basis.shape[1:]
    width = slot_column.shape[1]
    return pl.pallas_call(
        functools.partial(kl_kernel, part, owners),
        out_shape=jax.ShapeDtypeStruct((rows // shares, width), kind),
        in_specs=[VMEM] * (3 + owners),
        out_specs=VMEM,
        scratch_shapes=[pltpu.VMEM((freqs, width), jnp.bfloat16)],
        compiler_params=SMALL,
        cost_estimate=pl.CostEstimate(
            flops=2 * kl_basis.size * width // shares,
            bytes_accessed=2 * kl_basis.size,
            transcendentals=0,
        ),
        name="kl_project",
    )(slot_column, rows_column, kl_basis, *blocks)


def unpack(scalars, mine, got, owner_slots, modes):
    rows, width = mine.shape
    return pl.pallas_call(
        unpack_kernel,
        out_shape=jax.ShapeDtypeStruct((owner_slots, rows, modes), jnp.float32),
        in_specs=[VMEM] * 3,
        out_specs=VMEM,
        scratch_shapes=[pltpu.VMEM((rows, width + modes + LANES), jnp.float32)],
        compiler_params=SMALL,
        cost_estimate=pl.CostEstimate(
            flops=rows * width, bytes_accessed=10 * rows * width, transcendentals=0
        ),
        name="unpack",
    )(scalars, mine, got)


def pairs(axis, step):
    return [(i, i ^ step) for i in range(lax.axis_size(axis))]


def shards(panels, svd_basis, kl_basis, slot_of_m, svd_keep, kl_keep):
    owner_slots, modes = kl_basis.shape[0], svd_basis.shape[2]
    owners = lax.axis_size("ma")
    width = -(-min(OWNER_BUDGET, owner_slots * modes) // LANES) * LANES
    mine, send, slot_column, rows_column, scalars = project(
        panels, svd_basis, slot_of_m, svd_keep, kl_keep, owner_slots, width
    )
    got = lax.ppermute(send, "pa", pairs("pa", 1))
    summed = [(mine[step] + got[step]).astype(jnp.bfloat16) for step in range(owners)]
    blocks = [summed[0]] + [
        lax.ppermute(summed[step], "ma", pairs("ma", step)) for step in range(1, owners)
    ]
    send = kl_project(1, jnp.bfloat16, slot_column, rows_column, kl_basis, blocks)
    got = lax.ppermute(send, "af", pairs("af", 1))
    mine = kl_project(0, jnp.float32, slot_column, rows_column, kl_basis, blocks)
    return unpack(scalars, mine, got, owner_slots, modes)


def kernels_fit(mesh, args):
    panels, svd_basis, kl_basis = args[:3]
    slots = panels.shape[0] // mesh.shape["grp"]
    freqs = svd_basis.shape[0] // (mesh.shape["af"] * mesh.shape["ma"])
    owner_slots = kl_basis.shape[0] // (mesh.shape["pa"] * mesh.shape["ma"])
    share_rows = kl_basis.shape[1] // mesh.shape["af"]
    return (
        freqs % GROUP == 0
        and slots % (GROUP * mesh.shape["pa"]) == 0
        and owner_slots == 4
        and svd_basis.shape[2] == 2 * LANES
        and share_rows % GROUP == 0
        and mesh.shape["pa"] == 2
        and mesh.shape["af"] == 2
        and mesh.shape["ma"] in (2, 4)
    )


def solution(mesh):
    in_specs = (
        P("grp", ("af", "ma"), "pa"),
        P(("af", "ma"), "pa", None),
        P(("pa", "ma"), None, "af"),
        P(),
        P(),
        P(),
    )
    out_specs = P(("grp", "pa", "ma"), "af", None)

    def run(*args):
        body = shards if kernels_fit(mesh, args) else shards_plain
        mapped = jax.shard_map(
            body, mesh=mesh, in_specs=in_specs, out_specs=out_specs, check_vma=False
        )
        return mapped(*args)

    return run
```

```python
import functools

import jax
import jax.numpy as jnp
from jax import lax
from jax.experimental import pallas as pl
from jax.experimental.pallas import tpu as pltpu
from jax.sharding import PartitionSpec as P

LANES = 128
GROUP = 16
PACKED = 8
PER_COPY = 2
LATER = 16
EARLY = 8
OWNER_BUDGET = 576
MIB = 2**20


def shards_plain(panels, svd_basis, kl_basis, slot_of_m, svd_keep, kl_keep):
    slot_count = slot_of_m.shape[0]
    order_slots = jnp.argsort(slot_of_m)
    keep_slots = jnp.take(svd_keep, order_slots, axis=0)
    modes_slots = jnp.take(kl_keep, order_slots, axis=0)
    width_modes = svd_basis.shape[2]
    owner_rows = kl_basis.shape[0]
    slot_rows = slot_count // lax.axis_size("pa")
    slot_start = lax.axis_index("pa") * slot_rows
    owner_start = slot_start + lax.axis_index("ma") * owner_rows
    modes_owner = lax.dynamic_slice_in_dim(modes_slots, owner_start, owner_rows, 0)
    chosen = jnp.take(panels, order_slots, axis=0)
    summed = lax.psum_scatter(
        jnp.einsum("mfb,fbr->mfr", chosen, svd_basis, preferred_element_type=jnp.float32),
        "pa",
        scatter_dimension=0,
        tiled=True,
    )
    keep_here = lax.dynamic_slice_in_dim(keep_slots, slot_start, slot_rows, 0)
    columns = jnp.arange(width_modes, dtype=jnp.int32)
    retained = jnp.where(columns[None, None, :] < keep_here[:, None, None], summed, 0.0).astype(
        jnp.bfloat16
    )
    relaid = lax.all_to_all(retained, "ma", split_axis=0, concat_axis=1, tiled=True)
    partial_sums = jnp.einsum("mkf,mfr->mkr", kl_basis, relaid, preferred_element_type=jnp.float32)
    modes = jnp.arange(kl_basis.shape[1], dtype=jnp.int32)
    partial_sums = jnp.where(modes[None, :, None] < modes_owner[:, None, None], partial_sums, 0.0)
    return lax.psum_scatter(partial_sums, "af", scatter_dimension=1, tiled=True)


def cyclic(value, count):
    return lax.rem(value + count, count)


def place_of(slot, owner_slots, half_slots):
    half = cyclic(lax.div(slot, half_slots) - lax.axis_index("pa"), lax.axis_size("pa"))
    within = lax.rem(slot, half_slots)
    owner = lax.div(within, owner_slots) ^ lax.axis_index("ma")
    return half * half_slots + owner * owner_slots + lax.rem(within, owner_slots)


def offsets_of(keep_place, tile_place, shift_place, owner_slots):
    @pl.loop(0, keep_place.shape[0] // owner_slots)
    def _(at):
        offset = jnp.int32(0)
        for j in range(owner_slots):
            place = at * owner_slots + j
            tile = lax.div(offset, LANES)
            tile_place[place] = tile
            shift_place[place] = offset - tile * LANES
            offset = offset + keep_place[place]


def multiply_and_pack(lhs, basis_of, wait, first, out_v, pack_v, mine, send, line, tables):
    tile_place, shift_place, owner_slots = tables
    width, modes = mine.shape[-1], out_v.shape[-1]
    for k in range(PACKED):
        if k % PER_COPY == 0:
            wait(k // PER_COPY)
        out_v[k] = jnp.dot(lhs[first + k], basis_of(k), preferred_element_type=jnp.float32)
    lane = lax.broadcasted_iota(jnp.int32, (PACKED, LANES), 1)
    owners = mine.shape[0]
    rows = pl.ds(pl.multiple_of(line, PACKED), PACKED)
    for at in range(2 * owners):
        for j in range(owner_slots):
            place = at * owner_slots + j
            tile, shift = tile_place[place], shift_place[place]
            left = lane < shift
            before = None
            for t in range(modes // LANES + 1):
                lanes = pl.ds(pl.multiple_of((tile + t) * LANES, LANES), LANES)
                turned = before
                if t < modes // LANES:
                    turned = pltpu.roll(out_v[:, place, t * LANES : (t + 1) * LANES], shift, 1)
                if t == 0:
                    value = jnp.where(left, pack_v[at, :, lanes], turned)
                elif t < modes // LANES:
                    value = jnp.where(left, before, turned)
                else:
                    value = before
                pack_v[at, :, lanes] = value
                before = turned
        to = (mine, send)[at // owners]
        to[at % owners, rows, :] = pack_v[at, :, :width]


def first_kernel(
    owner_slots, slot_hbm, keep_hbm, rows_hbm, panels, basis,
    mine, send, slot_column, rows_column, scalars, lhs_later, basis_later,
    slot_s, keep_s, rows_s, keep_place, rows_place, tile_place, shift_place,
    panels_v, basis_v, lhs_v, out_v, pack_v, small_sem, panel_sem, basis_sem, later_sem,
):
    slots, all_freqs, depth = panels_v.shape
    freqs, later = basis_v.shape[0], basis_later.shape[0]
    groups = freqs // GROUP
    half_slots = slots // lax.axis_size("pa")

    table_copies = [
        pltpu.make_async_copy(slot_hbm, slot_s, small_sem.at[0]),
        pltpu.make_async_copy(keep_hbm, keep_s, small_sem.at[1]),
        pltpu.make_async_copy(rows_hbm, rows_s, small_sem.at[2]),
    ]
    for copy in table_copies:
        copy.start()

    def basis_copy(i):
        part = pl.ds(i * PER_COPY, PER_COPY)
        return pltpu.make_async_copy(basis.at[part], basis_v.at[part], basis_sem.at[i])

    later_copy = pltpu.make_async_copy(basis.at[pl.ds(freqs, later)], basis_later, later_sem)
    ahead = 4
    for i in range(ahead):
        basis_copy(i).start()
    for copy in table_copies:
        copy.wait()

    per_group = GROUP // PER_COPY
    for group in range(groups):
        part = pl.ds(group * GROUP, GROUP if group < groups - 1 else all_freqs - group * GROUP)

        @pl.loop(0, slots)
        def _(m):
            place = place_of(slot_s[m], owner_slots, half_slots)
            if group == 0:
                keep_place[place] = keep_s[m]
                rows_place[place] = rows_s[m]
            pltpu.make_async_copy(
                panels.at[m, part], panels_v.at[place, part], panel_sem.at[group]
            ).start()

        for i in range(ahead + group * per_group, min(ahead + (group + 1) * per_group, groups * per_group)):
            basis_copy(i).start()
    later_copy.start()

    offsets_of(keep_place, tile_place, shift_place, owner_slots)
    column = lax.broadcasted_iota(jnp.int32, slot_column.shape, 1)
    slot_at = jnp.full(slot_column.shape, owner_slots, jnp.int32)
    rows_at = jnp.zeros(slot_column.shape, jnp.int32)
    for j in range(owner_slots):
        keep = keep_place[j]
        offset = tile_place[j] * LANES + shift_place[j]
        within = (column >= offset) & (column < offset + keep)
        slot_at = jnp.where(within, j, slot_at)
        rows_at = jnp.where(within, rows_place[j], rows_at)
        scalars[j : j + 1, :] = jnp.full((1, LANES), offset, jnp.int32)
        scalars[owner_slots + j : owner_slots + j + 1, :] = jnp.full((1, LANES), keep, jnp.int32)
    slot_column[...] = slot_at
    rows_column[...] = rows_at

    side = GROUP * GROUP
    row = lax.broadcasted_iota(jnp.int32, (side, side), 0)
    column = lax.broadcasted_iota(jnp.int32, (side, side), 1)
    swap = (column == (row % GROUP) * GROUP + row // GROUP).astype(jnp.float32).astype(jnp.bfloat16)

    def turn(here, to):
        for block in range(slots // GROUP):
            blocks = slice(block * GROUP, (block + 1) * GROUP)
            tile = panels_v[blocks, here, :].reshape(side, depth)
            turned = jnp.dot(swap, tile, preferred_element_type=jnp.float32).astype(jnp.bfloat16)
            to[:, blocks, :] = turned.reshape(GROUP, GROUP, depth)

    def panels_wait(here, group):
        pltpu.make_async_copy(
            panels_v.at[:, here], panels_v.at[:, here], panel_sem.at[group]
        ).wait()

    @pl.loop(0, groups)
    def _(group):
        here = pl.ds(pl.multiple_of(group * GROUP, GROUP), GROUP)

        @pl.when(group < groups - 1)
        def _():
            panels_wait(here, group)

        @pl.when(group == groups - 1)
        def _():
            rest = pl.ds((groups - 1) * GROUP, all_freqs - (groups - 1) * GROUP)
            panels_wait(rest, groups - 1)
            turn(pl.ds(freqs, GROUP), lhs_later)

        turn(here, lhs_v)

        @pl.loop(0, GROUP // PACKED)
        def _(part):
            line = group * GROUP + part * PACKED
            multiply_and_pack(
                lhs_v,
                lambda k: basis_v[line + k],
                lambda c: basis_copy(line // PER_COPY + c).wait(),
                part * PACKED,
                out_v, pack_v, mine, send, line,
                (tile_place, shift_place, owner_slots),
            )

    later_copy.wait()


def second_kernel(
    start, owner_slots, slot_hbm, keep_hbm, basis, lhs, basis_early,
    mine, send,
    slot_s, keep_s, keep_place, tile_place, shift_place,
    basis_v, out_v, pack_v, small_sem, basis_sem,
):
    slots = lhs.shape[1]
    early, rest = basis_early.shape[0], basis_v.shape[0]
    half_slots = slots // lax.axis_size("pa")

    def basis_copy(i):
        part = pl.ds(start + early + i * PER_COPY, PER_COPY)
        return pltpu.make_async_copy(
            basis.at[part], basis_v.at[pl.ds(i * PER_COPY, PER_COPY)], basis_sem.at[i]
        )

    for i in range(rest // PER_COPY):
        basis_copy(i).start()
    table_copies = [
        pltpu.make_async_copy(slot_hbm, slot_s, small_sem.at[0]),
        pltpu.make_async_copy(keep_hbm, keep_s, small_sem.at[1]),
    ]
    for copy in table_copies:
        copy.start()
    for copy in table_copies:
        copy.wait()

    @pl.loop(0, slots)
    def _(m):
        keep_place[place_of(slot_s[m], owner_slots, half_slots)] = keep_s[m]

    offsets_of(keep_place, tile_place, shift_place, owner_slots)
    tables = (tile_place, shift_place, owner_slots)
    for line in range(0, early, PACKED):
        multiply_and_pack(
            lhs, lambda k: basis_early[line + k], lambda c: None, line,
            out_v, pack_v, mine, send, line, tables,
        )
    for line in range(0, rest, PACKED):
        multiply_and_pack(
            lhs,
            lambda k: basis_v[line + k],
            lambda c: basis_copy(line // PER_COPY + c).wait(),
            early + line,
            out_v, pack_v, mine, send, early + line, tables,
        )


def kl_kernel(part, owners, starts, slot_column, rows_column, kl, *refs):
    count = owners * len(starts)
    blocks, (out, packed_v) = refs[:count], refs[count:]
    owner_slots, rows, freqs = kl.shape
    shares = lax.axis_size("af")
    per_source = freqs // owners
    me = lax.axis_index("ma")
    for i, block in enumerate(blocks):
        source = me ^ (i % owners)
        at = pl.multiple_of(source * per_source + starts[i // owners], GROUP)
        packed_v[pl.ds(at, block.shape[0]), :] = block[...]
    share_rows, width = out.shape
    at = pl.multiple_of(cyclic(lax.axis_index("af") + part, shares) * share_rows, GROUP)
    lhs = kl[:, pl.ds(at, share_rows), :].reshape(owner_slots * share_rows, freqs)
    product = jnp.dot(lhs, packed_v[...], preferred_element_type=jnp.float32)
    line = lax.broadcasted_iota(jnp.int32, (share_rows, width), 0) + at
    slot_at = slot_column[0:1, :]
    total = jnp.zeros((share_rows, width), jnp.float32)
    for j in range(owner_slots):
        here = product[j * share_rows : (j + 1) * share_rows]
        total = jnp.where(slot_at == j, here, total)
    out[...] = jnp.where(line < rows_column[0:1, :], total, 0.0).astype(out.dtype)


def unpack_kernel(scalars, mine, got, out, sum_v):
    owner_slots, rows, modes = out.shape
    width = mine.shape[1]
    sum_v[:, :width] = mine[...] + got[...].astype(jnp.float32)
    lane = lax.broadcasted_iota(jnp.int32, (rows, LANES), 1)
    for j in range(owner_slots):
        offset = jnp.max(scalars[j : j + 1, :])
        keep = jnp.max(scalars[owner_slots + j : owner_slots + j + 1, :])
        tile = lax.div(offset, LANES)
        shift = offset - tile * LANES
        back = lax.rem(LANES - shift, LANES)
        turned = [
            pltpu.roll(
                sum_v[:, pl.ds(pl.multiple_of((tile + t) * LANES, LANES), LANES)], back, 1
            )
            for t in range(modes // LANES + 1)
        ]
        for t in range(modes // LANES):
            value = jnp.where(lane < LANES - shift, turned[t], turned[t + 1])
            value = jnp.where(lane < keep - t * LANES, value, 0.0)
            out[j, :, t * LANES : (t + 1) * LANES] = value


HBM = pl.BlockSpec(memory_space=pltpu.HBM)
VMEM = pl.BlockSpec(memory_space=pltpu.VMEM)
SMALL = pltpu.CompilerParams(vmem_limit_bytes=8 * MIB)


def in_hbm(operand):
    return pltpu.with_memory_space_constraint(operand, pltpu.HBM)


def project_cost(slots, freqs, depth, modes):
    return pl.CostEstimate(
        flops=2 * slots * freqs * depth * modes,
        bytes_accessed=2 * freqs * depth * (modes + slots),
        transcendentals=0,
    )


def project(panels, svd_basis, slot_of_m, svd_keep, kl_keep, owner_slots, width):
    slots, all_freqs, depth = panels.shape
    modes = svd_basis.shape[2]
    freqs = all_freqs - LATER
    owners, halves = lax.axis_size("ma"), lax.axis_size("pa")
    table = pltpu.SMEM((slots,), jnp.int32)
    wide = width + modes + LANES

    def packed(count):
        return jax.ShapeDtypeStruct((owners, count, width), jnp.float32)

    column = jax.ShapeDtypeStruct((8, width), jnp.int32)
    work = [
        pltpu.VMEM((PACKED, slots, modes), jnp.float32),
        pltpu.VMEM((halves * owners, PACKED, wide), jnp.float32),
    ]
    mine, send, slot_column, rows_column, scalars, lhs, early = pl.pallas_call(
        functools.partial(first_kernel, owner_slots),
        out_shape=(
            packed(freqs),
            packed(freqs),
            column,
            column,
            jax.ShapeDtypeStruct((8, LANES), jnp.int32),
            jax.ShapeDtypeStruct((LATER, slots, depth), jnp.bfloat16),
            jax.ShapeDtypeStruct((EARLY, depth, modes), jnp.bfloat16),
        ),
        in_specs=[HBM] * 5,
        out_specs=(VMEM,) * 7,
        scratch_shapes=[table] * 7
        + [
            pltpu.VMEM((slots, all_freqs, depth), jnp.bfloat16),
            pltpu.VMEM((freqs, depth, modes), jnp.bfloat16),
            pltpu.VMEM((GROUP, slots, depth), jnp.bfloat16),
        ]
        + work
        + [
            pltpu.SemaphoreType.DMA((3,)),
            pltpu.SemaphoreType.DMA((freqs // GROUP,)),
            pltpu.SemaphoreType.DMA((freqs // PER_COPY,)),
            pltpu.SemaphoreType.DMA,
        ],
        compiler_params=pltpu.CompilerParams(vmem_limit_bytes=44 * MIB),
        cost_estimate=project_cost(slots, freqs, depth, modes),
        name="project_first",
    )(*map(in_hbm, (slot_of_m, svd_keep, kl_keep, panels, svd_basis)))
    rest = LATER - EARLY
    second = pl.pallas_call(
        functools.partial(second_kernel, freqs, owner_slots),
        out_shape=(packed(LATER), packed(LATER)),
        in_specs=[HBM] * 3 + [VMEM] * 2,
        out_specs=(VMEM,) * 2,
        scratch_shapes=[table] * 5
        + [pltpu.VMEM((rest, depth, modes), jnp.bfloat16)]
        + work
        + [
            pltpu.SemaphoreType.DMA((2,)),
            pltpu.SemaphoreType.DMA((rest // PER_COPY,)),
        ],
        compiler_params=pltpu.CompilerParams(vmem_limit_bytes=16 * MIB),
        cost_estimate=project_cost(slots, LATER, depth, modes),
        name="project_second",
    )(*map(in_hbm, (slot_of_m, svd_keep, svd_basis)), lhs, early)
    return ((mine, send), tuple(second)), slot_column, rows_column, scalars


def kl_project(part, kind, slot_column, rows_column, kl_basis, blocks, starts):
    owners, shares = lax.axis_size("ma"), lax.axis_size("af")
    rows, freqs = kl_basis.shape[1:]
    width = slot_column.shape[1]
    return pl.pallas_call(
        functools.partial(kl_kernel, part, owners, starts),
        out_shape=jax.ShapeDtypeStruct((rows // shares, width), kind),
        in_specs=[VMEM] * (3 + len(blocks)),
        out_specs=VMEM,
        scratch_shapes=[pltpu.VMEM((freqs, width), jnp.bfloat16)],
        compiler_params=SMALL,
        cost_estimate=pl.CostEstimate(
            flops=2 * kl_basis.size * width // shares,
            bytes_accessed=2 * kl_basis.size,
            transcendentals=0,
        ),
        name="kl_project",
    )(slot_column, rows_column, kl_basis, *blocks)


def unpack(scalars, mine, got, owner_slots, modes):
    rows, width = mine.shape
    return pl.pallas_call(
        unpack_kernel,
        out_shape=jax.ShapeDtypeStruct((owner_slots, rows, modes), jnp.float32),
        in_specs=[VMEM] * 3,
        out_specs=VMEM,
        scratch_shapes=[pltpu.VMEM((rows, width + modes + LANES), jnp.float32)],
        compiler_params=SMALL,
        cost_estimate=pl.CostEstimate(
            flops=rows * width, bytes_accessed=10 * rows * width, transcendentals=0
        ),
        name="unpack",
    )(scalars, mine, got)


def pairs(axis, step):
    return [(i, i ^ step) for i in range(lax.axis_size(axis))]


def shards(panels, svd_basis, kl_basis, slot_of_m, svd_keep, kl_keep):
    owner_slots, modes = kl_basis.shape[0], svd_basis.shape[2]
    owners = lax.axis_size("ma")
    width = -(-min(OWNER_BUDGET, owner_slots * modes) // LANES) * LANES
    chunks, slot_column, rows_column, scalars = project(
        panels, svd_basis, slot_of_m, svd_keep, kl_keep, owner_slots, width
    )
    blocks, starts, start = [], [], 0
    for mine, send in chunks:
        got = lax.ppermute(send, "pa", pairs("pa", 1))
        summed = [(mine[step] + got[step]).astype(jnp.bfloat16) for step in range(owners)]
        blocks += [summed[0]] + [
            lax.ppermute(summed[step], "ma", pairs("ma", step)) for step in range(1, owners)
        ]
        starts.append(start)
        start += mine.shape[1]
    tables = (slot_column, rows_column, kl_basis, blocks, tuple(starts))
    send = kl_project(1, jnp.bfloat16, *tables)
    got = lax.ppermute(send, "af", pairs("af", 1))
    mine = kl_project(0, jnp.float32, *tables)
    return unpack(scalars, mine, got, owner_slots, modes)


def kernels_fit(mesh, args):
    panels, svd_basis, kl_basis = args[:3]
    slots = panels.shape[0] // mesh.shape["grp"]
    freqs = svd_basis.shape[0] // (mesh.shape["af"] * mesh.shape["ma"])
    owner_slots = kl_basis.shape[0] // (mesh.shape["pa"] * mesh.shape["ma"])
    share_rows = kl_basis.shape[1] // mesh.shape["af"]
    return (
        freqs % GROUP == 0
        and freqs > LATER
        and slots % (GROUP * mesh.shape["pa"]) == 0
        and owner_slots == 4
        and svd_basis.shape[2] == 2 * LANES
        and share_rows % GROUP == 0
        and mesh.shape["pa"] == 2
        and mesh.shape["af"] == 2
        and mesh.shape["ma"] in (2, 4)
    )


def solution(mesh):
    in_specs = (
        P("grp", ("af", "ma"), "pa"),
        P(("af", "ma"), "pa", None),
        P(("pa", "ma"), None, "af"),
        P(),
        P(),
        P(),
    )
    out_specs = P(("grp", "pa", "ma"), "af", None)

    def run(*args):
        body = shards if kernels_fit(mesh, args) else shards_plain
        mapped = jax.shard_map(
            body, mesh=mesh, in_specs=in_specs, out_specs=out_specs, check_vma=False
        )
        return mapped(*args)

    return run
```

```python
import functools

import jax
import jax.numpy as jnp
from jax import lax
from jax.experimental import pallas as pl
from jax.experimental.pallas import tpu as pltpu
from jax.sharding import PartitionSpec as P

LANES = 128
GROUP = 16
PACKED = 8
PER_COPY = 2
OWNER_BUDGET = 576
MIB = 2**20


def shards_plain(panels, svd_basis, kl_basis, slot_of_m, svd_keep, kl_keep):
    slot_count = slot_of_m.shape[0]
    order_slots = jnp.argsort(slot_of_m)
    keep_slots = jnp.take(svd_keep, order_slots, axis=0)
    modes_slots = jnp.take(kl_keep, order_slots, axis=0)
    width_modes = svd_basis.shape[2]
    owner_rows = kl_basis.shape[0]
    slot_rows = slot_count // lax.axis_size("pa")
    slot_start = lax.axis_index("pa") * slot_rows
    owner_start = slot_start + lax.axis_index("ma") * owner_rows
    modes_owner = lax.dynamic_slice_in_dim(modes_slots, owner_start, owner_rows, 0)
    chosen = jnp.take(panels, order_slots, axis=0)
    summed = lax.psum_scatter(
        jnp.einsum("mfb,fbr->mfr", chosen, svd_basis, preferred_element_type=jnp.float32),
        "pa",
        scatter_dimension=0,
        tiled=True,
    )
    keep_here = lax.dynamic_slice_in_dim(keep_slots, slot_start, slot_rows, 0)
    columns = jnp.arange(width_modes, dtype=jnp.int32)
    retained = jnp.where(columns[None, None, :] < keep_here[:, None, None], summed, 0.0).astype(
        jnp.bfloat16
    )
    relaid = lax.all_to_all(retained, "ma", split_axis=0, concat_axis=1, tiled=True)
    partial_sums = jnp.einsum("mkf,mfr->mkr", kl_basis, relaid, preferred_element_type=jnp.float32)
    modes = jnp.arange(kl_basis.shape[1], dtype=jnp.int32)
    partial_sums = jnp.where(modes[None, :, None] < modes_owner[:, None, None], partial_sums, 0.0)
    return lax.psum_scatter(partial_sums, "af", scatter_dimension=1, tiled=True)


def cyclic(value, count):
    return lax.rem(value + count, count)


def place_of(slot, owner_slots, half_slots):
    half = cyclic(lax.div(slot, half_slots) - lax.axis_index("pa"), lax.axis_size("pa"))
    within = lax.rem(slot, half_slots)
    owner = lax.div(within, owner_slots) ^ lax.axis_index("ma")
    return half * half_slots + owner * owner_slots + lax.rem(within, owner_slots)


def offsets_of(keep_place, tile_place, shift_place, owner_slots):
    @pl.loop(0, keep_place.shape[0] // owner_slots)
    def _(at):
        offset = jnp.int32(0)
        for j in range(owner_slots):
            place = at * owner_slots + j
            tile = lax.div(offset, LANES)
            tile_place[place] = tile
            shift_place[place] = offset - tile * LANES
            offset = offset + keep_place[place]


def multiply_and_pack(lhs, basis_of, wait, first, out_v, mine, send, line, tables):
    tile_place, shift_place, owner_slots = tables
    slots = lhs.shape[1]
    tiles = out_v.shape[0] // (PACKED * slots)
    last = mine.shape[-1] // LANES - 1
    for k in range(PACKED):
        if k % PER_COPY == 0:
            wait(k // PER_COPY)
        product = jnp.dot(lhs[first + k], basis_of(k), preferred_element_type=jnp.float32)
        for t in range(tiles):
            at = (t * PACKED + k) * slots
            out_v[at : at + slots, :] = product[:, t * LANES : (t + 1) * LANES]
    lane = lax.broadcasted_iota(jnp.int32, (PACKED, LANES), 1)
    owners = mine.shape[0]
    rows = pl.ds(pl.multiple_of(line, PACKED), PACKED)
    for at in range(2 * owners):
        to, owner = (mine, send)[at // owners], at % owners
        values, tile_before = None, None
        for j in range(owner_slots):
            place = at * owner_slots + j
            tile, shift = tile_place[place], shift_place[place]
            left = lane < shift
            turned = [
                pltpu.roll(
                    out_v[pl.ds(t * PACKED * slots + place, PACKED, stride=slots), :], shift, 1
                )
                for t in range(tiles)
            ]
            shared = turned[0]
            if j > 0:
                step = tile - tile_before
                shared = values[0]
                for t in range(1, tiles + 1):
                    shared = jnp.where(step == t, values[t], shared)
            values = (
                [jnp.where(left, shared, turned[0])]
                + [jnp.where(left, turned[t - 1], turned[t]) for t in range(1, tiles)]
                + [turned[tiles - 1]]
            )
            tile_before = tile
            for t in reversed(range(tiles + 1)):
                at_lane = pl.multiple_of(jnp.minimum(tile + t, last) * LANES, LANES)
                to[owner, rows, pl.ds(at_lane, LANES)] = values[t]


def project_kernel(
    owner_slots, slot_hbm, keep_hbm, rows_hbm, panels, basis,
    mine, send, slot_column, rows_column, scalars,
    slot_s, keep_s, rows_s, keep_place, rows_place, tile_place, shift_place,
    panels_v, basis_v, lhs_v, out_v, small_sem, panel_sem, basis_sem,
):
    slots, freqs, depth = panels_v.shape
    groups = freqs // GROUP
    half_slots = slots // lax.axis_size("pa")

    table_copies = [
        pltpu.make_async_copy(slot_hbm, slot_s, small_sem.at[0]),
        pltpu.make_async_copy(keep_hbm, keep_s, small_sem.at[1]),
        pltpu.make_async_copy(rows_hbm, rows_s, small_sem.at[2]),
    ]
    for copy in table_copies:
        copy.start()

    def basis_copy(i):
        part = pl.ds(i * PER_COPY, PER_COPY)
        return pltpu.make_async_copy(basis.at[part], basis_v.at[part], basis_sem.at[i])

    ahead = 4
    for i in range(ahead):
        basis_copy(i).start()
    for copy in table_copies:
        copy.wait()

    per_group = GROUP // PER_COPY
    for group in range(groups):
        part = pl.ds(group * GROUP, GROUP)

        @pl.loop(0, slots)
        def _(m):
            place = place_of(slot_s[m], owner_slots, half_slots)
            if group == 0:
                keep_place[place] = keep_s[m]
                rows_place[place] = rows_s[m]
            pltpu.make_async_copy(
                panels.at[m, part], panels_v.at[place, part], panel_sem.at[group]
            ).start()

        for i in range(ahead + group * per_group, min(ahead + (group + 1) * per_group, groups * per_group)):
            basis_copy(i).start()

    offsets_of(keep_place, tile_place, shift_place, owner_slots)
    column = lax.broadcasted_iota(jnp.int32, slot_column.shape, 1)
    slot_at = jnp.full(slot_column.shape, owner_slots, jnp.int32)
    rows_at = jnp.zeros(slot_column.shape, jnp.int32)
    for j in range(owner_slots):
        keep = keep_place[j]
        offset = tile_place[j] * LANES + shift_place[j]
        within = (column >= offset) & (column < offset + keep)
        slot_at = jnp.where(within, j, slot_at)
        rows_at = jnp.where(within, rows_place[j], rows_at)
        scalars[j : j + 1, :] = jnp.full((1, LANES), offset, jnp.int32)
        scalars[owner_slots + j : owner_slots + j + 1, :] = jnp.full((1, LANES), keep, jnp.int32)
    slot_column[...] = slot_at
    rows_column[...] = rows_at

    side = GROUP * GROUP
    row = lax.broadcasted_iota(jnp.int32, (side, side), 0)
    column = lax.broadcasted_iota(jnp.int32, (side, side), 1)
    swap = (column == (row % GROUP) * GROUP + row // GROUP).astype(jnp.float32).astype(jnp.bfloat16)

    @pl.loop(0, groups)
    def _(group):
        here = pl.ds(pl.multiple_of(group * GROUP, GROUP), GROUP)
        pltpu.make_async_copy(
            panels_v.at[:, here], panels_v.at[:, here], panel_sem.at[group]
        ).wait()
        for block in range(slots // GROUP):
            blocks = slice(block * GROUP, (block + 1) * GROUP)
            tile = panels_v[blocks, here, :].reshape(side, depth)
            turned = jnp.dot(swap, tile, preferred_element_type=jnp.float32).astype(jnp.bfloat16)
            lhs_v[:, blocks, :] = turned.reshape(GROUP, GROUP, depth)

        @pl.loop(0, GROUP // PACKED)
        def _(part):
            line = group * GROUP + part * PACKED
            multiply_and_pack(
                lhs_v,
                lambda k: basis_v[line + k],
                lambda c: basis_copy(line // PER_COPY + c).wait(),
                part * PACKED,
                out_v, mine, send, line,
                (tile_place, shift_place, owner_slots),
            )


def kl_kernel(part, owners, slot_column, rows_column, kl, *refs):
    blocks, (out, packed_v) = refs[:owners], refs[owners:]
    owner_slots, rows, freqs = kl.shape
    shares = lax.axis_size("af")
    per_source = freqs // owners
    me = lax.axis_index("ma")
    for step in range(owners):
        source = me ^ step
        at = pl.multiple_of(source * per_source, GROUP)
        packed_v[pl.ds(at, per_source), :] = blocks[step][...]
    share_rows, width = out.shape
    at = pl.multiple_of(cyclic(lax.axis_index("af") + part, shares) * share_rows, GROUP)
    lhs = kl[:, pl.ds(at, share_rows), :].reshape(owner_slots * share_rows, freqs)
    product = jnp.dot(lhs, packed_v[...], preferred_element_type=jnp.float32)
    line = lax.broadcasted_iota(jnp.int32, (share_rows, width), 0) + at
    slot_at = slot_column[0:1, :]
    total = jnp.zeros((share_rows, width), jnp.float32)
    for j in range(owner_slots):
        here = product[j * share_rows : (j + 1) * share_rows]
        total = jnp.where(slot_at == j, here, total)
    out[...] = jnp.where(line < rows_column[0:1, :], total, 0.0).astype(out.dtype)


def unpack_kernel(scalars, mine, got, out, sum_v):
    owner_slots, rows, modes = out.shape
    width = mine.shape[1]
    sum_v[:, :width] = mine[...] + got[...].astype(jnp.float32)
    lane = lax.broadcasted_iota(jnp.int32, (rows, LANES), 1)
    for j in range(owner_slots):
        offset = jnp.max(scalars[j : j + 1, :])
        keep = jnp.max(scalars[owner_slots + j : owner_slots + j + 1, :])
        tile = lax.div(offset, LANES)
        shift = offset - tile * LANES
        back = lax.rem(LANES - shift, LANES)
        turned = [
            pltpu.roll(
                sum_v[:, pl.ds(pl.multiple_of((tile + t) * LANES, LANES), LANES)], back, 1
            )
            for t in range(modes // LANES + 1)
        ]
        for t in range(modes // LANES):
            value = jnp.where(lane < LANES - shift, turned[t], turned[t + 1])
            value = jnp.where(lane < keep - t * LANES, value, 0.0)
            out[j, :, t * LANES : (t + 1) * LANES] = value


HBM = pl.BlockSpec(memory_space=pltpu.HBM)
VMEM = pl.BlockSpec(memory_space=pltpu.VMEM)
SMALL = pltpu.CompilerParams(vmem_limit_bytes=8 * MIB)


def in_hbm(operand):
    return pltpu.with_memory_space_constraint(operand, pltpu.HBM)


def project(panels, svd_basis, slot_of_m, svd_keep, kl_keep, owner_slots, width):
    slots, freqs, depth = panels.shape
    modes = svd_basis.shape[2]
    packed = jax.ShapeDtypeStruct((lax.axis_size("ma"), freqs, width), jnp.float32)
    column = jax.ShapeDtypeStruct((8, width), jnp.int32)
    return pl.pallas_call(
        functools.partial(project_kernel, owner_slots),
        out_shape=(packed, packed, column, column, jax.ShapeDtypeStruct((8, LANES), jnp.int32)),
        in_specs=[HBM] * 5,
        out_specs=(VMEM,) * 5,
        scratch_shapes=[pltpu.SMEM((slots,), jnp.int32)] * 7
        + [
            pltpu.VMEM((slots, freqs, depth), jnp.bfloat16),
            pltpu.VMEM((freqs, depth, modes), jnp.bfloat16),
            pltpu.VMEM((GROUP, slots, depth), jnp.bfloat16),
            pltpu.VMEM((modes // LANES * PACKED * slots, LANES), jnp.float32),
            pltpu.SemaphoreType.DMA((3,)),
            pltpu.SemaphoreType.DMA((freqs // GROUP,)),
            pltpu.SemaphoreType.DMA((freqs // PER_COPY,)),
        ],
        compiler_params=pltpu.CompilerParams(vmem_limit_bytes=48 * MIB),
        cost_estimate=pl.CostEstimate(
            flops=2 * slots * freqs * depth * modes,
            bytes_accessed=2 * freqs * depth * (modes + slots),
            transcendentals=0,
        ),
        name="project",
    )(*map(in_hbm, (slot_of_m, svd_keep, kl_keep, panels, svd_basis)))


def kl_project(part, kind, slot_column, rows_column, kl_basis, blocks):
    owners, shares = lax.axis_size("ma"), lax.axis_size("af")
    rows, freqs = kl_basis.shape[1:]
    width = slot_column.shape[1]
    return pl.pallas_call(
        functools.partial(kl_kernel, part, owners),
        out_shape=jax.ShapeDtypeStruct((rows // shares, width), kind),
        in_specs=[VMEM] * (3 + owners),
        out_specs=VMEM,
        scratch_shapes=[pltpu.VMEM((freqs, width), jnp.bfloat16)],
        compiler_params=SMALL,
        cost_estimate=pl.CostEstimate(
            flops=2 * kl_basis.size * width // shares,
            bytes_accessed=2 * kl_basis.size,
            transcendentals=0,
        ),
        name="kl_project",
    )(slot_column, rows_column, kl_basis, *blocks)


def unpack(scalars, mine, got, owner_slots, modes):
    rows, width = mine.shape
    return pl.pallas_call(
        unpack_kernel,
        out_shape=jax.ShapeDtypeStruct((owner_slots, rows, modes), jnp.float32),
        in_specs=[VMEM] * 3,
        out_specs=VMEM,
        scratch_shapes=[pltpu.VMEM((rows, width + modes + LANES), jnp.float32)],
        compiler_params=SMALL,
        cost_estimate=pl.CostEstimate(
            flops=rows * width, bytes_accessed=10 * rows * width, transcendentals=0
        ),
        name="unpack",
    )(scalars, mine, got)


def pairs(axis, step):
    return [(i, i ^ step) for i in range(lax.axis_size(axis))]


def shards(panels, svd_basis, kl_basis, slot_of_m, svd_keep, kl_keep):
    owner_slots, modes = kl_basis.shape[0], svd_basis.shape[2]
    owners = lax.axis_size("ma")
    width = -(-min(OWNER_BUDGET, owner_slots * modes) // LANES) * LANES
    mine, send, slot_column, rows_column, scalars = project(
        panels, svd_basis, slot_of_m, svd_keep, kl_keep, owner_slots, width
    )
    got = lax.ppermute(send, "pa", pairs("pa", 1))
    summed = [(mine[step] + got[step]).astype(jnp.bfloat16) for step in range(owners)]
    blocks = [summed[0]] + [
        lax.ppermute(summed[step], "ma", pairs("ma", step)) for step in range(1, owners)
    ]
    tables = (slot_column, rows_column, kl_basis, blocks)
    send = kl_project(1, jnp.bfloat16, *tables)
    got = lax.ppermute(send, "af", pairs("af", 1))
    mine = kl_project(0, jnp.float32, *tables)
    return unpack(scalars, mine, got, owner_slots, modes)


def kernels_fit(mesh, args):
    panels, svd_basis, kl_basis = args[:3]
    slots = panels.shape[0] // mesh.shape["grp"]
    freqs = svd_basis.shape[0] // (mesh.shape["af"] * mesh.shape["ma"])
    owner_slots = kl_basis.shape[0] // (mesh.shape["pa"] * mesh.shape["ma"])
    share_rows = kl_basis.shape[1] // mesh.shape["af"]
    return (
        freqs % GROUP == 0
        and slots % (GROUP * mesh.shape["pa"]) == 0
        and owner_slots == 4
        and svd_basis.shape[2] == 2 * LANES
        and share_rows % GROUP == 0
        and mesh.shape["pa"] == 2
        and mesh.shape["af"] == 2
        and mesh.shape["ma"] in (2, 4)
    )


def solution(mesh):
    in_specs = (
        P("grp", ("af", "ma"), "pa"),
        P(("af", "ma"), "pa", None),
        P(("pa", "ma"), None, "af"),
        P(),
        P(),
        P(),
    )
    out_specs = P(("grp", "pa", "ma"), "af", None)

    def run(*args):
        body = shards if kernels_fit(mesh, args) else shards_plain
        mapped = jax.shard_map(
            body, mesh=mesh, in_specs=in_specs, out_specs=out_specs, check_vma=False
        )
        return mapped(*args)

    return run
```

```python
import functools

import jax
import jax.numpy as jnp
from jax import lax
from jax.experimental import pallas as pl
from jax.experimental.pallas import tpu as pltpu
from jax.sharding import PartitionSpec as P

LANES = 128
GROUP = 16
PACKED = 16
BATCH = 2
PER_COPY = 4
OWNER_BUDGET = 576
MIB = 2**20


def shards_plain(panels, svd_basis, kl_basis, slot_of_m, svd_keep, kl_keep):
    slot_count = slot_of_m.shape[0]
    order_slots = jnp.argsort(slot_of_m)
    keep_slots = jnp.take(svd_keep, order_slots, axis=0)
    modes_slots = jnp.take(kl_keep, order_slots, axis=0)
    width_modes = svd_basis.shape[2]
    owner_rows = kl_basis.shape[0]
    slot_rows = slot_count // lax.axis_size("pa")
    slot_start = lax.axis_index("pa") * slot_rows
    owner_start = slot_start + lax.axis_index("ma") * owner_rows
    modes_owner = lax.dynamic_slice_in_dim(modes_slots, owner_start, owner_rows, 0)
    chosen = jnp.take(panels, order_slots, axis=0)
    summed = lax.psum_scatter(
        jnp.einsum("mfb,fbr->mfr", chosen, svd_basis, preferred_element_type=jnp.float32),
        "pa",
        scatter_dimension=0,
        tiled=True,
    )
    keep_here = lax.dynamic_slice_in_dim(keep_slots, slot_start, slot_rows, 0)
    columns = jnp.arange(width_modes, dtype=jnp.int32)
    retained = jnp.where(columns[None, None, :] < keep_here[:, None, None], summed, 0.0).astype(
        jnp.bfloat16
    )
    relaid = lax.all_to_all(retained, "ma", split_axis=0, concat_axis=1, tiled=True)
    partial_sums = jnp.einsum("mkf,mfr->mkr", kl_basis, relaid, preferred_element_type=jnp.float32)
    modes = jnp.arange(kl_basis.shape[1], dtype=jnp.int32)
    partial_sums = jnp.where(modes[None, :, None] < modes_owner[:, None, None], partial_sums, 0.0)
    return lax.psum_scatter(partial_sums, "af", scatter_dimension=1, tiled=True)


def cyclic(value, count):
    return lax.rem(value + count, count)


def place_of(slot, owner_slots, half_slots):
    half = cyclic(lax.div(slot, half_slots) - lax.axis_index("pa"), lax.axis_size("pa"))
    within = lax.rem(slot, half_slots)
    owner = lax.div(within, owner_slots) ^ lax.axis_index("ma")
    return half * half_slots + owner * owner_slots + lax.rem(within, owner_slots)


def offsets_of(keep_place, tile_place, shift_place, owner_slots):
    @pl.loop(0, keep_place.shape[0] // owner_slots)
    def _(at):
        offset = jnp.int32(0)
        for j in range(owner_slots):
            place = at * owner_slots + j
            tile = lax.div(offset, LANES)
            tile_place[place] = tile
            shift_place[place] = offset - tile * LANES
            offset = offset + keep_place[place]


def pack(out_v, mine, send, line, tables):
    tile_place, shift_place, owner_slots = tables
    owners, _, width = mine.shape
    slots = 2 * owners * owner_slots
    tiles = out_v.shape[0] // (PACKED * slots)
    last = width // LANES - 1
    lane = lax.broadcasted_iota(jnp.int32, (PACKED, LANES), 1)
    rows = pl.ds(pl.multiple_of(line, PACKED), PACKED)
    for begin in range(0, 2 * owners, BATCH):
        turned = {
            place: pltpu.roll(
                out_v[pl.ds(place, tiles * PACKED, stride=slots), :], shift_place[place], 1
            )
            for place in range(begin * owner_slots, (begin + BATCH) * owner_slots)
        }
        for at in range(begin, begin + BATCH):
            to, owner = (mine, send)[at // owners], at % owners
            values, tile_before = None, None
            for j in range(owner_slots):
                place = at * owner_slots + j
                tile = tile_place[place]
                left = lane < shift_place[place]
                moved = [turned[place][t * PACKED : (t + 1) * PACKED] for t in range(tiles)]
                shared = moved[0]
                if j > 0:
                    step = tile - tile_before
                    shared = values[0]
                    for t in range(1, tiles + 1):
                        shared = jnp.where(step == t, values[t], shared)
                values = (
                    [jnp.where(left, shared, moved[0])]
                    + [jnp.where(left, moved[t - 1], moved[t]) for t in range(1, tiles)]
                    + [moved[tiles - 1]]
                )
                tile_before = tile
                for t in reversed(range(tiles + 1)):
                    at_lane = pl.multiple_of(jnp.minimum(tile + t, last) * LANES, LANES)
                    to[owner, rows, pl.ds(at_lane, LANES)] = values[t]


def project_kernel(
    owner_slots, slot_hbm, keep_hbm, rows_hbm, panels, basis,
    mine, send, slot_column, rows_column, scalars,
    slot_s, keep_s, rows_s, keep_place, rows_place, tile_place, shift_place,
    panels_v, basis_v, lhs_v, out_v, small_sem, panel_sem, basis_sem,
):
    slots, freqs, depth = panels_v.shape
    groups = freqs // GROUP
    half_slots = slots // lax.axis_size("pa")

    table_copies = [
        pltpu.make_async_copy(slot_hbm, slot_s, small_sem.at[0]),
        pltpu.make_async_copy(keep_hbm, keep_s, small_sem.at[1]),
        pltpu.make_async_copy(rows_hbm, rows_s, small_sem.at[2]),
    ]
    for copy in table_copies:
        copy.start()

    def basis_copy(i):
        part = pl.ds(i * PER_COPY, PER_COPY)
        return pltpu.make_async_copy(basis.at[part], basis_v.at[part], basis_sem.at[i])

    ahead = 2
    for i in range(ahead):
        basis_copy(i).start()
    for copy in table_copies:
        copy.wait()

    per_group = GROUP // PER_COPY
    for group in range(groups):
        part = pl.ds(group * GROUP, GROUP)

        @pl.loop(0, slots)
        def _(m):
            place = place_of(slot_s[m], owner_slots, half_slots)
            if group == 0:
                keep_place[place] = keep_s[m]
                rows_place[place] = rows_s[m]
            pltpu.make_async_copy(
                panels.at[m, part], panels_v.at[place, part], panel_sem.at[group]
            ).start()

        for i in range(ahead + group * per_group, min(ahead + (group + 1) * per_group, groups * per_group)):
            basis_copy(i).start()

    offsets_of(keep_place, tile_place, shift_place, owner_slots)
    column = lax.broadcasted_iota(jnp.int32, slot_column.shape, 1)
    slot_at = jnp.full(slot_column.shape, owner_slots, jnp.int32)
    rows_at = jnp.zeros(slot_column.shape, jnp.int32)
    for j in range(owner_slots):
        keep = keep_place[j]
        offset = tile_place[j] * LANES + shift_place[j]
        within = (column >= offset) & (column < offset + keep)
        slot_at = jnp.where(within, j, slot_at)
        rows_at = jnp.where(within, rows_place[j], rows_at)
        scalars[j : j + 1, :] = jnp.full((1, LANES), offset, jnp.int32)
        scalars[owner_slots + j : owner_slots + j + 1, :] = jnp.full((1, LANES), keep, jnp.int32)
    slot_column[...] = slot_at
    rows_column[...] = rows_at

    side = GROUP * GROUP
    row = lax.broadcasted_iota(jnp.int32, (side, side), 0)
    column = lax.broadcasted_iota(jnp.int32, (side, side), 1)
    swap = (column == (row % GROUP) * GROUP + row // GROUP).astype(jnp.float32).astype(jnp.bfloat16)

    @pl.loop(0, groups)
    def _(group):
        here = pl.ds(pl.multiple_of(group * GROUP, GROUP), GROUP)
        pltpu.make_async_copy(
            panels_v.at[:, here], panels_v.at[:, here], panel_sem.at[group]
        ).wait()
        for block in range(slots // GROUP):
            blocks = slice(block * GROUP, (block + 1) * GROUP)
            tile = panels_v[blocks, here, :].reshape(side, depth)
            turned = jnp.dot(swap, tile, preferred_element_type=jnp.float32).astype(jnp.bfloat16)
            lhs_v[:, blocks, :] = turned.reshape(GROUP, GROUP, depth)

        @pl.loop(0, per_group)
        def _(i):
            basis_copy(group * per_group + i).wait()
            for k in range(PER_COPY):
                f = i * PER_COPY + k
                product = jnp.dot(
                    lhs_v[f], basis_v[group * GROUP + f], preferred_element_type=jnp.float32
                )
                for t in range(product.shape[1] // LANES):
                    at = pl.multiple_of((t * PACKED + f) * slots, slots)
                    out_v[pl.ds(at, slots), :] = product[:, t * LANES : (t + 1) * LANES]

        pack(out_v, mine, send, group * GROUP, (tile_place, shift_place, owner_slots))


def kl_kernel(part, owners, slot_column, rows_column, kl, *refs):
    blocks, (out, packed_v) = refs[:owners], refs[owners:]
    owner_slots, rows, freqs = kl.shape
    shares = lax.axis_size("af")
    per_source = freqs // owners
    me = lax.axis_index("ma")
    for step in range(owners):
        source = me ^ step
        at = pl.multiple_of(source * per_source, GROUP)
        packed_v[pl.ds(at, per_source), :] = blocks[step][...]
    share_rows, width = out.shape
    at = pl.multiple_of(cyclic(lax.axis_index("af") + part, shares) * share_rows, GROUP)
    lhs = kl[:, pl.ds(at, share_rows), :].reshape(owner_slots * share_rows, freqs)
    product = jnp.dot(lhs, packed_v[...], preferred_element_type=jnp.float32)
    line = lax.broadcasted_iota(jnp.int32, (share_rows, width), 0) + at
    slot_at = slot_column[0:1, :]
    total = jnp.zeros((share_rows, width), jnp.float32)
    for j in range(owner_slots):
        here = product[j * share_rows : (j + 1) * share_rows]
        total = jnp.where(slot_at == j, here, total)
    out[...] = jnp.where(line < rows_column[0:1, :], total, 0.0).astype(out.dtype)


def unpack_kernel(scalars, mine, got, out, sum_v):
    owner_slots, rows, modes = out.shape
    width = mine.shape[1]
    sum_v[:, :width] = mine[...] + got[...].astype(jnp.float32)
    lane = lax.broadcasted_iota(jnp.int32, (rows, LANES), 1)
    for j in range(owner_slots):
        offset = jnp.max(scalars[j : j + 1, :])
        keep = jnp.max(scalars[owner_slots + j : owner_slots + j + 1, :])
        tile = lax.div(offset, LANES)
        shift = offset - tile * LANES
        back = lax.rem(LANES - shift, LANES)
        turned = [
            pltpu.roll(
                sum_v[:, pl.ds(pl.multiple_of((tile + t) * LANES, LANES), LANES)], back, 1
            )
            for t in range(modes // LANES + 1)
        ]
        for t in range(modes // LANES):
            value = jnp.where(lane < LANES - shift, turned[t], turned[t + 1])
            value = jnp.where(lane < keep - t * LANES, value, 0.0)
            out[j, :, t * LANES : (t + 1) * LANES] = value


HBM = pl.BlockSpec(memory_space=pltpu.HBM)
VMEM = pl.BlockSpec(memory_space=pltpu.VMEM)
SMALL = pltpu.CompilerParams(vmem_limit_bytes=8 * MIB)


def in_hbm(operand):
    return pltpu.with_memory_space_constraint(operand, pltpu.HBM)


def project(panels, svd_basis, slot_of_m, svd_keep, kl_keep, owner_slots, width):
    slots, freqs, depth = panels.shape
    modes = svd_basis.shape[2]
    packed = jax.ShapeDtypeStruct((lax.axis_size("ma"), freqs, width), jnp.float32)
    column = jax.ShapeDtypeStruct((8, width), jnp.int32)
    return pl.pallas_call(
        functools.partial(project_kernel, owner_slots),
        out_shape=(packed, packed, column, column, jax.ShapeDtypeStruct((8, LANES), jnp.int32)),
        in_specs=[HBM] * 5,
        out_specs=(VMEM,) * 5,
        scratch_shapes=[pltpu.SMEM((slots,), jnp.int32)] * 7
        + [
            pltpu.VMEM((slots, freqs, depth), jnp.bfloat16),
            pltpu.VMEM((freqs, depth, modes), jnp.bfloat16),
            pltpu.VMEM((GROUP, slots, depth), jnp.bfloat16),
            pltpu.VMEM((modes // LANES * PACKED * slots, LANES), jnp.float32),
            pltpu.SemaphoreType.DMA((3,)),
            pltpu.SemaphoreType.DMA((freqs // GROUP,)),
            pltpu.SemaphoreType.DMA((freqs // PER_COPY,)),
        ],
        compiler_params=pltpu.CompilerParams(vmem_limit_bytes=48 * MIB),
        cost_estimate=pl.CostEstimate(
            flops=2 * slots * freqs * depth * modes,
            bytes_accessed=2 * freqs * depth * (modes + slots),
            transcendentals=0,
        ),
        name="project",
    )(*map(in_hbm, (slot_of_m, svd_keep, kl_keep, panels, svd_basis)))


def kl_project(part, kind, slot_column, rows_column, kl_basis, blocks):
    owners, shares = lax.axis_size("ma"), lax.axis_size("af")
    rows, freqs = kl_basis.shape[1:]
    width = slot_column.shape[1]
    return pl.pallas_call(
        functools.partial(kl_kernel, part, owners),
        out_shape=jax.ShapeDtypeStruct((rows // shares, width), kind),
        in_specs=[VMEM] * (3 + owners),
        out_specs=VMEM,
        scratch_shapes=[pltpu.VMEM((freqs, width), jnp.bfloat16)],
        compiler_params=SMALL,
        cost_estimate=pl.CostEstimate(
            flops=2 * kl_basis.size * width // shares,
            bytes_accessed=2 * kl_basis.size,
            transcendentals=0,
        ),
        name="kl_project",
    )(slot_column, rows_column, kl_basis, *blocks)


def unpack(scalars, mine, got, owner_slots, modes):
    rows, width = mine.shape
    return pl.pallas_call(
        unpack_kernel,
        out_shape=jax.ShapeDtypeStruct((owner_slots, rows, modes), jnp.float32),
        in_specs=[VMEM] * 3,
        out_specs=VMEM,
        scratch_shapes=[pltpu.VMEM((rows, width + modes + LANES), jnp.float32)],
        compiler_params=SMALL,
        cost_estimate=pl.CostEstimate(
            flops=rows * width, bytes_accessed=10 * rows * width, transcendentals=0
        ),
        name="unpack",
    )(scalars, mine, got)


def pairs(axis, step):
    return [(i, i ^ step) for i in range(lax.axis_size(axis))]


def shards(panels, svd_basis, kl_basis, slot_of_m, svd_keep, kl_keep):
    owner_slots, modes = kl_basis.shape[0], svd_basis.shape[2]
    owners = lax.axis_size("ma")
    width = -(-min(OWNER_BUDGET, owner_slots * modes) // LANES) * LANES
    mine, send, slot_column, rows_column, scalars = project(
        panels, svd_basis, slot_of_m, svd_keep, kl_keep, owner_slots, width
    )
    got = lax.ppermute(send, "pa", pairs("pa", 1))
    summed = [(mine[step] + got[step]).astype(jnp.bfloat16) for step in range(owners)]
    blocks = [summed[0]] + [
        lax.ppermute(summed[step], "ma", pairs("ma", step)) for step in range(1, owners)
    ]
    tables = (slot_column, rows_column, kl_basis, blocks)
    send = kl_project(1, jnp.bfloat16, *tables)
    got = lax.ppermute(send, "af", pairs("af", 1))
    mine = kl_project(0, jnp.float32, *tables)
    return unpack(scalars, mine, got, owner_slots, modes)


def kernels_fit(mesh, args):
    panels, svd_basis, kl_basis = args[:3]
    slots = panels.shape[0] // mesh.shape["grp"]
    freqs = svd_basis.shape[0] // (mesh.shape["af"] * mesh.shape["ma"])
    owner_slots = kl_basis.shape[0] // (mesh.shape["pa"] * mesh.shape["ma"])
    share_rows = kl_basis.shape[1] // mesh.shape["af"]
    return (
        freqs % GROUP == 0
        and slots % (GROUP * mesh.shape["pa"]) == 0
        and owner_slots == 4
        and svd_basis.shape[2] == 2 * LANES
        and share_rows % GROUP == 0
        and mesh.shape["pa"] == 2
        and mesh.shape["af"] == 2
        and mesh.shape["ma"] in (2, 4)
    )


def solution(mesh):
    in_specs = (
        P("grp", ("af", "ma"), "pa"),
        P(("af", "ma"), "pa", None),
        P(("pa", "ma"), None, "af"),
        P(),
        P(),
        P(),
    )
    out_specs = P(("grp", "pa", "ma"), "af", None)

    def run(*args):
        body = shards if kernels_fit(mesh, args) else shards_plain
        mapped = jax.shard_map(
            body, mesh=mesh, in_specs=in_specs, out_specs=out_specs, check_vma=False
        )
        return mapped(*args)

    return run
```

```python
import functools

import jax
import jax.numpy as jnp
from jax import lax
from jax.experimental import pallas as pl
from jax.experimental.pallas import tpu as pltpu
from jax.sharding import PartitionSpec as P

LANES = 128
GROUP = 16
PER_COPY = 4
OWNER_BUDGET = 576
MIB = 2**20


def shards_plain(panels, svd_basis, kl_basis, slot_of_m, svd_keep, kl_keep):
    slot_count = slot_of_m.shape[0]
    order_slots = jnp.argsort(slot_of_m)
    keep_slots = jnp.take(svd_keep, order_slots, axis=0)
    modes_slots = jnp.take(kl_keep, order_slots, axis=0)
    width_modes = svd_basis.shape[2]
    owner_rows = kl_basis.shape[0]
    slot_rows = slot_count // lax.axis_size("pa")
    slot_start = lax.axis_index("pa") * slot_rows
    owner_start = slot_start + lax.axis_index("ma") * owner_rows
    modes_owner = lax.dynamic_slice_in_dim(modes_slots, owner_start, owner_rows, 0)
    chosen = jnp.take(panels, order_slots, axis=0)
    summed = lax.psum_scatter(
        jnp.einsum("mfb,fbr->mfr", chosen, svd_basis, preferred_element_type=jnp.float32),
        "pa",
        scatter_dimension=0,
        tiled=True,
    )
    keep_here = lax.dynamic_slice_in_dim(keep_slots, slot_start, slot_rows, 0)
    columns = jnp.arange(width_modes, dtype=jnp.int32)
    retained = jnp.where(columns[None, None, :] < keep_here[:, None, None], summed, 0.0).astype(
        jnp.bfloat16
    )
    relaid = lax.all_to_all(retained, "ma", split_axis=0, concat_axis=1, tiled=True)
    partial_sums = jnp.einsum("mkf,mfr->mkr", kl_basis, relaid, preferred_element_type=jnp.float32)
    modes = jnp.arange(kl_basis.shape[1], dtype=jnp.int32)
    partial_sums = jnp.where(modes[None, :, None] < modes_owner[:, None, None], partial_sums, 0.0)
    return lax.psum_scatter(partial_sums, "af", scatter_dimension=1, tiled=True)


def cyclic(value, count):
    return lax.rem(value + count, count)


def place_of(slot, owner_slots, half_slots):
    half = cyclic(lax.div(slot, half_slots) - lax.axis_index("pa"), lax.axis_size("pa"))
    within = lax.rem(slot, half_slots)
    owner = lax.div(within, owner_slots) ^ lax.axis_index("ma")
    return half * half_slots + owner * owner_slots + lax.rem(within, owner_slots)


def offsets_of(keep_place, tile_place, shift_place, owner_slots):
    @pl.loop(0, keep_place.shape[0] // owner_slots)
    def _(at):
        offset = jnp.int32(0)
        for j in range(owner_slots):
            place = at * owner_slots + j
            tile = lax.div(offset, LANES)
            tile_place[place] = tile
            shift_place[place] = offset - tile * LANES
            offset = offset + keep_place[place]


def pack(out_v, mine, send, line, tables, owners_at):
    tile_place, shift_place, owner_slots = tables
    owners, width_tiles = mine.shape[:2]
    slots = 2 * owners * owner_slots
    tiles = out_v.shape[0] // (GROUP * slots)
    lane = lax.broadcasted_iota(jnp.int32, (GROUP, LANES), 1)
    rows = pl.ds(pl.multiple_of(line, GROUP), GROUP)
    turned = {
        place: pltpu.roll(
            out_v[pl.ds(place, tiles * GROUP, stride=slots), :], shift_place[place], 1
        )
        for place in range(owners_at[0] * owner_slots, (owners_at[-1] + 1) * owner_slots)
    }
    for at in owners_at:
        to, owner = (mine, send)[at // owners], at % owners
        values, tile_before = None, None
        for j in range(owner_slots):
            place = at * owner_slots + j
            tile = tile_place[place]
            left = lane < shift_place[place]
            moved = [turned[place][t * GROUP : (t + 1) * GROUP] for t in range(tiles)]
            shared = moved[0]
            if j > 0:
                step = tile - tile_before
                shared = values[0]
                for t in range(1, tiles + 1):
                    shared = jnp.where(step == t, values[t], shared)
            values = (
                [jnp.where(left, shared, moved[0])]
                + [jnp.where(left, moved[t - 1], moved[t]) for t in range(1, tiles)]
                + [moved[tiles - 1]]
            )
            tile_before = tile
            for t in reversed(range(tiles + 1)):
                to[owner, jnp.minimum(tile + t, width_tiles - 1), rows, :] = values[t]


def project_kernel(
    owner_slots, slot_hbm, keep_hbm, rows_hbm, panels, basis,
    mine, send, slot_column, rows_column, scalars,
    slot_s, keep_s, rows_s, keep_place, rows_place, tile_place, shift_place,
    panels_v, basis_v, lhs_v, out_even, out_odd, small_sem, panel_sem, basis_sem,
):
    slots, freqs, depth = panels_v.shape
    groups = freqs // GROUP
    half_slots = slots // lax.axis_size("pa")

    table_copies = [
        pltpu.make_async_copy(slot_hbm, slot_s, small_sem.at[0]),
        pltpu.make_async_copy(keep_hbm, keep_s, small_sem.at[1]),
        pltpu.make_async_copy(rows_hbm, rows_s, small_sem.at[2]),
    ]
    for copy in table_copies:
        copy.start()

    def basis_copy(i):
        part = pl.ds(i * PER_COPY, PER_COPY)
        return pltpu.make_async_copy(basis.at[part], basis_v.at[part], basis_sem.at[i])

    ahead = 2
    for i in range(ahead):
        basis_copy(i).start()
    for copy in table_copies:
        copy.wait()

    per_group = GROUP // PER_COPY
    for group in range(groups):
        part = pl.ds(group * GROUP, GROUP)

        @pl.loop(0, slots)
        def _(m):
            place = place_of(slot_s[m], owner_slots, half_slots)
            if group == 0:
                keep_place[place] = keep_s[m]
                rows_place[place] = rows_s[m]
            pltpu.make_async_copy(
                panels.at[m, part], panels_v.at[place, part], panel_sem.at[group]
            ).start()

        for i in range(ahead + group * per_group, min(ahead + (group + 1) * per_group, groups * per_group)):
            basis_copy(i).start()

    offsets_of(keep_place, tile_place, shift_place, owner_slots)
    column = lax.broadcasted_iota(jnp.int32, slot_column.shape, 1)
    slot_at = jnp.full(slot_column.shape, owner_slots, jnp.int32)
    rows_at = jnp.zeros(slot_column.shape, jnp.int32)
    for j in range(owner_slots):
        keep = keep_place[j]
        offset = tile_place[j] * LANES + shift_place[j]
        within = (column >= offset) & (column < offset + keep)
        slot_at = jnp.where(within, j, slot_at)
        rows_at = jnp.where(within, rows_place[j], rows_at)
        scalars[j : j + 1, :] = jnp.full((1, LANES), offset, jnp.int32)
        scalars[owner_slots + j : owner_slots + j + 1, :] = jnp.full((1, LANES), keep, jnp.int32)
    slot_column[...] = slot_at
    rows_column[...] = rows_at

    side = GROUP * GROUP
    row = lax.broadcasted_iota(jnp.int32, (side, side), 0)
    column = lax.broadcasted_iota(jnp.int32, (side, side), 1)
    swap = (column == (row % GROUP) * GROUP + row // GROUP).astype(jnp.float32).astype(jnp.bfloat16)

    tables = (tile_place, shift_place, owner_slots)
    all_owners = range(mine.shape[0] * lax.axis_size("pa"))
    share = len(all_owners) // per_group

    def group_step(group, out_v, out_before):
        here = pl.ds(pl.multiple_of(group * GROUP, GROUP), GROUP)
        pltpu.make_async_copy(
            panels_v.at[:, here], panels_v.at[:, here], panel_sem.at[group]
        ).wait()
        for block in range(slots // GROUP):
            blocks = slice(block * GROUP, (block + 1) * GROUP)
            tile = panels_v[blocks, here, :].reshape(side, depth)
            turned = jnp.dot(swap, tile, preferred_element_type=jnp.float32).astype(jnp.bfloat16)
            lhs_v[:, blocks, :] = turned.reshape(GROUP, GROUP, depth)
        for i in range(per_group):
            basis_copy(group * per_group + i).wait()
            for f in range(i * PER_COPY, (i + 1) * PER_COPY):
                product = jnp.dot(
                    lhs_v[f], basis_v[group * GROUP + f], preferred_element_type=jnp.float32
                )
                for t in range(product.shape[1] // LANES):
                    at = (t * GROUP + f) * slots
                    out_v[at : at + slots, :] = product[:, t * LANES : (t + 1) * LANES]
            line = jnp.maximum(group - 1, 0) * GROUP
            pack(out_before, mine, send, line, tables, all_owners[i * share : (i + 1) * share])

    @pl.loop(0, groups // 2)
    def _(pair):
        group_step(2 * pair, out_even, out_odd)
        group_step(2 * pair + 1, out_odd, out_even)

    for i in range(per_group):
        part = all_owners[i * share : (i + 1) * share]
        pack(out_odd, mine, send, (groups - 1) * GROUP, tables, part)


def kl_kernel(part, owners, slot_column, rows_column, kl, *refs):
    blocks, (out, packed_v) = refs[:owners], refs[owners:]
    owner_slots, rows, freqs = kl.shape
    shares = lax.axis_size("af")
    per_source = freqs // owners
    me = lax.axis_index("ma")
    for step in range(owners):
        source = me ^ step
        at = pl.multiple_of(source * per_source, GROUP)
        for t in range(blocks[step].shape[0]):
            packed_v[pl.ds(at, per_source), t * LANES : (t + 1) * LANES] = blocks[step][t]
    share_rows, width = out.shape
    at = pl.multiple_of(cyclic(lax.axis_index("af") + part, shares) * share_rows, GROUP)
    lhs = kl[:, pl.ds(at, share_rows), :].reshape(owner_slots * share_rows, freqs)
    product = jnp.dot(lhs, packed_v[...], preferred_element_type=jnp.float32)
    line = lax.broadcasted_iota(jnp.int32, (share_rows, width), 0) + at
    slot_at = slot_column[0:1, :]
    total = jnp.zeros((share_rows, width), jnp.float32)
    for j in range(owner_slots):
        here = product[j * share_rows : (j + 1) * share_rows]
        total = jnp.where(slot_at == j, here, total)
    out[...] = jnp.where(line < rows_column[0:1, :], total, 0.0).astype(out.dtype)


def unpack_kernel(scalars, mine, got, out, sum_v):
    owner_slots, rows, modes = out.shape
    width = mine.shape[1]
    sum_v[:, :width] = mine[...] + got[...].astype(jnp.float32)
    lane = lax.broadcasted_iota(jnp.int32, (rows, LANES), 1)
    for j in range(owner_slots):
        offset = jnp.max(scalars[j : j + 1, :])
        keep = jnp.max(scalars[owner_slots + j : owner_slots + j + 1, :])
        tile = lax.div(offset, LANES)
        shift = offset - tile * LANES
        back = lax.rem(LANES - shift, LANES)
        turned = [
            pltpu.roll(
                sum_v[:, pl.ds(pl.multiple_of((tile + t) * LANES, LANES), LANES)], back, 1
            )
            for t in range(modes // LANES + 1)
        ]
        for t in range(modes // LANES):
            value = jnp.where(lane < LANES - shift, turned[t], turned[t + 1])
            value = jnp.where(lane < keep - t * LANES, value, 0.0)
            out[j, :, t * LANES : (t + 1) * LANES] = value


HBM = pl.BlockSpec(memory_space=pltpu.HBM)
VMEM = pl.BlockSpec(memory_space=pltpu.VMEM)
SMALL = pltpu.CompilerParams(vmem_limit_bytes=8 * MIB)


def in_hbm(operand):
    return pltpu.with_memory_space_constraint(operand, pltpu.HBM)


def project(panels, svd_basis, slot_of_m, svd_keep, kl_keep, owner_slots, width):
    slots, freqs, depth = panels.shape
    modes = svd_basis.shape[2]
    packed = jax.ShapeDtypeStruct(
        (lax.axis_size("ma"), width // LANES, freqs, LANES), jnp.float32
    )
    column = jax.ShapeDtypeStruct((8, width), jnp.int32)
    return pl.pallas_call(
        functools.partial(project_kernel, owner_slots),
        out_shape=(packed, packed, column, column, jax.ShapeDtypeStruct((8, LANES), jnp.int32)),
        in_specs=[HBM] * 5,
        out_specs=(VMEM,) * 5,
        scratch_shapes=[pltpu.SMEM((slots,), jnp.int32)] * 7
        + [
            pltpu.VMEM((slots, freqs, depth), jnp.bfloat16),
            pltpu.VMEM((freqs, depth, modes), jnp.bfloat16),
            pltpu.VMEM((GROUP, slots, depth), jnp.bfloat16),
            pltpu.VMEM((modes // LANES * GROUP * slots, LANES), jnp.float32),
            pltpu.VMEM((modes // LANES * GROUP * slots, LANES), jnp.float32),
            pltpu.SemaphoreType.DMA((3,)),
            pltpu.SemaphoreType.DMA((freqs // GROUP,)),
            pltpu.SemaphoreType.DMA((freqs // PER_COPY,)),
        ],
        compiler_params=pltpu.CompilerParams(vmem_limit_bytes=48 * MIB),
        cost_estimate=pl.CostEstimate(
            flops=2 * slots * freqs * depth * modes,
            bytes_accessed=2 * freqs * depth * (modes + slots),
            transcendentals=0,
        ),
        name="project",
    )(*map(in_hbm, (slot_of_m, svd_keep, kl_keep, panels, svd_basis)))


def kl_project(part, kind, slot_column, rows_column, kl_basis, blocks):
    owners, shares = lax.axis_size("ma"), lax.axis_size("af")
    rows, freqs = kl_basis.shape[1:]
    width = slot_column.shape[1]
    return pl.pallas_call(
        functools.partial(kl_kernel, part, owners),
        out_shape=jax.ShapeDtypeStruct((rows // shares, width), kind),
        in_specs=[VMEM] * (3 + owners),
        out_specs=VMEM,
        scratch_shapes=[pltpu.VMEM((freqs, width), jnp.bfloat16)],
        compiler_params=SMALL,
        cost_estimate=pl.CostEstimate(
            flops=2 * kl_basis.size * width // shares,
            bytes_accessed=2 * kl_basis.size,
            transcendentals=0,
        ),
        name="kl_project",
    )(slot_column, rows_column, kl_basis, *blocks)


def unpack(scalars, mine, got, owner_slots, modes):
    rows, width = mine.shape
    return pl.pallas_call(
        unpack_kernel,
        out_shape=jax.ShapeDtypeStruct((owner_slots, rows, modes), jnp.float32),
        in_specs=[VMEM] * 3,
        out_specs=VMEM,
        scratch_shapes=[pltpu.VMEM((rows, width + modes + LANES), jnp.float32)],
        compiler_params=SMALL,
        cost_estimate=pl.CostEstimate(
            flops=rows * width, bytes_accessed=10 * rows * width, transcendentals=0
        ),
        name="unpack",
    )(scalars, mine, got)


def pairs(axis, step):
    return [(i, i ^ step) for i in range(lax.axis_size(axis))]


def shards(panels, svd_basis, kl_basis, slot_of_m, svd_keep, kl_keep):
    owner_slots, modes = kl_basis.shape[0], svd_basis.shape[2]
    owners = lax.axis_size("ma")
    width = -(-min(OWNER_BUDGET, owner_slots * modes) // LANES) * LANES
    mine, send, slot_column, rows_column, scalars = project(
        panels, svd_basis, slot_of_m, svd_keep, kl_keep, owner_slots, width
    )
    got = lax.ppermute(send, "pa", pairs("pa", 1))
    summed = [(mine[step] + got[step]).astype(jnp.bfloat16) for step in range(owners)]
    blocks = [summed[0]] + [
        lax.ppermute(summed[step], "ma", pairs("ma", step)) for step in range(1, owners)
    ]
    tables = (slot_column, rows_column, kl_basis, blocks)
    send = kl_project(1, jnp.bfloat16, *tables)
    got = lax.ppermute(send, "af", pairs("af", 1))
    mine = kl_project(0, jnp.float32, *tables)
    return unpack(scalars, mine, got, owner_slots, modes)


def kernels_fit(mesh, args):
    panels, svd_basis, kl_basis = args[:3]
    slots = panels.shape[0] // mesh.shape["grp"]
    freqs = svd_basis.shape[0] // (mesh.shape["af"] * mesh.shape["ma"])
    owner_slots = kl_basis.shape[0] // (mesh.shape["pa"] * mesh.shape["ma"])
    share_rows = kl_basis.shape[1] // mesh.shape["af"]
    return (
        freqs % (2 * GROUP) == 0
        and slots % (GROUP * mesh.shape["pa"]) == 0
        and owner_slots == 4
        and svd_basis.shape[2] == 2 * LANES
        and share_rows % GROUP == 0
        and mesh.shape["pa"] == 2
        and mesh.shape["af"] == 2
        and mesh.shape["ma"] in (2, 4)
    )


def solution(mesh):
    in_specs = (
        P("grp", ("af", "ma"), "pa"),
        P(("af", "ma"), "pa", None),
        P(("pa", "ma"), None, "af"),
        P(),
        P(),
        P(),
    )
    out_specs = P(("grp", "pa", "ma"), "af", None)

    def run(*args):
        body = shards if kernels_fit(mesh, args) else shards_plain
        mapped = jax.shard_map(
            body, mesh=mesh, in_specs=in_specs, out_specs=out_specs, check_vma=False
        )
        return mapped(*args)

    return run
```

```python
import functools

import jax
import jax.numpy as jnp
from jax import lax
from jax.experimental import pallas as pl
from jax.experimental.pallas import tpu as pltpu
from jax.sharding import PartitionSpec as P

LANES = 128
GROUP = 16
PER_COPY = 4
OWNER_BUDGET = 576
MIB = 2**20


def shards_plain(panels, svd_basis, kl_basis, slot_of_m, svd_keep, kl_keep):
    slot_count = slot_of_m.shape[0]
    order_slots = jnp.argsort(slot_of_m)
    keep_slots = jnp.take(svd_keep, order_slots, axis=0)
    modes_slots = jnp.take(kl_keep, order_slots, axis=0)
    width_modes = svd_basis.shape[2]
    owner_rows = kl_basis.shape[0]
    slot_rows = slot_count // lax.axis_size("pa")
    slot_start = lax.axis_index("pa") * slot_rows
    owner_start = slot_start + lax.axis_index("ma") * owner_rows
    modes_owner = lax.dynamic_slice_in_dim(modes_slots, owner_start, owner_rows, 0)
    chosen = jnp.take(panels, order_slots, axis=0)
    summed = lax.psum_scatter(
        jnp.einsum("mfb,fbr->mfr", chosen, svd_basis, preferred_element_type=jnp.float32),
        "pa",
        scatter_dimension=0,
        tiled=True,
    )
    keep_here = lax.dynamic_slice_in_dim(keep_slots, slot_start, slot_rows, 0)
    columns = jnp.arange(width_modes, dtype=jnp.int32)
    retained = jnp.where(columns[None, None, :] < keep_here[:, None, None], summed, 0.0).astype(
        jnp.bfloat16
    )
    relaid = lax.all_to_all(retained, "ma", split_axis=0, concat_axis=1, tiled=True)
    partial_sums = jnp.einsum("mkf,mfr->mkr", kl_basis, relaid, preferred_element_type=jnp.float32)
    modes = jnp.arange(kl_basis.shape[1], dtype=jnp.int32)
    partial_sums = jnp.where(modes[None, :, None] < modes_owner[:, None, None], partial_sums, 0.0)
    return lax.psum_scatter(partial_sums, "af", scatter_dimension=1, tiled=True)


def cyclic(value, count):
    return lax.rem(value + count, count)


def on_ring(z):
    return z ^ (z // 2) if isinstance(z, int) else z ^ lax.shift_right_logical(z, 1)


def far_step(owners):
    return owners // 2


def place_of(slot, owner_slots, half_slots):
    half = cyclic(lax.div(slot, half_slots) - lax.axis_index("pa"), lax.axis_size("pa"))
    within = lax.rem(slot, half_slots)
    owner = on_ring(lax.div(within, owner_slots)) - on_ring(lax.axis_index("ma"))
    owner = cyclic(owner, lax.axis_size("ma"))
    return half * half_slots + owner * owner_slots + lax.rem(within, owner_slots)


def offsets_of(keep_place, tile_place, shift_place, owner_slots):
    @pl.loop(0, keep_place.shape[0] // owner_slots)
    def _(at):
        offset = jnp.int32(0)
        for j in range(owner_slots):
            place = at * owner_slots + j
            tile = lax.div(offset, LANES)
            tile_place[place] = tile
            shift_place[place] = offset - tile * LANES
            offset = offset + keep_place[place]


def pack(out_v, mine, far, near, line, tables, owners_at):
    tile_place, shift_place, owner_slots = tables
    owners, width_tiles = mine.shape[:2]
    slots = 2 * owners * owner_slots
    tiles = out_v.shape[0] // (GROUP * slots)
    lane = lax.broadcasted_iota(jnp.int32, (GROUP, LANES), 1)
    rows = pl.ds(pl.multiple_of(line, GROUP), GROUP)
    turned = {
        place: pltpu.roll(
            out_v[pl.ds(place, tiles * GROUP, stride=slots), :], shift_place[place], 1
        )
        for place in range(owners_at[0] * owner_slots, (owners_at[-1] + 1) * owner_slots)
    }
    for at in owners_at:
        to, owner = mine, at % owners
        if at >= owners:
            first = far_step(owners)
            to, owner = (far, 0) if owner == first else (near, owner - (owner > first))
        values, tile_before = None, None
        for j in range(owner_slots):
            place = at * owner_slots + j
            tile = tile_place[place]
            left = lane < shift_place[place]
            moved = [turned[place][t * GROUP : (t + 1) * GROUP] for t in range(tiles)]
            shared = moved[0]
            if j > 0:
                step = tile - tile_before
                shared = values[0]
                for t in range(1, tiles + 1):
                    shared = jnp.where(step == t, values[t], shared)
            values = (
                [jnp.where(left, shared, moved[0])]
                + [jnp.where(left, moved[t - 1], moved[t]) for t in range(1, tiles)]
                + [moved[tiles - 1]]
            )
            tile_before = tile
            for t in reversed(range(tiles + 1)):
                to[owner, jnp.minimum(tile + t, width_tiles - 1), rows, :] = values[t]


def project_kernel(
    owner_slots, slot_hbm, keep_hbm, rows_hbm, panels, basis,
    mine, far, near, slot_column, rows_column, scalars,
    slot_s, keep_s, rows_s, keep_place, rows_place, tile_place, shift_place,
    panels_v, basis_v, lhs_v, out_even, out_odd, small_sem, panel_sem, basis_sem,
):
    slots, freqs, depth = panels_v.shape
    groups = freqs // GROUP
    half_slots = slots // lax.axis_size("pa")

    table_copies = [
        pltpu.make_async_copy(slot_hbm, slot_s, small_sem.at[0]),
        pltpu.make_async_copy(keep_hbm, keep_s, small_sem.at[1]),
        pltpu.make_async_copy(rows_hbm, rows_s, small_sem.at[2]),
    ]
    for copy in table_copies:
        copy.start()

    def basis_copy(i):
        part = pl.ds(i * PER_COPY, PER_COPY)
        return pltpu.make_async_copy(basis.at[part], basis_v.at[part], basis_sem.at[i])

    ahead = 2
    for i in range(ahead):
        basis_copy(i).start()
    for copy in table_copies:
        copy.wait()

    per_group = GROUP // PER_COPY
    for group in range(groups):
        part = pl.ds(group * GROUP, GROUP)

        @pl.loop(0, slots)
        def _(m):
            place = place_of(slot_s[m], owner_slots, half_slots)
            if group == 0:
                keep_place[place] = keep_s[m]
                rows_place[place] = rows_s[m]
            pltpu.make_async_copy(
                panels.at[m, part], panels_v.at[place, part], panel_sem.at[group]
            ).start()

        for i in range(ahead + group * per_group, min(ahead + (group + 1) * per_group, groups * per_group)):
            basis_copy(i).start()

    offsets_of(keep_place, tile_place, shift_place, owner_slots)
    column = lax.broadcasted_iota(jnp.int32, slot_column.shape, 1)
    slot_at = jnp.full(slot_column.shape, owner_slots, jnp.int32)
    rows_at = jnp.zeros(slot_column.shape, jnp.int32)
    for j in range(owner_slots):
        keep = keep_place[j]
        offset = tile_place[j] * LANES + shift_place[j]
        within = (column >= offset) & (column < offset + keep)
        slot_at = jnp.where(within, j, slot_at)
        rows_at = jnp.where(within, rows_place[j], rows_at)
        scalars[j : j + 1, :] = jnp.full((1, LANES), offset, jnp.int32)
        scalars[owner_slots + j : owner_slots + j + 1, :] = jnp.full((1, LANES), keep, jnp.int32)
    slot_column[...] = slot_at
    rows_column[...] = rows_at

    side = GROUP * GROUP
    row = lax.broadcasted_iota(jnp.int32, (side, side), 0)
    column = lax.broadcasted_iota(jnp.int32, (side, side), 1)
    swap = (column == (row % GROUP) * GROUP + row // GROUP).astype(jnp.float32).astype(jnp.bfloat16)

    tables = (tile_place, shift_place, owner_slots)
    all_owners = range(mine.shape[0] * lax.axis_size("pa"))
    share = len(all_owners) // per_group

    def group_step(group, out_v, out_before):
        here = pl.ds(pl.multiple_of(group * GROUP, GROUP), GROUP)
        pltpu.make_async_copy(
            panels_v.at[:, here], panels_v.at[:, here], panel_sem.at[group]
        ).wait()
        for block in range(slots // GROUP):
            blocks = slice(block * GROUP, (block + 1) * GROUP)
            tile = panels_v[blocks, here, :].reshape(side, depth)
            turned = jnp.dot(swap, tile, preferred_element_type=jnp.float32).astype(jnp.bfloat16)
            lhs_v[:, blocks, :] = turned.reshape(GROUP, GROUP, depth)
        for i in range(per_group):
            basis_copy(group * per_group + i).wait()
            for f in range(i * PER_COPY, (i + 1) * PER_COPY):
                product = jnp.dot(
                    lhs_v[f], basis_v[group * GROUP + f], preferred_element_type=jnp.float32
                )
                for t in range(product.shape[1] // LANES):
                    at = (t * GROUP + f) * slots
                    out_v[at : at + slots, :] = product[:, t * LANES : (t + 1) * LANES]
            line = jnp.maximum(group - 1, 0) * GROUP
            pack(out_before, mine, far, near, line, tables, all_owners[i * share : (i + 1) * share])

    @pl.loop(0, groups // 2)
    def _(pair):
        group_step(2 * pair, out_even, out_odd)
        group_step(2 * pair + 1, out_odd, out_even)

    for i in range(per_group):
        part = all_owners[i * share : (i + 1) * share]
        pack(out_odd, mine, far, near, (groups - 1) * GROUP, tables, part)


def sum_kernel(steps, mine, got, *out):
    for i, step in enumerate(steps):
        out[i][...] = (mine[step] + got[i]).astype(out[i].dtype)


def kl_kernel(part, owners, slot_column, rows_column, kl, *refs):
    blocks, (out, packed_v) = refs[:owners], refs[owners:]
    owner_slots, rows, freqs = kl.shape
    shares = lax.axis_size("af")
    per_source = freqs // owners
    me = lax.axis_index("ma")
    for step in range(owners):
        source = on_ring(cyclic(on_ring(me) - step, owners))
        at = pl.multiple_of(source * per_source, GROUP)
        for t in range(blocks[step].shape[0]):
            packed_v[pl.ds(at, per_source), t * LANES : (t + 1) * LANES] = blocks[step][t]
    share_rows, width = out.shape
    at = pl.multiple_of(cyclic(lax.axis_index("af") + part, shares) * share_rows, GROUP)
    lhs = kl[:, pl.ds(at, share_rows), :].reshape(owner_slots * share_rows, freqs)
    product = jnp.dot(lhs, packed_v[...], preferred_element_type=jnp.float32)
    line = lax.broadcasted_iota(jnp.int32, (share_rows, width), 0) + at
    slot_at = slot_column[0:1, :]
    total = jnp.zeros((share_rows, width), jnp.float32)
    for j in range(owner_slots):
        here = product[j * share_rows : (j + 1) * share_rows]
        total = jnp.where(slot_at == j, here, total)
    out[...] = jnp.where(line < rows_column[0:1, :], total, 0.0).astype(out.dtype)


def unpack_kernel(scalars, mine, got, out, sum_v):
    owner_slots, rows, modes = out.shape
    width = mine.shape[1]
    sum_v[:, :width] = mine[...] + got[...].astype(jnp.float32)
    lane = lax.broadcasted_iota(jnp.int32, (rows, LANES), 1)
    for j in range(owner_slots):
        offset = jnp.max(scalars[j : j + 1, :])
        keep = jnp.max(scalars[owner_slots + j : owner_slots + j + 1, :])
        tile = lax.div(offset, LANES)
        shift = offset - tile * LANES
        back = lax.rem(LANES - shift, LANES)
        turned = [
            pltpu.roll(
                sum_v[:, pl.ds(pl.multiple_of((tile + t) * LANES, LANES), LANES)], back, 1
            )
            for t in range(modes // LANES + 1)
        ]
        for t in range(modes // LANES):
            value = jnp.where(lane < LANES - shift, turned[t], turned[t + 1])
            value = jnp.where(lane < keep - t * LANES, value, 0.0)
            out[j, :, t * LANES : (t + 1) * LANES] = value


HBM = pl.BlockSpec(memory_space=pltpu.HBM)
VMEM = pl.BlockSpec(memory_space=pltpu.VMEM)
SMALL = pltpu.CompilerParams(vmem_limit_bytes=8 * MIB)


def in_hbm(operand):
    return pltpu.with_memory_space_constraint(operand, pltpu.HBM)


def project(panels, svd_basis, slot_of_m, svd_keep, kl_keep, owner_slots, width):
    slots, freqs, depth = panels.shape
    modes = svd_basis.shape[2]
    owners = lax.axis_size("ma")

    def packed(count):
        return jax.ShapeDtypeStruct((count, width // LANES, freqs, LANES), jnp.float32)

    column = jax.ShapeDtypeStruct((8, width), jnp.int32)
    return pl.pallas_call(
        functools.partial(project_kernel, owner_slots),
        out_shape=(
            packed(owners),
            packed(1),
            packed(owners - 1),
            column,
            column,
            jax.ShapeDtypeStruct((8, LANES), jnp.int32),
        ),
        in_specs=[HBM] * 5,
        out_specs=(VMEM,) * 6,
        scratch_shapes=[pltpu.SMEM((slots,), jnp.int32)] * 7
        + [
            pltpu.VMEM((slots, freqs, depth), jnp.bfloat16),
            pltpu.VMEM((freqs, depth, modes), jnp.bfloat16),
            pltpu.VMEM((GROUP, slots, depth), jnp.bfloat16),
            pltpu.VMEM((modes // LANES * GROUP * slots, LANES), jnp.float32),
            pltpu.VMEM((modes // LANES * GROUP * slots, LANES), jnp.float32),
            pltpu.SemaphoreType.DMA((3,)),
            pltpu.SemaphoreType.DMA((freqs // GROUP,)),
            pltpu.SemaphoreType.DMA((freqs // PER_COPY,)),
        ],
        compiler_params=pltpu.CompilerParams(vmem_limit_bytes=48 * MIB),
        cost_estimate=pl.CostEstimate(
            flops=2 * slots * freqs * depth * modes,
            bytes_accessed=2 * freqs * depth * (modes + slots),
            transcendentals=0,
        ),
        name="project",
    )(*map(in_hbm, (slot_of_m, svd_keep, kl_keep, panels, svd_basis)))


def sum_pair(steps, mine, got):
    kind = jax.ShapeDtypeStruct(mine.shape[1:], jnp.bfloat16)
    return pl.pallas_call(
        functools.partial(sum_kernel, steps),
        out_shape=(kind,) * len(steps),
        in_specs=[VMEM] * 2,
        out_specs=(VMEM,) * len(steps),
        compiler_params=SMALL,
        cost_estimate=pl.CostEstimate(
            flops=got.size, bytes_accessed=10 * got.size, transcendentals=0
        ),
        name="sum_pair",
    )(mine, got)


def kl_project(part, kind, slot_column, rows_column, kl_basis, blocks):
    owners, shares = lax.axis_size("ma"), lax.axis_size("af")
    rows, freqs = kl_basis.shape[1:]
    width = slot_column.shape[1]
    return pl.pallas_call(
        functools.partial(kl_kernel, part, owners),
        out_shape=jax.ShapeDtypeStruct((rows // shares, width), kind),
        in_specs=[VMEM] * (3 + owners),
        out_specs=VMEM,
        scratch_shapes=[pltpu.VMEM((freqs, width), jnp.bfloat16)],
        compiler_params=SMALL,
        cost_estimate=pl.CostEstimate(
            flops=2 * kl_basis.size * width // shares,
            bytes_accessed=2 * kl_basis.size,
            transcendentals=0,
        ),
        name="kl_project",
    )(slot_column, rows_column, kl_basis, *blocks)


def unpack(scalars, mine, got, owner_slots, modes):
    rows, width = mine.shape
    return pl.pallas_call(
        unpack_kernel,
        out_shape=jax.ShapeDtypeStruct((owner_slots, rows, modes), jnp.float32),
        in_specs=[VMEM] * 3,
        out_specs=VMEM,
        scratch_shapes=[pltpu.VMEM((rows, width + modes + LANES), jnp.float32)],
        compiler_params=SMALL,
        cost_estimate=pl.CostEstimate(
            flops=rows * width, bytes_accessed=10 * rows * width, transcendentals=0
        ),
        name="unpack",
    )(scalars, mine, got)


def pairs(axis):
    return [(i, i ^ 1) for i in range(lax.axis_size(axis))]


def ring(step):
    size = lax.axis_size("ma")
    return [(i, on_ring((on_ring(i) + step) % size)) for i in range(size)]


def shards(panels, svd_basis, kl_basis, slot_of_m, svd_keep, kl_keep):
    owner_slots, modes = kl_basis.shape[0], svd_basis.shape[2]
    owners = lax.axis_size("ma")
    width = -(-min(OWNER_BUDGET, owner_slots * modes) // LANES) * LANES
    mine, far, near, slot_column, rows_column, scalars = project(
        panels, svd_basis, slot_of_m, svd_keep, kl_keep, owner_slots, width
    )
    first = far_step(owners)
    others = [step for step in range(owners) if step != first]
    got_far = lax.ppermute(far, "pa", pairs("pa"))
    near, got_far = lax.optimization_barrier((near, got_far))
    got_near = lax.ppermute(near, "pa", pairs("pa"))
    summed = dict(zip([first], sum_pair([first], mine, got_far)))
    summed |= zip(others, sum_pair(others, mine, got_near))
    blocks = {
        step: lax.ppermute(summed[step], "ma", ring(step)) if step else summed[step]
        for step in [first] + others
    }
    tables = (slot_column, rows_column, kl_basis, [blocks[step] for step in range(owners)])
    send = kl_project(1, jnp.bfloat16, *tables)
    got = lax.ppermute(send, "af", pairs("af"))
    mine = kl_project(0, jnp.float32, *tables)
    return unpack(scalars, mine, got, owner_slots, modes)


def kernels_fit(mesh, args):
    panels, svd_basis, kl_basis = args[:3]
    slots = panels.shape[0] // mesh.shape["grp"]
    freqs = svd_basis.shape[0] // (mesh.shape["af"] * mesh.shape["ma"])
    owner_slots = kl_basis.shape[0] // (mesh.shape["pa"] * mesh.shape["ma"])
    share_rows = kl_basis.shape[1] // mesh.shape["af"]
    return (
        freqs % (2 * GROUP) == 0
        and slots % (GROUP * mesh.shape["pa"]) == 0
        and owner_slots == 4
        and svd_basis.shape[2] == 2 * LANES
        and share_rows % GROUP == 0
        and mesh.shape["pa"] == 2
        and mesh.shape["af"] == 2
        and mesh.shape["ma"] == 4
    )


def solution(mesh):
    in_specs = (
        P("grp", ("af", "ma"), "pa"),
        P(("af", "ma"), "pa", None),
        P(("pa", "ma"), None, "af"),
        P(),
        P(),
        P(),
    )
    out_specs = P(("grp", "pa", "ma"), "af", None)

    def run(*args):
        body = shards if kernels_fit(mesh, args) else shards_plain
        mapped = jax.shard_map(
            body, mesh=mesh, in_specs=in_specs, out_specs=out_specs, check_vma=False
        )
        return mapped(*args)

    return run
```

```python
import functools

import jax
import jax.numpy as jnp
from jax import lax
from jax.experimental import pallas as pl
from jax.experimental.pallas import tpu as pltpu
from jax.sharding import PartitionSpec as P

LANES = 128
GROUP = 16
PER_COPY = 8
OWNER_BUDGET = 576
MIB = 2**20


def shards_plain(panels, svd_basis, kl_basis, slot_of_m, svd_keep, kl_keep):
    slot_count = slot_of_m.shape[0]
    order_slots = jnp.argsort(slot_of_m)
    keep_slots = jnp.take(svd_keep, order_slots, axis=0)
    modes_slots = jnp.take(kl_keep, order_slots, axis=0)
    width_modes = svd_basis.shape[2]
    owner_rows = kl_basis.shape[0]
    slot_rows = slot_count // lax.axis_size("pa")
    slot_start = lax.axis_index("pa") * slot_rows
    owner_start = slot_start + lax.axis_index("ma") * owner_rows
    modes_owner = lax.dynamic_slice_in_dim(modes_slots, owner_start, owner_rows, 0)
    chosen = jnp.take(panels, order_slots, axis=0)
    summed = lax.psum_scatter(
        jnp.einsum("mfb,fbr->mfr", chosen, svd_basis, preferred_element_type=jnp.float32),
        "pa",
        scatter_dimension=0,
        tiled=True,
    )
    keep_here = lax.dynamic_slice_in_dim(keep_slots, slot_start, slot_rows, 0)
    columns = jnp.arange(width_modes, dtype=jnp.int32)
    retained = jnp.where(columns[None, None, :] < keep_here[:, None, None], summed, 0.0).astype(
        jnp.bfloat16
    )
    relaid = lax.all_to_all(retained, "ma", split_axis=0, concat_axis=1, tiled=True)
    partial_sums = jnp.einsum("mkf,mfr->mkr", kl_basis, relaid, preferred_element_type=jnp.float32)
    modes = jnp.arange(kl_basis.shape[1], dtype=jnp.int32)
    partial_sums = jnp.where(modes[None, :, None] < modes_owner[:, None, None], partial_sums, 0.0)
    return lax.psum_scatter(partial_sums, "af", scatter_dimension=1, tiled=True)


def cyclic(value, count):
    return lax.rem(value + count, count)


def on_ring(z):
    return z ^ (z // 2) if isinstance(z, int) else z ^ lax.shift_right_logical(z, 1)


def far_step(owners):
    return owners // 2


def place_of(slot, owner_slots, half_slots):
    half = cyclic(lax.div(slot, half_slots) - lax.axis_index("pa"), lax.axis_size("pa"))
    within = lax.rem(slot, half_slots)
    owner = on_ring(lax.div(within, owner_slots)) - on_ring(lax.axis_index("ma"))
    owner = cyclic(owner, lax.axis_size("ma"))
    return half * half_slots + owner * owner_slots + lax.rem(within, owner_slots)


def offsets_of(keep_place, tile_place, shift_place, owner_slots):
    @pl.loop(0, keep_place.shape[0] // owner_slots)
    def _(at):
        offset = jnp.int32(0)
        for j in range(owner_slots):
            place = at * owner_slots + j
            tile = lax.div(offset, LANES)
            tile_place[place] = tile
            shift_place[place] = offset - tile * LANES
            offset = offset + keep_place[place]


def pack(out_v, mine, far, near, line, tables, owners_at):
    tile_place, shift_place, owner_slots = tables
    owners, width_tiles = mine.shape[:2]
    slots = 2 * owners * owner_slots
    tiles = out_v.shape[0] // (GROUP * slots)
    lane = lax.broadcasted_iota(jnp.int32, (GROUP, LANES), 1)
    rows = pl.ds(pl.multiple_of(line, GROUP), GROUP)
    turned = {
        place: pltpu.roll(
            out_v[pl.ds(place, tiles * GROUP, stride=slots), :], shift_place[place], 1
        )
        for place in range(owners_at[0] * owner_slots, (owners_at[-1] + 1) * owner_slots)
    }
    for at in owners_at:
        to, owner = mine, at % owners
        if at >= owners:
            first = far_step(owners)
            to, owner = (far, 0) if owner == first else (near, owner - (owner > first))
        values, tile_before = None, None
        for j in range(owner_slots):
            place = at * owner_slots + j
            tile = tile_place[place]
            left = lane < shift_place[place]
            moved = [turned[place][t * GROUP : (t + 1) * GROUP] for t in range(tiles)]
            shared = moved[0]
            if j > 0:
                step = tile - tile_before
                shared = values[0]
                for t in range(1, tiles + 1):
                    shared = jnp.where(step == t, values[t], shared)
            values = (
                [jnp.where(left, shared, moved[0])]
                + [jnp.where(left, moved[t - 1], moved[t]) for t in range(1, tiles)]
                + [moved[tiles - 1]]
            )
            tile_before = tile
            for t in reversed(range(tiles + 1)):
                to[owner, jnp.minimum(tile + t, width_tiles - 1), rows, :] = values[t]


def project_kernel(
    owner_slots, slot_hbm, keep_hbm, rows_hbm, panels, basis,
    mine, far, near, slot_column, rows_column, scalars,
    slot_s, keep_s, rows_s, keep_place, rows_place, tile_place, shift_place,
    panels_v, basis_v, lhs_v, out_even, out_odd, small_sem, panel_sem, basis_sem,
):
    slots, freqs, depth = panels_v.shape
    groups = freqs // GROUP
    half_slots = slots // lax.axis_size("pa")

    table_copies = [
        pltpu.make_async_copy(slot_hbm, slot_s, small_sem.at[0]),
        pltpu.make_async_copy(keep_hbm, keep_s, small_sem.at[1]),
        pltpu.make_async_copy(rows_hbm, rows_s, small_sem.at[2]),
    ]
    for copy in table_copies:
        copy.start()

    def basis_copy(i):
        part = pl.ds(i * PER_COPY, PER_COPY)
        return pltpu.make_async_copy(basis.at[part], basis_v.at[part], basis_sem.at[i])

    ahead = 1
    for i in range(ahead):
        basis_copy(i).start()
    for copy in table_copies:
        copy.wait()

    per_group = GROUP // PER_COPY
    for group in range(groups):
        part = pl.ds(group * GROUP, GROUP)

        @pl.loop(0, slots)
        def _(m):
            place = place_of(slot_s[m], owner_slots, half_slots)
            if group == 0:
                keep_place[place] = keep_s[m]
                rows_place[place] = rows_s[m]
            pltpu.make_async_copy(
                panels.at[m, part], panels_v.at[place, part], panel_sem.at[group]
            ).start()

        for i in range(ahead + group * per_group, min(ahead + (group + 1) * per_group, groups * per_group)):
            basis_copy(i).start()

    offsets_of(keep_place, tile_place, shift_place, owner_slots)
    column = lax.broadcasted_iota(jnp.int32, slot_column.shape, 1)
    slot_at = jnp.full(slot_column.shape, owner_slots, jnp.int32)
    rows_at = jnp.zeros(slot_column.shape, jnp.int32)
    for j in range(owner_slots):
        keep = keep_place[j]
        offset = tile_place[j] * LANES + shift_place[j]
        within = (column >= offset) & (column < offset + keep)
        slot_at = jnp.where(within, j, slot_at)
        rows_at = jnp.where(within, rows_place[j], rows_at)
        scalars[j : j + 1, :] = jnp.full((1, LANES), offset, jnp.int32)
        scalars[owner_slots + j : owner_slots + j + 1, :] = jnp.full((1, LANES), keep, jnp.int32)
    slot_column[...] = slot_at
    rows_column[...] = rows_at

    side = GROUP * GROUP
    row = lax.broadcasted_iota(jnp.int32, (side, side), 0)
    column = lax.broadcasted_iota(jnp.int32, (side, side), 1)
    swap = (column == (row % GROUP) * GROUP + row // GROUP).astype(jnp.float32).astype(jnp.bfloat16)

    tables = (tile_place, shift_place, owner_slots)
    all_owners = range(mine.shape[0] * lax.axis_size("pa"))
    share = len(all_owners) // per_group

    def group_step(group, out_v, out_before):
        here = pl.ds(pl.multiple_of(group * GROUP, GROUP), GROUP)
        pltpu.make_async_copy(
            panels_v.at[:, here], panels_v.at[:, here], panel_sem.at[group]
        ).wait()
        for block in range(slots // GROUP):
            blocks = slice(block * GROUP, (block + 1) * GROUP)
            tile = panels_v[blocks, here, :].reshape(side, depth)
            turned = jnp.dot(swap, tile, preferred_element_type=jnp.float32).astype(jnp.bfloat16)
            lhs_v[:, blocks, :] = turned.reshape(GROUP, GROUP, depth)
        for i in range(per_group):
            basis_copy(group * per_group + i).wait()
            for f in range(i * PER_COPY, (i + 1) * PER_COPY):
                product = jnp.dot(
                    lhs_v[f], basis_v[group * GROUP + f], preferred_element_type=jnp.float32
                )
                for t in range(product.shape[1] // LANES):
                    at = (t * GROUP + f) * slots
                    out_v[at : at + slots, :] = product[:, t * LANES : (t + 1) * LANES]
            line = jnp.maximum(group - 1, 0) * GROUP
            pack(out_before, mine, far, near, line, tables, all_owners[i * share : (i + 1) * share])

    @pl.loop(0, groups // 2)
    def _(pair):
        group_step(2 * pair, out_even, out_odd)
        group_step(2 * pair + 1, out_odd, out_even)

    for i in range(per_group):
        part = all_owners[i * share : (i + 1) * share]
        pack(out_odd, mine, far, near, (groups - 1) * GROUP, tables, part)


def sum_kernel(steps, mine, got, *out):
    for i, step in enumerate(steps):
        out[i][...] = (mine[step] + got[i]).astype(out[i].dtype)


def kl_kernel(part, owners, slot_column, rows_column, kl, *refs):
    blocks, (out, packed_v) = refs[:owners], refs[owners:]
    owner_slots, rows, freqs = kl.shape
    shares = lax.axis_size("af")
    per_source = freqs // owners
    me = lax.axis_index("ma")
    for step in range(owners):
        source = on_ring(cyclic(on_ring(me) - step, owners))
        at = pl.multiple_of(source * per_source, GROUP)
        for t in range(blocks[step].shape[0]):
            packed_v[pl.ds(at, per_source), t * LANES : (t + 1) * LANES] = blocks[step][t]
    share_rows, width = out.shape
    at = pl.multiple_of(cyclic(lax.axis_index("af") + part, shares) * share_rows, GROUP)
    lhs = kl[:, pl.ds(at, share_rows), :].reshape(owner_slots * share_rows, freqs)
    product = jnp.dot(lhs, packed_v[...], preferred_element_type=jnp.float32)
    line = lax.broadcasted_iota(jnp.int32, (share_rows, width), 0) + at
    slot_at = slot_column[0:1, :]
    total = jnp.zeros((share_rows, width), jnp.float32)
    for j in range(owner_slots):
        here = product[j * share_rows : (j + 1) * share_rows]
        total = jnp.where(slot_at == j, here, total)
    out[...] = jnp.where(line < rows_column[0:1, :], total, 0.0).astype(out.dtype)


def unpack_kernel(scalars, mine, got, out, sum_v):
    owner_slots, rows, modes = out.shape
    width = mine.shape[1]
    sum_v[:, :width] = mine[...] + got[...].astype(jnp.float32)
    lane = lax.broadcasted_iota(jnp.int32, (rows, LANES), 1)
    for j in range(owner_slots):
        offset = jnp.max(scalars[j : j + 1, :])
        keep = jnp.max(scalars[owner_slots + j : owner_slots + j + 1, :])
        tile = lax.div(offset, LANES)
        shift = offset - tile * LANES
        back = lax.rem(LANES - shift, LANES)
        turned = [
            pltpu.roll(
                sum_v[:, pl.ds(pl.multiple_of((tile + t) * LANES, LANES), LANES)], back, 1
            )
            for t in range(modes // LANES + 1)
        ]
        for t in range(modes // LANES):
            value = jnp.where(lane < LANES - shift, turned[t], turned[t + 1])
            value = jnp.where(lane < keep - t * LANES, value, 0.0)
            out[j, :, t * LANES : (t + 1) * LANES] = value


HBM = pl.BlockSpec(memory_space=pltpu.HBM)
VMEM = pl.BlockSpec(memory_space=pltpu.VMEM)
SMALL = pltpu.CompilerParams(vmem_limit_bytes=8 * MIB)


def in_hbm(operand):
    return pltpu.with_memory_space_constraint(operand, pltpu.HBM)


def project(panels, svd_basis, slot_of_m, svd_keep, kl_keep, owner_slots, width):
    slots, freqs, depth = panels.shape
    modes = svd_basis.shape[2]
    owners = lax.axis_size("ma")

    def packed(count):
        return jax.ShapeDtypeStruct((count, width // LANES, freqs, LANES), jnp.float32)

    column = jax.ShapeDtypeStruct((8, width), jnp.int32)
    return pl.pallas_call(
        functools.partial(project_kernel, owner_slots),
        out_shape=(
            packed(owners),
            packed(1),
            packed(owners - 1),
            column,
            column,
            jax.ShapeDtypeStruct((8, LANES), jnp.int32),
        ),
        in_specs=[HBM] * 5,
        out_specs=(VMEM,) * 6,
        scratch_shapes=[pltpu.SMEM((slots,), jnp.int32)] * 7
        + [
            pltpu.VMEM((slots, freqs, depth), jnp.bfloat16),
            pltpu.VMEM((freqs, depth, modes), jnp.bfloat16),
            pltpu.VMEM((GROUP, slots, depth), jnp.bfloat16),
            pltpu.VMEM((modes // LANES * GROUP * slots, LANES), jnp.float32),
            pltpu.VMEM((modes // LANES * GROUP * slots, LANES), jnp.float32),
            pltpu.SemaphoreType.DMA((3,)),
            pltpu.SemaphoreType.DMA((freqs // GROUP,)),
            pltpu.SemaphoreType.DMA((freqs // PER_COPY,)),
        ],
        compiler_params=pltpu.CompilerParams(vmem_limit_bytes=48 * MIB),
        cost_estimate=pl.CostEstimate(
            flops=2 * slots * freqs * depth * modes,
            bytes_accessed=2 * freqs * depth * (modes + slots),
            transcendentals=0,
        ),
        name="project",
    )(*map(in_hbm, (slot_of_m, svd_keep, kl_keep, panels, svd_basis)))


def sum_pair(steps, mine, got):
    kind = jax.ShapeDtypeStruct(mine.shape[1:], jnp.bfloat16)
    return pl.pallas_call(
        functools.partial(sum_kernel, steps),
        out_shape=(kind,) * len(steps),
        in_specs=[VMEM] * 2,
        out_specs=(VMEM,) * len(steps),
        compiler_params=SMALL,
        cost_estimate=pl.CostEstimate(
            flops=got.size, bytes_accessed=10 * got.size, transcendentals=0
        ),
        name="sum_pair",
    )(mine, got)


def kl_project(part, kind, slot_column, rows_column, kl_basis, blocks):
    owners, shares = lax.axis_size("ma"), lax.axis_size("af")
    rows, freqs = kl_basis.shape[1:]
    width = slot_column.shape[1]
    return pl.pallas_call(
        functools.partial(kl_kernel, part, owners),
        out_shape=jax.ShapeDtypeStruct((rows // shares, width), kind),
        in_specs=[VMEM] * (3 + owners),
        out_specs=VMEM,
        scratch_shapes=[pltpu.VMEM((freqs, width), jnp.bfloat16)],
        compiler_params=SMALL,
        cost_estimate=pl.CostEstimate(
            flops=2 * kl_basis.size * width // shares,
            bytes_accessed=2 * kl_basis.size,
            transcendentals=0,
        ),
        name="kl_project",
    )(slot_column, rows_column, kl_basis, *blocks)


def unpack(scalars, mine, got, owner_slots, modes):
    rows, width = mine.shape
    return pl.pallas_call(
        unpack_kernel,
        out_shape=jax.ShapeDtypeStruct((owner_slots, rows, modes), jnp.float32),
        in_specs=[VMEM] * 3,
        out_specs=VMEM,
        scratch_shapes=[pltpu.VMEM((rows, width + modes + LANES), jnp.float32)],
        compiler_params=SMALL,
        cost_estimate=pl.CostEstimate(
            flops=rows * width, bytes_accessed=10 * rows * width, transcendentals=0
        ),
        name="unpack",
    )(scalars, mine, got)


def pairs(axis):
    return [(i, i ^ 1) for i in range(lax.axis_size(axis))]


def ring(step):
    size = lax.axis_size("ma")
    return [(i, on_ring((on_ring(i) + step) % size)) for i in range(size)]


def shards(panels, svd_basis, kl_basis, slot_of_m, svd_keep, kl_keep):
    owner_slots, modes = kl_basis.shape[0], svd_basis.shape[2]
    owners = lax.axis_size("ma")
    width = -(-min(OWNER_BUDGET, owner_slots * modes) // LANES) * LANES
    mine, far, near, slot_column, rows_column, scalars = project(
        panels, svd_basis, slot_of_m, svd_keep, kl_keep, owner_slots, width
    )
    first = far_step(owners)
    others = [step for step in range(owners) if step != first]
    got_far = lax.ppermute(far, "pa", pairs("pa"))
    near, got_far = lax.optimization_barrier((near, got_far))
    got_near = lax.ppermute(near, "pa", pairs("pa"))
    summed = dict(zip([first], sum_pair([first], mine, got_far)))
    summed |= zip(others, sum_pair(others, mine, got_near))
    blocks = {
        step: lax.ppermute(summed[step], "ma", ring(step)) if step else summed[step]
        for step in [first] + others
    }
    tables = (slot_column, rows_column, kl_basis, [blocks[step] for step in range(owners)])
    send = kl_project(1, jnp.bfloat16, *tables)
    got = lax.ppermute(send, "af", pairs("af"))
    mine = kl_project(0, jnp.float32, *tables)
    return unpack(scalars, mine, got, owner_slots, modes)


def kernels_fit(mesh, args):
    panels, svd_basis, kl_basis = args[:3]
    slots = panels.shape[0] // mesh.shape["grp"]
    freqs = svd_basis.shape[0] // (mesh.shape["af"] * mesh.shape["ma"])
    owner_slots = kl_basis.shape[0] // (mesh.shape["pa"] * mesh.shape["ma"])
    share_rows = kl_basis.shape[1] // mesh.shape["af"]
    return (
        freqs % (2 * GROUP) == 0
        and slots % (GROUP * mesh.shape["pa"]) == 0
        and owner_slots == 4
        and svd_basis.shape[2] == 2 * LANES
        and share_rows % GROUP == 0
        and mesh.shape["pa"] == 2
        and mesh.shape["af"] == 2
        and mesh.shape["ma"] == 4
    )


def solution(mesh):
    in_specs = (
        P("grp", ("af", "ma"), "pa"),
        P(("af", "ma"), "pa", None),
        P(("pa", "ma"), None, "af"),
        P(),
        P(),
        P(),
    )
    out_specs = P(("grp", "pa", "ma"), "af", None)

    def run(*args):
        body = shards if kernels_fit(mesh, args) else shards_plain
        mapped = jax.shard_map(
            body, mesh=mesh, in_specs=in_specs, out_specs=out_specs, check_vma=False
        )
        return mapped(*args)

    return run
```

```python
import functools

import jax
import jax.numpy as jnp
from jax import lax
from jax.experimental import pallas as pl
from jax.experimental.pallas import tpu as pltpu
from jax.sharding import PartitionSpec as P

LANES = 128
GROUP = 16
PER_COPY = 8
OWNER_BUDGET = 576
MIB = 2**20


def shards_plain(panels, svd_basis, kl_basis, slot_of_m, svd_keep, kl_keep):
    slot_count = slot_of_m.shape[0]
    order_slots = jnp.argsort(slot_of_m)
    keep_slots = jnp.take(svd_keep, order_slots, axis=0)
    modes_slots = jnp.take(kl_keep, order_slots, axis=0)
    width_modes = svd_basis.shape[2]
    owner_rows = kl_basis.shape[0]
    slot_rows = slot_count // lax.axis_size("pa")
    slot_start = lax.axis_index("pa") * slot_rows
    owner_start = slot_start + lax.axis_index("ma") * owner_rows
    modes_owner = lax.dynamic_slice_in_dim(modes_slots, owner_start, owner_rows, 0)
    chosen = jnp.take(panels, order_slots, axis=0)
    summed = lax.psum_scatter(
        jnp.einsum("mfb,fbr->mfr", chosen, svd_basis, preferred_element_type=jnp.float32),
        "pa",
        scatter_dimension=0,
        tiled=True,
    )
    keep_here = lax.dynamic_slice_in_dim(keep_slots, slot_start, slot_rows, 0)
    columns = jnp.arange(width_modes, dtype=jnp.int32)
    retained = jnp.where(columns[None, None, :] < keep_here[:, None, None], summed, 0.0).astype(
        jnp.bfloat16
    )
    relaid = lax.all_to_all(retained, "ma", split_axis=0, concat_axis=1, tiled=True)
    partial_sums = jnp.einsum("mkf,mfr->mkr", kl_basis, relaid, preferred_element_type=jnp.float32)
    modes = jnp.arange(kl_basis.shape[1], dtype=jnp.int32)
    partial_sums = jnp.where(modes[None, :, None] < modes_owner[:, None, None], partial_sums, 0.0)
    return lax.psum_scatter(partial_sums, "af", scatter_dimension=1, tiled=True)


def cyclic(value, count):
    return lax.rem(value + count, count)


def on_ring(z):
    return z ^ (z // 2) if isinstance(z, int) else z ^ lax.shift_right_logical(z, 1)


def far_step(owners):
    return owners // 2


def place_of(slot, owner_slots, half_slots):
    half = cyclic(lax.div(slot, half_slots) - lax.axis_index("pa"), lax.axis_size("pa"))
    within = lax.rem(slot, half_slots)
    owner = on_ring(lax.div(within, owner_slots)) - on_ring(lax.axis_index("ma"))
    owner = cyclic(owner, lax.axis_size("ma"))
    return half * half_slots + owner * owner_slots + lax.rem(within, owner_slots)


def offsets_of(keep_place, tile_place, shift_place, owner_slots):
    @pl.loop(0, keep_place.shape[0] // owner_slots)
    def _(at):
        offset = jnp.int32(0)
        for j in range(owner_slots):
            place = at * owner_slots + j
            tile = lax.div(offset, LANES)
            tile_place[place] = tile
            shift_place[place] = offset - tile * LANES
            offset = offset + keep_place[place]


def pack(out_v, mine, far, near, line, tables, owners_at):
    tile_place, shift_place, owner_slots = tables
    owners, width_tiles = mine.shape[:2]
    slots = 2 * owners * owner_slots
    tiles = out_v.shape[0] // (GROUP * slots)
    lane = lax.broadcasted_iota(jnp.int32, (GROUP, LANES), 1)
    rows = pl.ds(pl.multiple_of(line, GROUP), GROUP)
    turned = {
        place: pltpu.roll(
            out_v[pl.ds(place, tiles * GROUP, stride=slots), :], shift_place[place], 1
        )
        for place in range(owners_at[0] * owner_slots, (owners_at[-1] + 1) * owner_slots)
    }
    for at in owners_at:
        to, owner = mine, at % owners
        if at >= owners:
            first = far_step(owners)
            to, owner = (far, 0) if owner == first else (near, owner - (owner > first))
        values, tile_before = None, None
        for j in range(owner_slots):
            place = at * owner_slots + j
            tile = tile_place[place]
            left = lane < shift_place[place]
            moved = [turned[place][t * GROUP : (t + 1) * GROUP] for t in range(tiles)]
            shared = moved[0]
            if j > 0:
                step = tile - tile_before
                shared = values[0]
                for t in range(1, tiles + 1):
                    shared = jnp.where(step == t, values[t], shared)
            values = (
                [jnp.where(left, shared, moved[0])]
                + [jnp.where(left, moved[t - 1], moved[t]) for t in range(1, tiles)]
                + [moved[tiles - 1]]
            )
            tile_before = tile
            for t in reversed(range(tiles + 1)):
                to[owner, jnp.minimum(tile + t, width_tiles - 1), rows, :] = values[t]


def project_kernel(
    owner_slots, slot_hbm, keep_hbm, rows_hbm, panels, basis,
    mine, far, near, slot_column, rows_column, scalars,
    slot_s, keep_s, rows_s, keep_place, rows_place, tile_place, shift_place,
    panels_v, basis_v, lhs_v, out_even, out_odd, small_sem, panel_sem, basis_sem,
):
    slots, freqs, depth = panels_v.shape
    groups = freqs // GROUP
    half_slots = slots // lax.axis_size("pa")

    table_copies = [
        pltpu.make_async_copy(slot_hbm, slot_s, small_sem.at[0]),
        pltpu.make_async_copy(keep_hbm, keep_s, small_sem.at[1]),
        pltpu.make_async_copy(rows_hbm, rows_s, small_sem.at[2]),
    ]
    for copy in table_copies:
        copy.start()

    def basis_copy(i):
        part = pl.ds(i * PER_COPY, PER_COPY)
        return pltpu.make_async_copy(basis.at[part], basis_v.at[part], basis_sem.at[i])

    ahead = 1
    for i in range(ahead):
        basis_copy(i).start()
    for copy in table_copies:
        copy.wait()

    per_group = GROUP // PER_COPY
    for group in range(groups):
        part = pl.ds(group * GROUP, GROUP)

        @pl.loop(0, slots)
        def _(m):
            place = place_of(slot_s[m], owner_slots, half_slots)
            if group == 0:
                keep_place[place] = keep_s[m]
                rows_place[place] = rows_s[m]
            pltpu.make_async_copy(
                panels.at[m, part], panels_v.at[place, part], panel_sem.at[group]
            ).start()

        for i in range(ahead + group * per_group, min(ahead + (group + 1) * per_group, groups * per_group)):
            basis_copy(i).start()

    offsets_of(keep_place, tile_place, shift_place, owner_slots)
    column = lax.broadcasted_iota(jnp.int32, slot_column.shape, 1)
    slot_at = jnp.full(slot_column.shape, owner_slots, jnp.int32)
    rows_at = jnp.zeros(slot_column.shape, jnp.int32)
    for j in range(owner_slots):
        keep = keep_place[j]
        offset = tile_place[j] * LANES + shift_place[j]
        within = (column >= offset) & (column < offset + keep)
        slot_at = jnp.where(within, j, slot_at)
        rows_at = jnp.where(within, rows_place[j], rows_at)
        scalars[j : j + 1, :] = jnp.full((1, LANES), offset, jnp.int32)
        scalars[owner_slots + j : owner_slots + j + 1, :] = jnp.full((1, LANES), keep, jnp.int32)
    slot_column[...] = slot_at
    rows_column[...] = rows_at

    side = GROUP * GROUP
    row = lax.broadcasted_iota(jnp.int32, (side, side), 0)
    column = lax.broadcasted_iota(jnp.int32, (side, side), 1)
    swap = (column == (row % GROUP) * GROUP + row // GROUP).astype(jnp.float32).astype(jnp.bfloat16)

    tables = (tile_place, shift_place, owner_slots)
    all_owners = range(mine.shape[0] * lax.axis_size("pa"))
    share = len(all_owners) // per_group

    def group_step(group, out_v, out_before):
        here = pl.ds(pl.multiple_of(group * GROUP, GROUP), GROUP)
        pltpu.make_async_copy(
            panels_v.at[:, here], panels_v.at[:, here], panel_sem.at[group]
        ).wait()
        for block in range(slots // GROUP):
            blocks = slice(block * GROUP, (block + 1) * GROUP)
            tile = panels_v[blocks, here, :].reshape(side, depth)
            turned = jnp.dot(swap, tile, preferred_element_type=jnp.float32).astype(jnp.bfloat16)
            lhs_v[:, blocks, :] = turned.reshape(GROUP, GROUP, depth)
        for i in range(per_group):
            basis_copy(group * per_group + i).wait()
            for f in range(i * PER_COPY, (i + 1) * PER_COPY):
                product = jnp.dot(
                    lhs_v[f], basis_v[group * GROUP + f], preferred_element_type=jnp.float32
                )
                for t in range(product.shape[1] // LANES):
                    at = (t * GROUP + f) * slots
                    out_v[at : at + slots, :] = product[:, t * LANES : (t + 1) * LANES]
            line = jnp.maximum(group - 1, 0) * GROUP
            pack(out_before, mine, far, near, line, tables, all_owners[i * share : (i + 1) * share])

    @pl.loop(0, groups // 2)
    def _(pair):
        group_step(2 * pair, out_even, out_odd)
        group_step(2 * pair + 1, out_odd, out_even)

    for i in range(per_group):
        part = all_owners[i * share : (i + 1) * share]
        pack(out_odd, mine, far, near, (groups - 1) * GROUP, tables, part)


def folded_rows(rows, width):
    whole, rest = divmod(width, LANES)
    return rows * whole + (rows if rest > LANES // 2 else rows // 2 if rest else 0)


def fold(tiles, out, width):
    rows = tiles[0].shape[0]
    lane = lax.broadcasted_iota(jnp.int32, (rows // 2, LANES), 1)
    for t, tile in enumerate(tiles):
        if t == len(tiles) - 1 and out.shape[0] < rows * len(tiles):
            low, high = tile[: rows // 2], tile[rows // 2 :]
            tile = jnp.where(lane < LANES // 2, low, pltpu.roll(high, LANES // 2, 1))
        out[t * rows : t * rows + tile.shape[0], :] = tile.astype(out.dtype)


def unfold(block, rows):
    count = block.shape[0] // rows
    tiles = [block[t * rows : (t + 1) * rows, :] for t in range(count)]
    if count * rows < block.shape[0]:
        low = block[count * rows :, :].astype(jnp.float32)
        high = pltpu.roll(low, LANES // 2, 1)
        tiles.append(jnp.concatenate([low, high], axis=0).astype(block.dtype))
    return tiles


def sum_kernel(steps, width, mine, got, *out):
    for i, step in enumerate(steps):
        tiles = [mine[step, t] + got[i, t] for t in range(mine.shape[1])]
        fold(tiles, out[i], width)


def kl_kernel(part, owners, width, slot_column, rows_column, kl, *refs):
    blocks, (out, packed_v) = refs[:owners], refs[owners:]
    owner_slots, rows, freqs = kl.shape
    shares = lax.axis_size("af")
    per_source = freqs // owners
    me = lax.axis_index("ma")
    for step in range(owners):
        source = on_ring(cyclic(on_ring(me) - step, owners))
        at = pl.multiple_of(source * per_source, GROUP)
        for t, tile in enumerate(unfold(blocks[step], per_source)):
            packed_v[pl.ds(at, per_source), t * LANES : (t + 1) * LANES] = tile
    share_rows = rows // shares
    at = pl.multiple_of(cyclic(lax.axis_index("af") + part, shares) * share_rows, GROUP)
    lhs = kl[:, pl.ds(at, share_rows), :].reshape(owner_slots * share_rows, freqs)
    product = jnp.dot(lhs, packed_v[...], preferred_element_type=jnp.float32)
    line = lax.broadcasted_iota(jnp.int32, (share_rows, LANES), 0) + at
    tiles = []
    for t in range(packed_v.shape[1] // LANES):
        lanes = slice(t * LANES, (t + 1) * LANES)
        slot_at = slot_column[0:1, lanes]
        total = jnp.zeros((share_rows, LANES), jnp.float32)
        for j in range(owner_slots):
            here = product[j * share_rows : (j + 1) * share_rows, lanes]
            total = jnp.where(slot_at == j, here, total)
        tiles.append(jnp.where(line < rows_column[0:1, lanes], total, 0.0))
    fold(tiles, out, width)


def unpack_kernel(scalars, mine, got, out, sum_v, out_v, sems):
    owner_slots, rows, modes = out_v.shape
    places = [
        [jnp.max(scalars[k * owner_slots + j : k * owner_slots + j + 1, :]) for k in range(2)]
        for j in range(owner_slots)
    ]
    for t, (a, b) in enumerate(zip(unfold(mine, rows), unfold(got, rows))):
        sum_v[t] = a + b.astype(jnp.float32)
    lane = lax.broadcasted_iota(jnp.int32, (rows, LANES), 1)
    copies = []
    for j, (offset, keep) in enumerate(places):
        tile = lax.div(offset, LANES)
        shift = offset - tile * LANES
        back = lax.rem(LANES - shift, LANES)
        turned = [pltpu.roll(sum_v[tile + t], back, 1) for t in range(modes // LANES + 1)]
        for t in range(modes // LANES):
            value = jnp.where(lane < LANES - shift, turned[t], turned[t + 1])
            value = jnp.where(lane < keep - t * LANES, value, 0.0)
            out_v[j, :, t * LANES : (t + 1) * LANES] = value
        copy = pltpu.make_async_copy(out_v.at[j], out.at[j], sems.at[j])
        copy.start()
        copies.append(copy)
    for copy in copies:
        copy.wait()


HBM = pl.BlockSpec(memory_space=pltpu.HBM)
VMEM = pl.BlockSpec(memory_space=pltpu.VMEM)
SMALL = pltpu.CompilerParams(vmem_limit_bytes=8 * MIB)


def in_hbm(operand):
    return pltpu.with_memory_space_constraint(operand, pltpu.HBM)


def project(panels, svd_basis, slot_of_m, svd_keep, kl_keep, owner_slots, width):
    slots, freqs, depth = panels.shape
    modes = svd_basis.shape[2]
    owners = lax.axis_size("ma")

    def packed(count):
        return jax.ShapeDtypeStruct((count, width // LANES, freqs, LANES), jnp.float32)

    column = jax.ShapeDtypeStruct((8, width), jnp.int32)
    return pl.pallas_call(
        functools.partial(project_kernel, owner_slots),
        out_shape=(
            packed(owners),
            packed(1),
            packed(owners - 1),
            column,
            column,
            jax.ShapeDtypeStruct((8, LANES), jnp.int32),
        ),
        in_specs=[HBM] * 5,
        out_specs=(VMEM,) * 6,
        scratch_shapes=[pltpu.SMEM((slots,), jnp.int32)] * 7
        + [
            pltpu.VMEM((slots, freqs, depth), jnp.bfloat16),
            pltpu.VMEM((freqs, depth, modes), jnp.bfloat16),
            pltpu.VMEM((GROUP, slots, depth), jnp.bfloat16),
            pltpu.VMEM((modes // LANES * GROUP * slots, LANES), jnp.float32),
            pltpu.VMEM((modes // LANES * GROUP * slots, LANES), jnp.float32),
            pltpu.SemaphoreType.DMA((3,)),
            pltpu.SemaphoreType.DMA((freqs // GROUP,)),
            pltpu.SemaphoreType.DMA((freqs // PER_COPY,)),
        ],
        compiler_params=pltpu.CompilerParams(vmem_limit_bytes=48 * MIB),
        cost_estimate=pl.CostEstimate(
            flops=2 * slots * freqs * depth * modes,
            bytes_accessed=2 * freqs * depth * (modes + slots),
            transcendentals=0,
        ),
        name="project",
    )(*map(in_hbm, (slot_of_m, svd_keep, kl_keep, panels, svd_basis)))


def sum_pair(steps, width, mine, got):
    kind = jax.ShapeDtypeStruct((folded_rows(mine.shape[2], width), LANES), jnp.bfloat16)
    return pl.pallas_call(
        functools.partial(sum_kernel, steps, width),
        out_shape=(kind,) * len(steps),
        in_specs=[VMEM] * 2,
        out_specs=(VMEM,) * len(steps),
        compiler_params=SMALL,
        cost_estimate=pl.CostEstimate(
            flops=got.size, bytes_accessed=10 * got.size, transcendentals=0
        ),
        name="sum_pair",
    )(mine, got)


def kl_project(part, kind, width, slot_column, rows_column, kl_basis, blocks):
    owners, shares = lax.axis_size("ma"), lax.axis_size("af")
    rows, freqs = kl_basis.shape[1:]
    wide = slot_column.shape[1]
    return pl.pallas_call(
        functools.partial(kl_kernel, part, owners, width),
        out_shape=jax.ShapeDtypeStruct((folded_rows(rows // shares, width), LANES), kind),
        in_specs=[VMEM] * (3 + owners),
        out_specs=VMEM,
        scratch_shapes=[pltpu.VMEM((freqs, wide), jnp.bfloat16)],
        compiler_params=SMALL,
        cost_estimate=pl.CostEstimate(
            flops=2 * kl_basis.size * wide // shares,
            bytes_accessed=2 * kl_basis.size,
            transcendentals=0,
        ),
        name="kl_project",
    )(slot_column, rows_column, kl_basis, *blocks)


def unpack(scalars, mine, got, owner_slots, rows, modes, width):
    tiles = -(-width // LANES) + modes // LANES + 1
    return pl.pallas_call(
        unpack_kernel,
        out_shape=jax.ShapeDtypeStruct((owner_slots, rows, modes), jnp.float32),
        in_specs=[VMEM] * 3,
        out_specs=HBM,
        scratch_shapes=[
            pltpu.VMEM((tiles, rows, LANES), jnp.float32),
            pltpu.VMEM((owner_slots, rows, modes), jnp.float32),
            pltpu.SemaphoreType.DMA((owner_slots,)),
        ],
        compiler_params=SMALL,
        cost_estimate=pl.CostEstimate(
            flops=mine.size, bytes_accessed=10 * mine.size, transcendentals=0
        ),
        name="unpack",
    )(scalars, mine, got)


def pairs(axis):
    return [(i, i ^ 1) for i in range(lax.axis_size(axis))]


def ring(step):
    size = lax.axis_size("ma")
    return [(i, on_ring((on_ring(i) + step) % size)) for i in range(size)]


def shards(panels, svd_basis, kl_basis, slot_of_m, svd_keep, kl_keep):
    owner_slots, modes = kl_basis.shape[0], svd_basis.shape[2]
    owners = lax.axis_size("ma")
    width = min(OWNER_BUDGET, owner_slots * modes)
    wide = -(-width // LANES) * LANES
    mine, far, near, slot_column, rows_column, scalars = project(
        panels, svd_basis, slot_of_m, svd_keep, kl_keep, owner_slots, wide
    )
    first = far_step(owners)
    others = [step for step in range(owners) if step != first]
    got_far = lax.ppermute(far, "pa", pairs("pa"))
    near, got_far = lax.optimization_barrier((near, got_far))
    got_near = lax.ppermute(near, "pa", pairs("pa"))
    summed = dict(zip([first], sum_pair([first], width, mine, got_far)))
    summed |= zip(others, sum_pair(others, width, mine, got_near))
    blocks = {
        step: lax.ppermute(summed[step], "ma", ring(step)) if step else summed[step]
        for step in [first] + others
    }
    tables = (width, slot_column, rows_column, kl_basis, [blocks[step] for step in range(owners)])
    send = kl_project(1, jnp.bfloat16, *tables)
    got = lax.ppermute(send, "af", pairs("af"))
    mine = kl_project(0, jnp.float32, *tables)
    rows = kl_basis.shape[1] // lax.axis_size("af")
    return unpack(scalars, mine, got, owner_slots, rows, modes, width)


def kernels_fit(mesh, args):
    panels, svd_basis, kl_basis = args[:3]
    slots = panels.shape[0] // mesh.shape["grp"]
    freqs = svd_basis.shape[0] // (mesh.shape["af"] * mesh.shape["ma"])
    owner_slots = kl_basis.shape[0] // (mesh.shape["pa"] * mesh.shape["ma"])
    share_rows = kl_basis.shape[1] // mesh.shape["af"]
    return (
        freqs % (2 * GROUP) == 0
        and slots % (GROUP * mesh.shape["pa"]) == 0
        and owner_slots == 4
        and svd_basis.shape[2] == 2 * LANES
        and share_rows % (2 * GROUP) == 0
        and mesh.shape["pa"] == 2
        and mesh.shape["af"] == 2
        and mesh.shape["ma"] == 4
    )


def solution(mesh):
    in_specs = (
        P("grp", ("af", "ma"), "pa"),
        P(("af", "ma"), "pa", None),
        P(("pa", "ma"), None, "af"),
        P(),
        P(),
        P(),
    )
    out_specs = P(("grp", "pa", "ma"), "af", None)

    def run(*args):
        body = shards if kernels_fit(mesh, args) else shards_plain
        mapped = jax.shard_map(
            body, mesh=mesh, in_specs=in_specs, out_specs=out_specs, check_vma=False
        )
        return mapped(*args)

    return run
```

```python
import functools

import jax
import jax.numpy as jnp
from jax import lax
from jax.experimental import pallas as pl
from jax.experimental.pallas import tpu as pltpu
from jax.sharding import PartitionSpec as P

LANES = 128
GROUP = 16
PER_COPY = 8
OWNER_BUDGET = 576
MIB = 2**20


def shards_plain(panels, svd_basis, kl_basis, slot_of_m, svd_keep, kl_keep):
    slot_count = slot_of_m.shape[0]
    order_slots = jnp.argsort(slot_of_m)
    keep_slots = jnp.take(svd_keep, order_slots, axis=0)
    modes_slots = jnp.take(kl_keep, order_slots, axis=0)
    width_modes = svd_basis.shape[2]
    owner_rows = kl_basis.shape[0]
    slot_rows = slot_count // lax.axis_size("pa")
    slot_start = lax.axis_index("pa") * slot_rows
    owner_start = slot_start + lax.axis_index("ma") * owner_rows
    modes_owner = lax.dynamic_slice_in_dim(modes_slots, owner_start, owner_rows, 0)
    chosen = jnp.take(panels, order_slots, axis=0)
    summed = lax.psum_scatter(
        jnp.einsum("mfb,fbr->mfr", chosen, svd_basis, preferred_element_type=jnp.float32),
        "pa",
        scatter_dimension=0,
        tiled=True,
    )
    keep_here = lax.dynamic_slice_in_dim(keep_slots, slot_start, slot_rows, 0)
    columns = jnp.arange(width_modes, dtype=jnp.int32)
    retained = jnp.where(columns[None, None, :] < keep_here[:, None, None], summed, 0.0).astype(
        jnp.bfloat16
    )
    relaid = lax.all_to_all(retained, "ma", split_axis=0, concat_axis=1, tiled=True)
    partial_sums = jnp.einsum("mkf,mfr->mkr", kl_basis, relaid, preferred_element_type=jnp.float32)
    modes = jnp.arange(kl_basis.shape[1], dtype=jnp.int32)
    partial_sums = jnp.where(modes[None, :, None] < modes_owner[:, None, None], partial_sums, 0.0)
    return lax.psum_scatter(partial_sums, "af", scatter_dimension=1, tiled=True)


def cyclic(value, count):
    return lax.rem(value + count, count)


FIRST = 1


def place_of(slot, owner_slots, half_slots):
    half = cyclic(lax.div(slot, half_slots) - lax.axis_index("pa"), lax.axis_size("pa"))
    within = lax.rem(slot, half_slots)
    owner = cyclic(lax.div(within, owner_slots) - lax.axis_index("ma"), lax.axis_size("ma"))
    return half * half_slots + owner * owner_slots + lax.rem(within, owner_slots)


def offsets_of(keep_place, tile_place, shift_place, owner_slots):
    @pl.loop(0, keep_place.shape[0] // owner_slots)
    def _(at):
        offset = jnp.int32(0)
        for j in range(owner_slots):
            place = at * owner_slots + j
            tile = lax.div(offset, LANES)
            tile_place[place] = tile
            shift_place[place] = offset - tile * LANES
            offset = offset + keep_place[place]


def pack(out_v, mine, early, late, line, tables, owners_at):
    tile_place, shift_place, owner_slots = tables
    owners, width_tiles = mine.shape[:2]
    slots = 2 * owners * owner_slots
    tiles = out_v.shape[0] // (GROUP * slots)
    lane = lax.broadcasted_iota(jnp.int32, (GROUP, LANES), 1)
    rows = pl.ds(pl.multiple_of(line, GROUP), GROUP)
    turned = {
        place: pltpu.roll(
            out_v[pl.ds(place, tiles * GROUP, stride=slots), :], shift_place[place], 1
        )
        for place in range(owners_at[0] * owner_slots, (owners_at[-1] + 1) * owner_slots)
    }
    for at in owners_at:
        to, owner = mine, at % owners
        if at >= owners:
            to, owner = (early, 0) if owner == FIRST else (late, owner - (owner > FIRST))
        values, tile_before = None, None
        for j in range(owner_slots):
            place = at * owner_slots + j
            tile = tile_place[place]
            left = lane < shift_place[place]
            moved = [turned[place][t * GROUP : (t + 1) * GROUP] for t in range(tiles)]
            shared = moved[0]
            if j > 0:
                step = tile - tile_before
                shared = values[0]
                for t in range(1, tiles + 1):
                    shared = jnp.where(step == t, values[t], shared)
            values = (
                [jnp.where(left, shared, moved[0])]
                + [jnp.where(left, moved[t - 1], moved[t]) for t in range(1, tiles)]
                + [moved[tiles - 1]]
            )
            tile_before = tile
            for t in reversed(range(tiles + 1)):
                to[owner, jnp.minimum(tile + t, width_tiles - 1), rows, :] = values[t]


def project_kernel(
    owner_slots, slot_hbm, keep_hbm, rows_hbm, panels, basis,
    mine, early, late, slot_column, rows_column, scalars,
    slot_s, keep_s, rows_s, keep_place, rows_place, tile_place, shift_place,
    panels_v, basis_v, lhs_v, out_even, out_odd, small_sem, panel_sem, basis_sem,
):
    slots, freqs, depth = panels_v.shape
    groups = freqs // GROUP
    half_slots = slots // lax.axis_size("pa")

    table_copies = [
        pltpu.make_async_copy(slot_hbm, slot_s, small_sem.at[0]),
        pltpu.make_async_copy(keep_hbm, keep_s, small_sem.at[1]),
        pltpu.make_async_copy(rows_hbm, rows_s, small_sem.at[2]),
    ]
    for copy in table_copies:
        copy.start()

    def basis_copy(i):
        part = pl.ds(i * PER_COPY, PER_COPY)
        return pltpu.make_async_copy(basis.at[part], basis_v.at[part], basis_sem.at[i])

    ahead = 1
    for i in range(ahead):
        basis_copy(i).start()
    for copy in table_copies:
        copy.wait()

    per_group = GROUP // PER_COPY
    for group in range(groups):
        part = pl.ds(group * GROUP, GROUP)

        @pl.loop(0, slots)
        def _(m):
            place = place_of(slot_s[m], owner_slots, half_slots)
            if group == 0:
                keep_place[place] = keep_s[m]
                rows_place[place] = rows_s[m]
            pltpu.make_async_copy(
                panels.at[m, part], panels_v.at[place, part], panel_sem.at[group]
            ).start()

        for i in range(ahead + group * per_group, min(ahead + (group + 1) * per_group, groups * per_group)):
            basis_copy(i).start()

    offsets_of(keep_place, tile_place, shift_place, owner_slots)
    column = lax.broadcasted_iota(jnp.int32, slot_column.shape, 1)
    slot_at = jnp.full(slot_column.shape, owner_slots, jnp.int32)
    rows_at = jnp.zeros(slot_column.shape, jnp.int32)
    for j in range(owner_slots):
        keep = keep_place[j]
        offset = tile_place[j] * LANES + shift_place[j]
        within = (column >= offset) & (column < offset + keep)
        slot_at = jnp.where(within, j, slot_at)
        rows_at = jnp.where(within, rows_place[j], rows_at)
        scalars[j : j + 1, :] = jnp.full((1, LANES), offset, jnp.int32)
        scalars[owner_slots + j : owner_slots + j + 1, :] = jnp.full((1, LANES), keep, jnp.int32)
    slot_column[...] = slot_at
    rows_column[...] = rows_at

    side = GROUP * GROUP
    row = lax.broadcasted_iota(jnp.int32, (side, side), 0)
    column = lax.broadcasted_iota(jnp.int32, (side, side), 1)
    swap = (column == (row % GROUP) * GROUP + row // GROUP).astype(jnp.float32).astype(jnp.bfloat16)

    tables = (tile_place, shift_place, owner_slots)
    all_owners = range(mine.shape[0] * lax.axis_size("pa"))
    share = len(all_owners) // per_group

    def group_step(group, out_v, out_before):
        here = pl.ds(pl.multiple_of(group * GROUP, GROUP), GROUP)
        pltpu.make_async_copy(
            panels_v.at[:, here], panels_v.at[:, here], panel_sem.at[group]
        ).wait()
        for block in range(slots // GROUP):
            blocks = slice(block * GROUP, (block + 1) * GROUP)
            tile = panels_v[blocks, here, :].reshape(side, depth)
            turned = jnp.dot(swap, tile, preferred_element_type=jnp.float32).astype(jnp.bfloat16)
            lhs_v[:, blocks, :] = turned.reshape(GROUP, GROUP, depth)
        for i in range(per_group):
            basis_copy(group * per_group + i).wait()
            for f in range(i * PER_COPY, (i + 1) * PER_COPY):
                product = jnp.dot(
                    lhs_v[f], basis_v[group * GROUP + f], preferred_element_type=jnp.float32
                )
                for t in range(product.shape[1] // LANES):
                    at = (t * GROUP + f) * slots
                    out_v[at : at + slots, :] = product[:, t * LANES : (t + 1) * LANES]
            line = jnp.maximum(group - 1, 0) * GROUP
            pack(out_before, mine, early, late, line, tables, all_owners[i * share : (i + 1) * share])

    @pl.loop(0, groups // 2)
    def _(pair):
        group_step(2 * pair, out_even, out_odd)
        group_step(2 * pair + 1, out_odd, out_even)

    for i in range(per_group):
        part = all_owners[i * share : (i + 1) * share]
        pack(out_odd, mine, early, late, (groups - 1) * GROUP, tables, part)


def folded_rows(rows, width):
    whole, rest = divmod(width, LANES)
    return rows * whole + (rows if rest > LANES // 2 else rows // 2 if rest else 0)


def fold(tiles, out, width):
    rows = tiles[0].shape[0]
    lane = lax.broadcasted_iota(jnp.int32, (rows // 2, LANES), 1)
    for t, tile in enumerate(tiles):
        if t == len(tiles) - 1 and out.shape[0] < rows * len(tiles):
            low, high = tile[: rows // 2], tile[rows // 2 :]
            tile = jnp.where(lane < LANES // 2, low, pltpu.roll(high, LANES // 2, 1))
        out[t * rows : t * rows + tile.shape[0], :] = tile.astype(out.dtype)


def unfold(block, rows):
    count = block.shape[0] // rows
    tiles = [block[t * rows : (t + 1) * rows, :] for t in range(count)]
    if count * rows < block.shape[0]:
        low = block[count * rows :, :].astype(jnp.float32)
        high = pltpu.roll(low, LANES // 2, 1)
        tiles.append(jnp.concatenate([low, high], axis=0).astype(block.dtype))
    return tiles


def sum_kernel(steps, width, mine, got, *out):
    for i, step in enumerate(steps):
        tiles = [mine[step, t] + got[i, t] for t in range(mine.shape[1])]
        fold(tiles, out[i], width)


def kl_kernel(part, owners, width, slot_column, rows_column, kl, *refs):
    blocks, (out, packed_v) = refs[:owners], refs[owners:]
    owner_slots, rows, freqs = kl.shape
    shares = lax.axis_size("af")
    per_source = freqs // owners
    me = lax.axis_index("ma")
    for step in range(owners):
        source = cyclic(me - step, owners)
        at = pl.multiple_of(source * per_source, GROUP)
        for t, tile in enumerate(unfold(blocks[step], per_source)):
            packed_v[pl.ds(at, per_source), t * LANES : (t + 1) * LANES] = tile
    share_rows = rows // shares
    at = pl.multiple_of(cyclic(lax.axis_index("af") + part, shares) * share_rows, GROUP)
    lhs = kl[:, pl.ds(at, share_rows), :].reshape(owner_slots * share_rows, freqs)
    product = jnp.dot(lhs, packed_v[...], preferred_element_type=jnp.float32)
    line = lax.broadcasted_iota(jnp.int32, (share_rows, LANES), 0) + at
    tiles = []
    for t in range(packed_v.shape[1] // LANES):
        lanes = slice(t * LANES, (t + 1) * LANES)
        slot_at = slot_column[0:1, lanes]
        total = jnp.zeros((share_rows, LANES), jnp.float32)
        for j in range(owner_slots):
            here = product[j * share_rows : (j + 1) * share_rows, lanes]
            total = jnp.where(slot_at == j, here, total)
        tiles.append(jnp.where(line < rows_column[0:1, lanes], total, 0.0))
    fold(tiles, out, width)


def unpack_kernel(scalars, mine, got, out, sum_v, out_v, sems):
    owner_slots, rows, modes = out_v.shape
    places = [
        [jnp.max(scalars[k * owner_slots + j : k * owner_slots + j + 1, :]) for k in range(2)]
        for j in range(owner_slots)
    ]
    for t, (a, b) in enumerate(zip(unfold(mine, rows), unfold(got, rows))):
        sum_v[t] = a + b.astype(jnp.float32)
    lane = lax.broadcasted_iota(jnp.int32, (rows, LANES), 1)
    copies = []
    for j, (offset, keep) in enumerate(places):
        tile = lax.div(offset, LANES)
        shift = offset - tile * LANES
        back = lax.rem(LANES - shift, LANES)
        turned = [pltpu.roll(sum_v[tile + t], back, 1) for t in range(modes // LANES + 1)]
        for t in range(modes // LANES):
            value = jnp.where(lane < LANES - shift, turned[t], turned[t + 1])
            value = jnp.where(lane < keep - t * LANES, value, 0.0)
            out_v[j, :, t * LANES : (t + 1) * LANES] = value
        copy = pltpu.make_async_copy(out_v.at[j], out.at[j], sems.at[j])
        copy.start()
        copies.append(copy)
    for copy in copies:
        copy.wait()


HBM = pl.BlockSpec(memory_space=pltpu.HBM)
VMEM = pl.BlockSpec(memory_space=pltpu.VMEM)
SMALL = pltpu.CompilerParams(vmem_limit_bytes=8 * MIB)


def in_hbm(operand):
    return pltpu.with_memory_space_constraint(operand, pltpu.HBM)


def project(panels, svd_basis, slot_of_m, svd_keep, kl_keep, owner_slots, width):
    slots, freqs, depth = panels.shape
    modes = svd_basis.shape[2]
    owners = lax.axis_size("ma")

    def packed(count):
        return jax.ShapeDtypeStruct((count, width // LANES, freqs, LANES), jnp.float32)

    column = jax.ShapeDtypeStruct((8, width), jnp.int32)
    return pl.pallas_call(
        functools.partial(project_kernel, owner_slots),
        out_shape=(
            packed(owners),
            packed(1),
            packed(owners - 1),
            column,
            column,
            jax.ShapeDtypeStruct((8, LANES), jnp.int32),
        ),
        in_specs=[HBM] * 5,
        out_specs=(VMEM,) * 6,
        scratch_shapes=[pltpu.SMEM((slots,), jnp.int32)] * 7
        + [
            pltpu.VMEM((slots, freqs, depth), jnp.bfloat16),
            pltpu.VMEM((freqs, depth, modes), jnp.bfloat16),
            pltpu.VMEM((GROUP, slots, depth), jnp.bfloat16),
            pltpu.VMEM((modes // LANES * GROUP * slots, LANES), jnp.float32),
            pltpu.VMEM((modes // LANES * GROUP * slots, LANES), jnp.float32),
            pltpu.SemaphoreType.DMA((3,)),
            pltpu.SemaphoreType.DMA((freqs // GROUP,)),
            pltpu.SemaphoreType.DMA((freqs // PER_COPY,)),
        ],
        compiler_params=pltpu.CompilerParams(vmem_limit_bytes=48 * MIB),
        cost_estimate=pl.CostEstimate(
            flops=2 * slots * freqs * depth * modes,
            bytes_accessed=2 * freqs * depth * (modes + slots),
            transcendentals=0,
        ),
        name="project",
    )(*map(in_hbm, (slot_of_m, svd_keep, kl_keep, panels, svd_basis)))


def sum_pair(steps, width, mine, got):
    kind = jax.ShapeDtypeStruct((folded_rows(mine.shape[2], width), LANES), jnp.bfloat16)
    return pl.pallas_call(
        functools.partial(sum_kernel, steps, width),
        out_shape=(kind,) * len(steps),
        in_specs=[VMEM] * 2,
        out_specs=(VMEM,) * len(steps),
        compiler_params=SMALL,
        cost_estimate=pl.CostEstimate(
            flops=got.size, bytes_accessed=10 * got.size, transcendentals=0
        ),
        name="sum_pair",
    )(mine, got)


def kl_project(part, kind, width, slot_column, rows_column, kl_basis, blocks):
    owners, shares = lax.axis_size("ma"), lax.axis_size("af")
    rows, freqs = kl_basis.shape[1:]
    wide = slot_column.shape[1]
    return pl.pallas_call(
        functools.partial(kl_kernel, part, owners, width),
        out_shape=jax.ShapeDtypeStruct((folded_rows(rows // shares, width), LANES), kind),
        in_specs=[VMEM] * (3 + owners),
        out_specs=VMEM,
        scratch_shapes=[pltpu.VMEM((freqs, wide), jnp.bfloat16)],
        compiler_params=SMALL,
        cost_estimate=pl.CostEstimate(
            flops=2 * kl_basis.size * wide // shares,
            bytes_accessed=2 * kl_basis.size,
            transcendentals=0,
        ),
        name="kl_project",
    )(slot_column, rows_column, kl_basis, *blocks)


def unpack(scalars, mine, got, owner_slots, rows, modes, width):
    tiles = -(-width // LANES) + modes // LANES + 1
    return pl.pallas_call(
        unpack_kernel,
        out_shape=jax.ShapeDtypeStruct((owner_slots, rows, modes), jnp.float32),
        in_specs=[VMEM] * 3,
        out_specs=HBM,
        scratch_shapes=[
            pltpu.VMEM((tiles, rows, LANES), jnp.float32),
            pltpu.VMEM((owner_slots, rows, modes), jnp.float32),
            pltpu.SemaphoreType.DMA((owner_slots,)),
        ],
        compiler_params=SMALL,
        cost_estimate=pl.CostEstimate(
            flops=mine.size, bytes_accessed=10 * mine.size, transcendentals=0
        ),
        name="unpack",
    )(scalars, mine, got)


def pairs(axis):
    return [(i, i ^ 1) for i in range(lax.axis_size(axis))]


def ring(step):
    size = lax.axis_size("ma")
    return [(i, (i + step) % size) for i in range(size)]


def shards(panels, svd_basis, kl_basis, slot_of_m, svd_keep, kl_keep):
    owner_slots, modes = kl_basis.shape[0], svd_basis.shape[2]
    owners = lax.axis_size("ma")
    width = min(OWNER_BUDGET, owner_slots * modes)
    wide = -(-width // LANES) * LANES
    mine, early, late, slot_column, rows_column, scalars = project(
        panels, svd_basis, slot_of_m, svd_keep, kl_keep, owner_slots, wide
    )
    others = [step for step in range(owners) if step != FIRST]
    got_early = lax.ppermute(early, "pa", pairs("pa"))
    late, got_early = lax.optimization_barrier((late, got_early))
    got_late = lax.ppermute(late, "pa", pairs("pa"))
    summed = dict(zip([FIRST], sum_pair([FIRST], width, mine, got_early)))
    summed |= zip(others, sum_pair(others, width, mine, got_late))
    blocks = {
        step: lax.ppermute(summed[step], "ma", ring(step)) if step else summed[step]
        for step in [FIRST] + others
    }
    tables = (width, slot_column, rows_column, kl_basis, [blocks[step] for step in range(owners)])
    send = kl_project(1, jnp.bfloat16, *tables)
    got = lax.ppermute(send, "af", pairs("af"))
    mine = kl_project(0, jnp.float32, *tables)
    rows = kl_basis.shape[1] // lax.axis_size("af")
    return unpack(scalars, mine, got, owner_slots, rows, modes, width)


def kernels_fit(mesh, args):
    panels, svd_basis, kl_basis = args[:3]
    slots = panels.shape[0] // mesh.shape["grp"]
    freqs = svd_basis.shape[0] // (mesh.shape["af"] * mesh.shape["ma"])
    owner_slots = kl_basis.shape[0] // (mesh.shape["pa"] * mesh.shape["ma"])
    share_rows = kl_basis.shape[1] // mesh.shape["af"]
    return (
        freqs % (2 * GROUP) == 0
        and slots % (GROUP * mesh.shape["pa"]) == 0
        and owner_slots == 4
        and svd_basis.shape[2] == 2 * LANES
        and share_rows % (2 * GROUP) == 0
        and mesh.shape["pa"] == 2
        and mesh.shape["af"] == 2
        and mesh.shape["ma"] == 4
    )


def solution(mesh):
    in_specs = (
        P("grp", ("af", "ma"), "pa"),
        P(("af", "ma"), "pa", None),
        P(("pa", "ma"), None, "af"),
        P(),
        P(),
        P(),
    )
    out_specs = P(("grp", "pa", "ma"), "af", None)

    def run(*args):
        body = shards if kernels_fit(mesh, args) else shards_plain
        mapped = jax.shard_map(
            body, mesh=mesh, in_specs=in_specs, out_specs=out_specs, check_vma=False
        )
        return mapped(*args)

    return run
```

```python
import functools

import jax
import jax.numpy as jnp
from jax import lax
from jax.experimental import pallas as pl
from jax.experimental.pallas import tpu as pltpu
from jax.sharding import PartitionSpec as P

LANES = 128
GROUP = 16
COPIES = ((8, 8), (8, 4, 2, 2))
OWNER_BUDGET = 576
MIB = 2**20


def shards_plain(panels, svd_basis, kl_basis, slot_of_m, svd_keep, kl_keep):
    slot_count = slot_of_m.shape[0]
    order_slots = jnp.argsort(slot_of_m)
    keep_slots = jnp.take(svd_keep, order_slots, axis=0)
    modes_slots = jnp.take(kl_keep, order_slots, axis=0)
    width_modes = svd_basis.shape[2]
    owner_rows = kl_basis.shape[0]
    slot_rows = slot_count // lax.axis_size("pa")
    slot_start = lax.axis_index("pa") * slot_rows
    owner_start = slot_start + lax.axis_index("ma") * owner_rows
    modes_owner = lax.dynamic_slice_in_dim(modes_slots, owner_start, owner_rows, 0)
    chosen = jnp.take(panels, order_slots, axis=0)
    summed = lax.psum_scatter(
        jnp.einsum("mfb,fbr->mfr", chosen, svd_basis, preferred_element_type=jnp.float32),
        "pa",
        scatter_dimension=0,
        tiled=True,
    )
    keep_here = lax.dynamic_slice_in_dim(keep_slots, slot_start, slot_rows, 0)
    columns = jnp.arange(width_modes, dtype=jnp.int32)
    retained = jnp.where(columns[None, None, :] < keep_here[:, None, None], summed, 0.0).astype(
        jnp.bfloat16
    )
    relaid = lax.all_to_all(retained, "ma", split_axis=0, concat_axis=1, tiled=True)
    partial_sums = jnp.einsum("mkf,mfr->mkr", kl_basis, relaid, preferred_element_type=jnp.float32)
    modes = jnp.arange(kl_basis.shape[1], dtype=jnp.int32)
    partial_sums = jnp.where(modes[None, :, None] < modes_owner[:, None, None], partial_sums, 0.0)
    return lax.psum_scatter(partial_sums, "af", scatter_dimension=1, tiled=True)


def cyclic(value, count):
    return lax.rem(value + count, count)


def on_ring(z):
    return z ^ (z // 2) if isinstance(z, int) else z ^ lax.shift_right_logical(z, 1)


def far_step(owners):
    return owners // 2


def place_of(slot, owner_slots, half_slots):
    half = cyclic(lax.div(slot, half_slots) - lax.axis_index("pa"), lax.axis_size("pa"))
    within = lax.rem(slot, half_slots)
    owner = on_ring(lax.div(within, owner_slots)) - on_ring(lax.axis_index("ma"))
    owner = cyclic(owner, lax.axis_size("ma"))
    return half * half_slots + owner * owner_slots + lax.rem(within, owner_slots)


def offsets_of(keep_place, tile_place, shift_place, owner_slots):
    @pl.loop(0, keep_place.shape[0] // owner_slots)
    def _(at):
        offset = jnp.int32(0)
        for j in range(owner_slots):
            place = at * owner_slots + j
            tile = lax.div(offset, LANES)
            tile_place[place] = tile
            shift_place[place] = offset - tile * LANES
            offset = offset + keep_place[place]


def pack(out_v, mine, far, near, line, tables, owners_at):
    tile_place, shift_place, owner_slots = tables
    owners, width_tiles = mine.shape[:2]
    slots = 2 * owners * owner_slots
    tiles = out_v.shape[0] // (GROUP * slots)
    lane = lax.broadcasted_iota(jnp.int32, (GROUP, LANES), 1)
    rows = pl.ds(pl.multiple_of(line, GROUP), GROUP)
    turned = {
        place: pltpu.roll(
            out_v[pl.ds(place, tiles * GROUP, stride=slots), :], shift_place[place], 1
        )
        for place in range(owners_at[0] * owner_slots, (owners_at[-1] + 1) * owner_slots)
    }
    for at in owners_at:
        to, owner = mine, at % owners
        if at >= owners:
            first = far_step(owners)
            to, owner = (far, 0) if owner == first else (near, owner - (owner > first))
        values, tile_before = None, None
        for j in range(owner_slots):
            place = at * owner_slots + j
            tile = tile_place[place]
            left = lane < shift_place[place]
            moved = [turned[place][t * GROUP : (t + 1) * GROUP] for t in range(tiles)]
            shared = moved[0]
            if j > 0:
                step = tile - tile_before
                shared = values[0]
                for t in range(1, tiles + 1):
                    shared = jnp.where(step == t, values[t], shared)
            values = (
                [jnp.where(left, shared, moved[0])]
                + [jnp.where(left, moved[t - 1], moved[t]) for t in range(1, tiles)]
                + [moved[tiles - 1]]
            )
            tile_before = tile
            for t in reversed(range(tiles + 1)):
                to[owner, jnp.minimum(tile + t, width_tiles - 1), rows, :] = values[t]


def project_kernel(
    owner_slots, slot_hbm, keep_hbm, rows_hbm, panels, basis,
    mine, far, near, slot_column, rows_column, scalars,
    slot_s, keep_s, rows_s, keep_place, rows_place, tile_place, shift_place,
    panels_v, basis_v, lhs_v, out_even, out_odd, small_sem, panel_sem, basis_sem,
):
    slots, freqs, depth = panels_v.shape
    groups = freqs // GROUP
    half_slots = slots // lax.axis_size("pa")

    table_copies = [
        pltpu.make_async_copy(slot_hbm, slot_s, small_sem.at[0]),
        pltpu.make_async_copy(keep_hbm, keep_s, small_sem.at[1]),
        pltpu.make_async_copy(rows_hbm, rows_s, small_sem.at[2]),
    ]
    for copy in table_copies:
        copy.start()

    def basis_copies(group, parity):
        found, first = [], 0
        for i, count in enumerate(COPIES[parity]):
            part = pl.ds(group * GROUP + first, count)
            sem = basis_sem.at[group * len(COPIES[1]) + i]
            copy = pltpu.make_async_copy(basis.at[part], basis_v.at[part], sem)
            found.append((copy, first, count))
            first += count
        return found

    basis_copies(0, 0)[0][0].start()
    for copy in table_copies:
        copy.wait()

    for group in range(groups):
        part = pl.ds(group * GROUP, GROUP)

        @pl.loop(0, slots)
        def _(m):
            place = place_of(slot_s[m], owner_slots, half_slots)
            if group == 0:
                keep_place[place] = keep_s[m]
                rows_place[place] = rows_s[m]
            pltpu.make_async_copy(
                panels.at[m, part], panels_v.at[place, part], panel_sem.at[group]
            ).start()

        for copy, _, _ in basis_copies(group, group % 2)[1 if group == 0 else 0 :]:
            copy.start()

    offsets_of(keep_place, tile_place, shift_place, owner_slots)
    column = lax.broadcasted_iota(jnp.int32, slot_column.shape, 1)
    slot_at = jnp.full(slot_column.shape, owner_slots, jnp.int32)
    rows_at = jnp.zeros(slot_column.shape, jnp.int32)
    for j in range(owner_slots):
        keep = keep_place[j]
        offset = tile_place[j] * LANES + shift_place[j]
        within = (column >= offset) & (column < offset + keep)
        slot_at = jnp.where(within, j, slot_at)
        rows_at = jnp.where(within, rows_place[j], rows_at)
        scalars[j : j + 1, :] = jnp.full((1, LANES), offset, jnp.int32)
        scalars[owner_slots + j : owner_slots + j + 1, :] = jnp.full((1, LANES), keep, jnp.int32)
    slot_column[...] = slot_at
    rows_column[...] = rows_at

    side = GROUP * GROUP
    row = lax.broadcasted_iota(jnp.int32, (side, side), 0)
    column = lax.broadcasted_iota(jnp.int32, (side, side), 1)
    swap = (column == (row % GROUP) * GROUP + row // GROUP).astype(jnp.float32).astype(jnp.bfloat16)

    tables = (tile_place, shift_place, owner_slots)
    all_owners = range(mine.shape[0] * lax.axis_size("pa"))

    def group_step(group, parity, out_v, out_before):
        here = pl.ds(pl.multiple_of(group * GROUP, GROUP), GROUP)
        pltpu.make_async_copy(
            panels_v.at[:, here], panels_v.at[:, here], panel_sem.at[group]
        ).wait()
        for block in range(slots // GROUP):
            blocks = slice(block * GROUP, (block + 1) * GROUP)
            tile = panels_v[blocks, here, :].reshape(side, depth)
            turned = jnp.dot(swap, tile, preferred_element_type=jnp.float32).astype(jnp.bfloat16)
            lhs_v[:, blocks, :] = turned.reshape(GROUP, GROUP, depth)
        for i, (copy, first, count) in enumerate(basis_copies(group, parity)):
            copy.wait()
            for f in range(first, first + count):
                product = jnp.dot(
                    lhs_v[f], basis_v[group * GROUP + f], preferred_element_type=jnp.float32
                )
                for t in range(product.shape[1] // LANES):
                    at = (t * GROUP + f) * slots
                    out_v[at : at + slots, :] = product[:, t * LANES : (t + 1) * LANES]
            if i < 2:
                line = jnp.maximum(group - 1, 0) * GROUP
                half = len(all_owners) // 2
                part = all_owners[i * half : (i + 1) * half]
                pack(out_before, mine, far, near, line, tables, part)

    @pl.loop(0, groups // 2)
    def _(pair):
        group_step(2 * pair, 0, out_even, out_odd)
        group_step(2 * pair + 1, 1, out_odd, out_even)

    pack(out_odd, mine, far, near, (groups - 1) * GROUP, tables, all_owners)


def folded_rows(rows, width):
    whole, rest = divmod(width, LANES)
    return rows * whole + (rows if rest > LANES // 2 else rows // 2 if rest else 0)


def fold(tiles, out, width):
    rows = tiles[0].shape[0]
    lane = lax.broadcasted_iota(jnp.int32, (rows // 2, LANES), 1)
    for t, tile in enumerate(tiles):
        if t == len(tiles) - 1 and out.shape[0] < rows * len(tiles):
            low, high = tile[: rows // 2], tile[rows // 2 :]
            tile = jnp.where(lane < LANES // 2, low, pltpu.roll(high, LANES // 2, 1))
        out[t * rows : t * rows + tile.shape[0], :] = tile.astype(out.dtype)


def unfold(block, rows):
    count = block.shape[0] // rows
    tiles = [block[t * rows : (t + 1) * rows, :] for t in range(count)]
    if count * rows < block.shape[0]:
        low = block[count * rows :, :].astype(jnp.float32)
        high = pltpu.roll(low, LANES // 2, 1)
        tiles.append(jnp.concatenate([low, high], axis=0).astype(block.dtype))
    return tiles


def sum_kernel(steps, width, mine, got, *out):
    for i, step in enumerate(steps):
        tiles = [mine[step, t] + got[i, t] for t in range(mine.shape[1])]
        fold(tiles, out[i], width)


def kl_kernel(part, owners, width, slot_column, rows_column, kl, *refs):
    blocks, (out, packed_v) = refs[:owners], refs[owners:]
    owner_slots, rows, freqs = kl.shape
    shares = lax.axis_size("af")
    per_source = freqs // owners
    me = lax.axis_index("ma")
    for step in range(owners):
        source = on_ring(cyclic(on_ring(me) - step, owners))
        at = pl.multiple_of(source * per_source, GROUP)
        for t, tile in enumerate(unfold(blocks[step], per_source)):
            packed_v[pl.ds(at, per_source), t * LANES : (t + 1) * LANES] = tile
    share_rows = rows // shares
    at = pl.multiple_of(cyclic(lax.axis_index("af") + part, shares) * share_rows, GROUP)
    lhs = kl[:, pl.ds(at, share_rows), :].reshape(owner_slots * share_rows, freqs)
    product = jnp.dot(lhs, packed_v[...], preferred_element_type=jnp.float32)
    line = lax.broadcasted_iota(jnp.int32, (share_rows, LANES), 0) + at
    tiles = []
    for t in range(packed_v.shape[1] // LANES):
        lanes = slice(t * LANES, (t + 1) * LANES)
        slot_at = slot_column[0:1, lanes]
        total = jnp.zeros((share_rows, LANES), jnp.float32)
        for j in range(owner_slots):
            here = product[j * share_rows : (j + 1) * share_rows, lanes]
            total = jnp.where(slot_at == j, here, total)
        tiles.append(jnp.where(line < rows_column[0:1, lanes], total, 0.0))
    fold(tiles, out, width)


def unpack_kernel(scalars, mine, got, out, sum_v, out_v, sems):
    owner_slots, rows, modes = out_v.shape
    places = [
        [jnp.max(scalars[k * owner_slots + j : k * owner_slots + j + 1, :]) for k in range(2)]
        for j in range(owner_slots)
    ]
    for t, (a, b) in enumerate(zip(unfold(mine, rows), unfold(got, rows))):
        sum_v[t] = a + b.astype(jnp.float32)
    lane = lax.broadcasted_iota(jnp.int32, (rows, LANES), 1)
    copies = []
    for j, (offset, keep) in enumerate(places):
        tile = lax.div(offset, LANES)
        shift = offset - tile * LANES
        back = lax.rem(LANES - shift, LANES)
        turned = [pltpu.roll(sum_v[tile + t], back, 1) for t in range(modes // LANES + 1)]
        for t in range(modes // LANES):
            value = jnp.where(lane < LANES - shift, turned[t], turned[t + 1])
            value = jnp.where(lane < keep - t * LANES, value, 0.0)
            out_v[j, :, t * LANES : (t + 1) * LANES] = value
        copy = pltpu.make_async_copy(out_v.at[j], out.at[j], sems.at[j])
        copy.start()
        copies.append(copy)
    for copy in copies:
        copy.wait()


HBM = pl.BlockSpec(memory_space=pltpu.HBM)
VMEM = pl.BlockSpec(memory_space=pltpu.VMEM)
SMALL = pltpu.CompilerParams(vmem_limit_bytes=8 * MIB)


def in_hbm(operand):
    return pltpu.with_memory_space_constraint(operand, pltpu.HBM)


def project(panels, svd_basis, slot_of_m, svd_keep, kl_keep, owner_slots, width):
    slots, freqs, depth = panels.shape
    modes = svd_basis.shape[2]
    owners = lax.axis_size("ma")

    def packed(count):
        return jax.ShapeDtypeStruct((count, width // LANES, freqs, LANES), jnp.float32)

    column = jax.ShapeDtypeStruct((8, width), jnp.int32)
    return pl.pallas_call(
        functools.partial(project_kernel, owner_slots),
        out_shape=(
            packed(owners),
            packed(1),
            packed(owners - 1),
            column,
            column,
            jax.ShapeDtypeStruct((8, LANES), jnp.int32),
        ),
        in_specs=[HBM] * 5,
        out_specs=(VMEM,) * 6,
        scratch_shapes=[pltpu.SMEM((slots,), jnp.int32)] * 7
        + [
            pltpu.VMEM((slots, freqs, depth), jnp.bfloat16),
            pltpu.VMEM((freqs, depth, modes), jnp.bfloat16),
            pltpu.VMEM((GROUP, slots, depth), jnp.bfloat16),
            pltpu.VMEM((modes // LANES * GROUP * slots, LANES), jnp.float32),
            pltpu.VMEM((modes // LANES * GROUP * slots, LANES), jnp.float32),
            pltpu.SemaphoreType.DMA((3,)),
            pltpu.SemaphoreType.DMA((freqs // GROUP,)),
            pltpu.SemaphoreType.DMA((freqs // GROUP * len(COPIES[1]),)),
        ],
        compiler_params=pltpu.CompilerParams(vmem_limit_bytes=48 * MIB),
        cost_estimate=pl.CostEstimate(
            flops=2 * slots * freqs * depth * modes,
            bytes_accessed=2 * freqs * depth * (modes + slots),
            transcendentals=0,
        ),
        name="project",
    )(*map(in_hbm, (slot_of_m, svd_keep, kl_keep, panels, svd_basis)))


def sum_pair(steps, width, mine, got):
    kind = jax.ShapeDtypeStruct((folded_rows(mine.shape[2], width), LANES), jnp.bfloat16)
    return pl.pallas_call(
        functools.partial(sum_kernel, steps, width),
        out_shape=(kind,) * len(steps),
        in_specs=[VMEM] * 2,
        out_specs=(VMEM,) * len(steps),
        compiler_params=SMALL,
        cost_estimate=pl.CostEstimate(
            flops=got.size, bytes_accessed=10 * got.size, transcendentals=0
        ),
        name="sum_pair",
    )(mine, got)


def kl_project(part, kind, width, slot_column, rows_column, kl_basis, blocks):
    owners, shares = lax.axis_size("ma"), lax.axis_size("af")
    rows, freqs = kl_basis.shape[1:]
    wide = slot_column.shape[1]
    return pl.pallas_call(
        functools.partial(kl_kernel, part, owners, width),
        out_shape=jax.ShapeDtypeStruct((folded_rows(rows // shares, width), LANES), kind),
        in_specs=[VMEM] * (3 + owners),
        out_specs=VMEM,
        scratch_shapes=[pltpu.VMEM((freqs, wide), jnp.bfloat16)],
        compiler_params=SMALL,
        cost_estimate=pl.CostEstimate(
            flops=2 * kl_basis.size * wide // shares,
            bytes_accessed=2 * kl_basis.size,
            transcendentals=0,
        ),
        name="kl_project",
    )(slot_column, rows_column, kl_basis, *blocks)


def unpack(scalars, mine, got, owner_slots, rows, modes, width):
    tiles = -(-width // LANES) + modes // LANES + 1
    return pl.pallas_call(
        unpack_kernel,
        out_shape=jax.ShapeDtypeStruct((owner_slots, rows, modes), jnp.float32),
        in_specs=[VMEM] * 3,
        out_specs=HBM,
        scratch_shapes=[
            pltpu.VMEM((tiles, rows, LANES), jnp.float32),
            pltpu.VMEM((owner_slots, rows, modes), jnp.float32),
            pltpu.SemaphoreType.DMA((owner_slots,)),
        ],
        compiler_params=SMALL,
        cost_estimate=pl.CostEstimate(
            flops=mine.size, bytes_accessed=10 * mine.size, transcendentals=0
        ),
        name="unpack",
    )(scalars, mine, got)


def pairs(axis):
    return [(i, i ^ 1) for i in range(lax.axis_size(axis))]


def ring(step):
    size = lax.axis_size("ma")
    return [(i, on_ring((on_ring(i) + step) % size)) for i in range(size)]


def shards(panels, svd_basis, kl_basis, slot_of_m, svd_keep, kl_keep):
    owner_slots, modes = kl_basis.shape[0], svd_basis.shape[2]
    owners = lax.axis_size("ma")
    width = min(OWNER_BUDGET, owner_slots * modes)
    wide = -(-width // LANES) * LANES
    mine, far, near, slot_column, rows_column, scalars = project(
        panels, svd_basis, slot_of_m, svd_keep, kl_keep, owner_slots, wide
    )
    first = far_step(owners)
    others = [step for step in range(owners) if step != first]
    got_far = lax.ppermute(far, "pa", pairs("pa"))
    near, got_far = lax.optimization_barrier((near, got_far))
    got_near = lax.ppermute(near, "pa", pairs("pa"))
    summed = dict(zip([first], sum_pair([first], width, mine, got_far)))
    summed |= zip(others, sum_pair(others, width, mine, got_near))
    blocks = {
        step: lax.ppermute(summed[step], "ma", ring(step)) if step else summed[step]
        for step in [first] + others
    }
    tables = (width, slot_column, rows_column, kl_basis, [blocks[step] for step in range(owners)])
    send = kl_project(1, jnp.bfloat16, *tables)
    got = lax.ppermute(send, "af", pairs("af"))
    mine = kl_project(0, jnp.float32, *tables)
    rows = kl_basis.shape[1] // lax.axis_size("af")
    return unpack(scalars, mine, got, owner_slots, rows, modes, width)


def kernels_fit(mesh, args):
    panels, svd_basis, kl_basis = args[:3]
    slots = panels.shape[0] // mesh.shape["grp"]
    freqs = svd_basis.shape[0] // (mesh.shape["af"] * mesh.shape["ma"])
    owner_slots = kl_basis.shape[0] // (mesh.shape["pa"] * mesh.shape["ma"])
    share_rows = kl_basis.shape[1] // mesh.shape["af"]
    return (
        freqs % (2 * GROUP) == 0
        and slots % (GROUP * mesh.shape["pa"]) == 0
        and owner_slots == 4
        and svd_basis.shape[2] == 2 * LANES
        and share_rows % (2 * GROUP) == 0
        and mesh.shape["pa"] == 2
        and mesh.shape["af"] == 2
        and mesh.shape["ma"] == 4
    )


def solution(mesh):
    in_specs = (
        P("grp", ("af", "ma"), "pa"),
        P(("af", "ma"), "pa", None),
        P(("pa", "ma"), None, "af"),
        P(),
        P(),
        P(),
    )
    out_specs = P(("grp", "pa", "ma"), "af", None)

    def run(*args):
        body = shards if kernels_fit(mesh, args) else shards_plain
        mapped = jax.shard_map(
            body, mesh=mesh, in_specs=in_specs, out_specs=out_specs, check_vma=False
        )
        return mapped(*args)

    return run
```

```python
import functools

import jax
import jax.numpy as jnp
from jax import lax
from jax.experimental import pallas as pl
from jax.experimental.pallas import tpu as pltpu
from jax.sharding import PartitionSpec as P

LANES = 128
GROUP = 16
COPIES = ((8, 8), (8, 8))
UNITS = 2
SIDE = 256
OWNER_BUDGET = 576
MIB = 2**20


def shards_plain(panels, svd_basis, kl_basis, slot_of_m, svd_keep, kl_keep):
    slot_count = slot_of_m.shape[0]
    order_slots = jnp.argsort(slot_of_m)
    keep_slots = jnp.take(svd_keep, order_slots, axis=0)
    modes_slots = jnp.take(kl_keep, order_slots, axis=0)
    width_modes = svd_basis.shape[2]
    owner_rows = kl_basis.shape[0]
    slot_rows = slot_count // lax.axis_size("pa")
    slot_start = lax.axis_index("pa") * slot_rows
    owner_start = slot_start + lax.axis_index("ma") * owner_rows
    modes_owner = lax.dynamic_slice_in_dim(modes_slots, owner_start, owner_rows, 0)
    chosen = jnp.take(panels, order_slots, axis=0)
    summed = lax.psum_scatter(
        jnp.einsum("mfb,fbr->mfr", chosen, svd_basis, preferred_element_type=jnp.float32),
        "pa",
        scatter_dimension=0,
        tiled=True,
    )
    keep_here = lax.dynamic_slice_in_dim(keep_slots, slot_start, slot_rows, 0)
    columns = jnp.arange(width_modes, dtype=jnp.int32)
    retained = jnp.where(columns[None, None, :] < keep_here[:, None, None], summed, 0.0).astype(
        jnp.bfloat16
    )
    relaid = lax.all_to_all(retained, "ma", split_axis=0, concat_axis=1, tiled=True)
    partial_sums = jnp.einsum("mkf,mfr->mkr", kl_basis, relaid, preferred_element_type=jnp.float32)
    modes = jnp.arange(kl_basis.shape[1], dtype=jnp.int32)
    partial_sums = jnp.where(modes[None, :, None] < modes_owner[:, None, None], partial_sums, 0.0)
    return lax.psum_scatter(partial_sums, "af", scatter_dimension=1, tiled=True)


def cyclic(value, count):
    return lax.rem(value + count, count)


def on_ring(z):
    return z ^ (z // 2) if isinstance(z, int) else z ^ lax.shift_right_logical(z, 1)


def far_step(owners):
    return owners // 2


def place_of(slot, owner_slots, half_slots):
    half = cyclic(lax.div(slot, half_slots) - lax.axis_index("pa"), lax.axis_size("pa"))
    within = lax.rem(slot, half_slots)
    owner = on_ring(lax.div(within, owner_slots)) - on_ring(lax.axis_index("ma"))
    owner = cyclic(owner, lax.axis_size("ma"))
    return half * half_slots + owner * owner_slots + lax.rem(within, owner_slots)


def offsets_of(keep_place, tile_place, shift_place, owner_slots):
    @pl.loop(0, keep_place.shape[0] // owner_slots)
    def _(at):
        offset = jnp.int32(0)
        for j in range(owner_slots):
            place = at * owner_slots + j
            tile = lax.div(offset, LANES)
            tile_place[place] = tile
            shift_place[place] = offset - tile * LANES
            offset = offset + keep_place[place]


def pack(out_v, mine, far, near, line, tables, owners_at):
    tile_place, shift_place, owner_slots = tables
    owners, width_tiles = mine.shape[:2]
    slots = 2 * owners * owner_slots
    tiles = out_v.shape[0] // (GROUP * slots)
    lane = lax.broadcasted_iota(jnp.int32, (GROUP, LANES), 1)
    rows = pl.ds(pl.multiple_of(line, GROUP), GROUP)
    turned = {
        place: pltpu.roll(
            out_v[pl.ds(place, tiles * GROUP, stride=slots), :], shift_place[place], 1
        )
        for place in range(owners_at[0] * owner_slots, (owners_at[-1] + 1) * owner_slots)
    }
    for at in owners_at:
        to, owner = mine, at % owners
        if at >= owners:
            first = far_step(owners)
            to, owner = (far, 0) if owner == first else (near, owner - (owner > first))
        values, tile_before = None, None
        for j in range(owner_slots):
            place = at * owner_slots + j
            tile = tile_place[place]
            left = lane < shift_place[place]
            moved = [turned[place][t * GROUP : (t + 1) * GROUP] for t in range(tiles)]
            shared = moved[0]
            if j > 0:
                step = tile - tile_before
                shared = values[0]
                for t in range(1, tiles + 1):
                    shared = jnp.where(step == t, values[t], shared)
            values = (
                [jnp.where(left, shared, moved[0])]
                + [jnp.where(left, moved[t - 1], moved[t]) for t in range(1, tiles)]
                + [moved[tiles - 1]]
            )
            tile_before = tile
            for t in reversed(range(tiles + 1)):
                to[owner, jnp.minimum(tile + t, width_tiles - 1), rows, :] = values[t]


def products(lhs, basis, out_v, start, first, count, *totals):
    slots = lhs.shape[1]

    def store(pair, here):
        for unit, total in enumerate(here):
            product = pltpu.matmul_pop(total)
            for t in range(SIDE // LANES):
                at = (t * GROUP + pair + unit) * slots
                out_v[at : at + slots, :] = product[:, t * LANES : (t + 1) * LANES]

    before = None
    for pair in range(first, first + count, UNITS):
        here = totals[UNITS * ((pair // UNITS) % 2) :][:UNITS]
        for k in range(lhs.shape[2] // SIDE):
            depth = slice(k * SIDE, (k + 1) * SIDE)
            for unit, total in enumerate(here):
                pltpu.matmul_push_rhs(basis[start + pair + unit, depth, :], k % 2, unit)
                pltpu.matmul_acc_lhs(total, lhs[pair + unit, :, depth], load_staged_rhs=k % 2)
        if before:
            store(*before)
        before = pair, here
    store(*before)


def turn(swap, panels, here, lhs, *totals):
    def store(jobs, units):
        for (blocks, columns), total in zip(jobs, units):
            turned = pltpu.matmul_pop(total).astype(jnp.bfloat16)
            lhs[:, blocks, columns] = turned.reshape(GROUP, GROUP, SIDE)

    jobs = [
        (slice(block, block + GROUP), slice(column, column + SIDE))
        for block in range(0, panels.shape[0], GROUP)
        for column in range(0, panels.shape[2], SIDE)
    ]
    before = None
    for i in range(0, len(jobs), UNITS):
        reg = (i // UNITS) % 2
        now = jobs[i : i + UNITS], totals[UNITS * reg :][:UNITS]
        for unit, ((blocks, columns), total) in enumerate(zip(*now)):
            tile = panels[blocks, here, columns].reshape(SIDE, SIDE)
            pltpu.matmul_push_rhs(tile, reg, unit)
            pltpu.matmul_acc_lhs(total, swap, load_staged_rhs=reg)
        if before:
            store(*before)
        before = now
    store(*before)


def on_units(step, rows):
    pl.run_scoped(step, *[pltpu.ACC(i % UNITS)((rows, SIDE), jnp.float32) for i in range(2 * UNITS)])


def project_kernel(
    owner_slots, slot_hbm, keep_hbm, rows_hbm, panels, basis,
    mine, far, near, slot_column, rows_column, scalars,
    slot_s, keep_s, rows_s, keep_place, rows_place, tile_place, shift_place,
    panels_v, basis_v, lhs_v, out_even, out_odd, small_sem, panel_sem, basis_sem,
):
    slots, freqs, depth = panels_v.shape
    groups = freqs // GROUP
    half_slots = slots // lax.axis_size("pa")

    table_copies = [
        pltpu.make_async_copy(slot_hbm, slot_s, small_sem.at[0]),
        pltpu.make_async_copy(keep_hbm, keep_s, small_sem.at[1]),
        pltpu.make_async_copy(rows_hbm, rows_s, small_sem.at[2]),
    ]
    for copy in table_copies:
        copy.start()

    def basis_copies(group, parity):
        found, first = [], 0
        for i, count in enumerate(COPIES[parity]):
            part = pl.ds(group * GROUP + first, count)
            sem = basis_sem.at[group * len(COPIES[1]) + i]
            copy = pltpu.make_async_copy(basis.at[part], basis_v.at[part], sem)
            found.append((copy, first, count))
            first += count
        return found

    early_copies = basis_copies(0, 0)
    early_copies[0][0].start()
    for copy in table_copies:
        copy.wait()

    for group in range(groups):
        part = pl.ds(group * GROUP, GROUP)

        @pl.loop(0, slots)
        def _(m):
            place = place_of(slot_s[m], owner_slots, half_slots)
            if group == 0:
                keep_place[place] = keep_s[m]
                rows_place[place] = rows_s[m]
            pltpu.make_async_copy(
                panels.at[m, part], panels_v.at[place, part], panel_sem.at[group]
            ).start()

        for copy, _, _ in early_copies[1:] if group == 0 else basis_copies(group, group % 2):
            copy.start()

    offsets_of(keep_place, tile_place, shift_place, owner_slots)
    column = lax.broadcasted_iota(jnp.int32, slot_column.shape, 1)
    slot_at = jnp.full(slot_column.shape, owner_slots, jnp.int32)
    rows_at = jnp.zeros(slot_column.shape, jnp.int32)
    for j in range(owner_slots):
        keep = keep_place[j]
        offset = tile_place[j] * LANES + shift_place[j]
        within = (column >= offset) & (column < offset + keep)
        slot_at = jnp.where(within, j, slot_at)
        rows_at = jnp.where(within, rows_place[j], rows_at)
        scalars[j : j + 1, :] = jnp.full((1, LANES), offset, jnp.int32)
        scalars[owner_slots + j : owner_slots + j + 1, :] = jnp.full((1, LANES), keep, jnp.int32)
    slot_column[...] = slot_at
    rows_column[...] = rows_at

    side = GROUP * GROUP
    row = lax.broadcasted_iota(jnp.int32, (side, side), 0)
    column = lax.broadcasted_iota(jnp.int32, (side, side), 1)
    swap = (column == (row % GROUP) * GROUP + row // GROUP).astype(jnp.float32).astype(jnp.bfloat16)

    tables = (tile_place, shift_place, owner_slots)
    all_owners = range(mine.shape[0] * lax.axis_size("pa"))

    def group_step(group, parity, out_v, out_before):
        here = pl.ds(pl.multiple_of(group * GROUP, GROUP), GROUP)
        pltpu.make_async_copy(
            panels_v.at[:, here], panels_v.at[:, here], panel_sem.at[group]
        ).wait()
        on_units(functools.partial(turn, swap, panels_v, here, lhs_v), SIDE)
        for i, (copy, first, count) in enumerate(basis_copies(group, parity)):
            copy.wait()
            step = functools.partial(products, lhs_v, basis_v, out_v, group * GROUP, first, count)
            on_units(step, slots)
            if i < 2:
                line = jnp.maximum(group - 1, 0) * GROUP
                half = len(all_owners) // 2
                part = all_owners[i * half : (i + 1) * half]
                pack(out_before, mine, far, near, line, tables, part)

    @pl.loop(0, groups // 2)
    def _(pair):
        group_step(2 * pair, 0, out_even, out_odd)
        group_step(2 * pair + 1, 1, out_odd, out_even)

    pack(out_odd, mine, far, near, (groups - 1) * GROUP, tables, all_owners)


def folded_rows(rows, width):
    whole, rest = divmod(width, LANES)
    return rows * whole + (rows if rest > LANES // 2 else rows // 2 if rest else 0)


def fold(tiles, out, width):
    rows = tiles[0].shape[0]
    lane = lax.broadcasted_iota(jnp.int32, (rows // 2, LANES), 1)
    for t, tile in enumerate(tiles):
        if t == len(tiles) - 1 and out.shape[0] < rows * len(tiles):
            low, high = tile[: rows // 2], tile[rows // 2 :]
            tile = jnp.where(lane < LANES // 2, low, pltpu.roll(high, LANES // 2, 1))
        out[t * rows : t * rows + tile.shape[0], :] = tile.astype(out.dtype)


def unfold(block, rows):
    count = block.shape[0] // rows
    tiles = [block[t * rows : (t + 1) * rows, :] for t in range(count)]
    if count * rows < block.shape[0]:
        low = block[count * rows :, :].astype(jnp.float32)
        high = pltpu.roll(low, LANES // 2, 1)
        tiles.append(jnp.concatenate([low, high], axis=0).astype(block.dtype))
    return tiles


def sum_kernel(steps, width, mine, got, *out):
    for i, step in enumerate(steps):
        tiles = [mine[step, t] + got[i, t] for t in range(mine.shape[1])]
        fold(tiles, out[i], width)


def kl_kernel(part, owners, width, slot_column, rows_column, kl, *refs):
    blocks, (out, packed_v) = refs[:owners], refs[owners:]
    owner_slots, rows, freqs = kl.shape
    shares = lax.axis_size("af")
    per_source = freqs // owners
    me = lax.axis_index("ma")
    for step in range(owners):
        source = on_ring(cyclic(on_ring(me) - step, owners))
        at = pl.multiple_of(source * per_source, GROUP)
        for t, tile in enumerate(unfold(blocks[step], per_source)):
            packed_v[pl.ds(at, per_source), t * LANES : (t + 1) * LANES] = tile
    share_rows = rows // shares
    at = pl.multiple_of(cyclic(lax.axis_index("af") + part, shares) * share_rows, GROUP)
    lhs = kl[:, pl.ds(at, share_rows), :].reshape(owner_slots * share_rows, freqs)
    product = jnp.dot(lhs, packed_v[...], preferred_element_type=jnp.float32)
    line = lax.broadcasted_iota(jnp.int32, (share_rows, LANES), 0) + at
    tiles = []
    for t in range(packed_v.shape[1] // LANES):
        lanes = slice(t * LANES, (t + 1) * LANES)
        slot_at = slot_column[0:1, lanes]
        total = jnp.zeros((share_rows, LANES), jnp.float32)
        for j in range(owner_slots):
            here = product[j * share_rows : (j + 1) * share_rows, lanes]
            total = jnp.where(slot_at == j, here, total)
        tiles.append(jnp.where(line < rows_column[0:1, lanes], total, 0.0))
    fold(tiles, out, width)


def unpack_kernel(scalars, mine, got, out, sum_v, out_v, sems):
    owner_slots, rows, modes = out_v.shape
    places = [
        [jnp.max(scalars[k * owner_slots + j : k * owner_slots + j + 1, :]) for k in range(2)]
        for j in range(owner_slots)
    ]
    for t, (a, b) in enumerate(zip(unfold(mine, rows), unfold(got, rows))):
        sum_v[t] = a + b.astype(jnp.float32)
    lane = lax.broadcasted_iota(jnp.int32, (rows, LANES), 1)
    copies = []
    for j, (offset, keep) in enumerate(places):
        tile = lax.div(offset, LANES)
        shift = offset - tile * LANES
        back = lax.rem(LANES - shift, LANES)
        turned = [pltpu.roll(sum_v[tile + t], back, 1) for t in range(modes // LANES + 1)]
        for t in range(modes // LANES):
            value = jnp.where(lane < LANES - shift, turned[t], turned[t + 1])
            value = jnp.where(lane < keep - t * LANES, value, 0.0)
            out_v[j, :, t * LANES : (t + 1) * LANES] = value
        copy = pltpu.make_async_copy(out_v.at[j], out.at[j], sems.at[j])
        copy.start()
        copies.append(copy)
    for copy in copies:
        copy.wait()


HBM = pl.BlockSpec(memory_space=pltpu.HBM)
VMEM = pl.BlockSpec(memory_space=pltpu.VMEM)
SMALL = pltpu.CompilerParams(vmem_limit_bytes=8 * MIB)


def in_hbm(operand):
    return pltpu.with_memory_space_constraint(operand, pltpu.HBM)


def project(panels, svd_basis, slot_of_m, svd_keep, kl_keep, owner_slots, width):
    slots, freqs, depth = panels.shape
    modes = svd_basis.shape[2]
    owners = lax.axis_size("ma")

    def packed(count):
        return jax.ShapeDtypeStruct((count, width // LANES, freqs, LANES), jnp.float32)

    column = jax.ShapeDtypeStruct((8, width), jnp.int32)
    return pl.pallas_call(
        functools.partial(project_kernel, owner_slots),
        out_shape=(
            packed(owners),
            packed(1),
            packed(owners - 1),
            column,
            column,
            jax.ShapeDtypeStruct((8, LANES), jnp.int32),
        ),
        in_specs=[HBM] * 5,
        out_specs=(VMEM,) * 6,
        scratch_shapes=[pltpu.SMEM((slots,), jnp.int32)] * 7
        + [
            pltpu.VMEM((slots, freqs, depth), jnp.bfloat16),
            pltpu.VMEM((freqs, depth, modes), jnp.bfloat16),
            pltpu.VMEM((GROUP, slots, depth), jnp.bfloat16),
            pltpu.VMEM((modes // LANES * GROUP * slots, LANES), jnp.float32),
            pltpu.VMEM((modes // LANES * GROUP * slots, LANES), jnp.float32),
            pltpu.SemaphoreType.DMA((3,)),
            pltpu.SemaphoreType.DMA((freqs // GROUP,)),
            pltpu.SemaphoreType.DMA((freqs // GROUP * len(COPIES[1]),)),
        ],
        compiler_params=pltpu.CompilerParams(vmem_limit_bytes=48 * MIB),
        cost_estimate=pl.CostEstimate(
            flops=2 * slots * freqs * depth * modes,
            bytes_accessed=2 * freqs * depth * (modes + slots),
            transcendentals=0,
        ),
        name="project",
    )(*map(in_hbm, (slot_of_m, svd_keep, kl_keep, panels, svd_basis)))


def sum_pair(steps, width, mine, got):
    kind = jax.ShapeDtypeStruct((folded_rows(mine.shape[2], width), LANES), jnp.bfloat16)
    return pl.pallas_call(
        functools.partial(sum_kernel, steps, width),
        out_shape=(kind,) * len(steps),
        in_specs=[VMEM] * 2,
        out_specs=(VMEM,) * len(steps),
        compiler_params=SMALL,
        cost_estimate=pl.CostEstimate(
            flops=got.size, bytes_accessed=10 * got.size, transcendentals=0
        ),
        name="sum_pair",
    )(mine, got)


def kl_project(part, kind, width, slot_column, rows_column, kl_basis, blocks):
    owners, shares = lax.axis_size("ma"), lax.axis_size("af")
    rows, freqs = kl_basis.shape[1:]
    wide = slot_column.shape[1]
    return pl.pallas_call(
        functools.partial(kl_kernel, part, owners, width),
        out_shape=jax.ShapeDtypeStruct((folded_rows(rows // shares, width), LANES), kind),
        in_specs=[VMEM] * (3 + owners),
        out_specs=VMEM,
        scratch_shapes=[pltpu.VMEM((freqs, wide), jnp.bfloat16)],
        compiler_params=SMALL,
        cost_estimate=pl.CostEstimate(
            flops=2 * kl_basis.size * wide // shares,
            bytes_accessed=2 * kl_basis.size,
            transcendentals=0,
        ),
        name="kl_project",
    )(slot_column, rows_column, kl_basis, *blocks)


def unpack(scalars, mine, got, owner_slots, rows, modes, width):
    tiles = -(-width // LANES) + modes // LANES + 1
    return pl.pallas_call(
        unpack_kernel,
        out_shape=jax.ShapeDtypeStruct((owner_slots, rows, modes), jnp.float32),
        in_specs=[VMEM] * 3,
        out_specs=HBM,
        scratch_shapes=[
            pltpu.VMEM((tiles, rows, LANES), jnp.float32),
            pltpu.VMEM((owner_slots, rows, modes), jnp.float32),
            pltpu.SemaphoreType.DMA((owner_slots,)),
        ],
        compiler_params=SMALL,
        cost_estimate=pl.CostEstimate(
            flops=mine.size, bytes_accessed=10 * mine.size, transcendentals=0
        ),
        name="unpack",
    )(scalars, mine, got)


def pairs(axis):
    return [(i, i ^ 1) for i in range(lax.axis_size(axis))]


def ring(step):
    size = lax.axis_size("ma")
    return [(i, on_ring((on_ring(i) + step) % size)) for i in range(size)]


def shards(panels, svd_basis, kl_basis, slot_of_m, svd_keep, kl_keep):
    owner_slots, modes = kl_basis.shape[0], svd_basis.shape[2]
    owners = lax.axis_size("ma")
    width = min(OWNER_BUDGET, owner_slots * modes)
    wide = -(-width // LANES) * LANES
    mine, far, near, slot_column, rows_column, scalars = project(
        panels, svd_basis, slot_of_m, svd_keep, kl_keep, owner_slots, wide
    )
    first = far_step(owners)
    others = [step for step in range(owners) if step != first]
    got_far = lax.ppermute(far, "pa", pairs("pa"))
    near, got_far = lax.optimization_barrier((near, got_far))
    got_near = lax.ppermute(near, "pa", pairs("pa"))
    summed = dict(zip([first], sum_pair([first], width, mine, got_far)))
    summed |= zip(others, sum_pair(others, width, mine, got_near))
    blocks = {
        step: lax.ppermute(summed[step], "ma", ring(step)) if step else summed[step]
        for step in [first] + others
    }
    tables = (width, slot_column, rows_column, kl_basis, [blocks[step] for step in range(owners)])
    send = kl_project(1, jnp.bfloat16, *tables)
    got = lax.ppermute(send, "af", pairs("af"))
    mine = kl_project(0, jnp.float32, *tables)
    rows = kl_basis.shape[1] // lax.axis_size("af")
    return unpack(scalars, mine, got, owner_slots, rows, modes, width)


def kernels_fit(mesh, args):
    panels, svd_basis, kl_basis = args[:3]
    slots = panels.shape[0] // mesh.shape["grp"]
    freqs = svd_basis.shape[0] // (mesh.shape["af"] * mesh.shape["ma"])
    owner_slots = kl_basis.shape[0] // (mesh.shape["pa"] * mesh.shape["ma"])
    share_rows = kl_basis.shape[1] // mesh.shape["af"]
    return (
        freqs % (2 * GROUP) == 0
        and slots % (GROUP * mesh.shape["pa"]) == 0
        and owner_slots == 4
        and svd_basis.shape[2] == 2 * LANES
        and share_rows % (2 * GROUP) == 0
        and mesh.shape["pa"] == 2
        and mesh.shape["af"] == 2
        and mesh.shape["ma"] == 4
    )


def solution(mesh):
    in_specs = (
        P("grp", ("af", "ma"), "pa"),
        P(("af", "ma"), "pa", None),
        P(("pa", "ma"), None, "af"),
        P(),
        P(),
        P(),
    )
    out_specs = P(("grp", "pa", "ma"), "af", None)

    def run(*args):
        body = shards if kernels_fit(mesh, args) else shards_plain
        mapped = jax.shard_map(
            body, mesh=mesh, in_specs=in_specs, out_specs=out_specs, check_vma=False
        )
        return mapped(*args)

    return run
```

```python
import functools

import jax
import jax.numpy as jnp
from jax import lax
from jax.experimental import pallas as pl
from jax.experimental.pallas import tpu as pltpu
from jax.sharding import PartitionSpec as P

LANES = 128
GROUP = 16
COPIES = (8, 8)
OWNER_BUDGET = 576
MIB = 2**20


def shards_plain(panels, svd_basis, kl_basis, slot_of_m, svd_keep, kl_keep):
    slot_count = slot_of_m.shape[0]
    order_slots = jnp.argsort(slot_of_m)
    keep_slots = jnp.take(svd_keep, order_slots, axis=0)
    modes_slots = jnp.take(kl_keep, order_slots, axis=0)
    width_modes = svd_basis.shape[2]
    owner_rows = kl_basis.shape[0]
    slot_rows = slot_count // lax.axis_size("pa")
    slot_start = lax.axis_index("pa") * slot_rows
    owner_start = slot_start + lax.axis_index("ma") * owner_rows
    modes_owner = lax.dynamic_slice_in_dim(modes_slots, owner_start, owner_rows, 0)
    chosen = jnp.take(panels, order_slots, axis=0)
    summed = lax.psum_scatter(
        jnp.einsum("mfb,fbr->mfr", chosen, svd_basis, preferred_element_type=jnp.float32),
        "pa",
        scatter_dimension=0,
        tiled=True,
    )
    keep_here = lax.dynamic_slice_in_dim(keep_slots, slot_start, slot_rows, 0)
    columns = jnp.arange(width_modes, dtype=jnp.int32)
    retained = jnp.where(columns[None, None, :] < keep_here[:, None, None], summed, 0.0).astype(
        jnp.bfloat16
    )
    relaid = lax.all_to_all(retained, "ma", split_axis=0, concat_axis=1, tiled=True)
    partial_sums = jnp.einsum("mkf,mfr->mkr", kl_basis, relaid, preferred_element_type=jnp.float32)
    modes = jnp.arange(kl_basis.shape[1], dtype=jnp.int32)
    partial_sums = jnp.where(modes[None, :, None] < modes_owner[:, None, None], partial_sums, 0.0)
    return lax.psum_scatter(partial_sums, "af", scatter_dimension=1, tiled=True)


def cyclic(value, count):
    return lax.rem(value + count, count)


def on_ring(z):
    return z ^ (z // 2) if isinstance(z, int) else z ^ lax.shift_right_logical(z, 1)


def far_step(owners):
    return owners // 2


def place_of(slot, owner_slots, half_slots):
    half = cyclic(lax.div(slot, half_slots) - lax.axis_index("pa"), lax.axis_size("pa"))
    within = lax.rem(slot, half_slots)
    owner = on_ring(lax.div(within, owner_slots)) - on_ring(lax.axis_index("ma"))
    owner = cyclic(owner, lax.axis_size("ma"))
    return half * half_slots + owner * owner_slots + lax.rem(within, owner_slots)


def offsets_of(keep_place, tile_place, shift_place, owner_slots):
    @pl.loop(0, keep_place.shape[0] // owner_slots)
    def _(at):
        offset = jnp.int32(0)
        for j in range(owner_slots):
            place = at * owner_slots + j
            tile = lax.div(offset, LANES)
            tile_place[place] = tile
            shift_place[place] = offset - tile * LANES
            offset = offset + keep_place[place]


def pack(out_v, mine, far, near, line, tables, owners_at):
    tile_place, shift_place, owner_slots = tables
    owners, width_tiles = mine.shape[:2]
    slots = 2 * owners * owner_slots
    tiles = out_v.shape[0] // (GROUP * slots)
    lane = lax.broadcasted_iota(jnp.int32, (GROUP, LANES), 1)
    rows = pl.ds(pl.multiple_of(line, GROUP), GROUP)
    turned = {
        place: pltpu.roll(
            out_v[pl.ds(place, tiles * GROUP, stride=slots), :], shift_place[place], 1
        )
        for place in range(owners_at[0] * owner_slots, (owners_at[-1] + 1) * owner_slots)
    }
    for at in owners_at:
        to, owner = mine, at % owners
        if at >= owners:
            first = far_step(owners)
            to, owner = (far, 0) if owner == first else (near, owner - (owner > first))
        values, tile_before = None, None
        for j in range(owner_slots):
            place = at * owner_slots + j
            tile = tile_place[place]
            left = lane < shift_place[place]
            moved = [turned[place][t * GROUP : (t + 1) * GROUP] for t in range(tiles)]
            shared = moved[0]
            if j > 0:
                step = tile - tile_before
                shared = values[0]
                for t in range(1, tiles + 1):
                    shared = jnp.where(step == t, values[t], shared)
            values = (
                [jnp.where(left, shared, moved[0])]
                + [jnp.where(left, moved[t - 1], moved[t]) for t in range(1, tiles)]
                + [moved[tiles - 1]]
            )
            tile_before = tile
            for t in reversed(range(tiles + 1)):
                to[owner, jnp.minimum(tile + t, width_tiles - 1), rows, :] = values[t]


def project_kernel(
    owner_slots, slot_hbm, keep_hbm, rows_hbm, panels, basis,
    mine, far, near, slot_column, rows_column, scalars,
    slot_s, keep_s, rows_s, order_place, keep_place, rows_place, tile_place, shift_place,
    panels_v, basis_v, lhs_v, out_even, out_odd, small_sem, panel_sem, basis_sem,
):
    slots, freqs, depth = panels_v.shape
    groups = freqs // GROUP
    half_slots = slots // lax.axis_size("pa")

    table_copies = [
        pltpu.make_async_copy(slot_hbm, slot_s, small_sem.at[0]),
        pltpu.make_async_copy(keep_hbm, keep_s, small_sem.at[1]),
        pltpu.make_async_copy(rows_hbm, rows_s, small_sem.at[2]),
    ]
    for copy in table_copies:
        copy.start()

    def panels_copy(group):
        part = pl.ds(group * GROUP, GROUP)
        return pltpu.make_async_copy(panels.at[:, part], panels_v.at[:, part], panel_sem.at[group])

    def basis_copy(group, i):
        part = pl.ds(group * GROUP + sum(COPIES[:i]), COPIES[i])
        sem = basis_sem.at[group * len(COPIES) + i]
        return pltpu.make_async_copy(basis.at[part], basis_v.at[part], sem)

    for group in range(groups):
        panels_copy(group).start()
        for i in range(len(COPIES)):
            basis_copy(group, i).start()
    for copy in table_copies:
        copy.wait()

    @pl.loop(0, slots)
    def _(m):
        place = place_of(slot_s[m], owner_slots, half_slots)
        order_place[place] = m
        keep_place[place] = keep_s[m]
        rows_place[place] = rows_s[m]

    offsets_of(keep_place, tile_place, shift_place, owner_slots)
    column = lax.broadcasted_iota(jnp.int32, slot_column.shape, 1)
    slot_at = jnp.full(slot_column.shape, owner_slots, jnp.int32)
    rows_at = jnp.zeros(slot_column.shape, jnp.int32)
    for j in range(owner_slots):
        keep = keep_place[j]
        offset = tile_place[j] * LANES + shift_place[j]
        within = (column >= offset) & (column < offset + keep)
        slot_at = jnp.where(within, j, slot_at)
        rows_at = jnp.where(within, rows_place[j], rows_at)
        scalars[j : j + 1, :] = jnp.full((1, LANES), offset, jnp.int32)
        scalars[owner_slots + j : owner_slots + j + 1, :] = jnp.full((1, LANES), keep, jnp.int32)
    slot_column[...] = slot_at
    rows_column[...] = rows_at

    side = GROUP * GROUP
    row = lax.broadcasted_iota(jnp.int32, (side, side), 0)
    column = lax.broadcasted_iota(jnp.int32, (side, side), 1)
    swap = (column == (row % GROUP) * GROUP + row // GROUP).astype(jnp.float32).astype(jnp.bfloat16)

    tables = (tile_place, shift_place, owner_slots)
    all_owners = range(mine.shape[0] * lax.axis_size("pa"))

    def group_step(group, out_v, out_before):
        here = pl.ds(pl.multiple_of(group * GROUP, GROUP), GROUP)
        panels_copy(group).wait()
        for block in range(0, slots, GROUP):
            tile = jnp.concatenate(
                [panels_v[order_place[place], here, :] for place in range(block, block + GROUP)]
            )
            turned = jnp.dot(swap, tile, preferred_element_type=jnp.float32).astype(jnp.bfloat16)
            lhs_v[:, block : block + GROUP, :] = turned.reshape(GROUP, GROUP, depth)
        for i in range(len(COPIES)):
            basis_copy(group, i).wait()
            for f in range(sum(COPIES[:i]), sum(COPIES[: i + 1])):
                product = jnp.dot(
                    lhs_v[f], basis_v[group * GROUP + f], preferred_element_type=jnp.float32
                )
                for t in range(product.shape[1] // LANES):
                    at = (t * GROUP + f) * slots
                    out_v[at : at + slots, :] = product[:, t * LANES : (t + 1) * LANES]
            line = jnp.maximum(group - 1, 0) * GROUP
            share = len(all_owners) // len(COPIES)
            part = all_owners[i * share : (i + 1) * share]
            pack(out_before, mine, far, near, line, tables, part)

    @pl.loop(0, groups // 2)
    def _(pair):
        group_step(2 * pair, out_even, out_odd)
        group_step(2 * pair + 1, out_odd, out_even)

    pack(out_odd, mine, far, near, (groups - 1) * GROUP, tables, all_owners)


def folded_rows(rows, width):
    whole, rest = divmod(width, LANES)
    return rows * whole + (rows if rest > LANES // 2 else rows // 2 if rest else 0)


def fold(tiles, out, width):
    rows = tiles[0].shape[0]
    lane = lax.broadcasted_iota(jnp.int32, (rows // 2, LANES), 1)
    for t, tile in enumerate(tiles):
        if t == len(tiles) - 1 and out.shape[0] < rows * len(tiles):
            low, high = tile[: rows // 2], tile[rows // 2 :]
            tile = jnp.where(lane < LANES // 2, low, pltpu.roll(high, LANES // 2, 1))
        out[t * rows : t * rows + tile.shape[0], :] = tile.astype(out.dtype)


def unfold(block, rows):
    count = block.shape[0] // rows
    tiles = [block[t * rows : (t + 1) * rows, :] for t in range(count)]
    if count * rows < block.shape[0]:
        low = block[count * rows :, :].astype(jnp.float32)
        high = pltpu.roll(low, LANES // 2, 1)
        tiles.append(jnp.concatenate([low, high], axis=0).astype(block.dtype))
    return tiles


def sum_kernel(steps, width, mine, got, *out):
    for i, step in enumerate(steps):
        tiles = [mine[step, t] + got[i, t] for t in range(mine.shape[1])]
        fold(tiles, out[i], width)


def kl_kernel(part, owners, width, slot_column, rows_column, kl, *refs):
    blocks, (out, packed_v) = refs[:owners], refs[owners:]
    owner_slots, rows, freqs = kl.shape
    shares = lax.axis_size("af")
    per_source = freqs // owners
    me = lax.axis_index("ma")
    for step in range(owners):
        source = on_ring(cyclic(on_ring(me) - step, owners))
        at = pl.multiple_of(source * per_source, GROUP)
        for t, tile in enumerate(unfold(blocks[step], per_source)):
            packed_v[pl.ds(at, per_source), t * LANES : (t + 1) * LANES] = tile
    share_rows = rows // shares
    at = pl.multiple_of(cyclic(lax.axis_index("af") + part, shares) * share_rows, GROUP)
    lhs = kl[:, pl.ds(at, share_rows), :].reshape(owner_slots * share_rows, freqs)
    product = jnp.dot(lhs, packed_v[...], preferred_element_type=jnp.float32)
    line = lax.broadcasted_iota(jnp.int32, (share_rows, LANES), 0) + at
    tiles = []
    for t in range(packed_v.shape[1] // LANES):
        lanes = slice(t * LANES, (t + 1) * LANES)
        slot_at = slot_column[0:1, lanes]
        total = jnp.zeros((share_rows, LANES), jnp.float32)
        for j in range(owner_slots):
            here = product[j * share_rows : (j + 1) * share_rows, lanes]
            total = jnp.where(slot_at == j, here, total)
        tiles.append(jnp.where(line < rows_column[0:1, lanes], total, 0.0))
    fold(tiles, out, width)


def unpack_kernel(scalars, mine, got, out, sum_v, out_v, sems):
    owner_slots, rows, modes = out_v.shape
    places = [
        [jnp.max(scalars[k * owner_slots + j : k * owner_slots + j + 1, :]) for k in range(2)]
        for j in range(owner_slots)
    ]
    for t, (a, b) in enumerate(zip(unfold(mine, rows), unfold(got, rows))):
        sum_v[t] = a + b.astype(jnp.float32)
    lane = lax.broadcasted_iota(jnp.int32, (rows, LANES), 1)
    copies = []
    for j, (offset, keep) in enumerate(places):
        tile = lax.div(offset, LANES)
        shift = offset - tile * LANES
        back = lax.rem(LANES - shift, LANES)
        turned = [pltpu.roll(sum_v[tile + t], back, 1) for t in range(modes // LANES + 1)]
        for t in range(modes // LANES):
            value = jnp.where(lane < LANES - shift, turned[t], turned[t + 1])
            value = jnp.where(lane < keep - t * LANES, value, 0.0)
            out_v[j, :, t * LANES : (t + 1) * LANES] = value
        copy = pltpu.make_async_copy(out_v.at[j], out.at[j], sems.at[j])
        copy.start()
        copies.append(copy)
    for copy in copies:
        copy.wait()


HBM = pl.BlockSpec(memory_space=pltpu.HBM)
VMEM = pl.BlockSpec(memory_space=pltpu.VMEM)
SMALL = pltpu.CompilerParams(vmem_limit_bytes=8 * MIB)


def in_hbm(operand):
    return pltpu.with_memory_space_constraint(operand, pltpu.HBM)


def project(panels, svd_basis, slot_of_m, svd_keep, kl_keep, owner_slots, width):
    slots, freqs, depth = panels.shape
    modes = svd_basis.shape[2]
    owners = lax.axis_size("ma")

    def packed(count):
        return jax.ShapeDtypeStruct((count, width // LANES, freqs, LANES), jnp.float32)

    column = jax.ShapeDtypeStruct((8, width), jnp.int32)
    return pl.pallas_call(
        functools.partial(project_kernel, owner_slots),
        out_shape=(
            packed(owners),
            packed(1),
            packed(owners - 1),
            column,
            column,
            jax.ShapeDtypeStruct((8, LANES), jnp.int32),
        ),
        in_specs=[HBM] * 5,
        out_specs=(VMEM,) * 6,
        scratch_shapes=[pltpu.SMEM((slots,), jnp.int32)] * 8
        + [
            pltpu.VMEM((slots, freqs, depth), jnp.bfloat16),
            pltpu.VMEM((freqs, depth, modes), jnp.bfloat16),
            pltpu.VMEM((GROUP, slots, depth), jnp.bfloat16),
            pltpu.VMEM((modes // LANES * GROUP * slots, LANES), jnp.float32),
            pltpu.VMEM((modes // LANES * GROUP * slots, LANES), jnp.float32),
            pltpu.SemaphoreType.DMA((3,)),
            pltpu.SemaphoreType.DMA((freqs // GROUP,)),
            pltpu.SemaphoreType.DMA((freqs // GROUP * len(COPIES),)),
        ],
        compiler_params=pltpu.CompilerParams(vmem_limit_bytes=48 * MIB),
        cost_estimate=pl.CostEstimate(
            flops=2 * slots * freqs * depth * modes,
            bytes_accessed=2 * freqs * depth * (modes + slots),
            transcendentals=0,
        ),
        name="project",
    )(*map(in_hbm, (slot_of_m, svd_keep, kl_keep, panels, svd_basis)))


def sum_pair(steps, width, mine, got):
    kind = jax.ShapeDtypeStruct((folded_rows(mine.shape[2], width), LANES), jnp.bfloat16)
    return pl.pallas_call(
        functools.partial(sum_kernel, steps, width),
        out_shape=(kind,) * len(steps),
        in_specs=[VMEM] * 2,
        out_specs=(VMEM,) * len(steps),
        compiler_params=SMALL,
        cost_estimate=pl.CostEstimate(
            flops=got.size, bytes_accessed=10 * got.size, transcendentals=0
        ),
        name="sum_pair",
    )(mine, got)


def kl_project(part, kind, width, slot_column, rows_column, kl_basis, blocks):
    owners, shares = lax.axis_size("ma"), lax.axis_size("af")
    rows, freqs = kl_basis.shape[1:]
    wide = slot_column.shape[1]
    return pl.pallas_call(
        functools.partial(kl_kernel, part, owners, width),
        out_shape=jax.ShapeDtypeStruct((folded_rows(rows // shares, width), LANES), kind),
        in_specs=[VMEM] * (3 + owners),
        out_specs=VMEM,
        scratch_shapes=[pltpu.VMEM((freqs, wide), jnp.bfloat16)],
        compiler_params=SMALL,
        cost_estimate=pl.CostEstimate(
            flops=2 * kl_basis.size * wide // shares,
            bytes_accessed=2 * kl_basis.size,
            transcendentals=0,
        ),
        name="kl_project",
    )(slot_column, rows_column, kl_basis, *blocks)


def unpack(scalars, mine, got, owner_slots, rows, modes, width):
    tiles = -(-width // LANES) + modes // LANES + 1
    return pl.pallas_call(
        unpack_kernel,
        out_shape=jax.ShapeDtypeStruct((owner_slots, rows, modes), jnp.float32),
        in_specs=[VMEM] * 3,
        out_specs=HBM,
        scratch_shapes=[
            pltpu.VMEM((tiles, rows, LANES), jnp.float32),
            pltpu.VMEM((owner_slots, rows, modes), jnp.float32),
            pltpu.SemaphoreType.DMA((owner_slots,)),
        ],
        compiler_params=SMALL,
        cost_estimate=pl.CostEstimate(
            flops=mine.size, bytes_accessed=10 * mine.size, transcendentals=0
        ),
        name="unpack",
    )(scalars, mine, got)


def pairs(axis):
    return [(i, i ^ 1) for i in range(lax.axis_size(axis))]


def ring(step):
    size = lax.axis_size("ma")
    return [(i, on_ring((on_ring(i) + step) % size)) for i in range(size)]


def shards(panels, svd_basis, kl_basis, slot_of_m, svd_keep, kl_keep):
    owner_slots, modes = kl_basis.shape[0], svd_basis.shape[2]
    owners = lax.axis_size("ma")
    width = min(OWNER_BUDGET, owner_slots * modes)
    wide = -(-width // LANES) * LANES
    mine, far, near, slot_column, rows_column, scalars = project(
        panels, svd_basis, slot_of_m, svd_keep, kl_keep, owner_slots, wide
    )
    first = far_step(owners)
    others = [step for step in range(owners) if step != first]
    got_far = lax.ppermute(far, "pa", pairs("pa"))
    near, got_far = lax.optimization_barrier((near, got_far))
    got_near = lax.ppermute(near, "pa", pairs("pa"))
    summed = dict(zip([first], sum_pair([first], width, mine, got_far)))
    summed |= zip(others, sum_pair(others, width, mine, got_near))
    blocks = {
        step: lax.ppermute(summed[step], "ma", ring(step)) if step else summed[step]
        for step in [first] + others
    }
    tables = (width, slot_column, rows_column, kl_basis, [blocks[step] for step in range(owners)])
    send = kl_project(1, jnp.bfloat16, *tables)
    got = lax.ppermute(send, "af", pairs("af"))
    mine = kl_project(0, jnp.float32, *tables)
    rows = kl_basis.shape[1] // lax.axis_size("af")
    return unpack(scalars, mine, got, owner_slots, rows, modes, width)


def kernels_fit(mesh, args):
    panels, svd_basis, kl_basis = args[:3]
    slots = panels.shape[0] // mesh.shape["grp"]
    freqs = svd_basis.shape[0] // (mesh.shape["af"] * mesh.shape["ma"])
    owner_slots = kl_basis.shape[0] // (mesh.shape["pa"] * mesh.shape["ma"])
    share_rows = kl_basis.shape[1] // mesh.shape["af"]
    return (
        freqs % (2 * GROUP) == 0
        and slots % (GROUP * mesh.shape["pa"]) == 0
        and owner_slots == 4
        and svd_basis.shape[2] == 2 * LANES
        and share_rows % (2 * GROUP) == 0
        and mesh.shape["pa"] == 2
        and mesh.shape["af"] == 2
        and mesh.shape["ma"] == 4
    )


def solution(mesh):
    in_specs = (
        P("grp", ("af", "ma"), "pa"),
        P(("af", "ma"), "pa", None),
        P(("pa", "ma"), None, "af"),
        P(),
        P(),
        P(),
    )
    out_specs = P(("grp", "pa", "ma"), "af", None)

    def run(*args):
        body = shards if kernels_fit(mesh, args) else shards_plain
        mapped = jax.shard_map(
            body, mesh=mesh, in_specs=in_specs, out_specs=out_specs, check_vma=False
        )
        return mapped(*args)

    return run
```

```python
import functools

import jax
import jax.numpy as jnp
from jax import lax
from jax.experimental import pallas as pl
from jax.experimental.pallas import tpu as pltpu
from jax.sharding import PartitionSpec as P

LANES = 128
GROUP = 16
TOGETHER = 8
OWNER_BUDGET = 576
MIB = 2**20


def shards_plain(panels, svd_basis, kl_basis, slot_of_m, svd_keep, kl_keep):
    slot_count = slot_of_m.shape[0]
    order_slots = jnp.argsort(slot_of_m)
    keep_slots = jnp.take(svd_keep, order_slots, axis=0)
    modes_slots = jnp.take(kl_keep, order_slots, axis=0)
    width_modes = svd_basis.shape[2]
    owner_rows = kl_basis.shape[0]
    slot_rows = slot_count // lax.axis_size("pa")
    slot_start = lax.axis_index("pa") * slot_rows
    owner_start = slot_start + lax.axis_index("ma") * owner_rows
    modes_owner = lax.dynamic_slice_in_dim(modes_slots, owner_start, owner_rows, 0)
    chosen = jnp.take(panels, order_slots, axis=0)
    summed = lax.psum_scatter(
        jnp.einsum("mfb,fbr->mfr", chosen, svd_basis, preferred_element_type=jnp.float32),
        "pa",
        scatter_dimension=0,
        tiled=True,
    )
    keep_here = lax.dynamic_slice_in_dim(keep_slots, slot_start, slot_rows, 0)
    columns = jnp.arange(width_modes, dtype=jnp.int32)
    retained = jnp.where(columns[None, None, :] < keep_here[:, None, None], summed, 0.0).astype(
        jnp.bfloat16
    )
    relaid = lax.all_to_all(retained, "ma", split_axis=0, concat_axis=1, tiled=True)
    partial_sums = jnp.einsum("mkf,mfr->mkr", kl_basis, relaid, preferred_element_type=jnp.float32)
    modes = jnp.arange(kl_basis.shape[1], dtype=jnp.int32)
    partial_sums = jnp.where(modes[None, :, None] < modes_owner[:, None, None], partial_sums, 0.0)
    return lax.psum_scatter(partial_sums, "af", scatter_dimension=1, tiled=True)


def cyclic(value, count):
    return lax.rem(value + count, count)


def on_ring(z):
    return z ^ (z // 2) if isinstance(z, int) else z ^ lax.shift_right_logical(z, 1)


def far_step(owners):
    return owners // 2


def place_of(slot, owner_slots, half_slots):
    half = cyclic(lax.div(slot, half_slots) - lax.axis_index("pa"), lax.axis_size("pa"))
    within = lax.rem(slot, half_slots)
    owner = on_ring(lax.div(within, owner_slots)) - on_ring(lax.axis_index("ma"))
    owner = cyclic(owner, lax.axis_size("ma"))
    return half * half_slots + owner * owner_slots + lax.rem(within, owner_slots)


def offsets_of(keep_place, tile_place, shift_place, owner_slots):
    @pl.loop(0, keep_place.shape[0] // owner_slots)
    def _(at):
        offset = jnp.int32(0)
        for j in range(owner_slots):
            place = at * owner_slots + j
            tile = lax.div(offset, LANES)
            tile_place[place] = tile
            shift_place[place] = offset - tile * LANES
            offset = offset + keep_place[place]


def pack(out_v, mine, far, near, line, tables, owners_at):
    tile_place, shift_place, owner_slots = tables
    owners, width_tiles = mine.shape[:2]
    slots = 2 * owners * owner_slots
    tiles = out_v.shape[0] // (GROUP * slots)
    lane = lax.broadcasted_iota(jnp.int32, (GROUP, LANES), 1)
    rows = pl.ds(pl.multiple_of(line, GROUP), GROUP)
    turned = {
        place: pltpu.roll(
            out_v[pl.ds(place, tiles * GROUP, stride=slots), :], shift_place[place], 1
        )
        for place in range(owners_at[0] * owner_slots, (owners_at[-1] + 1) * owner_slots)
    }
    for at in owners_at:
        to, owner = mine, at % owners
        if at >= owners:
            first = far_step(owners)
            to, owner = (far, 0) if owner == first else (near, owner - (owner > first))
        values, tile_before = None, None
        for j in range(owner_slots):
            place = at * owner_slots + j
            tile = tile_place[place]
            left = lane < shift_place[place]
            moved = [turned[place][t * GROUP : (t + 1) * GROUP] for t in range(tiles)]
            shared = moved[0]
            if j > 0:
                step = tile - tile_before
                shared = values[0]
                for t in range(1, tiles + 1):
                    shared = jnp.where(step == t, values[t], shared)
            values = (
                [jnp.where(left, shared, moved[0])]
                + [jnp.where(left, moved[t - 1], moved[t]) for t in range(1, tiles)]
                + [moved[tiles - 1]]
            )
            tile_before = tile
            for t in reversed(range(tiles + 1)):
                to[owner, jnp.minimum(tile + t, width_tiles - 1), rows, :] = values[t]


def project_kernel(
    owner_slots, slot_hbm, keep_hbm, rows_hbm, panels, basis,
    mine, far, near, slot_column, rows_column, scalars,
    slot_s, keep_s, rows_s, place_m, keep_place, rows_place, tile_place, shift_place,
    panels_v, basis_v, lhs_v, out_even, out_odd, small_sem, panel_sem, basis_sem,
):
    slots, freqs, depth = panels_v.shape
    groups, waits = freqs // GROUP, GROUP // TOGETHER
    half_slots = slots // lax.axis_size("pa")

    table_copies = [
        pltpu.make_async_copy(slot_hbm, slot_s, small_sem.at[0]),
        pltpu.make_async_copy(keep_hbm, keep_s, small_sem.at[1]),
        pltpu.make_async_copy(rows_hbm, rows_s, small_sem.at[2]),
    ]
    for copy in table_copies:
        copy.start()

    def start_basis(group, i):
        first = group * GROUP + i * TOGETHER

        @pl.loop(first, first + TOGETHER)
        def _(f):
            sem = basis_sem.at[group * waits + i]
            pltpu.make_async_copy(basis.at[f], basis_v.at[f], sem).start()

    def wait_basis(group, i):
        part = pl.ds(group * GROUP + i * TOGETHER, TOGETHER)
        sem = basis_sem.at[group * waits + i]
        pltpu.make_async_copy(basis_v.at[part], basis_v.at[part], sem).wait()

    start_basis(0, 0)
    for copy in table_copies:
        copy.wait()

    @pl.loop(0, slots)
    def _(m):
        place = place_of(slot_s[m], owner_slots, half_slots)
        place_m[m] = place
        keep_place[place] = keep_s[m]
        rows_place[place] = rows_s[m]

    for group in range(groups):
        part = pl.ds(group * GROUP, GROUP)

        @pl.loop(0, slots)
        def _(m):
            pltpu.make_async_copy(
                panels.at[m, part], panels_v.at[place_m[m], part], panel_sem.at[group]
            ).start()

        for i in range(1 if group == 0 else 0, waits):
            start_basis(group, i)

    offsets_of(keep_place, tile_place, shift_place, owner_slots)
    column = lax.broadcasted_iota(jnp.int32, slot_column.shape, 1)
    slot_at = jnp.full(slot_column.shape, owner_slots, jnp.int32)
    rows_at = jnp.zeros(slot_column.shape, jnp.int32)
    for j in range(owner_slots):
        keep = keep_place[j]
        offset = tile_place[j] * LANES + shift_place[j]
        within = (column >= offset) & (column < offset + keep)
        slot_at = jnp.where(within, j, slot_at)
        rows_at = jnp.where(within, rows_place[j], rows_at)
        scalars[j : j + 1, :] = jnp.full((1, LANES), offset, jnp.int32)
        scalars[owner_slots + j : owner_slots + j + 1, :] = jnp.full((1, LANES), keep, jnp.int32)
    slot_column[...] = slot_at
    rows_column[...] = rows_at

    side = GROUP * GROUP
    row = lax.broadcasted_iota(jnp.int32, (side, side), 0)
    column = lax.broadcasted_iota(jnp.int32, (side, side), 1)
    swap = (column == (row % GROUP) * GROUP + row // GROUP).astype(jnp.float32).astype(jnp.bfloat16)

    tables = (tile_place, shift_place, owner_slots)
    all_owners = range(mine.shape[0] * lax.axis_size("pa"))

    def group_step(group, out_v, out_before):
        here = pl.ds(pl.multiple_of(group * GROUP, GROUP), GROUP)
        pltpu.make_async_copy(
            panels_v.at[:, here], panels_v.at[:, here], panel_sem.at[group]
        ).wait()
        for block in range(0, slots, GROUP):
            tile = panels_v[block : block + GROUP, here, :].reshape(side, depth)
            turned = jnp.dot(swap, tile, preferred_element_type=jnp.float32).astype(jnp.bfloat16)
            lhs_v[:, block : block + GROUP, :] = turned.reshape(GROUP, GROUP, depth)
        for i in range(waits):
            wait_basis(group, i)
            for f in range(i * TOGETHER, (i + 1) * TOGETHER):
                product = jnp.dot(
                    lhs_v[f], basis_v[group * GROUP + f], preferred_element_type=jnp.float32
                )
                for t in range(product.shape[1] // LANES):
                    at = (t * GROUP + f) * slots
                    out_v[at : at + slots, :] = product[:, t * LANES : (t + 1) * LANES]
            line = jnp.maximum(group - 1, 0) * GROUP
            share = len(all_owners) // waits
            part = all_owners[i * share : (i + 1) * share]
            pack(out_before, mine, far, near, line, tables, part)

    @pl.loop(0, groups // 2)
    def _(pair):
        group_step(2 * pair, out_even, out_odd)
        group_step(2 * pair + 1, out_odd, out_even)

    pack(out_odd, mine, far, near, (groups - 1) * GROUP, tables, all_owners)


def folded_rows(rows, width):
    whole, rest = divmod(width, LANES)
    return rows * whole + (rows if rest > LANES // 2 else rows // 2 if rest else 0)


def fold(tiles, out, width):
    rows = tiles[0].shape[0]
    lane = lax.broadcasted_iota(jnp.int32, (rows // 2, LANES), 1)
    for t, tile in enumerate(tiles):
        if t == len(tiles) - 1 and out.shape[0] < rows * len(tiles):
            low, high = tile[: rows // 2], tile[rows // 2 :]
            tile = jnp.where(lane < LANES // 2, low, pltpu.roll(high, LANES // 2, 1))
        out[t * rows : t * rows + tile.shape[0], :] = tile.astype(out.dtype)


def unfold(block, rows):
    count = block.shape[0] // rows
    tiles = [block[t * rows : (t + 1) * rows, :] for t in range(count)]
    if count * rows < block.shape[0]:
        low = block[count * rows :, :].astype(jnp.float32)
        high = pltpu.roll(low, LANES // 2, 1)
        tiles.append(jnp.concatenate([low, high], axis=0).astype(block.dtype))
    return tiles


def sum_kernel(steps, width, mine, got, *out):
    for i, step in enumerate(steps):
        tiles = [mine[step, t] + got[i, t] for t in range(mine.shape[1])]
        fold(tiles, out[i], width)


def kl_kernel(part, owners, width, slot_column, rows_column, kl, *refs):
    blocks, (out, packed_v) = refs[:owners], refs[owners:]
    owner_slots, rows, freqs = kl.shape
    shares = lax.axis_size("af")
    per_source = freqs // owners
    me = lax.axis_index("ma")
    for step in range(owners):
        source = on_ring(cyclic(on_ring(me) - step, owners))
        at = pl.multiple_of(source * per_source, GROUP)
        for t, tile in enumerate(unfold(blocks[step], per_source)):
            packed_v[pl.ds(at, per_source), t * LANES : (t + 1) * LANES] = tile
    share_rows = rows // shares
    at = pl.multiple_of(cyclic(lax.axis_index("af") + part, shares) * share_rows, GROUP)
    lhs = kl[:, pl.ds(at, share_rows), :].reshape(owner_slots * share_rows, freqs)
    product = jnp.dot(lhs, packed_v[...], preferred_element_type=jnp.float32)
    line = lax.broadcasted_iota(jnp.int32, (share_rows, LANES), 0) + at
    tiles = []
    for t in range(packed_v.shape[1] // LANES):
        lanes = slice(t * LANES, (t + 1) * LANES)
        slot_at = slot_column[0:1, lanes]
        total = jnp.zeros((share_rows, LANES), jnp.float32)
        for j in range(owner_slots):
            here = product[j * share_rows : (j + 1) * share_rows, lanes]
            total = jnp.where(slot_at == j, here, total)
        tiles.append(jnp.where(line < rows_column[0:1, lanes], total, 0.0))
    fold(tiles, out, width)


def unpack_kernel(scalars, mine, got, out, sum_v, out_v, sems):
    owner_slots, rows, modes = out_v.shape
    places = [
        [jnp.max(scalars[k * owner_slots + j : k * owner_slots + j + 1, :]) for k in range(2)]
        for j in range(owner_slots)
    ]
    for t, (a, b) in enumerate(zip(unfold(mine, rows), unfold(got, rows))):
        sum_v[t] = a + b.astype(jnp.float32)
    lane = lax.broadcasted_iota(jnp.int32, (rows, LANES), 1)
    copies = []
    for j, (offset, keep) in enumerate(places):
        tile = lax.div(offset, LANES)
        shift = offset - tile * LANES
        back = lax.rem(LANES - shift, LANES)
        turned = [pltpu.roll(sum_v[tile + t], back, 1) for t in range(modes // LANES + 1)]
        for t in range(modes // LANES):
            value = jnp.where(lane < LANES - shift, turned[t], turned[t + 1])
            value = jnp.where(lane < keep - t * LANES, value, 0.0)
            out_v[j, :, t * LANES : (t + 1) * LANES] = value
        copy = pltpu.make_async_copy(out_v.at[j], out.at[j], sems.at[j])
        copy.start()
        copies.append(copy)
    for copy in copies:
        copy.wait()


HBM = pl.BlockSpec(memory_space=pltpu.HBM)
VMEM = pl.BlockSpec(memory_space=pltpu.VMEM)
SMALL = pltpu.CompilerParams(vmem_limit_bytes=8 * MIB)


def in_hbm(operand):
    return pltpu.with_memory_space_constraint(operand, pltpu.HBM)


def project(panels, svd_basis, slot_of_m, svd_keep, kl_keep, owner_slots, width):
    slots, freqs, depth = panels.shape
    modes = svd_basis.shape[2]
    owners = lax.axis_size("ma")

    def packed(count):
        return jax.ShapeDtypeStruct((count, width // LANES, freqs, LANES), jnp.float32)

    column = jax.ShapeDtypeStruct((8, width), jnp.int32)
    return pl.pallas_call(
        functools.partial(project_kernel, owner_slots),
        out_shape=(
            packed(owners),
            packed(1),
            packed(owners - 1),
            column,
            column,
            jax.ShapeDtypeStruct((8, LANES), jnp.int32),
        ),
        in_specs=[HBM] * 5,
        out_specs=(VMEM,) * 6,
        scratch_shapes=[pltpu.SMEM((slots,), jnp.int32)] * 8
        + [
            pltpu.VMEM((slots, freqs, depth), jnp.bfloat16),
            pltpu.VMEM((freqs, depth, modes), jnp.bfloat16),
            pltpu.VMEM((GROUP, slots, depth), jnp.bfloat16),
            pltpu.VMEM((modes // LANES * GROUP * slots, LANES), jnp.float32),
            pltpu.VMEM((modes // LANES * GROUP * slots, LANES), jnp.float32),
            pltpu.SemaphoreType.DMA((3,)),
            pltpu.SemaphoreType.DMA((freqs // GROUP,)),
            pltpu.SemaphoreType.DMA((freqs // TOGETHER,)),
        ],
        compiler_params=pltpu.CompilerParams(vmem_limit_bytes=48 * MIB),
        cost_estimate=pl.CostEstimate(
            flops=2 * slots * freqs * depth * modes,
            bytes_accessed=2 * freqs * depth * (modes + slots),
            transcendentals=0,
        ),
        name="project",
    )(*map(in_hbm, (slot_of_m, svd_keep, kl_keep, panels, svd_basis)))


def sum_pair(steps, width, mine, got):
    kind = jax.ShapeDtypeStruct((folded_rows(mine.shape[2], width), LANES), jnp.bfloat16)
    return pl.pallas_call(
        functools.partial(sum_kernel, steps, width),
        out_shape=(kind,) * len(steps),
        in_specs=[VMEM] * 2,
        out_specs=(VMEM,) * len(steps),
        compiler_params=SMALL,
        cost_estimate=pl.CostEstimate(
            flops=got.size, bytes_accessed=10 * got.size, transcendentals=0
        ),
        name="sum_pair",
    )(mine, got)


def kl_project(part, kind, width, slot_column, rows_column, kl_basis, blocks):
    owners, shares = lax.axis_size("ma"), lax.axis_size("af")
    rows, freqs = kl_basis.shape[1:]
    wide = slot_column.shape[1]
    return pl.pallas_call(
        functools.partial(kl_kernel, part, owners, width),
        out_shape=jax.ShapeDtypeStruct((folded_rows(rows // shares, width), LANES), kind),
        in_specs=[VMEM] * (3 + owners),
        out_specs=VMEM,
        scratch_shapes=[pltpu.VMEM((freqs, wide), jnp.bfloat16)],
        compiler_params=SMALL,
        cost_estimate=pl.CostEstimate(
            flops=2 * kl_basis.size * wide // shares,
            bytes_accessed=2 * kl_basis.size,
            transcendentals=0,
        ),
        name="kl_project",
    )(slot_column, rows_column, kl_basis, *blocks)


def unpack(scalars, mine, got, owner_slots, rows, modes, width):
    tiles = -(-width // LANES) + modes // LANES + 1
    return pl.pallas_call(
        unpack_kernel,
        out_shape=jax.ShapeDtypeStruct((owner_slots, rows, modes), jnp.float32),
        in_specs=[VMEM] * 3,
        out_specs=HBM,
        scratch_shapes=[
            pltpu.VMEM((tiles, rows, LANES), jnp.float32),
            pltpu.VMEM((owner_slots, rows, modes), jnp.float32),
            pltpu.SemaphoreType.DMA((owner_slots,)),
        ],
        compiler_params=SMALL,
        cost_estimate=pl.CostEstimate(
            flops=mine.size, bytes_accessed=10 * mine.size, transcendentals=0
        ),
        name="unpack",
    )(scalars, mine, got)


def pairs(axis):
    return [(i, i ^ 1) for i in range(lax.axis_size(axis))]


def ring(step):
    size = lax.axis_size("ma")
    return [(i, on_ring((on_ring(i) + step) % size)) for i in range(size)]


def shards(panels, svd_basis, kl_basis, slot_of_m, svd_keep, kl_keep):
    owner_slots, modes = kl_basis.shape[0], svd_basis.shape[2]
    owners = lax.axis_size("ma")
    width = min(OWNER_BUDGET, owner_slots * modes)
    wide = -(-width // LANES) * LANES
    mine, far, near, slot_column, rows_column, scalars = project(
        panels, svd_basis, slot_of_m, svd_keep, kl_keep, owner_slots, wide
    )
    first = far_step(owners)
    others = [step for step in range(owners) if step != first]
    got_far = lax.ppermute(far, "pa", pairs("pa"))
    near, got_far = lax.optimization_barrier((near, got_far))
    got_near = lax.ppermute(near, "pa", pairs("pa"))
    summed = dict(zip([first], sum_pair([first], width, mine, got_far)))
    summed |= zip(others, sum_pair(others, width, mine, got_near))
    blocks = {
        step: lax.ppermute(summed[step], "ma", ring(step)) if step else summed[step]
        for step in [first] + others
    }
    tables = (width, slot_column, rows_column, kl_basis, [blocks[step] for step in range(owners)])
    send = kl_project(1, jnp.bfloat16, *tables)
    got = lax.ppermute(send, "af", pairs("af"))
    mine = kl_project(0, jnp.float32, *tables)
    rows = kl_basis.shape[1] // lax.axis_size("af")
    return unpack(scalars, mine, got, owner_slots, rows, modes, width)


def kernels_fit(mesh, args):
    panels, svd_basis, kl_basis = args[:3]
    slots = panels.shape[0] // mesh.shape["grp"]
    freqs = svd_basis.shape[0] // (mesh.shape["af"] * mesh.shape["ma"])
    owner_slots = kl_basis.shape[0] // (mesh.shape["pa"] * mesh.shape["ma"])
    share_rows = kl_basis.shape[1] // mesh.shape["af"]
    return (
        freqs % (2 * GROUP) == 0
        and slots % (GROUP * mesh.shape["pa"]) == 0
        and owner_slots == 4
        and svd_basis.shape[2] == 2 * LANES
        and share_rows % (2 * GROUP) == 0
        and mesh.shape["pa"] == 2
        and mesh.shape["af"] == 2
        and mesh.shape["ma"] == 4
    )


def solution(mesh):
    in_specs = (
        P("grp", ("af", "ma"), "pa"),
        P(("af", "ma"), "pa", None),
        P(("pa", "ma"), None, "af"),
        P(),
        P(),
        P(),
    )
    out_specs = P(("grp", "pa", "ma"), "af", None)

    def run(*args):
        body = shards if kernels_fit(mesh, args) else shards_plain
        mapped = jax.shard_map(
            body, mesh=mesh, in_specs=in_specs, out_specs=out_specs, check_vma=False
        )
        return mapped(*args)

    return run
```

```python
import functools

import jax
import jax.numpy as jnp
from jax import lax
from jax.experimental import pallas as pl
from jax.experimental.pallas import tpu as pltpu
from jax.sharding import PartitionSpec as P

LANES = 128
GROUP = 16
PER_COPY = 8
OWNER_BUDGET = 576
MIB = 2**20


def shards_plain(panels, svd_basis, kl_basis, slot_of_m, svd_keep, kl_keep):
    slot_count = slot_of_m.shape[0]
    order_slots = jnp.argsort(slot_of_m)
    keep_slots = jnp.take(svd_keep, order_slots, axis=0)
    modes_slots = jnp.take(kl_keep, order_slots, axis=0)
    width_modes = svd_basis.shape[2]
    owner_rows = kl_basis.shape[0]
    slot_rows = slot_count // lax.axis_size("pa")
    slot_start = lax.axis_index("pa") * slot_rows
    owner_start = slot_start + lax.axis_index("ma") * owner_rows
    modes_owner = lax.dynamic_slice_in_dim(modes_slots, owner_start, owner_rows, 0)
    chosen = jnp.take(panels, order_slots, axis=0)
    summed = lax.psum_scatter(
        jnp.einsum("mfb,fbr->mfr", chosen, svd_basis, preferred_element_type=jnp.float32),
        "pa",
        scatter_dimension=0,
        tiled=True,
    )
    keep_here = lax.dynamic_slice_in_dim(keep_slots, slot_start, slot_rows, 0)
    columns = jnp.arange(width_modes, dtype=jnp.int32)
    retained = jnp.where(columns[None, None, :] < keep_here[:, None, None], summed, 0.0).astype(
        jnp.bfloat16
    )
    relaid = lax.all_to_all(retained, "ma", split_axis=0, concat_axis=1, tiled=True)
    partial_sums = jnp.einsum("mkf,mfr->mkr", kl_basis, relaid, preferred_element_type=jnp.float32)
    modes = jnp.arange(kl_basis.shape[1], dtype=jnp.int32)
    partial_sums = jnp.where(modes[None, :, None] < modes_owner[:, None, None], partial_sums, 0.0)
    return lax.psum_scatter(partial_sums, "af", scatter_dimension=1, tiled=True)


def cyclic(value, count):
    return lax.rem(value + count, count)


def on_ring(z):
    return z ^ (z // 2) if isinstance(z, int) else z ^ lax.shift_right_logical(z, 1)


def far_step(owners):
    return owners // 2


def place_of(slot, owner_slots, half_slots):
    half = cyclic(lax.div(slot, half_slots) - lax.axis_index("pa"), lax.axis_size("pa"))
    within = lax.rem(slot, half_slots)
    owner = on_ring(lax.div(within, owner_slots)) - on_ring(lax.axis_index("ma"))
    owner = cyclic(owner, lax.axis_size("ma"))
    return half * half_slots + owner * owner_slots + lax.rem(within, owner_slots)


def offsets_of(keep_place, tile_place, shift_place, owner_slots):
    @pl.loop(0, keep_place.shape[0] // owner_slots)
    def _(at):
        offset = jnp.int32(0)
        for j in range(owner_slots):
            place = at * owner_slots + j
            tile = lax.div(offset, LANES)
            tile_place[place] = tile
            shift_place[place] = offset - tile * LANES
            offset = offset + keep_place[place]


def pack(out_v, mine, far, near, line, tables, owners_at):
    tile_place, shift_place, owner_slots = tables
    owners, width_tiles = mine.shape[:2]
    slots = 2 * owners * owner_slots
    tiles = out_v.shape[0] // (GROUP * slots)
    lane = lax.broadcasted_iota(jnp.int32, (GROUP, LANES), 1)
    rows = slice(line, line + GROUP)
    turned = {
        place: pltpu.roll(
            out_v[pl.ds(place, tiles * GROUP, stride=slots), :], shift_place[place], 1
        )
        for place in range(owners_at[0] * owner_slots, (owners_at[-1] + 1) * owner_slots)
    }
    for at in owners_at:
        to, owner = mine, at % owners
        if at >= owners:
            first = far_step(owners)
            to, owner = (far, 0) if owner == first else (near, owner - (owner > first))
        values, tile_before = None, None
        for j in range(owner_slots):
            place = at * owner_slots + j
            tile = tile_place[place]
            left = lane < shift_place[place]
            moved = [turned[place][t * GROUP : (t + 1) * GROUP] for t in range(tiles)]
            shared = moved[0]
            if j > 0:
                step = tile - tile_before
                shared = values[0]
                for t in range(1, tiles + 1):
                    shared = jnp.where(step == t, values[t], shared)
            values = (
                [jnp.where(left, shared, moved[0])]
                + [jnp.where(left, moved[t - 1], moved[t]) for t in range(1, tiles)]
                + [moved[tiles - 1]]
            )
            tile_before = tile
            for t in reversed(range(tiles + 1)):
                to[owner, jnp.minimum(tile + t, width_tiles - 1), rows, :] = values[t]


def project_kernel(
    owner_slots, slot_hbm, keep_hbm, rows_hbm, panels, basis,
    mine, far, near, slot_column, rows_column, scalars,
    slot_s, keep_s, rows_s, keep_place, rows_place, tile_place, shift_place,
    panels_v, basis_v, lhs_v, out_even, out_odd, small_sem, panel_sem, basis_sem,
):
    slots, freqs, depth = panels_v.shape
    groups = freqs // GROUP
    half_slots = slots // lax.axis_size("pa")

    table_copies = [
        pltpu.make_async_copy(slot_hbm, slot_s, small_sem.at[0]),
        pltpu.make_async_copy(keep_hbm, keep_s, small_sem.at[1]),
        pltpu.make_async_copy(rows_hbm, rows_s, small_sem.at[2]),
    ]
    for copy in table_copies:
        copy.start()

    def basis_copy(i):
        part = pl.ds(i * PER_COPY, PER_COPY)
        return pltpu.make_async_copy(basis.at[part], basis_v.at[part], basis_sem.at[i])

    ahead = 1
    for i in range(ahead):
        basis_copy(i).start()
    for copy in table_copies:
        copy.wait()

    per_group = GROUP // PER_COPY
    for group in range(groups):
        part = pl.ds(group * GROUP, GROUP)

        @pl.loop(0, slots)
        def _(m):
            place = place_of(slot_s[m], owner_slots, half_slots)
            if group == 0:
                keep_place[place] = keep_s[m]
                rows_place[place] = rows_s[m]
            pltpu.make_async_copy(
                panels.at[m, part], panels_v.at[place, part], panel_sem.at[group]
            ).start()

        for i in range(ahead + group * per_group, min(ahead + (group + 1) * per_group, groups * per_group)):
            basis_copy(i).start()

    offsets_of(keep_place, tile_place, shift_place, owner_slots)
    column = lax.broadcasted_iota(jnp.int32, slot_column.shape, 1)
    slot_at = jnp.full(slot_column.shape, owner_slots, jnp.int32)
    rows_at = jnp.zeros(slot_column.shape, jnp.int32)
    for j in range(owner_slots):
        keep = keep_place[j]
        offset = tile_place[j] * LANES + shift_place[j]
        within = (column >= offset) & (column < offset + keep)
        slot_at = jnp.where(within, j, slot_at)
        rows_at = jnp.where(within, rows_place[j], rows_at)
        scalars[j : j + 1, :] = jnp.full((1, LANES), offset, jnp.int32)
        scalars[owner_slots + j : owner_slots + j + 1, :] = jnp.full((1, LANES), keep, jnp.int32)
    slot_column[...] = slot_at
    rows_column[...] = rows_at

    side = GROUP * GROUP
    row = lax.broadcasted_iota(jnp.int32, (side, side), 0)
    column = lax.broadcasted_iota(jnp.int32, (side, side), 1)
    swap = (column == (row % GROUP) * GROUP + row // GROUP).astype(jnp.float32).astype(jnp.bfloat16)

    tables = (tile_place, shift_place, owner_slots)
    all_owners = range(mine.shape[0] * lax.axis_size("pa"))
    share = len(all_owners) // per_group

    def group_step(group, out_v, out_before):
        here = slice(group * GROUP, (group + 1) * GROUP)
        pltpu.make_async_copy(
            panels_v.at[:, here], panels_v.at[:, here], panel_sem.at[group]
        ).wait()
        for block in range(slots // GROUP):
            blocks = slice(block * GROUP, (block + 1) * GROUP)
            tile = panels_v[blocks, here, :].reshape(side, depth)
            turned = jnp.dot(swap, tile, preferred_element_type=jnp.float32).astype(jnp.bfloat16)
            lhs_v[:, blocks, :] = turned.reshape(GROUP, GROUP, depth)
        for i in range(per_group):
            basis_copy(group * per_group + i).wait()
            for f in range(i * PER_COPY, (i + 1) * PER_COPY):
                product = jnp.dot(
                    lhs_v[f], basis_v[group * GROUP + f], preferred_element_type=jnp.float32
                )
                for t in range(product.shape[1] // LANES):
                    at = (t * GROUP + f) * slots
                    out_v[at : at + slots, :] = product[:, t * LANES : (t + 1) * LANES]
            if group > 0:
                line = (group - 1) * GROUP
                pack(out_before, mine, far, near, line, tables, all_owners[i * share : (i + 1) * share])

    outs = (out_even, out_odd)
    for group in range(groups):
        group_step(group, outs[group % 2], outs[(group + 1) % 2])

    for i in range(per_group):
        part = all_owners[i * share : (i + 1) * share]
        pack(outs[(groups - 1) % 2], mine, far, near, (groups - 1) * GROUP, tables, part)


def folded_rows(rows, width):
    whole, rest = divmod(width, LANES)
    return rows * whole + (rows if rest > LANES // 2 else rows // 2 if rest else 0)


def fold(tiles, out, width):
    rows = tiles[0].shape[0]
    lane = lax.broadcasted_iota(jnp.int32, (rows // 2, LANES), 1)
    for t, tile in enumerate(tiles):
        if t == len(tiles) - 1 and out.shape[0] < rows * len(tiles):
            low, high = tile[: rows // 2], tile[rows // 2 :]
            tile = jnp.where(lane < LANES // 2, low, pltpu.roll(high, LANES // 2, 1))
        out[t * rows : t * rows + tile.shape[0], :] = tile.astype(out.dtype)


def unfold(block, rows):
    count = block.shape[0] // rows
    tiles = [block[t * rows : (t + 1) * rows, :] for t in range(count)]
    if count * rows < block.shape[0]:
        low = block[count * rows :, :].astype(jnp.float32)
        high = pltpu.roll(low, LANES // 2, 1)
        tiles.append(jnp.concatenate([low, high], axis=0).astype(block.dtype))
    return tiles


def sum_kernel(steps, width, mine, got, *out):
    for i, step in enumerate(steps):
        tiles = [mine[step, t] + got[i, t] for t in range(mine.shape[1])]
        fold(tiles, out[i], width)


def kl_kernel(part, owners, width, slot_column, rows_column, kl, *refs):
    blocks, (out, packed_v) = refs[:owners], refs[owners:]
    owner_slots, rows, freqs = kl.shape
    shares = lax.axis_size("af")
    per_source = freqs // owners
    me = lax.axis_index("ma")
    for step in range(owners):
        source = on_ring(cyclic(on_ring(me) - step, owners))
        at = pl.multiple_of(source * per_source, GROUP)
        for t, tile in enumerate(unfold(blocks[step], per_source)):
            packed_v[pl.ds(at, per_source), t * LANES : (t + 1) * LANES] = tile
    share_rows = rows // shares
    at = pl.multiple_of(cyclic(lax.axis_index("af") + part, shares) * share_rows, GROUP)
    lhs = kl[:, pl.ds(at, share_rows), :].reshape(owner_slots * share_rows, freqs)
    product = jnp.dot(lhs, packed_v[...], preferred_element_type=jnp.float32)
    line = lax.broadcasted_iota(jnp.int32, (share_rows, LANES), 0) + at
    tiles = []
    for t in range(packed_v.shape[1] // LANES):
        lanes = slice(t * LANES, (t + 1) * LANES)
        slot_at = slot_column[0:1, lanes]
        total = jnp.zeros((share_rows, LANES), jnp.float32)
        for j in range(owner_slots):
            here = product[j * share_rows : (j + 1) * share_rows, lanes]
            total = jnp.where(slot_at == j, here, total)
        tiles.append(jnp.where(line < rows_column[0:1, lanes], total, 0.0))
    fold(tiles, out, width)


def unpack_kernel(scalars, mine, got, out, sum_v, out_v, sems):
    owner_slots, rows, modes = out_v.shape
    places = [
        [jnp.max(scalars[k * owner_slots + j : k * owner_slots + j + 1, :]) for k in range(2)]
        for j in range(owner_slots)
    ]
    for t, (a, b) in enumerate(zip(unfold(mine, rows), unfold(got, rows))):
        sum_v[t] = a + b.astype(jnp.float32)
    lane = lax.broadcasted_iota(jnp.int32, (rows, LANES), 1)
    copies = []
    for j, (offset, keep) in enumerate(places):
        tile = lax.div(offset, LANES)
        shift = offset - tile * LANES
        back = lax.rem(LANES - shift, LANES)
        turned = [pltpu.roll(sum_v[tile + t], back, 1) for t in range(modes // LANES + 1)]
        for t in range(modes // LANES):
            value = jnp.where(lane < LANES - shift, turned[t], turned[t + 1])
            value = jnp.where(lane < keep - t * LANES, value, 0.0)
            out_v[j, :, t * LANES : (t + 1) * LANES] = value
        copy = pltpu.make_async_copy(out_v.at[j], out.at[j], sems.at[j])
        copy.start()
        copies.append(copy)
    for copy in copies:
        copy.wait()


HBM = pl.BlockSpec(memory_space=pltpu.HBM)
VMEM = pl.BlockSpec(memory_space=pltpu.VMEM)
SMALL = pltpu.CompilerParams(vmem_limit_bytes=8 * MIB)


def in_hbm(operand):
    return pltpu.with_memory_space_constraint(operand, pltpu.HBM)


def project(panels, svd_basis, slot_of_m, svd_keep, kl_keep, owner_slots, width):
    slots, freqs, depth = panels.shape
    modes = svd_basis.shape[2]
    owners = lax.axis_size("ma")

    def packed(count):
        return jax.ShapeDtypeStruct((count, width // LANES, freqs, LANES), jnp.float32)

    column = jax.ShapeDtypeStruct((8, width), jnp.int32)
    return pl.pallas_call(
        functools.partial(project_kernel, owner_slots),
        out_shape=(
            packed(owners),
            packed(1),
            packed(owners - 1),
            column,
            column,
            jax.ShapeDtypeStruct((8, LANES), jnp.int32),
        ),
        in_specs=[HBM] * 5,
        out_specs=(VMEM,) * 6,
        scratch_shapes=[pltpu.SMEM((slots,), jnp.int32)] * 7
        + [
            pltpu.VMEM((slots, freqs, depth), jnp.bfloat16),
            pltpu.VMEM((freqs, depth, modes), jnp.bfloat16),
            pltpu.VMEM((GROUP, slots, depth), jnp.bfloat16),
            pltpu.VMEM((modes // LANES * GROUP * slots, LANES), jnp.float32),
            pltpu.VMEM((modes // LANES * GROUP * slots, LANES), jnp.float32),
            pltpu.SemaphoreType.DMA((3,)),
            pltpu.SemaphoreType.DMA((freqs // GROUP,)),
            pltpu.SemaphoreType.DMA((freqs // PER_COPY,)),
        ],
        compiler_params=pltpu.CompilerParams(vmem_limit_bytes=48 * MIB),
        cost_estimate=pl.CostEstimate(
            flops=2 * slots * freqs * depth * modes,
            bytes_accessed=2 * freqs * depth * (modes + slots),
            transcendentals=0,
        ),
        name="project",
    )(*map(in_hbm, (slot_of_m, svd_keep, kl_keep, panels, svd_basis)))


def sum_pair(steps, width, mine, got):
    kind = jax.ShapeDtypeStruct((folded_rows(mine.shape[2], width), LANES), jnp.bfloat16)
    return pl.pallas_call(
        functools.partial(sum_kernel, steps, width),
        out_shape=(kind,) * len(steps),
        in_specs=[VMEM] * 2,
        out_specs=(VMEM,) * len(steps),
        compiler_params=SMALL,
        cost_estimate=pl.CostEstimate(
            flops=got.size, bytes_accessed=10 * got.size, transcendentals=0
        ),
        name="sum_pair",
    )(mine, got)


def kl_project(part, kind, width, slot_column, rows_column, kl_basis, blocks):
    owners, shares = lax.axis_size("ma"), lax.axis_size("af")
    rows, freqs = kl_basis.shape[1:]
    wide = slot_column.shape[1]
    return pl.pallas_call(
        functools.partial(kl_kernel, part, owners, width),
        out_shape=jax.ShapeDtypeStruct((folded_rows(rows // shares, width), LANES), kind),
        in_specs=[VMEM] * (3 + owners),
        out_specs=VMEM,
        scratch_shapes=[pltpu.VMEM((freqs, wide), jnp.bfloat16)],
        compiler_params=SMALL,
        cost_estimate=pl.CostEstimate(
            flops=2 * kl_basis.size * wide // shares,
            bytes_accessed=2 * kl_basis.size,
            transcendentals=0,
        ),
        name="kl_project",
    )(slot_column, rows_column, kl_basis, *blocks)


def unpack(scalars, mine, got, owner_slots, rows, modes, width):
    tiles = -(-width // LANES) + modes // LANES + 1
    return pl.pallas_call(
        unpack_kernel,
        out_shape=jax.ShapeDtypeStruct((owner_slots, rows, modes), jnp.float32),
        in_specs=[VMEM] * 3,
        out_specs=HBM,
        scratch_shapes=[
            pltpu.VMEM((tiles, rows, LANES), jnp.float32),
            pltpu.VMEM((owner_slots, rows, modes), jnp.float32),
            pltpu.SemaphoreType.DMA((owner_slots,)),
        ],
        compiler_params=SMALL,
        cost_estimate=pl.CostEstimate(
            flops=mine.size, bytes_accessed=10 * mine.size, transcendentals=0
        ),
        name="unpack",
    )(scalars, mine, got)


def pairs(axis):
    return [(i, i ^ 1) for i in range(lax.axis_size(axis))]


def ring(step):
    size = lax.axis_size("ma")
    return [(i, on_ring((on_ring(i) + step) % size)) for i in range(size)]


def shards(panels, svd_basis, kl_basis, slot_of_m, svd_keep, kl_keep):
    owner_slots, modes = kl_basis.shape[0], svd_basis.shape[2]
    owners = lax.axis_size("ma")
    width = min(OWNER_BUDGET, owner_slots * modes)
    wide = -(-width // LANES) * LANES
    mine, far, near, slot_column, rows_column, scalars = project(
        panels, svd_basis, slot_of_m, svd_keep, kl_keep, owner_slots, wide
    )
    first = far_step(owners)
    others = [step for step in range(owners) if step != first]
    got_far = lax.ppermute(far, "pa", pairs("pa"))
    near, got_far = lax.optimization_barrier((near, got_far))
    got_near = lax.ppermute(near, "pa", pairs("pa"))
    summed = dict(zip([first], sum_pair([first], width, mine, got_far)))
    summed |= zip(others, sum_pair(others, width, mine, got_near))
    blocks = {
        step: lax.ppermute(summed[step], "ma", ring(step)) if step else summed[step]
        for step in [first] + others
    }
    tables = (width, slot_column, rows_column, kl_basis, [blocks[step] for step in range(owners)])
    send = kl_project(1, jnp.bfloat16, *tables)
    got = lax.ppermute(send, "af", pairs("af"))
    mine = kl_project(0, jnp.float32, *tables)
    rows = kl_basis.shape[1] // lax.axis_size("af")
    return unpack(scalars, mine, got, owner_slots, rows, modes, width)


def kernels_fit(mesh, args):
    panels, svd_basis, kl_basis = args[:3]
    slots = panels.shape[0] // mesh.shape["grp"]
    freqs = svd_basis.shape[0] // (mesh.shape["af"] * mesh.shape["ma"])
    owner_slots = kl_basis.shape[0] // (mesh.shape["pa"] * mesh.shape["ma"])
    share_rows = kl_basis.shape[1] // mesh.shape["af"]
    return (
        freqs % GROUP == 0
        and freqs <= 8 * GROUP
        and slots % (GROUP * mesh.shape["pa"]) == 0
        and owner_slots == 4
        and svd_basis.shape[2] == 2 * LANES
        and share_rows % (2 * GROUP) == 0
        and mesh.shape["pa"] == 2
        and mesh.shape["af"] == 2
        and mesh.shape["ma"] == 4
    )


def solution(mesh):
    in_specs = (
        P("grp", ("af", "ma"), "pa"),
        P(("af", "ma"), "pa", None),
        P(("pa", "ma"), None, "af"),
        P(),
        P(),
        P(),
    )
    out_specs = P(("grp", "pa", "ma"), "af", None)

    def run(*args):
        body = shards if kernels_fit(mesh, args) else shards_plain
        mapped = jax.shard_map(
            body, mesh=mesh, in_specs=in_specs, out_specs=out_specs, check_vma=False
        )
        return mapped(*args)

    return run
```

```python
import functools

import jax
import jax.numpy as jnp
from jax import lax
from jax.experimental import pallas as pl
from jax.experimental.pallas import tpu as pltpu
from jax.sharding import PartitionSpec as P

LANES = 128
GROUP = 16
BATCH = 2
PER_COPY = 8
OWNER_BUDGET = 576
MIB = 2**20


def shards_plain(panels, svd_basis, kl_basis, slot_of_m, svd_keep, kl_keep):
    slot_count = slot_of_m.shape[0]
    order_slots = jnp.argsort(slot_of_m)
    keep_slots = jnp.take(svd_keep, order_slots, axis=0)
    modes_slots = jnp.take(kl_keep, order_slots, axis=0)
    width_modes = svd_basis.shape[2]
    owner_rows = kl_basis.shape[0]
    slot_rows = slot_count // lax.axis_size("pa")
    slot_start = lax.axis_index("pa") * slot_rows
    owner_start = slot_start + lax.axis_index("ma") * owner_rows
    modes_owner = lax.dynamic_slice_in_dim(modes_slots, owner_start, owner_rows, 0)
    chosen = jnp.take(panels, order_slots, axis=0)
    summed = lax.psum_scatter(
        jnp.einsum("mfb,fbr->mfr", chosen, svd_basis, preferred_element_type=jnp.float32),
        "pa",
        scatter_dimension=0,
        tiled=True,
    )
    keep_here = lax.dynamic_slice_in_dim(keep_slots, slot_start, slot_rows, 0)
    columns = jnp.arange(width_modes, dtype=jnp.int32)
    retained = jnp.where(columns[None, None, :] < keep_here[:, None, None], summed, 0.0).astype(
        jnp.bfloat16
    )
    relaid = lax.all_to_all(retained, "ma", split_axis=0, concat_axis=1, tiled=True)
    partial_sums = jnp.einsum("mkf,mfr->mkr", kl_basis, relaid, preferred_element_type=jnp.float32)
    modes = jnp.arange(kl_basis.shape[1], dtype=jnp.int32)
    partial_sums = jnp.where(modes[None, :, None] < modes_owner[:, None, None], partial_sums, 0.0)
    return lax.psum_scatter(partial_sums, "af", scatter_dimension=1, tiled=True)


def cyclic(value, count):
    return lax.rem(value + count, count)


def on_ring(z):
    return z ^ (z // 2) if isinstance(z, int) else z ^ lax.shift_right_logical(z, 1)


def far_step(owners):
    return owners // 2


def place_of(slot, owner_slots, half_slots):
    half = cyclic(lax.div(slot, half_slots) - lax.axis_index("pa"), lax.axis_size("pa"))
    within = lax.rem(slot, half_slots)
    owner = on_ring(lax.div(within, owner_slots)) - on_ring(lax.axis_index("ma"))
    owner = cyclic(owner, lax.axis_size("ma"))
    return half * half_slots + owner * owner_slots + lax.rem(within, owner_slots)


def offsets_of(keep_place, tile_place, shift_place, owner_slots):
    @pl.loop(0, keep_place.shape[0] // owner_slots)
    def _(at):
        offset = jnp.int32(0)
        for j in range(owner_slots):
            place = at * owner_slots + j
            tile = lax.div(offset, LANES)
            tile_place[place] = tile
            shift_place[place] = offset - tile * LANES
            offset = offset + keep_place[place]


def pack(out_v, mine, far, near, line, tables, owners_at):
    for i in range(0, len(owners_at), BATCH):
        pack_batch(out_v, mine, far, near, line, tables, owners_at[i : i + BATCH])


def pack_batch(out_v, mine, far, near, line, tables, owners_at):
    tile_place, shift_place, owner_slots = tables
    owners, width_tiles = mine.shape[:2]
    slots = 2 * owners * owner_slots
    tiles = out_v.shape[0] // (GROUP * slots)
    lane = lax.broadcasted_iota(jnp.int32, (GROUP, LANES), 1)
    rows = pl.ds(pl.multiple_of(line, GROUP), GROUP)
    turned = {
        place: pltpu.roll(
            out_v[pl.ds(place, tiles * GROUP, stride=slots), :], shift_place[place], 1
        )
        for place in range(owners_at[0] * owner_slots, (owners_at[-1] + 1) * owner_slots)
    }
    for at in owners_at:
        to, owner = mine, at % owners
        if at >= owners:
            first = far_step(owners)
            to, owner = (far, 0) if owner == first else (near, owner - (owner > first))
        values, tile_before = None, None
        for j in range(owner_slots):
            place = at * owner_slots + j
            tile = tile_place[place]
            left = lane < shift_place[place]
            moved = [turned[place][t * GROUP : (t + 1) * GROUP] for t in range(tiles)]
            shared = moved[0]
            if j > 0:
                step = tile - tile_before
                shared = values[0]
                for t in range(1, tiles + 1):
                    shared = jnp.where(step == t, values[t], shared)
            values = (
                [jnp.where(left, shared, moved[0])]
                + [jnp.where(left, moved[t - 1], moved[t]) for t in range(1, tiles)]
                + [moved[tiles - 1]]
            )
            tile_before = tile
            for t in reversed(range(tiles + 1)):
                to[owner, jnp.minimum(tile + t, width_tiles - 1), rows, :] = values[t]


def project_kernel(
    owner_slots, slot_hbm, keep_hbm, rows_hbm, panels, basis,
    mine, far, near, slot_column, rows_column, scalars,
    slot_s, keep_s, rows_s, place_m, keep_place, rows_place, tile_place, shift_place,
    panels_v, basis_v, lhs_v, out_even, out_odd, small_sem, panel_sem, basis_sem,
):
    slots, freqs, depth = panels_v.shape
    groups = freqs // GROUP
    half_slots = slots // lax.axis_size("pa")

    table_copies = [
        pltpu.make_async_copy(slot_hbm, slot_s, small_sem.at[0]),
        pltpu.make_async_copy(keep_hbm, keep_s, small_sem.at[1]),
        pltpu.make_async_copy(rows_hbm, rows_s, small_sem.at[2]),
    ]
    for copy in table_copies:
        copy.start()

    def basis_copy(i):
        part = pl.ds(i * PER_COPY, PER_COPY)
        return pltpu.make_async_copy(basis.at[part], basis_v.at[part], basis_sem.at[i])

    ahead = 1
    for i in range(ahead):
        basis_copy(i).start()
    for copy in table_copies:
        copy.wait()

    @pl.loop(0, slots)
    def _(m):
        place = place_of(slot_s[m], owner_slots, half_slots)
        place_m[m] = place
        keep_place[place] = keep_s[m]
        rows_place[place] = rows_s[m]

    per_group = GROUP // PER_COPY
    for group in range(groups):
        part = pl.ds(group * GROUP, GROUP)

        @pl.loop(0, slots)
        def _(m):
            pltpu.make_async_copy(
                panels.at[m, part], panels_v.at[place_m[m], part], panel_sem.at[group]
            ).start()

        for i in range(ahead + group * per_group, min(ahead + (group + 1) * per_group, groups * per_group)):
            basis_copy(i).start()

    offsets_of(keep_place, tile_place, shift_place, owner_slots)
    column = lax.broadcasted_iota(jnp.int32, slot_column.shape, 1)
    slot_at = jnp.full(slot_column.shape, owner_slots, jnp.int32)
    rows_at = jnp.zeros(slot_column.shape, jnp.int32)
    for j in range(owner_slots):
        keep = keep_place[j]
        offset = tile_place[j] * LANES + shift_place[j]
        within = (column >= offset) & (column < offset + keep)
        slot_at = jnp.where(within, j, slot_at)
        rows_at = jnp.where(within, rows_place[j], rows_at)
        scalars[j : j + 1, :] = jnp.full((1, LANES), offset, jnp.int32)
        scalars[owner_slots + j : owner_slots + j + 1, :] = jnp.full((1, LANES), keep, jnp.int32)
    slot_column[...] = slot_at
    rows_column[...] = rows_at

    side = GROUP * GROUP
    row = lax.broadcasted_iota(jnp.int32, (side, side), 0)
    column = lax.broadcasted_iota(jnp.int32, (side, side), 1)
    swap = (column == (row % GROUP) * GROUP + row // GROUP).astype(jnp.float32).astype(jnp.bfloat16)

    tables = (tile_place, shift_place, owner_slots)
    all_owners = range(mine.shape[0] * lax.axis_size("pa"))
    share = len(all_owners) // per_group

    def group_step(group, out_v, out_before):
        here = pl.ds(pl.multiple_of(group * GROUP, GROUP), GROUP)
        pltpu.make_async_copy(
            panels_v.at[:, here], panels_v.at[:, here], panel_sem.at[group]
        ).wait()
        for block in range(slots // GROUP):
            blocks = slice(block * GROUP, (block + 1) * GROUP)
            tile = panels_v[blocks, here, :].reshape(side, depth)
            turned = jnp.dot(swap, tile, preferred_element_type=jnp.float32).astype(jnp.bfloat16)
            lhs_v[:, blocks, :] = turned.reshape(GROUP, GROUP, depth)
        for i in range(per_group):
            basis_copy(group * per_group + i).wait()
            for f in range(i * PER_COPY, (i + 1) * PER_COPY):
                product = jnp.dot(
                    lhs_v[f], basis_v[group * GROUP + f], preferred_element_type=jnp.float32
                )
                for t in range(product.shape[1] // LANES):
                    at = (t * GROUP + f) * slots
                    out_v[at : at + slots, :] = product[:, t * LANES : (t + 1) * LANES]
            line = jnp.maximum(group - 1, 0) * GROUP
            pack(out_before, mine, far, near, line, tables, all_owners[i * share : (i + 1) * share])

    @pl.loop(0, groups // 2)
    def _(pair):
        group_step(2 * pair, out_even, out_odd)
        group_step(2 * pair + 1, out_odd, out_even)

    for i in range(per_group):
        part = all_owners[i * share : (i + 1) * share]
        pack(out_odd, mine, far, near, (groups - 1) * GROUP, tables, part)


def folded_rows(rows, width):
    whole, rest = divmod(width, LANES)
    return rows * whole + (rows if rest > LANES // 2 else rows // 2 if rest else 0)


def fold(tiles, out, width):
    rows = tiles[0].shape[0]
    lane = lax.broadcasted_iota(jnp.int32, (rows // 2, LANES), 1)
    for t, tile in enumerate(tiles):
        if t == len(tiles) - 1 and out.shape[0] < rows * len(tiles):
            low, high = tile[: rows // 2], tile[rows // 2 :]
            tile = jnp.where(lane < LANES // 2, low, pltpu.roll(high, LANES // 2, 1))
        out[t * rows : t * rows + tile.shape[0], :] = tile.astype(out.dtype)


def unfold(block, rows):
    count = block.shape[0] // rows
    tiles = [block[t * rows : (t + 1) * rows, :] for t in range(count)]
    if count * rows < block.shape[0]:
        low = block[count * rows :, :].astype(jnp.float32)
        high = pltpu.roll(low, LANES // 2, 1)
        tiles.append(jnp.concatenate([low, high], axis=0).astype(block.dtype))
    return tiles


def sum_kernel(steps, width, mine, got, *out):
    for i, step in enumerate(steps):
        tiles = [mine[step, t] + got[i, t] for t in range(mine.shape[1])]
        fold(tiles, out[i], width)


def kl_kernel(part, owners, width, slot_column, rows_column, kl, *refs):
    blocks, (out, packed_v) = refs[:owners], refs[owners:]
    owner_slots, rows, freqs = kl.shape
    shares = lax.axis_size("af")
    per_source = freqs // owners
    me = lax.axis_index("ma")
    for step in range(owners):
        source = on_ring(cyclic(on_ring(me) - step, owners))
        at = pl.multiple_of(source * per_source, GROUP)
        for t, tile in enumerate(unfold(blocks[step], per_source)):
            packed_v[pl.ds(at, per_source), t * LANES : (t + 1) * LANES] = tile
    share_rows = rows // shares
    at = pl.multiple_of(cyclic(lax.axis_index("af") + part, shares) * share_rows, GROUP)
    lhs = kl[:, pl.ds(at, share_rows), :].reshape(owner_slots * share_rows, freqs)
    product = jnp.dot(lhs, packed_v[...], preferred_element_type=jnp.float32)
    line = lax.broadcasted_iota(jnp.int32, (share_rows, LANES), 0) + at
    tiles = []
    for t in range(packed_v.shape[1] // LANES):
        lanes = slice(t * LANES, (t + 1) * LANES)
        slot_at = slot_column[0:1, lanes]
        total = jnp.zeros((share_rows, LANES), jnp.float32)
        for j in range(owner_slots):
            here = product[j * share_rows : (j + 1) * share_rows, lanes]
            total = jnp.where(slot_at == j, here, total)
        tiles.append(jnp.where(line < rows_column[0:1, lanes], total, 0.0))
    fold(tiles, out, width)


def unpack_kernel(scalars, mine, got, out, sum_v, out_v, sems):
    owner_slots, rows, modes = out_v.shape
    places = [
        [jnp.max(scalars[k * owner_slots + j : k * owner_slots + j + 1, :]) for k in range(2)]
        for j in range(owner_slots)
    ]
    for t, (a, b) in enumerate(zip(unfold(mine, rows), unfold(got, rows))):
        sum_v[t] = a + b.astype(jnp.float32)
    lane = lax.broadcasted_iota(jnp.int32, (rows, LANES), 1)
    copies = []
    for j, (offset, keep) in enumerate(places):
        tile = lax.div(offset, LANES)
        shift = offset - tile * LANES
        back = lax.rem(LANES - shift, LANES)
        turned = [pltpu.roll(sum_v[tile + t], back, 1) for t in range(modes // LANES + 1)]
        for t in range(modes // LANES):
            value = jnp.where(lane < LANES - shift, turned[t], turned[t + 1])
            value = jnp.where(lane < keep - t * LANES, value, 0.0)
            out_v[j, :, t * LANES : (t + 1) * LANES] = value
        copy = pltpu.make_async_copy(out_v.at[j], out.at[j], sems.at[j])
        copy.start()
        copies.append(copy)
    for copy in copies:
        copy.wait()


HBM = pl.BlockSpec(memory_space=pltpu.HBM)
VMEM = pl.BlockSpec(memory_space=pltpu.VMEM)
SMALL = pltpu.CompilerParams(vmem_limit_bytes=8 * MIB)


def in_hbm(operand):
    return pltpu.with_memory_space_constraint(operand, pltpu.HBM)


def project(panels, svd_basis, slot_of_m, svd_keep, kl_keep, owner_slots, width):
    slots, freqs, depth = panels.shape
    modes = svd_basis.shape[2]
    owners = lax.axis_size("ma")

    def packed(count):
        return jax.ShapeDtypeStruct((count, width // LANES, freqs, LANES), jnp.float32)

    column = jax.ShapeDtypeStruct((8, width), jnp.int32)
    return pl.pallas_call(
        functools.partial(project_kernel, owner_slots),
        out_shape=(
            packed(owners),
            packed(1),
            packed(owners - 1),
            column,
            column,
            jax.ShapeDtypeStruct((8, LANES), jnp.int32),
        ),
        in_specs=[HBM] * 5,
        out_specs=(VMEM,) * 6,
        scratch_shapes=[pltpu.SMEM((slots,), jnp.int32)] * 8
        + [
            pltpu.VMEM((slots, freqs, depth), jnp.bfloat16),
            pltpu.VMEM((freqs, depth, modes), jnp.bfloat16),
            pltpu.VMEM((GROUP, slots, depth), jnp.bfloat16),
            pltpu.VMEM((modes // LANES * GROUP * slots, LANES), jnp.float32),
            pltpu.VMEM((modes // LANES * GROUP * slots, LANES), jnp.float32),
            pltpu.SemaphoreType.DMA((3,)),
            pltpu.SemaphoreType.DMA((freqs // GROUP,)),
            pltpu.SemaphoreType.DMA((freqs // PER_COPY,)),
        ],
        compiler_params=pltpu.CompilerParams(vmem_limit_bytes=48 * MIB),
        cost_estimate=pl.CostEstimate(
            flops=2 * slots * freqs * depth * modes,
            bytes_accessed=2 * freqs * depth * (modes + slots),
            transcendentals=0,
        ),
        name="project",
    )(*map(in_hbm, (slot_of_m, svd_keep, kl_keep, panels, svd_basis)))


def sum_pair(steps, width, mine, got):
    kind = jax.ShapeDtypeStruct((folded_rows(mine.shape[2], width), LANES), jnp.bfloat16)
    return pl.pallas_call(
        functools.partial(sum_kernel, steps, width),
        out_shape=(kind,) * len(steps),
        in_specs=[VMEM] * 2,
        out_specs=(VMEM,) * len(steps),
        compiler_params=SMALL,
        cost_estimate=pl.CostEstimate(
            flops=got.size, bytes_accessed=10 * got.size, transcendentals=0
        ),
        name="sum_pair",
    )(mine, got)


def kl_project(part, kind, width, slot_column, rows_column, kl_basis, blocks):
    owners, shares = lax.axis_size("ma"), lax.axis_size("af")
    rows, freqs = kl_basis.shape[1:]
    wide = slot_column.shape[1]
    return pl.pallas_call(
        functools.partial(kl_kernel, part, owners, width),
        out_shape=jax.ShapeDtypeStruct((folded_rows(rows // shares, width), LANES), kind),
        in_specs=[VMEM] * (3 + owners),
        out_specs=VMEM,
        scratch_shapes=[pltpu.VMEM((freqs, wide), jnp.bfloat16)],
        compiler_params=SMALL,
        cost_estimate=pl.CostEstimate(
            flops=2 * kl_basis.size * wide // shares,
            bytes_accessed=2 * kl_basis.size,
            transcendentals=0,
        ),
        name="kl_project",
    )(slot_column, rows_column, kl_basis, *blocks)


def unpack(scalars, mine, got, owner_slots, rows, modes, width):
    tiles = -(-width // LANES) + modes // LANES + 1
    return pl.pallas_call(
        unpack_kernel,
        out_shape=jax.ShapeDtypeStruct((owner_slots, rows, modes), jnp.float32),
        in_specs=[VMEM] * 3,
        out_specs=HBM,
        scratch_shapes=[
            pltpu.VMEM((tiles, rows, LANES), jnp.float32),
            pltpu.VMEM((owner_slots, rows, modes), jnp.float32),
            pltpu.SemaphoreType.DMA((owner_slots,)),
        ],
        compiler_params=SMALL,
        cost_estimate=pl.CostEstimate(
            flops=mine.size, bytes_accessed=10 * mine.size, transcendentals=0
        ),
        name="unpack",
    )(scalars, mine, got)


def pairs(axis):
    return [(i, i ^ 1) for i in range(lax.axis_size(axis))]


def ring(step):
    size = lax.axis_size("ma")
    return [(i, on_ring((on_ring(i) + step) % size)) for i in range(size)]


def shards(panels, svd_basis, kl_basis, slot_of_m, svd_keep, kl_keep):
    owner_slots, modes = kl_basis.shape[0], svd_basis.shape[2]
    owners = lax.axis_size("ma")
    width = min(OWNER_BUDGET, owner_slots * modes)
    wide = -(-width // LANES) * LANES
    mine, far, near, slot_column, rows_column, scalars = project(
        panels, svd_basis, slot_of_m, svd_keep, kl_keep, owner_slots, wide
    )
    first = far_step(owners)
    others = [step for step in range(owners) if step != first]
    got_far = lax.ppermute(far, "pa", pairs("pa"))
    near, got_far = lax.optimization_barrier((near, got_far))
    got_near = lax.ppermute(near, "pa", pairs("pa"))
    summed = dict(zip([first], sum_pair([first], width, mine, got_far)))
    summed |= zip(others, sum_pair(others, width, mine, got_near))
    blocks = {
        step: lax.ppermute(summed[step], "ma", ring(step)) if step else summed[step]
        for step in [first] + others
    }
    tables = (width, slot_column, rows_column, kl_basis, [blocks[step] for step in range(owners)])
    send = kl_project(1, jnp.bfloat16, *tables)
    got = lax.ppermute(send, "af", pairs("af"))
    mine = kl_project(0, jnp.float32, *tables)
    rows = kl_basis.shape[1] // lax.axis_size("af")
    return unpack(scalars, mine, got, owner_slots, rows, modes, width)


def kernels_fit(mesh, args):
    panels, svd_basis, kl_basis = args[:3]
    slots = panels.shape[0] // mesh.shape["grp"]
    freqs = svd_basis.shape[0] // (mesh.shape["af"] * mesh.shape["ma"])
    owner_slots = kl_basis.shape[0] // (mesh.shape["pa"] * mesh.shape["ma"])
    share_rows = kl_basis.shape[1] // mesh.shape["af"]
    return (
        freqs % (2 * GROUP) == 0
        and slots % (GROUP * mesh.shape["pa"]) == 0
        and owner_slots == 4
        and svd_basis.shape[2] == 2 * LANES
        and share_rows % (2 * GROUP) == 0
        and mesh.shape["pa"] == 2
        and mesh.shape["af"] == 2
        and mesh.shape["ma"] == 4
    )


def solution(mesh):
    in_specs = (
        P("grp", ("af", "ma"), "pa"),
        P(("af", "ma"), "pa", None),
        P(("pa", "ma"), None, "af"),
        P(),
        P(),
        P(),
    )
    out_specs = P(("grp", "pa", "ma"), "af", None)

    def run(*args):
        body = shards if kernels_fit(mesh, args) else shards_plain
        mapped = jax.shard_map(
            body, mesh=mesh, in_specs=in_specs, out_specs=out_specs, check_vma=False
        )
        return mapped(*args)

    return run
```

```python
import functools

import jax
import jax.numpy as jnp
from jax import lax
from jax.experimental import pallas as pl
from jax.experimental.pallas import tpu as pltpu
from jax.sharding import PartitionSpec as P

LANES = 128
GROUP = 16
PER_COPY = 8
OWNER_BUDGET = 576
MIB = 2**20


def shards_plain(panels, svd_basis, kl_basis, slot_of_m, svd_keep, kl_keep):
    slot_count = slot_of_m.shape[0]
    order_slots = jnp.argsort(slot_of_m)
    keep_slots = jnp.take(svd_keep, order_slots, axis=0)
    modes_slots = jnp.take(kl_keep, order_slots, axis=0)
    width_modes = svd_basis.shape[2]
    owner_rows = kl_basis.shape[0]
    slot_rows = slot_count // lax.axis_size("pa")
    slot_start = lax.axis_index("pa") * slot_rows
    owner_start = slot_start + lax.axis_index("ma") * owner_rows
    modes_owner = lax.dynamic_slice_in_dim(modes_slots, owner_start, owner_rows, 0)
    chosen = jnp.take(panels, order_slots, axis=0)
    summed = lax.psum_scatter(
        jnp.einsum("mfb,fbr->mfr", chosen, svd_basis, preferred_element_type=jnp.float32),
        "pa",
        scatter_dimension=0,
        tiled=True,
    )
    keep_here = lax.dynamic_slice_in_dim(keep_slots, slot_start, slot_rows, 0)
    columns = jnp.arange(width_modes, dtype=jnp.int32)
    retained = jnp.where(columns[None, None, :] < keep_here[:, None, None], summed, 0.0).astype(
        jnp.bfloat16
    )
    relaid = lax.all_to_all(retained, "ma", split_axis=0, concat_axis=1, tiled=True)
    partial_sums = jnp.einsum("mkf,mfr->mkr", kl_basis, relaid, preferred_element_type=jnp.float32)
    modes = jnp.arange(kl_basis.shape[1], dtype=jnp.int32)
    partial_sums = jnp.where(modes[None, :, None] < modes_owner[:, None, None], partial_sums, 0.0)
    return lax.psum_scatter(partial_sums, "af", scatter_dimension=1, tiled=True)


def cyclic(value, count):
    return lax.rem(value + count, count)


def on_ring(z):
    return z ^ (z // 2) if isinstance(z, int) else z ^ lax.shift_right_logical(z, 1)


def far_step(owners):
    return owners // 2


def place_of(slot, owner_slots, half_slots):
    half = cyclic(lax.div(slot, half_slots) - lax.axis_index("pa"), lax.axis_size("pa"))
    within = lax.rem(slot, half_slots)
    owner = on_ring(lax.div(within, owner_slots)) - on_ring(lax.axis_index("ma"))
    owner = cyclic(owner, lax.axis_size("ma"))
    return half * half_slots + owner * owner_slots + lax.rem(within, owner_slots)


def offsets_of(keep_place, tile_place, shift_place, owner_slots):
    @pl.loop(0, keep_place.shape[0] // owner_slots)
    def _(at):
        offset = jnp.int32(0)
        for j in range(owner_slots):
            place = at * owner_slots + j
            tile = lax.div(offset, LANES)
            tile_place[place] = tile
            shift_place[place] = offset - tile * LANES
            offset = offset + keep_place[place]


def pack(out_v, mine, far, near, line, tables, owners_at):
    tile_place, shift_place, owner_slots = tables
    owners, width_tiles = mine.shape[:2]
    slots = 2 * owners * owner_slots
    tiles = out_v.shape[0] // (GROUP * slots)
    lane = lax.broadcasted_iota(jnp.int32, (GROUP, LANES), 1)
    rows = pl.ds(pl.multiple_of(line, GROUP), GROUP)
    turned = {
        place: pltpu.roll(
            out_v[pl.ds(place, tiles * GROUP, stride=slots), :], shift_place[place], 1
        )
        for place in range(owners_at[0] * owner_slots, (owners_at[-1] + 1) * owner_slots)
    }
    for at in owners_at:
        to, owner = mine, at % owners
        if at >= owners:
            first = far_step(owners)
            to, owner = (far, 0) if owner == first else (near, owner - (owner > first))
        values, tile_before = None, None
        for j in range(owner_slots):
            place = at * owner_slots + j
            tile = tile_place[place]
            left = lane < shift_place[place]
            moved = [turned[place][t * GROUP : (t + 1) * GROUP] for t in range(tiles)]
            shared = moved[0]
            if j > 0:
                step = tile - tile_before
                shared = values[0]
                for t in range(1, tiles + 1):
                    shared = jnp.where(step == t, values[t], shared)
            values = (
                [jnp.where(left, shared, moved[0])]
                + [jnp.where(left, moved[t - 1], moved[t]) for t in range(1, tiles)]
                + [moved[tiles - 1]]
            )
            tile_before = tile
            for t in reversed(range(tiles + 1)):
                to[owner, jnp.minimum(tile + t, width_tiles - 1), rows, :] = values[t]


def project_kernel(
    owner_slots, slot_hbm, keep_hbm, rows_hbm, panels, basis,
    mine, far, near, slot_column, rows_column, scalars,
    slot_s, keep_s, rows_s, keep_place, rows_place, tile_place, shift_place,
    panels_v, basis_v, lhs_v, out_even, out_odd, small_sem, panel_sem, basis_sem,
):
    slots, freqs, depth = panels_v.shape
    groups = freqs // GROUP
    half_slots = slots // lax.axis_size("pa")

    table_copies = [
        pltpu.make_async_copy(slot_hbm, slot_s, small_sem.at[0]),
        pltpu.make_async_copy(keep_hbm, keep_s, small_sem.at[1]),
        pltpu.make_async_copy(rows_hbm, rows_s, small_sem.at[2]),
    ]
    for copy in table_copies:
        copy.start()

    def basis_copy(i):
        part = pl.ds(i * PER_COPY, PER_COPY)
        return pltpu.make_async_copy(basis.at[part], basis_v.at[part], basis_sem.at[i])

    ahead = 1
    for i in range(ahead):
        basis_copy(i).start()
    for copy in table_copies:
        copy.wait()

    per_group = GROUP // PER_COPY
    for group in range(groups):
        part = pl.ds(group * GROUP, GROUP)

        @pl.loop(0, slots)
        def _(m):
            place = place_of(slot_s[m], owner_slots, half_slots)
            if group == 0:
                keep_place[place] = keep_s[m]
                rows_place[place] = rows_s[m]
            pltpu.make_async_copy(
                panels.at[m, part], panels_v.at[place, part], panel_sem.at[group]
            ).start()

        for i in range(ahead + group * per_group, min(ahead + (group + 1) * per_group, groups * per_group)):
            basis_copy(i).start()

    offsets_of(keep_place, tile_place, shift_place, owner_slots)
    column = lax.broadcasted_iota(jnp.int32, slot_column.shape, 1)
    slot_at = jnp.full(slot_column.shape, owner_slots, jnp.int32)
    rows_at = jnp.zeros(slot_column.shape, jnp.int32)
    for j in range(owner_slots):
        keep = keep_place[j]
        offset = tile_place[j] * LANES + shift_place[j]
        within = (column >= offset) & (column < offset + keep)
        slot_at = jnp.where(within, j, slot_at)
        rows_at = jnp.where(within, rows_place[j], rows_at)
        scalars[j : j + 1, :] = jnp.full((1, LANES), offset, jnp.int32)
        scalars[owner_slots + j : owner_slots + j + 1, :] = jnp.full((1, LANES), keep, jnp.int32)
    slot_column[...] = slot_at
    rows_column[...] = rows_at

    side = GROUP * GROUP
    row = lax.broadcasted_iota(jnp.int32, (side, side), 0)
    column = lax.broadcasted_iota(jnp.int32, (side, side), 1)
    swap = (column == (row % GROUP) * GROUP + row // GROUP).astype(jnp.float32).astype(jnp.bfloat16)

    tables = (tile_place, shift_place, owner_slots)
    all_owners = range(mine.shape[0] * lax.axis_size("pa"))

    def group_step(group, out_v, out_before):
        here = pl.ds(pl.multiple_of(group * GROUP, GROUP), GROUP)
        pltpu.make_async_copy(
            panels_v.at[:, here], panels_v.at[:, here], panel_sem.at[group]
        ).wait()
        for block in range(slots // GROUP):
            blocks = slice(block * GROUP, (block + 1) * GROUP)
            tile = panels_v[blocks, here, :].reshape(side, depth)
            turned = jnp.dot(swap, tile, preferred_element_type=jnp.float32).astype(jnp.bfloat16)
            lhs_v[:, blocks, :] = turned.reshape(GROUP, GROUP, depth)
        for i in range(per_group):
            basis_copy(group * per_group + i).wait()
            for f in range(i * PER_COPY, (i + 1) * PER_COPY):
                product = jnp.dot(
                    lhs_v[f], basis_v[group * GROUP + f], preferred_element_type=jnp.float32
                )
                for t in range(product.shape[1] // LANES):
                    at = (t * GROUP + f) * slots
                    out_v[at : at + slots, :] = product[:, t * LANES : (t + 1) * LANES]
            if i == 0:
                line = jnp.maximum(group - 1, 0) * GROUP
                pack(out_before, mine, far, near, line, tables, all_owners)

    @pl.loop(0, groups // 2)
    def _(pair):
        group_step(2 * pair, out_even, out_odd)
        group_step(2 * pair + 1, out_odd, out_even)

    pack(out_odd, mine, far, near, (groups - 1) * GROUP, tables, all_owners)


def folded_rows(rows, width):
    whole, rest = divmod(width, LANES)
    return rows * whole + (rows if rest > LANES // 2 else rows // 2 if rest else 0)


def fold(tiles, out, width):
    rows = tiles[0].shape[0]
    lane = lax.broadcasted_iota(jnp.int32, (rows // 2, LANES), 1)
    for t, tile in enumerate(tiles):
        if t == len(tiles) - 1 and out.shape[0] < rows * len(tiles):
            low, high = tile[: rows // 2], tile[rows // 2 :]
            tile = jnp.where(lane < LANES // 2, low, pltpu.roll(high, LANES // 2, 1))
        out[t * rows : t * rows + tile.shape[0], :] = tile.astype(out.dtype)


def unfold(block, rows):
    count = block.shape[0] // rows
    tiles = [block[t * rows : (t + 1) * rows, :] for t in range(count)]
    if count * rows < block.shape[0]:
        low = block[count * rows :, :].astype(jnp.float32)
        high = pltpu.roll(low, LANES // 2, 1)
        tiles.append(jnp.concatenate([low, high], axis=0).astype(block.dtype))
    return tiles


def sum_kernel(steps, width, mine, got, *out):
    for i, step in enumerate(steps):
        tiles = [mine[step, t] + got[i, t] for t in range(mine.shape[1])]
        fold(tiles, out[i], width)


def kl_kernel(part, owners, width, slot_column, rows_column, kl, *refs):
    blocks, (out, packed_v) = refs[:owners], refs[owners:]
    owner_slots, rows, freqs = kl.shape
    shares = lax.axis_size("af")
    per_source = freqs // owners
    me = lax.axis_index("ma")
    for step in range(owners):
        source = on_ring(cyclic(on_ring(me) - step, owners))
        at = pl.multiple_of(source * per_source, GROUP)
        for t, tile in enumerate(unfold(blocks[step], per_source)):
            packed_v[pl.ds(at, per_source), t * LANES : (t + 1) * LANES] = tile
    share_rows = rows // shares
    at = pl.multiple_of(cyclic(lax.axis_index("af") + part, shares) * share_rows, GROUP)
    lhs = kl[:, pl.ds(at, share_rows), :].reshape(owner_slots * share_rows, freqs)
    product = jnp.dot(lhs, packed_v[...], preferred_element_type=jnp.float32)
    line = lax.broadcasted_iota(jnp.int32, (share_rows, LANES), 0) + at
    tiles = []
    for t in range(packed_v.shape[1] // LANES):
        lanes = slice(t * LANES, (t + 1) * LANES)
        slot_at = slot_column[0:1, lanes]
        total = jnp.zeros((share_rows, LANES), jnp.float32)
        for j in range(owner_slots):
            here = product[j * share_rows : (j + 1) * share_rows, lanes]
            total = jnp.where(slot_at == j, here, total)
        tiles.append(jnp.where(line < rows_column[0:1, lanes], total, 0.0))
    fold(tiles, out, width)


def unpack_kernel(scalars, mine, got, out, sum_v, out_v, sems):
    owner_slots, rows, modes = out_v.shape
    places = [
        [jnp.max(scalars[k * owner_slots + j : k * owner_slots + j + 1, :]) for k in range(2)]
        for j in range(owner_slots)
    ]
    for t, (a, b) in enumerate(zip(unfold(mine, rows), unfold(got, rows))):
        sum_v[t] = a + b.astype(jnp.float32)
    lane = lax.broadcasted_iota(jnp.int32, (rows, LANES), 1)
    copies = []
    for j, (offset, keep) in enumerate(places):
        tile = lax.div(offset, LANES)
        shift = offset - tile * LANES
        back = lax.rem(LANES - shift, LANES)
        turned = [pltpu.roll(sum_v[tile + t], back, 1) for t in range(modes // LANES + 1)]
        for t in range(modes // LANES):
            value = jnp.where(lane < LANES - shift, turned[t], turned[t + 1])
            value = jnp.where(lane < keep - t * LANES, value, 0.0)
            out_v[j, :, t * LANES : (t + 1) * LANES] = value
        copy = pltpu.make_async_copy(out_v.at[j], out.at[j], sems.at[j])
        copy.start()
        copies.append(copy)
    for copy in copies:
        copy.wait()


HBM = pl.BlockSpec(memory_space=pltpu.HBM)
VMEM = pl.BlockSpec(memory_space=pltpu.VMEM)
SMALL = pltpu.CompilerParams(vmem_limit_bytes=8 * MIB)


def in_hbm(operand):
    return pltpu.with_memory_space_constraint(operand, pltpu.HBM)


def project(panels, svd_basis, slot_of_m, svd_keep, kl_keep, owner_slots, width):
    slots, freqs, depth = panels.shape
    modes = svd_basis.shape[2]
    owners = lax.axis_size("ma")

    def packed(count):
        return jax.ShapeDtypeStruct((count, width // LANES, freqs, LANES), jnp.float32)

    column = jax.ShapeDtypeStruct((8, width), jnp.int32)
    return pl.pallas_call(
        functools.partial(project_kernel, owner_slots),
        out_shape=(
            packed(owners),
            packed(1),
            packed(owners - 1),
            column,
            column,
            jax.ShapeDtypeStruct((8, LANES), jnp.int32),
        ),
        in_specs=[HBM] * 5,
        out_specs=(VMEM,) * 6,
        scratch_shapes=[pltpu.SMEM((slots,), jnp.int32)] * 7
        + [
            pltpu.VMEM((slots, freqs, depth), jnp.bfloat16),
            pltpu.VMEM((freqs, depth, modes), jnp.bfloat16),
            pltpu.VMEM((GROUP, slots, depth), jnp.bfloat16),
            pltpu.VMEM((modes // LANES * GROUP * slots, LANES), jnp.float32),
            pltpu.VMEM((modes // LANES * GROUP * slots, LANES), jnp.float32),
            pltpu.SemaphoreType.DMA((3,)),
            pltpu.SemaphoreType.DMA((freqs // GROUP,)),
            pltpu.SemaphoreType.DMA((freqs // PER_COPY,)),
        ],
        compiler_params=pltpu.CompilerParams(vmem_limit_bytes=48 * MIB),
        cost_estimate=pl.CostEstimate(
            flops=2 * slots * freqs * depth * modes,
            bytes_accessed=2 * freqs * depth * (modes + slots),
            transcendentals=0,
        ),
        name="project",
    )(*map(in_hbm, (slot_of_m, svd_keep, kl_keep, panels, svd_basis)))


def sum_pair(steps, width, mine, got):
    kind = jax.ShapeDtypeStruct((folded_rows(mine.shape[2], width), LANES), jnp.bfloat16)
    return pl.pallas_call(
        functools.partial(sum_kernel, steps, width),
        out_shape=(kind,) * len(steps),
        in_specs=[VMEM] * 2,
        out_specs=(VMEM,) * len(steps),
        compiler_params=SMALL,
        cost_estimate=pl.CostEstimate(
            flops=got.size, bytes_accessed=10 * got.size, transcendentals=0
        ),
        name="sum_pair",
    )(mine, got)


def kl_project(part, kind, width, slot_column, rows_column, kl_basis, blocks):
    owners, shares = lax.axis_size("ma"), lax.axis_size("af")
    rows, freqs = kl_basis.shape[1:]
    wide = slot_column.shape[1]
    return pl.pallas_call(
        functools.partial(kl_kernel, part, owners, width),
        out_shape=jax.ShapeDtypeStruct((folded_rows(rows // shares, width), LANES), kind),
        in_specs=[VMEM] * (3 + owners),
        out_specs=VMEM,
        scratch_shapes=[pltpu.VMEM((freqs, wide), jnp.bfloat16)],
        compiler_params=SMALL,
        cost_estimate=pl.CostEstimate(
            flops=2 * kl_basis.size * wide // shares,
            bytes_accessed=2 * kl_basis.size,
            transcendentals=0,
        ),
        name="kl_project",
    )(slot_column, rows_column, kl_basis, *blocks)


def unpack(scalars, mine, got, owner_slots, rows, modes, width):
    tiles = -(-width // LANES) + modes // LANES + 1
    return pl.pallas_call(
        unpack_kernel,
        out_shape=jax.ShapeDtypeStruct((owner_slots, rows, modes), jnp.float32),
        in_specs=[VMEM] * 3,
        out_specs=HBM,
        scratch_shapes=[
            pltpu.VMEM((tiles, rows, LANES), jnp.float32),
            pltpu.VMEM((owner_slots, rows, modes), jnp.float32),
            pltpu.SemaphoreType.DMA((owner_slots,)),
        ],
        compiler_params=SMALL,
        cost_estimate=pl.CostEstimate(
            flops=mine.size, bytes_accessed=10 * mine.size, transcendentals=0
        ),
        name="unpack",
    )(scalars, mine, got)


def pairs(axis):
    return [(i, i ^ 1) for i in range(lax.axis_size(axis))]


def ring(step):
    size = lax.axis_size("ma")
    return [(i, on_ring((on_ring(i) + step) % size)) for i in range(size)]


def shards(panels, svd_basis, kl_basis, slot_of_m, svd_keep, kl_keep):
    owner_slots, modes = kl_basis.shape[0], svd_basis.shape[2]
    owners = lax.axis_size("ma")
    width = min(OWNER_BUDGET, owner_slots * modes)
    wide = -(-width // LANES) * LANES
    mine, far, near, slot_column, rows_column, scalars = project(
        panels, svd_basis, slot_of_m, svd_keep, kl_keep, owner_slots, wide
    )
    first = far_step(owners)
    others = [step for step in range(owners) if step != first]
    got_far = lax.ppermute(far, "pa", pairs("pa"))
    near, got_far = lax.optimization_barrier((near, got_far))
    got_near = lax.ppermute(near, "pa", pairs("pa"))
    summed = dict(zip([first], sum_pair([first], width, mine, got_far)))
    summed |= zip(others, sum_pair(others, width, mine, got_near))
    blocks = {
        step: lax.ppermute(summed[step], "ma", ring(step)) if step else summed[step]
        for step in [first] + others
    }
    tables = (width, slot_column, rows_column, kl_basis, [blocks[step] for step in range(owners)])
    send = kl_project(1, jnp.bfloat16, *tables)
    got = lax.ppermute(send, "af", pairs("af"))
    mine = kl_project(0, jnp.float32, *tables)
    rows = kl_basis.shape[1] // lax.axis_size("af")
    return unpack(scalars, mine, got, owner_slots, rows, modes, width)


def kernels_fit(mesh, args):
    panels, svd_basis, kl_basis = args[:3]
    slots = panels.shape[0] // mesh.shape["grp"]
    freqs = svd_basis.shape[0] // (mesh.shape["af"] * mesh.shape["ma"])
    owner_slots = kl_basis.shape[0] // (mesh.shape["pa"] * mesh.shape["ma"])
    share_rows = kl_basis.shape[1] // mesh.shape["af"]
    return (
        freqs % (2 * GROUP) == 0
        and slots % (GROUP * mesh.shape["pa"]) == 0
        and owner_slots == 4
        and svd_basis.shape[2] == 2 * LANES
        and share_rows % (2 * GROUP) == 0
        and mesh.shape["pa"] == 2
        and mesh.shape["af"] == 2
        and mesh.shape["ma"] == 4
    )


def solution(mesh):
    in_specs = (
        P("grp", ("af", "ma"), "pa"),
        P(("af", "ma"), "pa", None),
        P(("pa", "ma"), None, "af"),
        P(),
        P(),
        P(),
    )
    out_specs = P(("grp", "pa", "ma"), "af", None)

    def run(*args):
        body = shards if kernels_fit(mesh, args) else shards_plain
        mapped = jax.shard_map(
            body, mesh=mesh, in_specs=in_specs, out_specs=out_specs, check_vma=False
        )
        return mapped(*args)

    return run
```

```python
import functools

import jax
import jax.numpy as jnp
from jax import lax
from jax.experimental import pallas as pl
from jax.experimental.pallas import tpu as pltpu
from jax.sharding import PartitionSpec as P

LANES = 128
GROUP = 16
PER_COPY = 8
OWNER_BUDGET = 576
MIB = 2**20


def shards_plain(panels, svd_basis, kl_basis, slot_of_m, svd_keep, kl_keep):
    slot_count = slot_of_m.shape[0]
    order_slots = jnp.argsort(slot_of_m)
    keep_slots = jnp.take(svd_keep, order_slots, axis=0)
    modes_slots = jnp.take(kl_keep, order_slots, axis=0)
    width_modes = svd_basis.shape[2]
    owner_rows = kl_basis.shape[0]
    slot_rows = slot_count // lax.axis_size("pa")
    slot_start = lax.axis_index("pa") * slot_rows
    owner_start = slot_start + lax.axis_index("ma") * owner_rows
    modes_owner = lax.dynamic_slice_in_dim(modes_slots, owner_start, owner_rows, 0)
    chosen = jnp.take(panels, order_slots, axis=0)
    summed = lax.psum_scatter(
        jnp.einsum("mfb,fbr->mfr", chosen, svd_basis, preferred_element_type=jnp.float32),
        "pa",
        scatter_dimension=0,
        tiled=True,
    )
    keep_here = lax.dynamic_slice_in_dim(keep_slots, slot_start, slot_rows, 0)
    columns = jnp.arange(width_modes, dtype=jnp.int32)
    retained = jnp.where(columns[None, None, :] < keep_here[:, None, None], summed, 0.0).astype(
        jnp.bfloat16
    )
    relaid = lax.all_to_all(retained, "ma", split_axis=0, concat_axis=1, tiled=True)
    partial_sums = jnp.einsum("mkf,mfr->mkr", kl_basis, relaid, preferred_element_type=jnp.float32)
    modes = jnp.arange(kl_basis.shape[1], dtype=jnp.int32)
    partial_sums = jnp.where(modes[None, :, None] < modes_owner[:, None, None], partial_sums, 0.0)
    return lax.psum_scatter(partial_sums, "af", scatter_dimension=1, tiled=True)


def cyclic(value, count):
    return lax.rem(value + count, count)


def on_ring(z):
    return z ^ (z // 2) if isinstance(z, int) else z ^ lax.shift_right_logical(z, 1)


def far_step(owners):
    return owners // 2


def place_of(slot, owner_slots, half_slots):
    half = cyclic(lax.div(slot, half_slots) - lax.axis_index("pa"), lax.axis_size("pa"))
    within = lax.rem(slot, half_slots)
    owner = on_ring(lax.div(within, owner_slots)) - on_ring(lax.axis_index("ma"))
    owner = cyclic(owner, lax.axis_size("ma"))
    return half * half_slots + owner * owner_slots + lax.rem(within, owner_slots)


def offsets_of(keep_place, tile_place, shift_place, owner_slots):
    @pl.loop(0, keep_place.shape[0] // owner_slots)
    def _(at):
        offset = jnp.int32(0)
        for j in range(owner_slots):
            place = at * owner_slots + j
            tile = lax.div(offset, LANES)
            tile_place[place] = tile
            shift_place[place] = offset - tile * LANES
            offset = offset + keep_place[place]


def pack(out_v, mine, far, near, line, tables, owners_at):
    tile_place, shift_place, owner_slots = tables
    owners, width_tiles = mine.shape[:2]
    slots = 2 * owners * owner_slots
    tiles = out_v.shape[0] // (GROUP * slots)
    lane = lax.broadcasted_iota(jnp.int32, (GROUP, LANES), 1)
    rows = pl.ds(pl.multiple_of(line, GROUP), GROUP)
    turned = {
        place: pltpu.roll(
            out_v[pl.ds(place, tiles * GROUP, stride=slots), :], shift_place[place], 1
        )
        for place in range(owners_at[0] * owner_slots, (owners_at[-1] + 1) * owner_slots)
    }
    for at in owners_at:
        to, owner = mine, at % owners
        if at >= owners:
            first = far_step(owners)
            to, owner = (far, 0) if owner == first else (near, owner - (owner > first))
        values, tile_before = None, None
        for j in range(owner_slots):
            place = at * owner_slots + j
            tile = tile_place[place]
            left = lane < shift_place[place]
            moved = [turned[place][t * GROUP : (t + 1) * GROUP] for t in range(tiles)]
            shared = moved[0]
            if j > 0:
                step = tile - tile_before
                shared = values[0]
                for t in range(1, tiles + 1):
                    shared = jnp.where(step == t, values[t], shared)
            values = (
                [jnp.where(left, shared, moved[0])]
                + [jnp.where(left, moved[t - 1], moved[t]) for t in range(1, tiles)]
                + [moved[tiles - 1]]
            )
            tile_before = tile
            for t in reversed(range(tiles + 1)):
                to[owner, jnp.minimum(tile + t, width_tiles - 1), rows, :] = values[t]


def project_kernel(
    owner_slots, slot_hbm, keep_hbm, rows_hbm, panels, basis,
    mine, far, near, slot_column, rows_column, scalars,
    slot_s, keep_s, rows_s, keep_place, rows_place, tile_place, shift_place,
    panels_v, basis_v, lhs_v, out_even, out_odd, small_sem, panel_sem, basis_sem,
):
    slots, freqs, depth = panels_v.shape
    groups = freqs // GROUP
    half_slots = slots // lax.axis_size("pa")

    table_copies = [
        pltpu.make_async_copy(slot_hbm, slot_s, small_sem.at[0]),
        pltpu.make_async_copy(keep_hbm, keep_s, small_sem.at[1]),
        pltpu.make_async_copy(rows_hbm, rows_s, small_sem.at[2]),
    ]
    for copy in table_copies:
        copy.start()

    def basis_copy(i):
        part = pl.ds(i * PER_COPY, PER_COPY)
        return pltpu.make_async_copy(basis.at[part], basis_v.at[part], basis_sem.at[i])

    ahead = 0
    for i in range(ahead):
        basis_copy(i).start()
    for copy in table_copies:
        copy.wait()

    per_group = GROUP // PER_COPY
    for group in range(groups):
        part = pl.ds(group * GROUP, GROUP)

        @pl.loop(0, slots)
        def _(m):
            place = place_of(slot_s[m], owner_slots, half_slots)
            if group == 0:
                keep_place[place] = keep_s[m]
                rows_place[place] = rows_s[m]
            pltpu.make_async_copy(
                panels.at[m, part], panels_v.at[place, part], panel_sem.at[group]
            ).start()

        for i in range(ahead + group * per_group, min(ahead + (group + 1) * per_group, groups * per_group)):
            basis_copy(i).start()

    offsets_of(keep_place, tile_place, shift_place, owner_slots)
    column = lax.broadcasted_iota(jnp.int32, slot_column.shape, 1)
    slot_at = jnp.full(slot_column.shape, owner_slots, jnp.int32)
    rows_at = jnp.zeros(slot_column.shape, jnp.int32)
    for j in range(owner_slots):
        keep = keep_place[j]
        offset = tile_place[j] * LANES + shift_place[j]
        within = (column >= offset) & (column < offset + keep)
        slot_at = jnp.where(within, j, slot_at)
        rows_at = jnp.where(within, rows_place[j], rows_at)
        scalars[j : j + 1, :] = jnp.full((1, LANES), offset, jnp.int32)
        scalars[owner_slots + j : owner_slots + j + 1, :] = jnp.full((1, LANES), keep, jnp.int32)
    slot_column[...] = slot_at
    rows_column[...] = rows_at

    side = GROUP * GROUP
    row = lax.broadcasted_iota(jnp.int32, (side, side), 0)
    column = lax.broadcasted_iota(jnp.int32, (side, side), 1)
    swap = (column == (row % GROUP) * GROUP + row // GROUP).astype(jnp.float32).astype(jnp.bfloat16)

    tables = (tile_place, shift_place, owner_slots)
    all_owners = range(mine.shape[0] * lax.axis_size("pa"))
    share = len(all_owners) // per_group

    def group_step(group, out_v, out_before):
        here = pl.ds(pl.multiple_of(group * GROUP, GROUP), GROUP)
        pltpu.make_async_copy(
            panels_v.at[:, here], panels_v.at[:, here], panel_sem.at[group]
        ).wait()
        for block in range(slots // GROUP):
            blocks = slice(block * GROUP, (block + 1) * GROUP)
            tile = panels_v[blocks, here, :].reshape(side, depth)
            turned = jnp.dot(swap, tile, preferred_element_type=jnp.float32).astype(jnp.bfloat16)
            lhs_v[:, blocks, :] = turned.reshape(GROUP, GROUP, depth)
        for i in range(per_group):
            basis_copy(group * per_group + i).wait()
            for f in range(i * PER_COPY, (i + 1) * PER_COPY):
                product = jnp.dot(
                    lhs_v[f], basis_v[group * GROUP + f], preferred_element_type=jnp.float32
                )
                for t in range(product.shape[1] // LANES):
                    at = (t * GROUP + f) * slots
                    out_v[at : at + slots, :] = product[:, t * LANES : (t + 1) * LANES]
            line = jnp.maximum(group - 1, 0) * GROUP
            pack(out_before, mine, far, near, line, tables, all_owners[i * share : (i + 1) * share])

    @pl.loop(0, groups // 2)
    def _(pair):
        group_step(2 * pair, out_even, out_odd)
        group_step(2 * pair + 1, out_odd, out_even)

    for i in range(per_group):
        part = all_owners[i * share : (i + 1) * share]
        pack(out_odd, mine, far, near, (groups - 1) * GROUP, tables, part)


def folded_rows(rows, width):
    whole, rest = divmod(width, LANES)
    return rows * whole + (rows if rest > LANES // 2 else rows // 2 if rest else 0)


def fold(tiles, out, width):
    rows = tiles[0].shape[0]
    lane = lax.broadcasted_iota(jnp.int32, (rows // 2, LANES), 1)
    for t, tile in enumerate(tiles):
        if t == len(tiles) - 1 and out.shape[0] < rows * len(tiles):
            low, high = tile[: rows // 2], tile[rows // 2 :]
            tile = jnp.where(lane < LANES // 2, low, pltpu.roll(high, LANES // 2, 1))
        out[t * rows : t * rows + tile.shape[0], :] = tile.astype(out.dtype)


def unfold(block, rows):
    count = block.shape[0] // rows
    tiles = [block[t * rows : (t + 1) * rows, :] for t in range(count)]
    if count * rows < block.shape[0]:
        low = block[count * rows :, :].astype(jnp.float32)
        high = pltpu.roll(low, LANES // 2, 1)
        tiles.append(jnp.concatenate([low, high], axis=0).astype(block.dtype))
    return tiles


def sum_kernel(steps, width, mine, got, *out):
    for i, step in enumerate(steps):
        tiles = [mine[step, t] + got[i, t] for t in range(mine.shape[1])]
        fold(tiles, out[i], width)


def kl_kernel(part, owners, width, slot_column, rows_column, kl, *refs):
    blocks, (out, packed_v) = refs[:owners], refs[owners:]
    owner_slots, rows, freqs = kl.shape
    shares = lax.axis_size("af")
    per_source = freqs // owners
    me = lax.axis_index("ma")
    for step in range(owners):
        source = on_ring(cyclic(on_ring(me) - step, owners))
        at = pl.multiple_of(source * per_source, GROUP)
        for t, tile in enumerate(unfold(blocks[step], per_source)):
            packed_v[pl.ds(at, per_source), t * LANES : (t + 1) * LANES] = tile
    share_rows = rows // shares
    at = pl.multiple_of(cyclic(lax.axis_index("af") + part, shares) * share_rows, GROUP)
    lhs = kl[:, pl.ds(at, share_rows), :].reshape(owner_slots * share_rows, freqs)
    product = jnp.dot(lhs, packed_v[...], preferred_element_type=jnp.float32)
    line = lax.broadcasted_iota(jnp.int32, (share_rows, LANES), 0) + at
    tiles = []
    for t in range(packed_v.shape[1] // LANES):
        lanes = slice(t * LANES, (t + 1) * LANES)
        slot_at = slot_column[0:1, lanes]
        total = jnp.zeros((share_rows, LANES), jnp.float32)
        for j in range(owner_slots):
            here = product[j * share_rows : (j + 1) * share_rows, lanes]
            total = jnp.where(slot_at == j, here, total)
        tiles.append(jnp.where(line < rows_column[0:1, lanes], total, 0.0))
    fold(tiles, out, width)


def unpack_kernel(scalars, mine, got, out, sum_v, out_v, sems):
    owner_slots, rows, modes = out_v.shape
    places = [
        [jnp.max(scalars[k * owner_slots + j : k * owner_slots + j + 1, :]) for k in range(2)]
        for j in range(owner_slots)
    ]
    for t, (a, b) in enumerate(zip(unfold(mine, rows), unfold(got, rows))):
        sum_v[t] = a + b.astype(jnp.float32)
    lane = lax.broadcasted_iota(jnp.int32, (rows, LANES), 1)
    copies = []
    for j, (offset, keep) in enumerate(places):
        tile = lax.div(offset, LANES)
        shift = offset - tile * LANES
        back = lax.rem(LANES - shift, LANES)
        turned = [pltpu.roll(sum_v[tile + t], back, 1) for t in range(modes // LANES + 1)]
        for t in range(modes // LANES):
            value = jnp.where(lane < LANES - shift, turned[t], turned[t + 1])
            value = jnp.where(lane < keep - t * LANES, value, 0.0)
            out_v[j, :, t * LANES : (t + 1) * LANES] = value
        copy = pltpu.make_async_copy(out_v.at[j], out.at[j], sems.at[j])
        copy.start()
        copies.append(copy)
    for copy in copies:
        copy.wait()


HBM = pl.BlockSpec(memory_space=pltpu.HBM)
VMEM = pl.BlockSpec(memory_space=pltpu.VMEM)
SMALL = pltpu.CompilerParams(vmem_limit_bytes=8 * MIB)


def in_hbm(operand):
    return pltpu.with_memory_space_constraint(operand, pltpu.HBM)


def project(panels, svd_basis, slot_of_m, svd_keep, kl_keep, owner_slots, width):
    slots, freqs, depth = panels.shape
    modes = svd_basis.shape[2]
    owners = lax.axis_size("ma")

    def packed(count):
        return jax.ShapeDtypeStruct((count, width // LANES, freqs, LANES), jnp.float32)

    column = jax.ShapeDtypeStruct((8, width), jnp.int32)
    return pl.pallas_call(
        functools.partial(project_kernel, owner_slots),
        out_shape=(
            packed(owners),
            packed(1),
            packed(owners - 1),
            column,
            column,
            jax.ShapeDtypeStruct((8, LANES), jnp.int32),
        ),
        in_specs=[HBM] * 5,
        out_specs=(VMEM,) * 6,
        scratch_shapes=[pltpu.SMEM((slots,), jnp.int32)] * 7
        + [
            pltpu.VMEM((slots, freqs, depth), jnp.bfloat16),
            pltpu.VMEM((freqs, depth, modes), jnp.bfloat16),
            pltpu.VMEM((GROUP, slots, depth), jnp.bfloat16),
            pltpu.VMEM((modes // LANES * GROUP * slots, LANES), jnp.float32),
            pltpu.VMEM((modes // LANES * GROUP * slots, LANES), jnp.float32),
            pltpu.SemaphoreType.DMA((3,)),
            pltpu.SemaphoreType.DMA((freqs // GROUP,)),
            pltpu.SemaphoreType.DMA((freqs // PER_COPY,)),
        ],
        compiler_params=pltpu.CompilerParams(vmem_limit_bytes=48 * MIB),
        cost_estimate=pl.CostEstimate(
            flops=2 * slots * freqs * depth * modes,
            bytes_accessed=2 * freqs * depth * (modes + slots),
            transcendentals=0,
        ),
        name="project",
    )(*map(in_hbm, (slot_of_m, svd_keep, kl_keep, panels, svd_basis)))


def sum_pair(steps, width, mine, got):
    kind = jax.ShapeDtypeStruct((folded_rows(mine.shape[2], width), LANES), jnp.bfloat16)
    return pl.pallas_call(
        functools.partial(sum_kernel, steps, width),
        out_shape=(kind,) * len(steps),
        in_specs=[VMEM] * 2,
        out_specs=(VMEM,) * len(steps),
        compiler_params=SMALL,
        cost_estimate=pl.CostEstimate(
            flops=got.size, bytes_accessed=10 * got.size, transcendentals=0
        ),
        name="sum_pair",
    )(mine, got)


def kl_project(part, kind, width, slot_column, rows_column, kl_basis, blocks):
    owners, shares = lax.axis_size("ma"), lax.axis_size("af")
    rows, freqs = kl_basis.shape[1:]
    wide = slot_column.shape[1]
    return pl.pallas_call(
        functools.partial(kl_kernel, part, owners, width),
        out_shape=jax.ShapeDtypeStruct((folded_rows(rows // shares, width), LANES), kind),
        in_specs=[VMEM] * (3 + owners),
        out_specs=VMEM,
        scratch_shapes=[pltpu.VMEM((freqs, wide), jnp.bfloat16)],
        compiler_params=SMALL,
        cost_estimate=pl.CostEstimate(
            flops=2 * kl_basis.size * wide // shares,
            bytes_accessed=2 * kl_basis.size,
            transcendentals=0,
        ),
        name="kl_project",
    )(slot_column, rows_column, kl_basis, *blocks)


def unpack(scalars, mine, got, owner_slots, rows, modes, width):
    tiles = -(-width // LANES) + modes // LANES + 1
    return pl.pallas_call(
        unpack_kernel,
        out_shape=jax.ShapeDtypeStruct((owner_slots, rows, modes), jnp.float32),
        in_specs=[VMEM] * 3,
        out_specs=HBM,
        scratch_shapes=[
            pltpu.VMEM((tiles, rows, LANES), jnp.float32),
            pltpu.VMEM((owner_slots, rows, modes), jnp.float32),
            pltpu.SemaphoreType.DMA((owner_slots,)),
        ],
        compiler_params=SMALL,
        cost_estimate=pl.CostEstimate(
            flops=mine.size, bytes_accessed=10 * mine.size, transcendentals=0
        ),
        name="unpack",
    )(scalars, mine, got)


def pairs(axis):
    return [(i, i ^ 1) for i in range(lax.axis_size(axis))]


def ring(step):
    size = lax.axis_size("ma")
    return [(i, on_ring((on_ring(i) + step) % size)) for i in range(size)]


def shards(panels, svd_basis, kl_basis, slot_of_m, svd_keep, kl_keep):
    owner_slots, modes = kl_basis.shape[0], svd_basis.shape[2]
    owners = lax.axis_size("ma")
    width = min(OWNER_BUDGET, owner_slots * modes)
    wide = -(-width // LANES) * LANES
    mine, far, near, slot_column, rows_column, scalars = project(
        panels, svd_basis, slot_of_m, svd_keep, kl_keep, owner_slots, wide
    )
    first = far_step(owners)
    others = [step for step in range(owners) if step != first]
    got_far = lax.ppermute(far, "pa", pairs("pa"))
    near, got_far = lax.optimization_barrier((near, got_far))
    got_near = lax.ppermute(near, "pa", pairs("pa"))
    summed = dict(zip([first], sum_pair([first], width, mine, got_far)))
    summed |= zip(others, sum_pair(others, width, mine, got_near))
    blocks = {
        step: lax.ppermute(summed[step], "ma", ring(step)) if step else summed[step]
        for step in [first] + others
    }
    tables = (width, slot_column, rows_column, kl_basis, [blocks[step] for step in range(owners)])
    send = kl_project(1, jnp.bfloat16, *tables)
    got = lax.ppermute(send, "af", pairs("af"))
    mine = kl_project(0, jnp.float32, *tables)
    rows = kl_basis.shape[1] // lax.axis_size("af")
    return unpack(scalars, mine, got, owner_slots, rows, modes, width)


def kernels_fit(mesh, args):
    panels, svd_basis, kl_basis = args[:3]
    slots = panels.shape[0] // mesh.shape["grp"]
    freqs = svd_basis.shape[0] // (mesh.shape["af"] * mesh.shape["ma"])
    owner_slots = kl_basis.shape[0] // (mesh.shape["pa"] * mesh.shape["ma"])
    share_rows = kl_basis.shape[1] // mesh.shape["af"]
    return (
        freqs % (2 * GROUP) == 0
        and slots % (GROUP * mesh.shape["pa"]) == 0
        and owner_slots == 4
        and svd_basis.shape[2] == 2 * LANES
        and share_rows % (2 * GROUP) == 0
        and mesh.shape["pa"] == 2
        and mesh.shape["af"] == 2
        and mesh.shape["ma"] == 4
    )


def solution(mesh):
    in_specs = (
        P("grp", ("af", "ma"), "pa"),
        P(("af", "ma"), "pa", None),
        P(("pa", "ma"), None, "af"),
        P(),
        P(),
        P(),
    )
    out_specs = P(("grp", "pa", "ma"), "af", None)

    def run(*args):
        body = shards if kernels_fit(mesh, args) else shards_plain
        mapped = jax.shard_map(
            body, mesh=mesh, in_specs=in_specs, out_specs=out_specs, check_vma=False
        )
        return mapped(*args)

    return run
```

```python
import functools

import jax
import jax.numpy as jnp
from jax import lax
from jax.experimental import pallas as pl
from jax.experimental.pallas import tpu as pltpu
from jax.sharding import PartitionSpec as P

LANES = 128
GROUP = 16
PER_COPY = 8
OWNER_BUDGET = 576
MIB = 2**20


def shards_plain(panels, svd_basis, kl_basis, slot_of_m, svd_keep, kl_keep):
    slot_count = slot_of_m.shape[0]
    order_slots = jnp.argsort(slot_of_m)
    keep_slots = jnp.take(svd_keep, order_slots, axis=0)
    modes_slots = jnp.take(kl_keep, order_slots, axis=0)
    width_modes = svd_basis.shape[2]
    owner_rows = kl_basis.shape[0]
    slot_rows = slot_count // lax.axis_size("pa")
    slot_start = lax.axis_index("pa") * slot_rows
    owner_start = slot_start + lax.axis_index("ma") * owner_rows
    modes_owner = lax.dynamic_slice_in_dim(modes_slots, owner_start, owner_rows, 0)
    chosen = jnp.take(panels, order_slots, axis=0)
    summed = lax.psum_scatter(
        jnp.einsum("mfb,fbr->mfr", chosen, svd_basis, preferred_element_type=jnp.float32),
        "pa",
        scatter_dimension=0,
        tiled=True,
    )
    keep_here = lax.dynamic_slice_in_dim(keep_slots, slot_start, slot_rows, 0)
    columns = jnp.arange(width_modes, dtype=jnp.int32)
    retained = jnp.where(columns[None, None, :] < keep_here[:, None, None], summed, 0.0).astype(
        jnp.bfloat16
    )
    relaid = lax.all_to_all(retained, "ma", split_axis=0, concat_axis=1, tiled=True)
    partial_sums = jnp.einsum("mkf,mfr->mkr", kl_basis, relaid, preferred_element_type=jnp.float32)
    modes = jnp.arange(kl_basis.shape[1], dtype=jnp.int32)
    partial_sums = jnp.where(modes[None, :, None] < modes_owner[:, None, None], partial_sums, 0.0)
    return lax.psum_scatter(partial_sums, "af", scatter_dimension=1, tiled=True)


def cyclic(value, count):
    return lax.rem(value + count, count)


def on_ring(z):
    return z ^ (z // 2) if isinstance(z, int) else z ^ lax.shift_right_logical(z, 1)


def far_step(owners):
    return owners // 2


def place_of(slot, owner_slots, half_slots):
    half = cyclic(lax.div(slot, half_slots) - lax.axis_index("pa"), lax.axis_size("pa"))
    within = lax.rem(slot, half_slots)
    owner = on_ring(lax.div(within, owner_slots)) - on_ring(lax.axis_index("ma"))
    owner = cyclic(owner, lax.axis_size("ma"))
    return half * half_slots + owner * owner_slots + lax.rem(within, owner_slots)


def offsets_of(keep_place, tile_place, shift_place, owner_slots):
    @pl.loop(0, keep_place.shape[0] // owner_slots)
    def _(at):
        offset = jnp.int32(0)
        for j in range(owner_slots):
            place = at * owner_slots + j
            tile = lax.div(offset, LANES)
            tile_place[place] = tile
            shift_place[place] = offset - tile * LANES
            offset = offset + keep_place[place]


def pack(out_v, mine, far, near, line, tables, owners_at):
    tile_place, shift_place, owner_slots = tables
    owners, width_tiles = mine.shape[:2]
    slots = 2 * owners * owner_slots
    tiles = out_v.shape[0] // (GROUP * slots)
    lane = lax.broadcasted_iota(jnp.int32, (GROUP, LANES), 1)
    rows = pl.ds(pl.multiple_of(line, GROUP), GROUP)
    turned = {
        place: pltpu.roll(
            out_v[pl.ds(place, tiles * GROUP, stride=slots), :], shift_place[place], 1
        )
        for place in range(owners_at[0] * owner_slots, (owners_at[-1] + 1) * owner_slots)
    }
    for at in owners_at:
        to, owner = mine, at % owners
        if at >= owners:
            first = far_step(owners)
            to, owner = (far, 0) if owner == first else (near, owner - (owner > first))
        values, tile_before = None, None
        for j in range(owner_slots):
            place = at * owner_slots + j
            tile = tile_place[place]
            left = lane < shift_place[place]
            moved = [turned[place][t * GROUP : (t + 1) * GROUP] for t in range(tiles)]
            shared = moved[0]
            if j > 0:
                step = tile - tile_before
                shared = values[0]
                for t in range(1, tiles + 1):
                    shared = jnp.where(step == t, values[t], shared)
            values = (
                [jnp.where(left, shared, moved[0])]
                + [jnp.where(left, moved[t - 1], moved[t]) for t in range(1, tiles)]
                + [moved[tiles - 1]]
            )
            tile_before = tile
            for t in reversed(range(tiles + 1)):
                to[owner, jnp.minimum(tile + t, width_tiles - 1), rows, :] = values[t]


def project_kernel(
    owner_slots, slot_hbm, keep_hbm, rows_hbm, panels, basis,
    mine, far, near, slot_column, rows_column, scalars,
    slot_s, keep_s, rows_s, keep_place, rows_place, tile_place, shift_place,
    panels_v, basis_v, lhs_v, out_even, out_odd, small_sem, panel_sem, basis_sem,
):
    slots, freqs, depth = panels_v.shape
    groups = freqs // GROUP
    half_slots = slots // lax.axis_size("pa")

    table_copies = [
        pltpu.make_async_copy(slot_hbm, slot_s, small_sem.at[0]),
        pltpu.make_async_copy(keep_hbm, keep_s, small_sem.at[1]),
        pltpu.make_async_copy(rows_hbm, rows_s, small_sem.at[2]),
    ]
    for copy in table_copies:
        copy.start()

    def basis_copy(i):
        part = pl.ds(i * PER_COPY, PER_COPY)
        return pltpu.make_async_copy(basis.at[part], basis_v.at[part], basis_sem.at[i])

    ahead = 2
    for i in range(ahead):
        basis_copy(i).start()
    for copy in table_copies:
        copy.wait()

    per_group = GROUP // PER_COPY
    for group in range(groups):
        part = pl.ds(group * GROUP, GROUP)

        @pl.loop(0, slots)
        def _(m):
            place = place_of(slot_s[m], owner_slots, half_slots)
            if group == 0:
                keep_place[place] = keep_s[m]
                rows_place[place] = rows_s[m]
            pltpu.make_async_copy(
                panels.at[m, part], panels_v.at[place, part], panel_sem.at[group]
            ).start()

        for i in range(ahead + group * per_group, min(ahead + (group + 1) * per_group, groups * per_group)):
            basis_copy(i).start()

    offsets_of(keep_place, tile_place, shift_place, owner_slots)
    column = lax.broadcasted_iota(jnp.int32, slot_column.shape, 1)
    slot_at = jnp.full(slot_column.shape, owner_slots, jnp.int32)
    rows_at = jnp.zeros(slot_column.shape, jnp.int32)
    for j in range(owner_slots):
        keep = keep_place[j]
        offset = tile_place[j] * LANES + shift_place[j]
        within = (column >= offset) & (column < offset + keep)
        slot_at = jnp.where(within, j, slot_at)
        rows_at = jnp.where(within, rows_place[j], rows_at)
        scalars[j : j + 1, :] = jnp.full((1, LANES), offset, jnp.int32)
        scalars[owner_slots + j : owner_slots + j + 1, :] = jnp.full((1, LANES), keep, jnp.int32)
    slot_column[...] = slot_at
    rows_column[...] = rows_at

    side = GROUP * GROUP
    row = lax.broadcasted_iota(jnp.int32, (side, side), 0)
    column = lax.broadcasted_iota(jnp.int32, (side, side), 1)
    swap = (column == (row % GROUP) * GROUP + row // GROUP).astype(jnp.float32).astype(jnp.bfloat16)

    tables = (tile_place, shift_place, owner_slots)
    all_owners = range(mine.shape[0] * lax.axis_size("pa"))
    share = len(all_owners) // per_group

    def group_step(group, out_v, out_before):
        here = pl.ds(pl.multiple_of(group * GROUP, GROUP), GROUP)
        pltpu.make_async_copy(
            panels_v.at[:, here], panels_v.at[:, here], panel_sem.at[group]
        ).wait()
        for block in range(slots // GROUP):
            blocks = slice(block * GROUP, (block + 1) * GROUP)
            tile = panels_v[blocks, here, :].reshape(side, depth)
            turned = jnp.dot(swap, tile, preferred_element_type=jnp.float32).astype(jnp.bfloat16)
            lhs_v[:, blocks, :] = turned.reshape(GROUP, GROUP, depth)
        for i in range(per_group):
            basis_copy(group * per_group + i).wait()
            for f in range(i * PER_COPY, (i + 1) * PER_COPY):
                product = jnp.dot(
                    lhs_v[f], basis_v[group * GROUP + f], preferred_element_type=jnp.float32
                )
                for t in range(product.shape[1] // LANES):
                    at = (t * GROUP + f) * slots
                    out_v[at : at + slots, :] = product[:, t * LANES : (t + 1) * LANES]
            line = jnp.maximum(group - 1, 0) * GROUP
            pack(out_before, mine, far, near, line, tables, all_owners[i * share : (i + 1) * share])

    @pl.loop(0, groups // 2)
    def _(pair):
        group_step(2 * pair, out_even, out_odd)
        group_step(2 * pair + 1, out_odd, out_even)

    for i in range(per_group):
        part = all_owners[i * share : (i + 1) * share]
        pack(out_odd, mine, far, near, (groups - 1) * GROUP, tables, part)


def folded_rows(rows, width):
    whole, rest = divmod(width, LANES)
    return rows * whole + (rows if rest > LANES // 2 else rows // 2 if rest else 0)


def fold(tiles, out, width):
    rows = tiles[0].shape[0]
    lane = lax.broadcasted_iota(jnp.int32, (rows // 2, LANES), 1)
    for t, tile in enumerate(tiles):
        if t == len(tiles) - 1 and out.shape[0] < rows * len(tiles):
            low, high = tile[: rows // 2], tile[rows // 2 :]
            tile = jnp.where(lane < LANES // 2, low, pltpu.roll(high, LANES // 2, 1))
        out[t * rows : t * rows + tile.shape[0], :] = tile.astype(out.dtype)


def unfold(block, rows):
    count = block.shape[0] // rows
    tiles = [block[t * rows : (t + 1) * rows, :] for t in range(count)]
    if count * rows < block.shape[0]:
        low = block[count * rows :, :].astype(jnp.float32)
        high = pltpu.roll(low, LANES // 2, 1)
        tiles.append(jnp.concatenate([low, high], axis=0).astype(block.dtype))
    return tiles


def sum_kernel(steps, width, mine, got, *out):
    for i, step in enumerate(steps):
        tiles = [mine[step, t] + got[i, t] for t in range(mine.shape[1])]
        fold(tiles, out[i], width)


def kl_kernel(part, owners, width, slot_column, rows_column, kl, *refs):
    blocks, (out, packed_v) = refs[:owners], refs[owners:]
    owner_slots, rows, freqs = kl.shape
    shares = lax.axis_size("af")
    per_source = freqs // owners
    me = lax.axis_index("ma")
    for step in range(owners):
        source = on_ring(cyclic(on_ring(me) - step, owners))
        at = pl.multiple_of(source * per_source, GROUP)
        for t, tile in enumerate(unfold(blocks[step], per_source)):
            packed_v[pl.ds(at, per_source), t * LANES : (t + 1) * LANES] = tile
    share_rows = rows // shares
    at = pl.multiple_of(cyclic(lax.axis_index("af") + part, shares) * share_rows, GROUP)
    lhs = kl[:, pl.ds(at, share_rows), :].reshape(owner_slots * share_rows, freqs)
    product = jnp.dot(lhs, packed_v[...], preferred_element_type=jnp.float32)
    line = lax.broadcasted_iota(jnp.int32, (share_rows, LANES), 0) + at
    tiles = []
    for t in range(packed_v.shape[1] // LANES):
        lanes = slice(t * LANES, (t + 1) * LANES)
        slot_at = slot_column[0:1, lanes]
        total = jnp.zeros((share_rows, LANES), jnp.float32)
        for j in range(owner_slots):
            here = product[j * share_rows : (j + 1) * share_rows, lanes]
            total = jnp.where(slot_at == j, here, total)
        tiles.append(jnp.where(line < rows_column[0:1, lanes], total, 0.0))
    fold(tiles, out, width)


def unpack_kernel(scalars, mine, got, out, sum_v, out_v, sems):
    owner_slots, rows, modes = out_v.shape
    places = [
        [jnp.max(scalars[k * owner_slots + j : k * owner_slots + j + 1, :]) for k in range(2)]
        for j in range(owner_slots)
    ]
    for t, (a, b) in enumerate(zip(unfold(mine, rows), unfold(got, rows))):
        sum_v[t] = a + b.astype(jnp.float32)
    lane = lax.broadcasted_iota(jnp.int32, (rows, LANES), 1)
    copies = []
    for j, (offset, keep) in enumerate(places):
        tile = lax.div(offset, LANES)
        shift = offset - tile * LANES
        back = lax.rem(LANES - shift, LANES)
        turned = [pltpu.roll(sum_v[tile + t], back, 1) for t in range(modes // LANES + 1)]
        for t in range(modes // LANES):
            value = jnp.where(lane < LANES - shift, turned[t], turned[t + 1])
            value = jnp.where(lane < keep - t * LANES, value, 0.0)
            out_v[j, :, t * LANES : (t + 1) * LANES] = value
        copy = pltpu.make_async_copy(out_v.at[j], out.at[j], sems.at[j])
        copy.start()
        copies.append(copy)
    for copy in copies:
        copy.wait()


HBM = pl.BlockSpec(memory_space=pltpu.HBM)
VMEM = pl.BlockSpec(memory_space=pltpu.VMEM)
SMALL = pltpu.CompilerParams(vmem_limit_bytes=8 * MIB)


def in_hbm(operand):
    return pltpu.with_memory_space_constraint(operand, pltpu.HBM)


def project(panels, svd_basis, slot_of_m, svd_keep, kl_keep, owner_slots, width):
    slots, freqs, depth = panels.shape
    modes = svd_basis.shape[2]
    owners = lax.axis_size("ma")

    def packed(count):
        return jax.ShapeDtypeStruct((count, width // LANES, freqs, LANES), jnp.float32)

    column = jax.ShapeDtypeStruct((8, width), jnp.int32)
    return pl.pallas_call(
        functools.partial(project_kernel, owner_slots),
        out_shape=(
            packed(owners),
            packed(1),
            packed(owners - 1),
            column,
            column,
            jax.ShapeDtypeStruct((8, LANES), jnp.int32),
        ),
        in_specs=[HBM] * 5,
        out_specs=(VMEM,) * 6,
        scratch_shapes=[pltpu.SMEM((slots,), jnp.int32)] * 7
        + [
            pltpu.VMEM((slots, freqs, depth), jnp.bfloat16),
            pltpu.VMEM((freqs, depth, modes), jnp.bfloat16),
            pltpu.VMEM((GROUP, slots, depth), jnp.bfloat16),
            pltpu.VMEM((modes // LANES * GROUP * slots, LANES), jnp.float32),
            pltpu.VMEM((modes // LANES * GROUP * slots, LANES), jnp.float32),
            pltpu.SemaphoreType.DMA((3,)),
            pltpu.SemaphoreType.DMA((freqs // GROUP,)),
            pltpu.SemaphoreType.DMA((freqs // PER_COPY,)),
        ],
        compiler_params=pltpu.CompilerParams(vmem_limit_bytes=48 * MIB),
        cost_estimate=pl.CostEstimate(
            flops=2 * slots * freqs * depth * modes,
            bytes_accessed=2 * freqs * depth * (modes + slots),
            transcendentals=0,
        ),
        name="project",
    )(*map(in_hbm, (slot_of_m, svd_keep, kl_keep, panels, svd_basis)))


def sum_pair(steps, width, mine, got):
    kind = jax.ShapeDtypeStruct((folded_rows(mine.shape[2], width), LANES), jnp.bfloat16)
    return pl.pallas_call(
        functools.partial(sum_kernel, steps, width),
        out_shape=(kind,) * len(steps),
        in_specs=[VMEM] * 2,
        out_specs=(VMEM,) * len(steps),
        compiler_params=SMALL,
        cost_estimate=pl.CostEstimate(
            flops=got.size, bytes_accessed=10 * got.size, transcendentals=0
        ),
        name="sum_pair",
    )(mine, got)


def kl_project(part, kind, width, slot_column, rows_column, kl_basis, blocks):
    owners, shares = lax.axis_size("ma"), lax.axis_size("af")
    rows, freqs = kl_basis.shape[1:]
    wide = slot_column.shape[1]
    return pl.pallas_call(
        functools.partial(kl_kernel, part, owners, width),
        out_shape=jax.ShapeDtypeStruct((folded_rows(rows // shares, width), LANES), kind),
        in_specs=[VMEM] * (3 + owners),
        out_specs=VMEM,
        scratch_shapes=[pltpu.VMEM((freqs, wide), jnp.bfloat16)],
        compiler_params=SMALL,
        cost_estimate=pl.CostEstimate(
            flops=2 * kl_basis.size * wide // shares,
            bytes_accessed=2 * kl_basis.size,
            transcendentals=0,
        ),
        name="kl_project",
    )(slot_column, rows_column, kl_basis, *blocks)


def unpack(scalars, mine, got, owner_slots, rows, modes, width):
    tiles = -(-width // LANES) + modes // LANES + 1
    return pl.pallas_call(
        unpack_kernel,
        out_shape=jax.ShapeDtypeStruct((owner_slots, rows, modes), jnp.float32),
        in_specs=[VMEM] * 3,
        out_specs=HBM,
        scratch_shapes=[
            pltpu.VMEM((tiles, rows, LANES), jnp.float32),
            pltpu.VMEM((owner_slots, rows, modes), jnp.float32),
            pltpu.SemaphoreType.DMA((owner_slots,)),
        ],
        compiler_params=SMALL,
        cost_estimate=pl.CostEstimate(
            flops=mine.size, bytes_accessed=10 * mine.size, transcendentals=0
        ),
        name="unpack",
    )(scalars, mine, got)


def pairs(axis):
    return [(i, i ^ 1) for i in range(lax.axis_size(axis))]


def ring(step):
    size = lax.axis_size("ma")
    return [(i, on_ring((on_ring(i) + step) % size)) for i in range(size)]


def shards(panels, svd_basis, kl_basis, slot_of_m, svd_keep, kl_keep):
    owner_slots, modes = kl_basis.shape[0], svd_basis.shape[2]
    owners = lax.axis_size("ma")
    width = min(OWNER_BUDGET, owner_slots * modes)
    wide = -(-width // LANES) * LANES
    mine, far, near, slot_column, rows_column, scalars = project(
        panels, svd_basis, slot_of_m, svd_keep, kl_keep, owner_slots, wide
    )
    first = far_step(owners)
    others = [step for step in range(owners) if step != first]
    got_far = lax.ppermute(far, "pa", pairs("pa"))
    near, got_far = lax.optimization_barrier((near, got_far))
    got_near = lax.ppermute(near, "pa", pairs("pa"))
    summed = dict(zip([first], sum_pair([first], width, mine, got_far)))
    summed |= zip(others, sum_pair(others, width, mine, got_near))
    blocks = {
        step: lax.ppermute(summed[step], "ma", ring(step)) if step else summed[step]
        for step in [first] + others
    }
    tables = (width, slot_column, rows_column, kl_basis, [blocks[step] for step in range(owners)])
    send = kl_project(1, jnp.bfloat16, *tables)
    got = lax.ppermute(send, "af", pairs("af"))
    mine = kl_project(0, jnp.float32, *tables)
    rows = kl_basis.shape[1] // lax.axis_size("af")
    return unpack(scalars, mine, got, owner_slots, rows, modes, width)


def kernels_fit(mesh, args):
    panels, svd_basis, kl_basis = args[:3]
    slots = panels.shape[0] // mesh.shape["grp"]
    freqs = svd_basis.shape[0] // (mesh.shape["af"] * mesh.shape["ma"])
    owner_slots = kl_basis.shape[0] // (mesh.shape["pa"] * mesh.shape["ma"])
    share_rows = kl_basis.shape[1] // mesh.shape["af"]
    return (
        freqs % (2 * GROUP) == 0
        and slots % (GROUP * mesh.shape["pa"]) == 0
        and owner_slots == 4
        and svd_basis.shape[2] == 2 * LANES
        and share_rows % (2 * GROUP) == 0
        and mesh.shape["pa"] == 2
        and mesh.shape["af"] == 2
        and mesh.shape["ma"] == 4
    )


def solution(mesh):
    in_specs = (
        P("grp", ("af", "ma"), "pa"),
        P(("af", "ma"), "pa", None),
        P(("pa", "ma"), None, "af"),
        P(),
        P(),
        P(),
    )
    out_specs = P(("grp", "pa", "ma"), "af", None)

    def run(*args):
        body = shards if kernels_fit(mesh, args) else shards_plain
        mapped = jax.shard_map(
            body, mesh=mesh, in_specs=in_specs, out_specs=out_specs, check_vma=False
        )
        return mapped(*args)

    return run
```

```python
import functools

import jax
import jax.numpy as jnp
from jax import lax
from jax.experimental import pallas as pl
from jax.experimental.pallas import tpu as pltpu
from jax.sharding import PartitionSpec as P

LANES = 128
GROUP = 16
PER_COPY = 8
OWNER_BUDGET = 576
MIB = 2**20


def shards_plain(panels, svd_basis, kl_basis, slot_of_m, svd_keep, kl_keep):
    slot_count = slot_of_m.shape[0]
    order_slots = jnp.argsort(slot_of_m)
    keep_slots = jnp.take(svd_keep, order_slots, axis=0)
    modes_slots = jnp.take(kl_keep, order_slots, axis=0)
    width_modes = svd_basis.shape[2]
    owner_rows = kl_basis.shape[0]
    slot_rows = slot_count // lax.axis_size("pa")
    slot_start = lax.axis_index("pa") * slot_rows
    owner_start = slot_start + lax.axis_index("ma") * owner_rows
    modes_owner = lax.dynamic_slice_in_dim(modes_slots, owner_start, owner_rows, 0)
    chosen = jnp.take(panels, order_slots, axis=0)
    summed = lax.psum_scatter(
        jnp.einsum("mfb,fbr->mfr", chosen, svd_basis, preferred_element_type=jnp.float32),
        "pa",
        scatter_dimension=0,
        tiled=True,
    )
    keep_here = lax.dynamic_slice_in_dim(keep_slots, slot_start, slot_rows, 0)
    columns = jnp.arange(width_modes, dtype=jnp.int32)
    retained = jnp.where(columns[None, None, :] < keep_here[:, None, None], summed, 0.0).astype(
        jnp.bfloat16
    )
    relaid = lax.all_to_all(retained, "ma", split_axis=0, concat_axis=1, tiled=True)
    partial_sums = jnp.einsum("mkf,mfr->mkr", kl_basis, relaid, preferred_element_type=jnp.float32)
    modes = jnp.arange(kl_basis.shape[1], dtype=jnp.int32)
    partial_sums = jnp.where(modes[None, :, None] < modes_owner[:, None, None], partial_sums, 0.0)
    return lax.psum_scatter(partial_sums, "af", scatter_dimension=1, tiled=True)


def cyclic(value, count):
    return lax.rem(value + count, count)


def on_ring(z):
    return z ^ (z // 2) if isinstance(z, int) else z ^ lax.shift_right_logical(z, 1)


def far_step(owners):
    return owners // 2


def place_of(slot, owner_slots, half_slots):
    half = cyclic(lax.div(slot, half_slots) - lax.axis_index("pa"), lax.axis_size("pa"))
    within = lax.rem(slot, half_slots)
    owner = on_ring(lax.div(within, owner_slots)) - on_ring(lax.axis_index("ma"))
    owner = cyclic(owner, lax.axis_size("ma"))
    return half * half_slots + owner * owner_slots + lax.rem(within, owner_slots)


def offsets_of(keep_place, tile_place, shift_place, owner_slots):
    @pl.loop(0, keep_place.shape[0] // owner_slots)
    def _(at):
        offset = jnp.int32(0)
        for j in range(owner_slots):
            place = at * owner_slots + j
            tile = lax.div(offset, LANES)
            tile_place[place] = tile
            shift_place[place] = offset - tile * LANES
            offset = offset + keep_place[place]


def pack(out_v, mine, far, near, line, tables, owners_at):
    tile_place, shift_place, owner_slots = tables
    owners, width_tiles = mine.shape[:2]
    slots = 2 * owners * owner_slots
    tiles = out_v.shape[0] // (GROUP * slots)
    lane = lax.broadcasted_iota(jnp.int32, (GROUP, LANES), 1)
    rows = pl.ds(pl.multiple_of(line, GROUP), GROUP)
    turned = {
        place: pltpu.roll(
            out_v[pl.ds(place, tiles * GROUP, stride=slots), :], shift_place[place], 1
        )
        for place in range(owners_at[0] * owner_slots, (owners_at[-1] + 1) * owner_slots)
    }
    for at in owners_at:
        to, owner = mine, at % owners
        if at >= owners:
            first = far_step(owners)
            to, owner = (far, 0) if owner == first else (near, owner - (owner > first))
        values, tile_before = None, None
        for j in range(owner_slots):
            place = at * owner_slots + j
            tile = tile_place[place]
            left = lane < shift_place[place]
            moved = [turned[place][t * GROUP : (t + 1) * GROUP] for t in range(tiles)]
            shared = moved[0]
            if j > 0:
                step = tile - tile_before
                shared = values[0]
                for t in range(1, tiles + 1):
                    shared = jnp.where(step == t, values[t], shared)
            values = (
                [jnp.where(left, shared, moved[0])]
                + [jnp.where(left, moved[t - 1], moved[t]) for t in range(1, tiles)]
                + [moved[tiles - 1]]
            )
            tile_before = tile
            for t in reversed(range(tiles + 1)):
                to[owner, jnp.minimum(tile + t, width_tiles - 1), rows, :] = values[t]


def project_kernel(
    owner_slots, slot_hbm, keep_hbm, rows_hbm, panels, basis,
    mine, far, near, slot_column, rows_column, scalars,
    slot_s, keep_s, rows_s, keep_place, rows_place, tile_place, shift_place,
    panels_v, basis_v, lhs_v, out_even, out_odd, small_sem, panel_sem, basis_sem,
):
    slots, freqs, depth = panels_v.shape
    groups = freqs // GROUP
    half_slots = slots // lax.axis_size("pa")

    table_copies = [
        pltpu.make_async_copy(slot_hbm, slot_s, small_sem.at[0]),
        pltpu.make_async_copy(keep_hbm, keep_s, small_sem.at[1]),
        pltpu.make_async_copy(rows_hbm, rows_s, small_sem.at[2]),
    ]
    for copy in table_copies:
        copy.start()

    def basis_copy(i):
        part = pl.ds(i * PER_COPY, PER_COPY)
        return pltpu.make_async_copy(basis.at[part], basis_v.at[part], basis_sem.at[i])

    ahead = 1
    for i in range(ahead):
        basis_copy(i).start()
    for copy in table_copies:
        copy.wait()

    per_group = GROUP // PER_COPY
    for group in range(groups):
        part = pl.ds(group * GROUP, GROUP)

        @pl.loop(0, slots)
        def _(m):
            place = place_of(slot_s[m], owner_slots, half_slots)
            if group == 0:
                keep_place[place] = keep_s[m]
                rows_place[place] = rows_s[m]
            pltpu.make_async_copy(
                panels.at[m, part], panels_v.at[place, part], panel_sem.at[group]
            ).start()

        for i in range(ahead + group * per_group, min(ahead + (group + 1) * per_group, groups * per_group)):
            basis_copy(i).start()

    offsets_of(keep_place, tile_place, shift_place, owner_slots)
    column = lax.broadcasted_iota(jnp.int32, slot_column.shape, 1)
    slot_at = jnp.full(slot_column.shape, owner_slots, jnp.int32)
    rows_at = jnp.zeros(slot_column.shape, jnp.int32)
    for j in range(owner_slots):
        keep = keep_place[j]
        offset = tile_place[j] * LANES + shift_place[j]
        within = (column >= offset) & (column < offset + keep)
        slot_at = jnp.where(within, j, slot_at)
        rows_at = jnp.where(within, rows_place[j], rows_at)
        scalars[j : j + 1, :] = jnp.full((1, LANES), offset, jnp.int32)
        scalars[owner_slots + j : owner_slots + j + 1, :] = jnp.full((1, LANES), keep, jnp.int32)
    slot_column[...] = slot_at
    rows_column[...] = rows_at

    side = GROUP * GROUP
    row = lax.broadcasted_iota(jnp.int32, (side, side), 0)
    column = lax.broadcasted_iota(jnp.int32, (side, side), 1)
    swap = (column == (row % GROUP) * GROUP + row // GROUP).astype(jnp.float32).astype(jnp.bfloat16)

    tables = (tile_place, shift_place, owner_slots)
    all_owners = range(mine.shape[0] * lax.axis_size("pa"))
    share = len(all_owners) // per_group

    def group_step(group, out_v, out_before):
        here = pl.ds(pl.multiple_of(group * GROUP, GROUP), GROUP)
        pltpu.make_async_copy(
            panels_v.at[:, here], panels_v.at[:, here], panel_sem.at[group]
        ).wait()
        for block in range(slots // GROUP):
            blocks = slice(block * GROUP, (block + 1) * GROUP)
            tile = panels_v[blocks, here, :].reshape(side, depth)
            turned = jnp.dot(swap, tile, preferred_element_type=jnp.float32).astype(jnp.bfloat16)
            lhs_v[:, blocks, :] = turned.reshape(GROUP, GROUP, depth)
        for i in range(per_group):
            basis_copy(group * per_group + i).wait()
            for f in range(i * PER_COPY, (i + 1) * PER_COPY):
                product = jnp.dot(
                    lhs_v[f], basis_v[group * GROUP + f], preferred_element_type=jnp.float32
                )
                for t in range(product.shape[1] // LANES):
                    at = (t * GROUP + f) * slots
                    out_v[at : at + slots, :] = product[:, t * LANES : (t + 1) * LANES]
            line = jnp.maximum(group - 1, 0) * GROUP
            pack(out_before, mine, far, near, line, tables, all_owners[i * share : (i + 1) * share])

    @pl.loop(0, groups // 2)
    def _(pair):
        group_step(2 * pair, out_even, out_odd)
        group_step(2 * pair + 1, out_odd, out_even)

    for i in range(per_group):
        part = all_owners[i * share : (i + 1) * share]
        pack(out_odd, mine, far, near, (groups - 1) * GROUP, tables, part)


def folded_rows(rows, width):
    whole, rest = divmod(width, LANES)
    return rows * whole + (rows if rest > LANES // 2 else rows // 2 if rest else 0)


def fold(tiles, out, width):
    rows = tiles[0].shape[0]
    lane = lax.broadcasted_iota(jnp.int32, (rows // 2, LANES), 1)
    for t, tile in enumerate(tiles):
        if t == len(tiles) - 1 and out.shape[0] < rows * len(tiles):
            low, high = tile[: rows // 2], tile[rows // 2 :]
            tile = jnp.where(lane < LANES // 2, low, pltpu.roll(high, LANES // 2, 1))
        out[t * rows : t * rows + tile.shape[0], :] = tile.astype(out.dtype)


def unfold(block, rows):
    count = block.shape[0] // rows
    tiles = [block[t * rows : (t + 1) * rows, :] for t in range(count)]
    if count * rows < block.shape[0]:
        low = block[count * rows :, :].astype(jnp.float32)
        high = pltpu.roll(low, LANES // 2, 1)
        tiles.append(jnp.concatenate([low, high], axis=0).astype(block.dtype))
    return tiles


def sum_kernel(steps, width, mine, got, *out):
    for i, step in enumerate(steps):
        tiles = [mine[step, t] + got[i, t] for t in range(mine.shape[1])]
        fold(tiles, out[i], width)


def kl_kernel(part, owners, width, slot_column, rows_column, kl, *refs):
    blocks, (out, packed_v) = refs[:owners], refs[owners:]
    owner_slots, rows, freqs = kl.shape
    shares = lax.axis_size("af")
    per_source = freqs // owners
    me = lax.axis_index("ma")
    for step in range(owners):
        source = on_ring(cyclic(on_ring(me) - step, owners))
        at = pl.multiple_of(source * per_source, GROUP)
        for t, tile in enumerate(unfold(blocks[step], per_source)):
            packed_v[pl.ds(at, per_source), t * LANES : (t + 1) * LANES] = tile
    share_rows = rows // shares
    at = pl.multiple_of(cyclic(lax.axis_index("af") + part, shares) * share_rows, GROUP)
    lhs = kl[:, pl.ds(at, share_rows), :].reshape(owner_slots * share_rows, freqs)
    product = jnp.dot(lhs, packed_v[...], preferred_element_type=jnp.float32)
    line = lax.broadcasted_iota(jnp.int32, (share_rows, LANES), 0) + at
    tiles = []
    for t in range(packed_v.shape[1] // LANES):
        lanes = slice(t * LANES, (t + 1) * LANES)
        slot_at = slot_column[0:1, lanes]
        total = jnp.zeros((share_rows, LANES), jnp.float32)
        for j in range(owner_slots):
            here = product[j * share_rows : (j + 1) * share_rows, lanes]
            total = jnp.where(slot_at == j, here, total)
        tiles.append(jnp.where(line < rows_column[0:1, lanes], total, 0.0))
    fold(tiles, out, width)


def unpack_kernel(scalars, mine, got, out, sum_v, out_v, sems):
    owner_slots, rows, modes = out_v.shape
    places = [
        [jnp.max(scalars[k * owner_slots + j : k * owner_slots + j + 1, :]) for k in range(2)]
        for j in range(owner_slots)
    ]
    for t, (a, b) in enumerate(zip(unfold(mine, rows), unfold(got, rows))):
        sum_v[t] = a + b.astype(jnp.float32)
    lane = lax.broadcasted_iota(jnp.int32, (rows, LANES), 1)
    copies = []
    for j, (offset, keep) in enumerate(places):
        tile = lax.div(offset, LANES)
        shift = offset - tile * LANES
        back = lax.rem(LANES - shift, LANES)
        turned = [pltpu.roll(sum_v[tile + t], back, 1) for t in range(modes // LANES + 1)]
        for t in range(modes // LANES):
            value = jnp.where(lane < LANES - shift, turned[t], turned[t + 1])
            value = jnp.where(lane < keep - t * LANES, value, 0.0)
            out_v[j, :, t * LANES : (t + 1) * LANES] = value
        copy = pltpu.make_async_copy(out_v.at[j], out.at[j], sems.at[j])
        copy.start()
        copies.append(copy)
    for copy in copies:
        copy.wait()


HBM = pl.BlockSpec(memory_space=pltpu.HBM)
VMEM = pl.BlockSpec(memory_space=pltpu.VMEM)
SMALL = pltpu.CompilerParams(vmem_limit_bytes=8 * MIB)


def in_hbm(operand):
    return pltpu.with_memory_space_constraint(operand, pltpu.HBM)


def project(panels, svd_basis, slot_of_m, svd_keep, kl_keep, owner_slots, width):
    slots, freqs, depth = panels.shape
    modes = svd_basis.shape[2]
    owners = lax.axis_size("ma")

    def packed(count):
        return jax.ShapeDtypeStruct((count, width // LANES, freqs, LANES), jnp.float32)

    column = jax.ShapeDtypeStruct((8, width), jnp.int32)
    return pl.pallas_call(
        functools.partial(project_kernel, owner_slots),
        out_shape=(
            packed(owners),
            packed(1),
            packed(owners - 1),
            column,
            column,
            jax.ShapeDtypeStruct((8, LANES), jnp.int32),
        ),
        in_specs=[HBM] * 5,
        out_specs=(VMEM,) * 6,
        scratch_shapes=[pltpu.SMEM((slots,), jnp.int32)] * 7
        + [
            pltpu.VMEM((slots, freqs, depth), jnp.bfloat16),
            pltpu.VMEM((freqs, depth, modes), jnp.bfloat16),
            pltpu.VMEM((GROUP, slots, depth), jnp.bfloat16),
            pltpu.VMEM((modes // LANES * GROUP * slots, LANES), jnp.float32),
            pltpu.VMEM((modes // LANES * GROUP * slots, LANES), jnp.float32),
            pltpu.SemaphoreType.DMA((3,)),
            pltpu.SemaphoreType.DMA((freqs // GROUP,)),
            pltpu.SemaphoreType.DMA((freqs // PER_COPY,)),
        ],
        compiler_params=pltpu.CompilerParams(vmem_limit_bytes=48 * MIB),
        cost_estimate=pl.CostEstimate(
            flops=2 * slots * freqs * depth * modes,
            bytes_accessed=2 * freqs * depth * (modes + slots),
            transcendentals=0,
        ),
        name="project",
    )(*map(in_hbm, (slot_of_m, svd_keep, kl_keep, panels, svd_basis)))


def sum_pair(steps, width, mine, got):
    kind = jax.ShapeDtypeStruct((folded_rows(mine.shape[2], width), LANES), jnp.bfloat16)
    return pl.pallas_call(
        functools.partial(sum_kernel, steps, width),
        out_shape=(kind,) * len(steps),
        in_specs=[VMEM] * 2,
        out_specs=(VMEM,) * len(steps),
        compiler_params=SMALL,
        cost_estimate=pl.CostEstimate(
            flops=got.size, bytes_accessed=10 * got.size, transcendentals=0
        ),
        name="sum_pair",
    )(mine, got)


def kl_project(part, kind, width, slot_column, rows_column, kl_basis, blocks):
    owners, shares = lax.axis_size("ma"), lax.axis_size("af")
    rows, freqs = kl_basis.shape[1:]
    wide = slot_column.shape[1]
    return pl.pallas_call(
        functools.partial(kl_kernel, part, owners, width),
        out_shape=jax.ShapeDtypeStruct((folded_rows(rows // shares, width), LANES), kind),
        in_specs=[VMEM] * (3 + owners),
        out_specs=VMEM,
        scratch_shapes=[pltpu.VMEM((freqs, wide), jnp.bfloat16)],
        compiler_params=SMALL,
        cost_estimate=pl.CostEstimate(
            flops=2 * kl_basis.size * wide // shares,
            bytes_accessed=2 * kl_basis.size,
            transcendentals=0,
        ),
        name="kl_project",
    )(slot_column, rows_column, kl_basis, *blocks)


def unpack(scalars, mine, got, owner_slots, rows, modes, width):
    tiles = -(-width // LANES) + modes // LANES + 1
    return pl.pallas_call(
        unpack_kernel,
        out_shape=jax.ShapeDtypeStruct((owner_slots, rows, modes), jnp.float32),
        in_specs=[VMEM] * 3,
        out_specs=HBM,
        scratch_shapes=[
            pltpu.VMEM((tiles, rows, LANES), jnp.float32),
            pltpu.VMEM((owner_slots, rows, modes), jnp.float32),
            pltpu.SemaphoreType.DMA((owner_slots,)),
        ],
        compiler_params=SMALL,
        cost_estimate=pl.CostEstimate(
            flops=mine.size, bytes_accessed=10 * mine.size, transcendentals=0
        ),
        name="unpack",
    )(scalars, mine, got)


def pairs(axis):
    return [(i, i ^ 1) for i in range(lax.axis_size(axis))]


def ring(step):
    size = lax.axis_size("ma")
    return [(i, on_ring((on_ring(i) + step) % size)) for i in range(size)]


def shards(panels, svd_basis, kl_basis, slot_of_m, svd_keep, kl_keep):
    owner_slots, modes = kl_basis.shape[0], svd_basis.shape[2]
    owners = lax.axis_size("ma")
    width = min(OWNER_BUDGET, owner_slots * modes)
    wide = -(-width // LANES) * LANES
    mine, far, near, slot_column, rows_column, scalars = project(
        panels, svd_basis, slot_of_m, svd_keep, kl_keep, owner_slots, wide
    )
    first = far_step(owners)
    others = [step for step in range(owners) if step != first]
    got_far = lax.ppermute(far, "pa", pairs("pa"))
    near, got_far = lax.optimization_barrier((near, got_far))
    got_near = lax.ppermute(near, "pa", pairs("pa"))
    summed = dict(zip([first], sum_pair([first], width, mine, got_far)))
    summed |= zip(others, sum_pair(others, width, mine, got_near))
    blocks = {
        step: lax.ppermute(summed[step], "ma", ring(step)) if step else summed[step]
        for step in [first] + others[::-1]
    }
    tables = (width, slot_column, rows_column, kl_basis, [blocks[step] for step in range(owners)])
    send = kl_project(1, jnp.bfloat16, *tables)
    got = lax.ppermute(send, "af", pairs("af"))
    mine = kl_project(0, jnp.float32, *tables)
    rows = kl_basis.shape[1] // lax.axis_size("af")
    return unpack(scalars, mine, got, owner_slots, rows, modes, width)


def kernels_fit(mesh, args):
    panels, svd_basis, kl_basis = args[:3]
    slots = panels.shape[0] // mesh.shape["grp"]
    freqs = svd_basis.shape[0] // (mesh.shape["af"] * mesh.shape["ma"])
    owner_slots = kl_basis.shape[0] // (mesh.shape["pa"] * mesh.shape["ma"])
    share_rows = kl_basis.shape[1] // mesh.shape["af"]
    return (
        freqs % (2 * GROUP) == 0
        and slots % (GROUP * mesh.shape["pa"]) == 0
        and owner_slots == 4
        and svd_basis.shape[2] == 2 * LANES
        and share_rows % (2 * GROUP) == 0
        and mesh.shape["pa"] == 2
        and mesh.shape["af"] == 2
        and mesh.shape["ma"] == 4
    )


def solution(mesh):
    in_specs = (
        P("grp", ("af", "ma"), "pa"),
        P(("af", "ma"), "pa", None),
        P(("pa", "ma"), None, "af"),
        P(),
        P(),
        P(),
    )
    out_specs = P(("grp", "pa", "ma"), "af", None)

    def run(*args):
        body = shards if kernels_fit(mesh, args) else shards_plain
        mapped = jax.shard_map(
            body, mesh=mesh, in_specs=in_specs, out_specs=out_specs, check_vma=False
        )
        return mapped(*args)

    return run
```
